32 devices in a mesh: seq: 2 (over x), exp: 8 (over z, core), dp: 2 (over y).
Axes of the slice: x: 2, y: 2, z: 4, core: 2. Of those that a mesh axis runs over, the one named last changes fastest.
Arguments:
- tokens: bfloat16 [16, 256, 2880], P(('exp', 'dp'), 'seq'), may hold values from -6 to 6
- segments: int32 [16, 256], P(('exp', 'dp')), may hold values from 0 to 1, as said below
- routes: int32 [16, 256, 4], P(('exp', 'dp'), 'seq'), may hold values from 0 to 7, all different within a row; in each aligned block of 128 rows (0 to 127, 128 to 255, ..., all dimensions but the last counted through in order) at most 72 rows name the same one
- gate_share: float32 [16, 256, 4], P(('exp', 'dp'), 'seq'), may hold values from 0.1 to 0.4
- attn_gain: float32 [2880], replicated, may hold values from 0.5 to 1.5
- query_weight: bfloat16 [2880, 4096], P(None, ('seq', 'exp', 'dp')), may hold values from -0.109375 to 0.109375
- query_bias: float32 [4096], replicated, may hold values from -1.8 to 1.8
- key_weight: bfloat16 [2880, 512], P(None, ('seq', 'exp', 'dp')), may hold values from -0.109375 to 0.109375
- key_bias: float32 [512], replicated, may hold values from -1.8 to 1.8
- value_weight: bfloat16 [2880, 512], P(None, ('seq', 'exp', 'dp')), may hold values from -0.109375 to 0.109375
- value_bias: float32 [512], replicated, may hold values from -1.8 to 1.8
- output_weight: bfloat16 [4096, 2880], P(('seq', 'exp', 'dp')), may hold values from -0.375 to 0.375
- output_bias: float32 [2880], replicated, may hold values from -1.8 to 1.8
- sink_logits: float32 [64], replicated, may hold values from -3 to 3
- moe_gain: float32 [2880], replicated, may hold values from 0.5 to 1.5
- gate_weight: bfloat16 [8, 2880, 2880], P('exp', None, ('seq', 'dp')), may hold values from -0.109375 to 0.109375
- gate_bias: float32 [8, 2880], P('exp', ('seq', 'dp')), may hold values from -0.6 to 0.6
- up_weight: bfloat16 [8, 2880, 2880], P('exp', None, ('seq', 'dp')), may hold values from -0.109375 to 0.109375
- up_bias: float32 [8, 2880], P('exp', ('seq', 'dp')), may hold values from -0.6 to 0.6
- down_weight: bfloat16 [8, 2880, 2880], P('exp', ('seq', 'dp')), may hold values from -0.109375 to 0.109375
- down_bias: float32 [8, 2880], P('exp'), may hold values from -0.6 to 0.6
- cotangent: bfloat16 [16, 256, 2880], P(('exp', 'dp'), 'seq'), may hold values from -6 to 6
Outputs:
- output: bfloat16 [16, 256, 2880], P(('exp', 'dp'), 'seq')
- input_grad: float32 [16, 256, 2880], P(('exp', 'dp'), 'seq')
- attn_gain_grad: float32 [2880], replicated
- query_weight_grad: float32 [2880, 4096], P(None, ('seq', 'exp', 'dp'))
- query_bias_grad: float32 [4096], replicated
- key_weight_grad: float32 [2880, 512], P(None, ('seq', 'exp', 'dp'))
- key_bias_grad: float32 [512], replicated
- value_weight_grad: float32 [2880, 512], P(None, ('seq', 'exp', 'dp'))
- value_bias_grad: float32 [512], replicated
- output_weight_grad: float32 [4096, 2880], P(('seq', 'exp', 'dp'))
- output_bias_grad: float32 [2880], replicated
- sink_grad: float32 [64], replicated
- moe_gain_grad: float32 [2880], replicated
- gate_weight_grad: float32 [8, 2880, 2880], P('exp', None, ('seq', 'dp'))
- gate_bias_grad: float32 [8, 2880], P('exp', ('seq', 'dp'))
- up_weight_grad: float32 [8, 2880, 2880], P('exp', None, ('seq', 'dp'))
- up_bias_grad: float32 [8, 2880], P('exp', ('seq', 'dp'))
- down_weight_grad: float32 [8, 2880, 2880], P('exp', ('seq', 'dp'))
- down_bias_grad: float32 [8, 2880], P('exp')
The draws below stay inside these ranges and needn't reach their ends.
Inputs may be any that keep to these rules, and one draw needn't show every extreme that they name: `segments`: along a sequence the numbers never fall; equal numbers mark one document. `routes`: each token names 4 different experts; among the tokens of one device no expert is named by more than 72 of them.
All inputs are finite; a program needn't handle non-finite values.
Results may differ from the reference program's by a relative error of at most 0.02.
Values may be sent and summed in bfloat16 or wider, within the bound.
A program may use at most 512 MiB of HBM per device.

```python
import math
import jax
import jax.numpy as jnp
import numpy as np
from jax import lax

D = 2880
HQ = 64
KV = 8
HD = 64
FF = 2880
TOPK = 4
TOK_DEV = 128
EXPERTS = 8
LEN = 256
SEQS = 16
TOKENS = 4096
CAP = 72


def draw_segments(key, part):
    key = jax.random.fold_in(key, 11)
    side_key, place_key = jax.random.split(key)
    reach = LEN * 7 // 32
    distance = jax.random.randint(place_key, (SEQS,), 1, reach)
    side = jax.random.randint(side_key, (SEQS,), 0, 2)
    boundary = jnp.where(side == 0, distance, LEN - distance)
    position = jnp.arange(LEN, dtype=jnp.int32)
    return (boundary[:, None] <= position[None, :]).astype(jnp.int32)


def levels(key, dims, cuts, smallest, top_value):
    def one(dim, shards_of):
        draws = jax.random.uniform(jax.random.fold_in(jax.random.fold_in(key, 6), dim), (shards_of,), jnp.float32, smallest / len(cuts), top_value / len(cuts))
        return jnp.repeat(jnp.exp(draws), dims[dim] // shards_of).reshape((-1,) + (1,) * (len(dims) - dim - 1))

    loudness = one(*cuts[0])
    for cut in cuts[1:]:
        loudness = loudness * one(*cut)
    return loudness


def routed_block(rng, own, number, rows, count, top, limit, skew):
    order = jax.random.permutation(rng, count)
    heavy_load, common = shares(count, rows * top, limit, skew, True), shares(count, rows * top, limit, skew, False)
    places = jnp.arange(count)

    def named(tallies, offset_by):
        used = int((tallies > 0).sum())
        fixed = max(1, used // 4)
        passed = fixed + (places - fixed + offset_by * (used - fixed)) % max(1, count - fixed)
        return jnp.zeros((count,), jnp.int32).at[order[jnp.where(places < fixed, places, passed)]].set(jnp.asarray(tallies, jnp.int32))

    tallies = jnp.where(number % 4 == 0, named(heavy_load, number // 4), named(common, number - number // 4 - 1))
    mixed = jax.random.permutation(jax.random.fold_in(own, 3), count)
    donor, taker = mixed[0:count // 2 * 2:2], mixed[1:count // 2 * 2:2]
    slack = jnp.minimum(tallies[donor] - 1, limit - tallies[taker]) // 2
    slack = jnp.where((donor == order[0]) | (taker == order[0]) | (tallies[taker] == 0), 0, jnp.maximum(slack, 0))
    passed = jax.random.randint(jax.random.fold_in(own, 4), (count // 2,), 0, 1 << 20) % (slack + 1)
    tallies = tallies.at[donor].add(-passed).at[taker].add(passed)
    members = jnp.searchsorted(jnp.cumsum(tallies), jnp.arange(rows * top), side="right").astype(jnp.int32)
    listing = members.reshape(top, rows).T
    listing = listing[jax.random.permutation(jax.random.fold_in(own, 1), rows)]
    offset_by = jax.random.randint(jax.random.fold_in(own, 2), (rows, 1), 0, top)
    return jnp.take_along_axis(listing, (jnp.arange(top)[None, :] + offset_by) % top, axis=1)


def shares(amount, total, most, skew, full):
    weights = [(1 << 20) // math.isqrt(rank ** skew) + 1 for rank in range(1, amount + 1)]
    largest = most if full else min(most, max(-(-total // amount), total * weights[0] // sum(weights)))
    least = 1 if total - largest >= amount - 1 else 0
    holding, rest = [largest] + [least] * (amount - 1), total - largest - least * (amount - 1)
    while rest > 0:
        movable = [i for i in range(1, amount) if holding[i] < largest] or [i for i in range(1, amount) if holding[i] < most]
        pool, remaining = sum([weights[i] for i in movable]), rest
        for i in movable:
            addition = min(most - holding[i], max(1, remaining * weights[i] // pool), rest)
            holding[i] = holding[i] + addition
            rest = rest - addition
    return np.array(holding)


def centred(own_key, dims, spread, most, cuts=(), kind=jnp.bfloat16):
    values = spread * jax.random.normal(own_key, dims, jnp.float32)
    if cuts:
        values = values * levels(own_key, dims, cuts, -0.22, 0.18)
    return jnp.clip(values, -most, most).astype(kind)


def setup_inputs(seed: int = 0) -> dict:
    seeds = jax.random.split(jax.random.key(seed), 23)
    tokens = centred(seeds[0], (SEQS, LEN, D), 1.0, 6.0, ((0, 16), (1, 2)))
    segments = draw_segments(jax.random.fold_in(seeds[22], 71), 0)
    routes_keys = jax.random.split(jax.random.fold_in(seeds[2], 1), SEQS * LEN // TOK_DEV)
    routes_turns = jax.random.permutation(jax.random.fold_in(seeds[2], 3), SEQS * LEN // TOK_DEV)
    routes = jax.vmap(lambda own, number: routed_block(jax.random.fold_in(seeds[2], 2), own, number, TOK_DEV, EXPERTS, TOPK, CAP, 1))(routes_keys, routes_turns).reshape((SEQS, LEN, TOPK))
    gate_share = jnp.clip(0.1 + 0.3 * jax.random.uniform(seeds[3], (SEQS, LEN, TOPK), jnp.float32) ** levels(seeds[3], (SEQS, LEN, TOPK), ((0, 16), (1, 2)), -0.2, 0.2), 0.1, 0.4)
    attn_gain = jnp.clip(1.0 + 0.1 * jax.random.normal(seeds[4], (D,), jnp.float32), 0.5, 1.5)
    query_weight = centred(seeds[5], (D, HQ * HD), D ** -0.5, 0.109375, ((1, 32),))
    query_bias = centred(seeds[6], (HQ * HD,), 0.3, 1.8, (), jnp.float32)
    key_weight = centred(seeds[7], (D, KV * HD), D ** -0.5, 0.109375, ((1, 32),))
    key_bias = centred(seeds[8], (KV * HD,), 0.3, 1.8, (), jnp.float32)
    value_weight = centred(seeds[9], (D, KV * HD), D ** -0.5, 0.109375, ((1, 32),))
    value_bias = centred(seeds[10], (KV * HD,), 0.3, 1.8, (), jnp.float32)
    output_weight = centred(seeds[11], (HQ * HD, D), (HQ * HD // 16) ** -0.5, 0.375, ((0, 32),))
    output_bias = centred(seeds[12], (D,), 0.3, 1.8, (), jnp.float32)
    sink_logits = centred(seeds[13], (HQ,), 1.0, 3.0, (), jnp.float32)
    moe_gain = jnp.clip(1.0 + 0.1 * jax.random.normal(seeds[14], (D,), jnp.float32), 0.5, 1.5)
    gate_weight = centred(seeds[15], (EXPERTS, D, FF), D ** -0.5, 0.109375, ((0, 8), (2, 4)))
    gate_bias = centred(seeds[16], (EXPERTS, FF), 0.1, 0.6, ((0, 8), (1, 4)), jnp.float32)
    up_weight = centred(seeds[17], (EXPERTS, D, FF), D ** -0.5, 0.109375, ((0, 8), (2, 4)))
    up_bias = centred(seeds[18], (EXPERTS, FF), 0.1, 0.6, ((0, 8), (1, 4)), jnp.float32)
    down_weight = centred(seeds[19], (EXPERTS, FF, D), FF ** -0.5, 0.109375, ((0, 8), (1, 4)))
    down_bias = centred(seeds[20], (EXPERTS, D), 0.1, 0.6, ((0, 8),), jnp.float32)
    cotangent = centred(seeds[21], (SEQS, LEN, D), 1.0, 6.0, ((0, 16), (1, 2)))
    return dict(tokens=tokens, segments=segments, routes=routes, gate_share=gate_share, attn_gain=attn_gain, query_weight=query_weight, query_bias=query_bias, key_weight=key_weight, key_bias=key_bias, value_weight=value_weight, value_bias=value_bias, output_weight=output_weight, output_bias=output_bias, sink_logits=sink_logits, moe_gain=moe_gain, gate_weight=gate_weight, gate_bias=gate_bias, up_weight=up_weight, up_bias=up_bias, down_weight=down_weight, down_bias=down_bias, cotangent=cotangent)


@jax.custom_vjp
def low(v):
    return lax.optimization_barrier(v.astype(jnp.bfloat16)).astype(jnp.float32)

@jax.custom_vjp
def low_back(v):
    return v

def low_keep(v):
    return (low(v), None)

def low_pass(kept, grad):
    return (grad,)

def back_keep(v):
    return (v, None)

def back_low(kept, grad):
    return (low(grad),)
low.defvjp(low_keep, low_pass)
low_back.defvjp(back_keep, back_low)
highest = lax.Precision.HIGHEST
norm_eps = 1e-05
rope_base = 150000.0
clip_level = 7.0
glu_alpha = 1.702
masked_score = -1000000000.0

def rms_apply(values, gain):
    return values * lax.rsqrt(lax.optimization_barrier(jnp.mean(values * values, axis=-1, keepdims=True)) + norm_eps) * gain

def rope_tables(position, width):
    exponent = jnp.arange(width // 2).astype(jnp.float32) * (2.0 / width)
    freqs = jnp.exp(-math.log(rope_base) * exponent)
    angles = position.astype(jnp.float32)[:, None] * freqs[None, :]
    return (jnp.cos(angles), jnp.sin(angles))

def rotate(values, cosine, sine):
    half = values.shape[-1] // 2
    first = values[..., :half]
    second = values[..., half:]
    return jnp.concatenate([first * cosine - second * sine, second * cosine + first * sine], axis=-1)

def swiglu(gate_pre, up_pre):
    gate_soft = clip_level * jnp.tanh(gate_pre / clip_level)
    up_soft = clip_level * jnp.tanh(up_pre / clip_level)
    return gate_soft * jax.nn.sigmoid(glu_alpha * gate_soft) * (up_soft + 1.0)

def attend_sequence(normed, segment, query_weight, query_bias, key_weight, key_bias, value_weight, value_bias, sink_logits):
    length = normed.shape[0]
    group = HQ // KV
    scale = 1.0 / math.sqrt(HD)
    query_lin = low_back(jnp.dot(normed, query_weight, precision=highest) + query_bias).reshape(length, HQ, HD)
    key_lin = low_back(jnp.dot(normed, key_weight, precision=highest) + key_bias).reshape(length, KV, HD)
    values = low(low_back(jnp.dot(normed, value_weight, precision=highest) + value_bias)).reshape(length, KV, HD)
    position = jnp.arange(length, dtype=jnp.int32)
    cosine, sine = rope_tables(position, HD)
    query_rot = low(rotate(query_lin, cosine[:, None], sine[:, None])).reshape(length, KV, group, HD)
    key_rot = low(rotate(key_lin, cosine[:, None], sine[:, None]))
    scores = low_back(jnp.einsum('qkgd,skd->kgqs', query_rot, key_rot, precision=highest) * scale)
    visible = (position[:, None] >= position[None, :]) & (segment[:, None] == segment[None, :])
    scores = jnp.where(visible[None, None], scores, masked_score)
    sink_grid = sink_logits.reshape(KV, group)[:, :, None]
    peak = jnp.maximum(lax.optimization_barrier(jnp.max(scores, axis=-1)), sink_grid)
    total = lax.optimization_barrier(jnp.sum(jnp.exp(scores - peak[..., None]), axis=-1)) + jnp.exp(sink_grid - peak)
    log_total = peak + jnp.log(total)
    probs = low(jnp.exp(scores - log_total[..., None]))
    mixed = jnp.einsum('kgqs,skd->qkgd', probs, values, precision=highest).reshape(length, HQ * HD)
    return low(low_back(mixed))

def route_table(routes, gate_share):
    blocks = TOKENS // TOK_DEV
    chosen = routes.reshape(blocks, TOK_DEV * TOPK).astype(jnp.int32)
    expert_hot = (chosen[:, :, None] == jnp.arange(EXPERTS, dtype=jnp.int32)[None, None, :]).astype(jnp.int32)
    slot_index = lax.optimization_barrier(jnp.sum((jnp.cumsum(expert_hot, axis=1) - expert_hot) * expert_hot, axis=2)).astype(jnp.int32)
    block_index = jnp.broadcast_to(jnp.arange(blocks, dtype=jnp.int32)[:, None], chosen.shape)
    token_index = (block_index * TOK_DEV + jnp.arange(TOK_DEV * TOPK, dtype=jnp.int32)[None, :] // TOPK).astype(jnp.int32)
    table = jnp.full((EXPERTS, blocks, CAP), TOKENS, jnp.int32).at[chosen, block_index, slot_index].set(token_index)
    weights = gate_share.reshape(blocks, TOK_DEV * TOPK)
    slot_gates = jnp.zeros((EXPERTS, blocks, CAP), weights.dtype).at[chosen, block_index, slot_index].set(weights)
    return (table.reshape(EXPERTS, blocks * CAP), slot_gates.reshape(EXPERTS, blocks * CAP))

def reference(tokens, segments, routes, gate_share, attn_gain, query_weight, query_bias, key_weight, key_bias, value_weight, value_bias, output_weight, output_bias, sink_logits, moe_gain, gate_weight, gate_bias, up_weight, up_bias, down_weight, down_bias, cotangent):
    table, slot_gates = route_table(routes, gate_share)

    def forward(block_in, norm_one, w_query, b_query, w_key, b_key, w_value, b_value, w_output, b_output, sink_row, norm_two, w_gate, b_gate, w_up, b_up, w_down, b_down):
        normed = low(rms_apply(block_in, norm_one))

        def one_sequence(inputs):
            return attend_sequence(inputs[0], inputs[1], w_query, b_query, w_key, b_key, w_value, b_value, sink_row)
        mixed = lax.map(jax.checkpoint(one_sequence), (normed, segments))
        attn_out = low_back(jnp.dot(mixed.reshape(TOKENS, HQ * HD), w_output, precision=highest) + b_output)
        hidden = block_in.reshape(TOKENS, D) + attn_out
        normed_moe = low(rms_apply(hidden, norm_two))
        padded = jnp.concatenate([normed_moe, jnp.zeros((1, D), normed_moe.dtype)], axis=0)

        def one_expert(inputs):
            index_rows, gate_mat, gate_vec, up_mat, up_vec, down_mat, down_vec = inputs
            picked = padded[index_rows]
            gate_pre = low_back(jnp.dot(picked, gate_mat, precision=highest) + gate_vec)
            up_pre = low_back(jnp.dot(picked, up_mat, precision=highest) + up_vec)
            activation = low(swiglu(gate_pre, up_pre))
            return low_back(low(jnp.dot(activation, down_mat, precision=highest) + down_vec))
        expert_out = lax.map(jax.checkpoint(one_expert), (table, w_gate, b_gate, w_up, b_up, w_down, b_down))
        weighted = (expert_out * slot_gates[:, :, None]).reshape(-1, D)
        moe_out = jnp.zeros((TOKENS + 1, D), weighted.dtype).at[table.reshape(-1)].add(weighted)[:TOKENS]
        return hidden + moe_out
    params = (tokens.astype(jnp.float32), attn_gain, query_weight.astype(jnp.float32), query_bias, key_weight.astype(jnp.float32), key_bias, value_weight.astype(jnp.float32), value_bias, output_weight.astype(jnp.float32), output_bias, sink_logits, moe_gain, gate_weight.astype(jnp.float32), gate_bias, up_weight.astype(jnp.float32), up_bias, down_weight.astype(jnp.float32), down_bias)
    result, pull = jax.vjp(forward, *params)
    grads = pull(cotangent.astype(jnp.float32).reshape(TOKENS, D))
    return (result.reshape(SEQS, LEN, D).astype(jnp.bfloat16), grads[0], grads[1], grads[2], grads[3], grads[4], grads[5], grads[6], grads[7], grads[8], grads[9], grads[10], grads[11], grads[12], grads[13], grads[14], grads[15], grads[16], grads[17])
```

```python
import math

import jax
import jax.numpy as jnp
from jax import lax
from jax.experimental import pallas as pl
from jax.experimental.pallas import tpu as pltpu
from jax.sharding import PartitionSpec as P

HD = 64


highest = lax.Precision.HIGHEST
norm_eps = 1e-05
rope_base = 150000.0
clip_level = 7.0
glu_alpha = 1.702
masked_score = -1000000000.0


def rms_apply(values, gain):
    return values * lax.rsqrt(jnp.mean(values * values, axis=-1, keepdims=True) + norm_eps) * gain


def rope_tables(position, width):
    exponent = jnp.arange(width // 2).astype(jnp.float32) * (2.0 / width)
    freqs = jnp.exp(-math.log(rope_base) * exponent)
    angles = position.astype(jnp.float32)[:, None] * freqs[None, :]
    return (jnp.cos(angles), jnp.sin(angles))


def rotate(values, cosine, sine):
    half = values.shape[-1] // 2
    first = values[..., :half]
    second = values[..., half:]
    return jnp.concatenate(
        [first * cosine - second * sine, second * cosine + first * sine], axis=-1
    )


def swiglu(gate_pre, up_pre):
    gate_soft = clip_level * jnp.tanh(gate_pre / clip_level)
    up_soft = clip_level * jnp.tanh(up_pre / clip_level)
    return gate_soft * jax.nn.sigmoid(glu_alpha * gate_soft) * (up_soft + 1.0)


def inner_rows(left, right):
    return lax.dot_general(
        left, right, (((0,), (0,)), ((), ())), preferred_element_type=jnp.float32
    )


def times_transposed(left, right):
    return lax.dot_general(
        left, right, (((1,), (1,)), ((), ())), preferred_element_type=jnp.float32
    )


def to_experts(outgoing):
    width = outgoing.shape[2]
    arrived = lax.all_to_all(outgoing, "exp", split_axis=0, concat_axis=0, tiled=True)
    arrived = lax.all_gather(arrived, ("seq", "dp"), axis=0, tiled=True)
    return arrived.reshape(-1, width)


def results_back(activation, down_matrix, down_vector, experts, capacity):
    width = down_matrix.shape[1]
    share = lax.psum_scatter(
        jnp.dot(activation, down_matrix, preferred_element_type=jnp.float32).astype(jnp.bfloat16),
        ("seq", "dp"),
        scatter_dimension=0,
        tiled=True,
    ).astype(jnp.float32)
    finished = (share + down_vector).astype(jnp.bfloat16).reshape(experts, capacity, width)
    return lax.all_to_all(finished, "exp", split_axis=0, concat_axis=0, tiled=True)


def gradients_back(gate_grad, up_grad, gate_matrix, up_matrix, experts, capacity):
    share = lax.psum_scatter(
        times_transposed(gate_grad, gate_matrix) + times_transposed(up_grad, up_matrix),
        ("seq", "dp"),
        scatter_dimension=0,
        tiled=True,
    )
    return lax.all_to_all(
        share.reshape(experts, capacity, share.shape[1]),
        "exp",
        split_axis=0,
        concat_axis=0,
        tiled=True,
    )


def local(
    tokens,
    segments,
    routes,
    gate_share,
    attn_gain,
    query_weight,
    query_bias,
    key_weight,
    key_bias,
    value_weight,
    value_bias,
    output_weight,
    output_bias,
    sink_logits,
    moe_gain,
    gate_weight,
    gate_bias,
    up_weight,
    up_bias,
    down_weight,
    down_bias,
    cotangent,
):
    count_rows = tokens.shape[1]
    width = tokens.shape[2]
    head_count = sink_logits.shape[0]
    kv_count = key_bias.shape[0] // HD
    group = head_count // kv_count
    scale = 1.0 / math.sqrt(HD)
    experts = lax.axis_size("exp")
    topk = routes.shape[2]
    capacity = count_rows * topk * 9 // (8 * experts)
    resid = tokens[0].astype(jnp.float32)
    full_query, full_key, full_value, full_output = (
        lax.all_gather(query_weight, ("seq", "exp", "dp"), axis=1, tiled=True),
        lax.all_gather(key_weight, ("seq", "exp", "dp"), axis=1, tiled=True),
        lax.all_gather(value_weight, ("seq", "exp", "dp"), axis=1, tiled=True),
        lax.all_gather(output_weight, ("seq", "exp", "dp"), axis=0, tiled=True),
    )
    attn_norm, attn_norm_pull = jax.vjp(rms_apply, resid, attn_gain)
    normed = attn_norm.astype(jnp.bfloat16)
    query_lin = jnp.dot(normed, full_query, preferred_element_type=jnp.float32) + query_bias
    key_lin = jnp.dot(normed, full_key, preferred_element_type=jnp.float32) + key_bias
    value_low = (
        jnp.dot(normed, full_value, preferred_element_type=jnp.float32) + value_bias
    ).astype(jnp.bfloat16)
    offset = lax.axis_index("seq") * count_rows
    position = offset + jnp.arange(count_rows, dtype=jnp.int32)
    cosine, sine = rope_tables(position, HD)
    cosine = cosine[:, None]
    sine = sine[:, None]
    query_rot = rotate(query_lin.reshape(count_rows, head_count, HD), cosine, sine).astype(
        jnp.bfloat16
    )
    key_rot = rotate(key_lin.reshape(count_rows, kv_count, HD), cosine, sine).astype(jnp.bfloat16)
    all_keys, all_values = (
        lax.all_gather(key_rot.reshape(count_rows, kv_count * HD), "seq", axis=0, tiled=True),
        lax.all_gather(value_low, "seq", axis=0, tiled=True),
    )
    seq_len = all_keys.shape[0]
    all_keys = all_keys.reshape(seq_len, kv_count, HD)
    all_values = all_values.reshape(seq_len, kv_count, HD)
    doc_ids = segments[0]
    own_ids = lax.dynamic_slice_in_dim(doc_ids, offset, count_rows, 0)
    key_place = jnp.arange(seq_len, dtype=jnp.int32)
    visible = (position[:, None] >= key_place[None, :]) & (own_ids[:, None] == doc_ids[None, :])
    query_group = query_rot.reshape(count_rows, kv_count, group, HD)
    sink_grid = sink_logits.reshape(kv_count, group)[:, :, None]

    def score_block():
        raw = (
            jnp.einsum("qkgd,skd->kgqs", query_group, all_keys, preferred_element_type=jnp.float32)
            * scale
        )
        return jnp.where(visible[None, None], raw, masked_score)

    scores = score_block()
    peak = jnp.maximum(jnp.max(scores, axis=-1), sink_grid)
    total = jnp.sum(jnp.exp(scores - peak[..., None]), axis=-1) + jnp.exp(sink_grid - peak)
    log_total = peak + jnp.log(total)
    probs = jnp.exp(scores - log_total[..., None])
    mixed = jnp.einsum(
        "kgqs,skd->qkgd", probs.astype(jnp.bfloat16), all_values, preferred_element_type=jnp.float32
    )
    mixed = mixed.reshape(count_rows, head_count * HD).astype(jnp.bfloat16)
    attn_out = jnp.dot(mixed, full_output, preferred_element_type=jnp.float32) + output_bias
    hidden = resid + attn_out
    moe_norm, moe_norm_pull = jax.vjp(rms_apply, hidden, moe_gain)
    normed_moe = moe_norm.astype(jnp.bfloat16)
    chosen = routes[0].reshape(-1)
    expert_hot = (chosen[:, None] == jnp.arange(experts, dtype=jnp.int32)[None, :]).astype(
        jnp.int32
    )
    slot_index = jnp.sum((jnp.cumsum(expert_hot, axis=0) - expert_hot) * expert_hot, axis=1)
    target = chosen * capacity + slot_index
    slot_hot = (
        target[:, None] == jnp.arange(experts * capacity, dtype=jnp.int32)[None, :]
    ).reshape(count_rows, topk, experts * capacity)
    dispatch = jnp.sum(slot_hot.astype(jnp.bfloat16), axis=1)
    weighted = jnp.sum(slot_hot.astype(jnp.float32) * gate_share[0][:, :, None], axis=1)
    outgoing = jnp.einsum("ts,td->sd", dispatch, normed_moe, preferred_element_type=jnp.float32)
    outgoing = outgoing.astype(jnp.bfloat16).reshape(experts, capacity, width)
    expert_rows = to_experts(outgoing)
    gate_pre = (
        jnp.dot(expert_rows, gate_weight[0], preferred_element_type=jnp.float32) + gate_bias[0]
    )
    up_pre = jnp.dot(expert_rows, up_weight[0], preferred_element_type=jnp.float32) + up_bias[0]
    act_full, swiglu_pull = jax.vjp(swiglu, gate_pre, up_pre)
    activation = act_full.astype(jnp.bfloat16)
    returned = results_back(activation, down_weight[0], down_bias[0], experts, capacity)
    moe_out = jnp.dot(
        weighted, returned.reshape(experts * capacity, width).astype(jnp.float32), precision=highest
    )
    output = (hidden + moe_out).astype(jnp.bfloat16)
    upstream = cotangent[0].astype(jnp.float32)
    grad_slots = jnp.einsum("ts,td->sd", weighted, upstream, precision=highest)
    grad_slots = grad_slots.astype(jnp.bfloat16).reshape(experts, capacity, width)
    grad_rows = to_experts(grad_slots)
    down_bias_grad = jnp.sum(grad_rows.astype(jnp.float32), axis=0)
    down_weight_grad = inner_rows(activation, grad_rows)
    act_grad = times_transposed(grad_rows, down_weight[0])
    gate_grad_full, up_grad_full = swiglu_pull(act_grad)
    gate_grad = gate_grad_full.astype(jnp.bfloat16)
    up_grad = up_grad_full.astype(jnp.bfloat16)
    gate_bias_grad = jnp.sum(gate_grad.astype(jnp.float32), axis=0)
    up_bias_grad = jnp.sum(up_grad.astype(jnp.float32), axis=0)
    gate_weight_grad = inner_rows(expert_rows, gate_grad)
    up_weight_grad = inner_rows(expert_rows, up_grad)
    rows_grad = gradients_back(gate_grad, up_grad, gate_weight[0], up_weight[0], experts, capacity)
    normed_moe_grad = jnp.einsum(
        "ts,sd->td",
        dispatch.astype(jnp.float32),
        rows_grad.reshape(experts * capacity, width),
        precision=highest,
    )
    hidden_norm_grad, moe_gain_grad = moe_norm_pull(normed_moe_grad)
    hidden_grad = upstream + hidden_norm_grad
    attn_out_grad = hidden_grad.astype(jnp.bfloat16)
    output_bias_grad = jnp.sum(attn_out_grad.astype(jnp.float32), axis=0)
    full_query, full_key, full_value, full_output = (
        lax.all_gather(query_weight, ("seq", "exp", "dp"), axis=1, tiled=True),
        lax.all_gather(key_weight, ("seq", "exp", "dp"), axis=1, tiled=True),
        lax.all_gather(value_weight, ("seq", "exp", "dp"), axis=1, tiled=True),
        lax.all_gather(output_weight, ("seq", "exp", "dp"), axis=0, tiled=True),
    )
    mixed_grad = (
        times_transposed(attn_out_grad, full_output)
        .astype(jnp.bfloat16)
        .reshape(count_rows, kv_count, group, HD)
    )
    scores = score_block()
    probs = jnp.exp(scores - log_total[..., None])
    prob_grad = jnp.einsum(
        "qkgd,skd->kgqs", mixed_grad, all_values, preferred_element_type=jnp.float32
    )
    delta = jnp.sum(probs * prob_grad, axis=-1)
    score_grad = (probs * (prob_grad - delta[..., None])).astype(jnp.bfloat16)
    sink_grad = -jnp.sum(jnp.exp(sink_grid - log_total) * delta, axis=-1).reshape(head_count)
    value_grad = jnp.einsum(
        "kgqs,qkgd->skd", probs.astype(jnp.bfloat16), mixed_grad, preferred_element_type=jnp.float32
    )
    key_grad = (
        jnp.einsum("kgqs,qkgd->skd", score_grad, query_group, preferred_element_type=jnp.float32)
        * scale
    )
    query_grad = (
        jnp.einsum("kgqs,skd->qkgd", score_grad, all_keys, preferred_element_type=jnp.float32)
        * scale
    )
    key_share, value_share = (
        lax.psum_scatter(
            key_grad.reshape(seq_len, kv_count * HD), "seq", scatter_dimension=0, tiled=True
        ),
        lax.psum_scatter(
            value_grad.reshape(seq_len, kv_count * HD), "seq", scatter_dimension=0, tiled=True
        ),
    )
    query_lin_grad = (
        rotate(query_grad.reshape(count_rows, head_count, HD), cosine, -sine)
        .reshape(count_rows, head_count * HD)
        .astype(jnp.bfloat16)
    )
    key_lin_grad = (
        rotate(key_share.reshape(count_rows, kv_count, HD), cosine, -sine)
        .reshape(count_rows, kv_count * HD)
        .astype(jnp.bfloat16)
    )
    value_lin_grad = value_share.astype(jnp.bfloat16)
    query_bias_grad = jnp.sum(query_lin_grad.astype(jnp.float32), axis=0)
    key_bias_grad = jnp.sum(key_lin_grad.astype(jnp.float32), axis=0)
    value_bias_grad = jnp.sum(value_lin_grad.astype(jnp.float32), axis=0)
    normed_grad = (
        times_transposed(query_lin_grad, full_query)
        + times_transposed(key_lin_grad, full_key)
        + times_transposed(value_lin_grad, full_value)
    )
    resid_norm_grad, attn_gain_grad = attn_norm_pull(normed_grad)
    input_grad = hidden_grad + resid_norm_grad
    query_weight_grad = inner_rows(normed, query_lin_grad)
    key_weight_grad = inner_rows(normed, key_lin_grad)
    value_weight_grad = inner_rows(normed, value_lin_grad)
    output_weight_grad = inner_rows(mixed, attn_out_grad)
    query_owned, key_owned, value_owned, output_owned = (
        lax.psum_scatter(query_weight_grad, ("seq", "exp", "dp"), scatter_dimension=1, tiled=True),
        lax.psum_scatter(key_weight_grad, ("seq", "exp", "dp"), scatter_dimension=1, tiled=True),
        lax.psum_scatter(value_weight_grad, ("seq", "exp", "dp"), scatter_dimension=1, tiled=True),
        lax.psum_scatter(output_weight_grad, ("seq", "exp", "dp"), scatter_dimension=0, tiled=True),
    )
    summed = lax.psum(
        (
            attn_gain_grad,
            query_bias_grad,
            key_bias_grad,
            value_bias_grad,
            output_bias_grad,
            sink_grad,
            moe_gain_grad,
        ),
        ("seq", "exp", "dp"),
    )
    return (
        output[None],
        input_grad[None],
        summed[0],
        query_owned,
        summed[1],
        key_owned,
        summed[2],
        value_owned,
        summed[3],
        output_owned,
        summed[4],
        summed[5],
        summed[6],
        gate_weight_grad[None],
        gate_bias_grad[None],
        up_weight_grad[None],
        up_bias_grad[None],
        down_weight_grad[None],
        down_bias_grad[None],
    )

MESH = pl.DeviceIdType.MESH
HERE = (0, 0, 0)
SIBLING = (0, 1, 0)
ACROSS = (1, 0, 0)
ALONG = (0, 0, 1)
NEAR = (0, 2, 0)
FAR = (0, 4, 0)
ENDS = (0, 6, 0)


def flip(place, mask):
    x, e, y = place
    if mask[0]:
        x = 1 - x
    if mask[2]:
        y = 1 - y
    step = 0
    for bit in (1, 2, 4):
        if mask[1] & bit:
            step = step + bit - 2 * bit * lax.rem(lax.div(e, bit), 2)
    return x, e + step, y


def both(left, right):
    return tuple(a ^ b for a, b in zip(left, right))


def place_here():
    return lax.axis_index("seq"), lax.axis_index("exp"), lax.axis_index("dp")


def block_of_all(place):
    x, e, y = place
    return (x * 8 + e) * 2 + y


def block_of_tokens(place):
    x, e, y = place
    return lax.rem(lax.div(e, 2), 2) * 2 + x


def block_of_heads(place):
    x, e, y = place
    return (lax.div(e, 4) * 2 + lax.rem(e, 2)) * 2 + y


GROUPS = {
    "all": (block_of_all, 32, SIBLING, ACROSS, ALONG, (NEAR, FAR, ENDS), 0.5),
    "tokens": (block_of_tokens, 4, None, ACROSS, NEAR, (), 0.5),
    "heads": (block_of_heads, 8, SIBLING, FAR, ALONG, (), 1.0),
}


def partners(group):
    _, _, sibling, first, second, line, _ = GROUPS[group]
    return ([sibling] if sibling else []) + [first, second] + list(line)


def copies(group):
    _, _, sibling, _, _, line, _ = GROUPS[group]
    rounds = 1 + len(line)
    return rounds * (8 if sibling else 4) + len(line)


class Sender:
    def __init__(self, place, send, recv):
        self.place, self.send, self.recv, self.started = place, send, recv, []

    def push(self, source, target, mask):
        number = len(self.started)
        copy = pltpu.make_async_remote_copy(
            src_ref=source,
            dst_ref=target,
            send_sem=self.send.at[number],
            recv_sem=self.recv.at[number],
            device_id=flip(self.place, mask),
            device_id_type=MESH,
        )
        copy.start()
        self.started.append(copy)
        return copy

    def finish(self):
        for copy in self.started:
            copy.wait_send()


def gather_steps(group, place, source, result, send, recv, local):
    index, _, sibling, first, second, line, share = GROUPS[group]
    rows = source.shape[0]
    cut = int(rows * share) // 16 * 16
    corner = both(first, second)
    out = Sender(place, send, recv)

    def at(mask):
        return result.at[index(flip(place, mask))]

    own = pltpu.make_async_copy(source, at(HERE), local.at[0])
    own.start()
    tails = []

    def pass_on(mask, block):
        if sibling:
            tails.append(out.push(block, at(mask), sibling))

    def plane(mask, block):
        ways = (out.push(block, at(mask), first), out.push(block, at(mask), second))
        pass_on(mask, block)
        return ways

    def turn(mask, ways):
        halves = []
        ways[0].wait_recv()
        seen = both(mask, first)
        if cut:
            halves.append(out.push(at(seen).at[:cut], at(seen).at[:cut], second))
        pass_on(seen, at(seen))
        ways[1].wait_recv()
        seen = both(mask, second)
        if cut < rows:
            halves.append(out.push(at(seen).at[cut:], at(seen).at[cut:], first))
        pass_on(seen, at(seen))
        return halves

    def close(mask, halves):
        for half in halves:
            half.wait_recv()
        pass_on(both(mask, corner), at(both(mask, corner)))

    reach = [out.push(source, at(HERE), mask) for mask in line]
    masks = [HERE] + list(line)
    ways, halves = {}, {}
    for step in range(len(masks) + 2):
        if step < len(masks):
            if step:
                reach[step - 1].wait_recv()
            ways[step] = plane(masks[step], at(masks[step]) if step else source)
            yield
        if 0 <= step - 1 < len(masks):
            halves[step - 1] = turn(masks[step - 1], ways[step - 1])
            yield
        if 0 <= step - 2 < len(masks):
            close(masks[step - 2], halves[step - 2])
            yield
    for copy in tails:
        copy.wait_recv()
    own.wait()
    out.finish()


def total(parts, low, high, store):
    def body(step, carry):
        rows = pl.ds(pl.multiple_of(low + step * 16, 16), 16)
        value = parts[0][rows].astype(jnp.float32)
        for part in parts[1:]:
            value = value + part[rows].astype(jnp.float32)
        store[rows] = value.astype(store.dtype)
        return carry

    if high > low:
        lax.fori_loop(0, (high - low) // 16, body, 0)


def scatter_steps(group, place, source, result, own, mate, side, arrive, ends, send, recv, local):
    index, _, sibling, first, second, line, share = GROUPS[group]
    rows = result.shape[0]
    cut = int(rows * (1.0 - share)) // 16 * 16
    corner = both(first, second)
    out = Sender(place, send, recv)
    masks = list(line)[::-1] + [HERE]
    corners = (corner, first, second, HERE)
    fetched, sent = {}, {}
    for step, mask in enumerate(masks):
        for spot, shift in enumerate(corners):
            seat = step * 4 + spot
            goal = both(mask, shift)
            if sibling:
                sent[seat] = out.push(
                    source.at[index(flip(place, both(goal, sibling)))], mate.at[seat], sibling
                )
            fetched[seat] = pltpu.make_async_copy(
                source.at[index(flip(place, goal))], own.at[seat], local.at[seat]
            )
            fetched[seat].start()
    yield

    def ready(seat):
        fetched[seat].wait()
        if sibling:
            sent[seat].wait_recv()
            return [own.at[seat], mate.at[seat]]
        return [own.at[seat]]

    def outward(step):
        seat = step * 4
        parts = ready(seat)
        if sibling:
            total(parts, 0, rows, own.at[seat])
        halves = []
        if cut:
            halves.append(out.push(own.at[seat].at[:cut], side.at[step].at[:cut], first))
        if cut < rows:
            halves.append(out.push(own.at[seat].at[cut:], side.at[step].at[cut:], second))
        return halves

    def inward(step, halves):
        by_first, by_second = ready(step * 4 + 1), ready(step * 4 + 2)
        for half in halves:
            half.wait_recv()
        total(by_second + [side.at[step]], 0, cut, own.at[step * 4 + 2])
        total(by_first + [side.at[step]], cut, rows, own.at[step * 4 + 1])
        if sibling:
            total(by_second, cut, rows, own.at[step * 4 + 2])
            total(by_first, 0, cut, own.at[step * 4 + 1])
        return (
            out.push(own.at[step * 4 + 1], arrive.at[step * 2], first),
            out.push(own.at[step * 4 + 2], arrive.at[step * 2 + 1], second),
        )

    def close(step, ways):
        parts = ready(step * 4 + 3)
        for way in ways:
            way.wait_recv()
        parts = parts + [arrive.at[step * 2], arrive.at[step * 2 + 1]]
        if masks[step] != HERE:
            total(parts, 0, rows, own.at[step * 4 + 3])
            return out.push(own.at[step * 4 + 3], ends.at[step], masks[step])
        for number, copy in enumerate(reach):
            copy.wait_recv()
            parts.append(ends.at[number])
        total(parts, 0, rows, result)

    halves, ways, reach = {}, {}, []
    for step in range(len(masks) + 2):
        if step < len(masks):
            halves[step] = outward(step)
            yield
        if 0 <= step - 1 < len(masks):
            ways[step - 1] = inward(step - 1, halves[step - 1])
            yield
        if 0 <= step - 2 < len(masks):
            copy = close(step - 2, ways[step - 2])
            if copy is not None:
                reach.append(copy)
            yield
    out.finish()


def exchange(jobs, collective, name):
    in_specs, out_specs, out_shape, scratch, plans = [], [], [], [], []
    for kind, group, array in jobs:
        _, blocks, sibling, _, _, line, _ = GROUPS[group]
        rounds = 1 + len(line)
        in_specs.append(pl.BlockSpec(memory_space=pl.ANY))
        sems = [pltpu.SemaphoreType.DMA((copies(group),)), pltpu.SemaphoreType.DMA((copies(group),))]
        if kind == "gather":
            shape = array.shape
            out_shape.append(jax.ShapeDtypeStruct((blocks,) + shape, array.dtype))
            out_specs.append(pl.BlockSpec(memory_space=pl.ANY))
            need = sems + [pltpu.SemaphoreType.DMA((1,))]
        else:
            shape = array.shape[1:]
            out_shape.append(jax.ShapeDtypeStruct(shape, jnp.float32))
            out_specs.append(pl.BlockSpec(memory_space=pltpu.VMEM))
            slots = [4 * rounds, 4 * rounds if sibling else 1, rounds, 2 * rounds, max(1, rounds - 1)]
            if not sibling:
                slots[1] = 1
            need = [
                pltpu.VMEM((count,) + (shape if count > 1 or number != 1 else (16, 128)), array.dtype)
                for number, count in enumerate(slots)
            ]
            need = need + sems + [pltpu.SemaphoreType.DMA((4 * rounds,))]
        plans.append((kind, group, len(need)))
        scratch += need
    greet = []
    for _, group, _ in jobs:
        greet += [mask for mask in partners(group) if mask not in greet]

    def body(*refs):
        count = len(jobs)
        sources, results, rest = refs[:count], refs[count : 2 * count], list(refs[2 * count :])
        place = place_here()
        barrier = pltpu.get_barrier_semaphore()
        for mask in greet:
            pl.semaphore_signal(barrier, inc=1, device_id=flip(place, mask), device_id_type=MESH)
        pl.semaphore_wait(barrier, len(greet))
        running = []
        for number, (kind, group, width) in enumerate(plans):
            own, rest = rest[:width], rest[width:]
            steps = gather_steps if kind == "gather" else scatter_steps
            running.append(steps(group, place, sources[number], results[number], *own))
        while running:
            for steps in list(running):
                if next(steps, "end") == "end":
                    running.remove(steps)

    return pl.pallas_call(
        body,
        out_shape=out_shape,
        in_specs=in_specs,
        out_specs=out_specs,
        scratch_shapes=scratch,
        compiler_params=pltpu.CompilerParams(
            collective_id=collective, has_side_effects=True, vmem_limit_bytes=60 * 1024 * 1024
        ),
        name=name,
    )(*[array for _, _, array in jobs])


def gather_all(array):
    return lax.all_gather(array, ("seq", "exp", "dp"), axis=0, tiled=False)


def pair_steps(mesh_exp, bit):
    return [(e, e ^ bit) for e in range(mesh_exp)]


def close_by(
    tokens,
    segments,
    routes,
    gate_share,
    attn_gain,
    query_weight,
    query_bias,
    key_weight,
    key_bias,
    value_weight,
    value_bias,
    output_weight,
    output_bias,
    sink_logits,
    moe_gain,
    gate_weight,
    gate_bias,
    up_weight,
    up_bias,
    down_weight,
    down_bias,
    cotangent,
):
    count_rows = tokens.shape[1]
    width = tokens.shape[2]
    head_count = sink_logits.shape[0]
    kv_count = key_bias.shape[0] // HD
    group = head_count // kv_count
    scale = 1.0 / math.sqrt(HD)
    experts = lax.axis_size("exp")
    devices = 4 * experts
    topk = routes.shape[2]
    capacity = count_rows * topk * 9 // (8 * experts)
    x, e, y = place_here()
    near_bit = lax.rem(lax.div(e, 2), 2)
    seq_len = 2 * count_rows
    own_cols = query_weight.shape[1]
    own_kv = key_weight.shape[1]

    chosen = routes[0].reshape(-1)
    expert_hot = (chosen[:, None] == jnp.arange(experts, dtype=jnp.int32)[None, :]).astype(
        jnp.int32
    )
    earlier = (jnp.cumsum(expert_hot, axis=0) - expert_hot).reshape(count_rows, topk, experts)
    named = expert_hot.reshape(count_rows, topk, experts)
    slot_table = jnp.sum((earlier + 1) * named, axis=1) - 1
    share_table = jnp.sum(named.astype(jnp.float32) * gate_share[0][:, :, None], axis=1)
    table = jnp.stack([slot_table.astype(jnp.float32).T, share_table.T])
    tables = gather_all(table)
    all_cotangents = gather_all(cotangent[0])

    resid = tokens[0].astype(jnp.float32)
    attn_norm, attn_norm_pull = jax.vjp(rms_apply, resid, attn_gain)
    normed = attn_norm.astype(jnp.bfloat16)
    kv_rows = jnp.concatenate([key_weight.T, value_weight.T], axis=0)
    group_tokens, group_query, group_kv, group_output = exchange(
        [
            ("gather", "tokens", normed),
            ("gather", "heads", query_weight.T),
            ("gather", "heads", kv_rows),
            ("gather", "heads", output_weight),
        ],
        0,
        "gather_attention",
    )
    block_tokens = 4 * count_rows
    held_tokens = group_tokens.reshape(block_tokens, width)
    held_query = group_query.reshape(-1, width)
    held_key = group_kv[:, :own_kv].reshape(-1, width)
    held_value = group_kv[:, own_kv:].reshape(-1, width)
    held_output = group_output.reshape(-1, width)
    held_kv = 2
    held_heads = held_kv * group

    def own_part(vector):
        parts = vector.reshape(2, 2, 2, -1)
        parts = lax.dynamic_index_in_dim(parts, x, 0, keepdims=False)
        return lax.dynamic_index_in_dim(parts, near_bit, 1, keepdims=False)

    query_lin = times_transposed(held_tokens, held_query) + own_part(query_bias).reshape(-1)
    key_lin = times_transposed(held_tokens, held_key) + own_part(key_bias).reshape(-1)
    value_low = (
        times_transposed(held_tokens, held_value) + own_part(value_bias).reshape(-1)
    ).astype(jnp.bfloat16)
    position = jnp.arange(seq_len, dtype=jnp.int32)
    cosine, sine = rope_tables(position, HD)
    cosine = cosine[None, :, None]
    sine = sine[None, :, None]
    query_rot = rotate(query_lin.reshape(2, seq_len, held_heads, HD), cosine, sine).astype(
        jnp.bfloat16
    )
    key_rot = rotate(key_lin.reshape(2, seq_len, held_kv, HD), cosine, sine).astype(jnp.bfloat16)
    values = value_low.reshape(2, seq_len, held_kv, HD)
    mine = segments[0]
    other = lax.ppermute(mine, "exp", pair_steps(experts, 2))
    doc_ids = jnp.where(near_bit == 0, jnp.stack([mine, other]), jnp.stack([other, mine]))
    visible = (position[:, None] >= position[None, :])[None] & (
        doc_ids[:, :, None] == doc_ids[:, None, :]
    )
    query_group = query_rot.reshape(2, seq_len, held_kv, group, HD)
    sink_grid = own_part(sink_logits).reshape(held_kv, group)[None, :, :, None]

    def score_block():
        raw = (
            jnp.einsum("bqkgd,bskd->bkgqs", query_group, key_rot, preferred_element_type=jnp.float32)
            * scale
        )
        return jnp.where(visible[:, None, None], raw, masked_score)

    scores = score_block()
    peak = jnp.maximum(jnp.max(scores, axis=-1), sink_grid)
    total_mass = jnp.sum(jnp.exp(scores - peak[..., None]), axis=-1) + jnp.exp(sink_grid - peak)
    log_total = peak + jnp.log(total_mass)
    probs = jnp.exp(scores - log_total[..., None])
    mixed = jnp.einsum(
        "bkgqs,bskd->bqkgd", probs.astype(jnp.bfloat16), values, preferred_element_type=jnp.float32
    )
    mixed = mixed.reshape(block_tokens, held_heads * HD).astype(jnp.bfloat16)
    attn_part = jnp.dot(mixed, held_output, preferred_element_type=jnp.float32)
    (attn_out,) = exchange(
        [("scatter", "tokens", attn_part.astype(jnp.bfloat16).reshape(4, count_rows, width))],
        1,
        "sum_attention",
    )
    hidden = resid + (attn_out + output_bias)
    moe_norm, moe_norm_pull = jax.vjp(rms_apply, hidden, moe_gain)
    normed_moe = moe_norm.astype(jnp.bfloat16)
    (all_normed,) = exchange([("gather", "all", normed_moe)], 2, "gather_rows")

    own_tables = lax.dynamic_index_in_dim(tables, e, 2, keepdims=False)
    slots = own_tables[:, 0].astype(jnp.int32)
    shares = own_tables[:, 1]
    seat_hot = slots[:, None, :] == jnp.arange(capacity, dtype=jnp.int32)[None, :, None]
    dispatch = seat_hot.astype(jnp.bfloat16)
    row_share = jnp.sum(jnp.where(seat_hot, shares[:, None, :], 0.0), axis=2)

    def to_rows(blocks):
        return jnp.einsum("bst,btd->bsd", dispatch, blocks, preferred_element_type=jnp.float32)

    def to_tokens(rows):
        return jnp.einsum(
            "bst,bsd->btd",
            dispatch,
            rows.astype(jnp.bfloat16).reshape(devices, capacity, width),
            preferred_element_type=jnp.float32,
        ).astype(jnp.bfloat16)

    row_count = devices * capacity
    expert_rows = to_rows(all_normed).astype(jnp.bfloat16).reshape(row_count, width)
    grad_rows = (
        (row_share[:, :, None] * to_rows(all_cotangents))
        .astype(jnp.bfloat16)
        .reshape(row_count, width)
    )
    gate_pre = (
        jnp.dot(expert_rows, gate_weight[0], preferred_element_type=jnp.float32) + gate_bias[0]
    )
    up_pre = jnp.dot(expert_rows, up_weight[0], preferred_element_type=jnp.float32) + up_bias[0]
    act_full, swiglu_pull = jax.vjp(swiglu, gate_pre, up_pre)
    activation = act_full.astype(jnp.bfloat16)
    act_grad = times_transposed(grad_rows, down_weight[0])
    gate_grad_full, up_grad_full = swiglu_pull(act_grad)
    gate_grad = gate_grad_full.astype(jnp.bfloat16)
    up_grad = up_grad_full.astype(jnp.bfloat16)
    rows_grad = times_transposed(gate_grad, gate_weight[0]) + times_transposed(
        up_grad, up_weight[0]
    )
    (normed_moe_grad,) = exchange([("scatter", "all", to_tokens(rows_grad))], 3, "sum_rows")
    once = jnp.where((x == 0) & (y == 0), 1.0, 0.0)
    finished = (
        jnp.dot(activation, down_weight[0], preferred_element_type=jnp.float32)
        + once * down_bias[0]
    )
    (moe_out,) = exchange(
        [("scatter", "all", to_tokens(row_share.reshape(row_count, 1) * finished))],
        4,
        "sum_results",
    )
    output = (hidden + moe_out).astype(jnp.bfloat16)
    down_bias_grad = jnp.sum(grad_rows.astype(jnp.float32), axis=0)
    down_weight_grad = inner_rows(activation, grad_rows)
    gate_bias_grad = jnp.sum(gate_grad.astype(jnp.float32), axis=0)
    up_bias_grad = jnp.sum(up_grad.astype(jnp.float32), axis=0)
    gate_weight_grad = inner_rows(expert_rows, gate_grad)
    up_weight_grad = inner_rows(expert_rows, up_grad)

    upstream = cotangent[0].astype(jnp.float32)
    hidden_norm_grad, moe_gain_grad = moe_norm_pull(normed_moe_grad)
    hidden_grad = upstream + hidden_norm_grad
    attn_out_grad = hidden_grad.astype(jnp.bfloat16)
    output_bias_grad = jnp.sum(attn_out_grad.astype(jnp.float32), axis=0)
    (group_grad,) = exchange([("gather", "tokens", attn_out_grad)], 5, "gather_gradient")
    held_grad = group_grad.reshape(block_tokens, width)
    mixed_grad = (
        times_transposed(held_grad, held_output)
        .astype(jnp.bfloat16)
        .reshape(2, seq_len, held_kv, group, HD)
    )
    scores = score_block()
    probs = jnp.exp(scores - log_total[..., None])
    prob_grad = jnp.einsum(
        "bqkgd,bskd->bkgqs", mixed_grad, values, preferred_element_type=jnp.float32
    )
    delta = jnp.sum(probs * prob_grad, axis=-1)
    score_grad = (probs * (prob_grad - delta[..., None])).astype(jnp.bfloat16)
    sink_part = -jnp.sum(jnp.exp(sink_grid - log_total) * delta, axis=(0, 3))
    value_grad = jnp.einsum(
        "bkgqs,bqkgd->bskd", probs.astype(jnp.bfloat16), mixed_grad, preferred_element_type=jnp.float32
    )
    key_grad = (
        jnp.einsum("bkgqs,bqkgd->bskd", score_grad, query_group, preferred_element_type=jnp.float32)
        * scale
    )
    query_grad = (
        jnp.einsum("bkgqs,bskd->bqkgd", score_grad, key_rot, preferred_element_type=jnp.float32)
        * scale
    )
    query_lin_grad = (
        rotate(query_grad.reshape(2, seq_len, held_heads, HD), cosine, -sine)
        .reshape(block_tokens, held_heads * HD)
        .astype(jnp.bfloat16)
    )
    key_lin_grad = (
        rotate(key_grad, cosine, -sine).reshape(block_tokens, held_kv * HD).astype(jnp.bfloat16)
    )
    value_lin_grad = value_grad.reshape(block_tokens, held_kv * HD).astype(jnp.bfloat16)
    normed_part = (
        jnp.dot(query_lin_grad, held_query, preferred_element_type=jnp.float32)
        + jnp.dot(key_lin_grad, held_key, preferred_element_type=jnp.float32)
        + jnp.dot(value_lin_grad, held_value, preferred_element_type=jnp.float32)
    )
    query_rows = inner_rows(query_lin_grad, held_tokens).astype(jnp.bfloat16)
    key_rows = inner_rows(key_lin_grad, held_tokens).astype(jnp.bfloat16)
    value_rows = inner_rows(value_lin_grad, held_tokens).astype(jnp.bfloat16)
    output_rows = inner_rows(mixed, held_grad).astype(jnp.bfloat16)
    own_blocks = held_query.shape[0] // own_cols
    kv_part = jnp.concatenate(
        [
            key_rows.reshape(own_blocks, own_kv, width),
            value_rows.reshape(own_blocks, own_kv, width),
        ],
        axis=1,
    )
    normed_grad, query_owned, kv_owned, output_owned = exchange(
        [
            ("scatter", "tokens", normed_part.astype(jnp.bfloat16).reshape(4, count_rows, width)),
            ("scatter", "heads", query_rows.reshape(own_blocks, own_cols, width)),
            ("scatter", "heads", kv_part),
            ("scatter", "heads", output_rows.reshape(own_blocks, own_cols, width)),
        ],
        6,
        "sum_weights",
    )
    resid_norm_grad, attn_gain_grad = attn_norm_pull(normed_grad)
    input_grad = hidden_grad + resid_norm_grad

    def spread(part):
        flat = part.reshape(1, 2, 1, -1)
        full = jnp.zeros((2, 2, 2, flat.shape[-1]), jnp.float32)
        return lax.dynamic_update_slice(full, flat, (x, 0, near_bit, 0)).reshape(-1)

    summed = lax.psum(
        (
            attn_gain_grad,
            spread(jnp.sum(query_lin_grad.astype(jnp.float32), axis=0)),
            spread(jnp.sum(key_lin_grad.astype(jnp.float32), axis=0)),
            spread(jnp.sum(value_lin_grad.astype(jnp.float32), axis=0)),
            output_bias_grad,
            spread(sink_part),
            moe_gain_grad,
        ),
        ("seq", "exp", "dp"),
    )
    return (
        output[None],
        input_grad[None],
        summed[0],
        query_owned.T,
        summed[1],
        kv_owned[:own_kv].T,
        summed[2],
        kv_owned[own_kv:].T,
        summed[3],
        output_owned,
        summed[4],
        summed[5],
        summed[6],
        gate_weight_grad[None],
        gate_bias_grad[None],
        up_weight_grad[None],
        up_bias_grad[None],
        down_weight_grad[None],
        down_bias_grad[None],
    )


def solution(mesh):
    placed = (
        P(("exp", "dp"), "seq", None),
        P(("exp", "dp"), None),
        P(("exp", "dp"), "seq", None),
        P(("exp", "dp"), "seq", None),
        P(),
        P(None, ("seq", "exp", "dp")),
        P(),
        P(None, ("seq", "exp", "dp")),
        P(),
        P(None, ("seq", "exp", "dp")),
        P(),
        P(("seq", "exp", "dp"), None),
        P(),
        P(),
        P(),
        P("exp", None, ("seq", "dp")),
        P("exp", ("seq", "dp")),
        P("exp", None, ("seq", "dp")),
        P("exp", ("seq", "dp")),
        P("exp", ("seq", "dp"), None),
        P("exp", None),
        P(("exp", "dp"), "seq", None),
    )
    shape = mesh.shape
    small = shape["seq"] == 2 and shape["dp"] == 2 and shape["exp"] == 8
    return jax.shard_map(
        close_by if small else local,
        mesh=mesh,
        in_specs=placed,
        out_specs=(
            P(("exp", "dp"), "seq", None),
            P(("exp", "dp"), "seq", None),
            P(),
            P(None, ("seq", "exp", "dp")),
            P(),
            P(None, ("seq", "exp", "dp")),
            P(),
            P(None, ("seq", "exp", "dp")),
            P(),
            P(("seq", "exp", "dp"), None),
            P(),
            P(),
            P(),
            P("exp", None, ("seq", "dp")),
            P("exp", ("seq", "dp")),
            P("exp", None, ("seq", "dp")),
            P("exp", ("seq", "dp")),
            P("exp", ("seq", "dp"), None),
            P("exp", None),
        ),
        check_vma=False,
    )
```

```python
import math

import jax
import jax.numpy as jnp
from jax import lax
from jax.experimental import pallas as pl
from jax.experimental.pallas import tpu as pltpu
from jax.sharding import PartitionSpec as P

HD = 64


highest = lax.Precision.HIGHEST
norm_eps = 1e-05
rope_base = 150000.0
clip_level = 7.0
glu_alpha = 1.702
masked_score = -1000000000.0


def rms_apply(values, gain):
    return values * lax.rsqrt(jnp.mean(values * values, axis=-1, keepdims=True) + norm_eps) * gain


def rope_tables(position, width):
    exponent = jnp.arange(width // 2).astype(jnp.float32) * (2.0 / width)
    freqs = jnp.exp(-math.log(rope_base) * exponent)
    angles = position.astype(jnp.float32)[:, None] * freqs[None, :]
    return (jnp.cos(angles), jnp.sin(angles))


def rotate(values, cosine, sine):
    half = values.shape[-1] // 2
    first = values[..., :half]
    second = values[..., half:]
    return jnp.concatenate(
        [first * cosine - second * sine, second * cosine + first * sine], axis=-1
    )


def swiglu(gate_pre, up_pre):
    gate_soft = clip_level * jnp.tanh(gate_pre / clip_level)
    up_soft = clip_level * jnp.tanh(up_pre / clip_level)
    return gate_soft * jax.nn.sigmoid(glu_alpha * gate_soft) * (up_soft + 1.0)


def inner_rows(left, right):
    return lax.dot_general(
        left, right, (((0,), (0,)), ((), ())), preferred_element_type=jnp.float32
    )


def times_transposed(left, right):
    return lax.dot_general(
        left, right, (((1,), (1,)), ((), ())), preferred_element_type=jnp.float32
    )


def to_experts(outgoing):
    width = outgoing.shape[2]
    arrived = lax.all_to_all(outgoing, "exp", split_axis=0, concat_axis=0, tiled=True)
    arrived = lax.all_gather(arrived, ("seq", "dp"), axis=0, tiled=True)
    return arrived.reshape(-1, width)


def results_back(activation, down_matrix, down_vector, experts, capacity):
    width = down_matrix.shape[1]
    share = lax.psum_scatter(
        jnp.dot(activation, down_matrix, preferred_element_type=jnp.float32).astype(jnp.bfloat16),
        ("seq", "dp"),
        scatter_dimension=0,
        tiled=True,
    ).astype(jnp.float32)
    finished = (share + down_vector).astype(jnp.bfloat16).reshape(experts, capacity, width)
    return lax.all_to_all(finished, "exp", split_axis=0, concat_axis=0, tiled=True)


def gradients_back(gate_grad, up_grad, gate_matrix, up_matrix, experts, capacity):
    share = lax.psum_scatter(
        times_transposed(gate_grad, gate_matrix) + times_transposed(up_grad, up_matrix),
        ("seq", "dp"),
        scatter_dimension=0,
        tiled=True,
    )
    return lax.all_to_all(
        share.reshape(experts, capacity, share.shape[1]),
        "exp",
        split_axis=0,
        concat_axis=0,
        tiled=True,
    )


def local(
    tokens,
    segments,
    routes,
    gate_share,
    attn_gain,
    query_weight,
    query_bias,
    key_weight,
    key_bias,
    value_weight,
    value_bias,
    output_weight,
    output_bias,
    sink_logits,
    moe_gain,
    gate_weight,
    gate_bias,
    up_weight,
    up_bias,
    down_weight,
    down_bias,
    cotangent,
):
    count_rows = tokens.shape[1]
    width = tokens.shape[2]
    head_count = sink_logits.shape[0]
    kv_count = key_bias.shape[0] // HD
    group = head_count // kv_count
    scale = 1.0 / math.sqrt(HD)
    experts = lax.axis_size("exp")
    topk = routes.shape[2]
    capacity = count_rows * topk * 9 // (8 * experts)
    resid = tokens[0].astype(jnp.float32)
    full_query, full_key, full_value, full_output = (
        lax.all_gather(query_weight, ("seq", "exp", "dp"), axis=1, tiled=True),
        lax.all_gather(key_weight, ("seq", "exp", "dp"), axis=1, tiled=True),
        lax.all_gather(value_weight, ("seq", "exp", "dp"), axis=1, tiled=True),
        lax.all_gather(output_weight, ("seq", "exp", "dp"), axis=0, tiled=True),
    )
    attn_norm, attn_norm_pull = jax.vjp(rms_apply, resid, attn_gain)
    normed = attn_norm.astype(jnp.bfloat16)
    query_lin = jnp.dot(normed, full_query, preferred_element_type=jnp.float32) + query_bias
    key_lin = jnp.dot(normed, full_key, preferred_element_type=jnp.float32) + key_bias
    value_low = (
        jnp.dot(normed, full_value, preferred_element_type=jnp.float32) + value_bias
    ).astype(jnp.bfloat16)
    offset = lax.axis_index("seq") * count_rows
    position = offset + jnp.arange(count_rows, dtype=jnp.int32)
    cosine, sine = rope_tables(position, HD)
    cosine = cosine[:, None]
    sine = sine[:, None]
    query_rot = rotate(query_lin.reshape(count_rows, head_count, HD), cosine, sine).astype(
        jnp.bfloat16
    )
    key_rot = rotate(key_lin.reshape(count_rows, kv_count, HD), cosine, sine).astype(jnp.bfloat16)
    all_keys, all_values = (
        lax.all_gather(key_rot.reshape(count_rows, kv_count * HD), "seq", axis=0, tiled=True),
        lax.all_gather(value_low, "seq", axis=0, tiled=True),
    )
    seq_len = all_keys.shape[0]
    all_keys = all_keys.reshape(seq_len, kv_count, HD)
    all_values = all_values.reshape(seq_len, kv_count, HD)
    doc_ids = segments[0]
    own_ids = lax.dynamic_slice_in_dim(doc_ids, offset, count_rows, 0)
    key_place = jnp.arange(seq_len, dtype=jnp.int32)
    visible = (position[:, None] >= key_place[None, :]) & (own_ids[:, None] == doc_ids[None, :])
    query_group = query_rot.reshape(count_rows, kv_count, group, HD)
    sink_grid = sink_logits.reshape(kv_count, group)[:, :, None]

    def score_block():
        raw = (
            jnp.einsum("qkgd,skd->kgqs", query_group, all_keys, preferred_element_type=jnp.float32)
            * scale
        )
        return jnp.where(visible[None, None], raw, masked_score)

    scores = score_block()
    peak = jnp.maximum(jnp.max(scores, axis=-1), sink_grid)
    total = jnp.sum(jnp.exp(scores - peak[..., None]), axis=-1) + jnp.exp(sink_grid - peak)
    log_total = peak + jnp.log(total)
    probs = jnp.exp(scores - log_total[..., None])
    mixed = jnp.einsum(
        "kgqs,skd->qkgd", probs.astype(jnp.bfloat16), all_values, preferred_element_type=jnp.float32
    )
    mixed = mixed.reshape(count_rows, head_count * HD).astype(jnp.bfloat16)
    attn_out = jnp.dot(mixed, full_output, preferred_element_type=jnp.float32) + output_bias
    hidden = resid + attn_out
    moe_norm, moe_norm_pull = jax.vjp(rms_apply, hidden, moe_gain)
    normed_moe = moe_norm.astype(jnp.bfloat16)
    chosen = routes[0].reshape(-1)
    expert_hot = (chosen[:, None] == jnp.arange(experts, dtype=jnp.int32)[None, :]).astype(
        jnp.int32
    )
    slot_index = jnp.sum((jnp.cumsum(expert_hot, axis=0) - expert_hot) * expert_hot, axis=1)
    target = chosen * capacity + slot_index
    slot_hot = (
        target[:, None] == jnp.arange(experts * capacity, dtype=jnp.int32)[None, :]
    ).reshape(count_rows, topk, experts * capacity)
    dispatch = jnp.sum(slot_hot.astype(jnp.bfloat16), axis=1)
    weighted = jnp.sum(slot_hot.astype(jnp.float32) * gate_share[0][:, :, None], axis=1)
    outgoing = jnp.einsum("ts,td->sd", dispatch, normed_moe, preferred_element_type=jnp.float32)
    outgoing = outgoing.astype(jnp.bfloat16).reshape(experts, capacity, width)
    expert_rows = to_experts(outgoing)
    gate_pre = (
        jnp.dot(expert_rows, gate_weight[0], preferred_element_type=jnp.float32) + gate_bias[0]
    )
    up_pre = jnp.dot(expert_rows, up_weight[0], preferred_element_type=jnp.float32) + up_bias[0]
    act_full, swiglu_pull = jax.vjp(swiglu, gate_pre, up_pre)
    activation = act_full.astype(jnp.bfloat16)
    returned = results_back(activation, down_weight[0], down_bias[0], experts, capacity)
    moe_out = jnp.dot(
        weighted, returned.reshape(experts * capacity, width).astype(jnp.float32), precision=highest
    )
    output = (hidden + moe_out).astype(jnp.bfloat16)
    upstream = cotangent[0].astype(jnp.float32)
    grad_slots = jnp.einsum("ts,td->sd", weighted, upstream, precision=highest)
    grad_slots = grad_slots.astype(jnp.bfloat16).reshape(experts, capacity, width)
    grad_rows = to_experts(grad_slots)
    down_bias_grad = jnp.sum(grad_rows.astype(jnp.float32), axis=0)
    down_weight_grad = inner_rows(activation, grad_rows)
    act_grad = times_transposed(grad_rows, down_weight[0])
    gate_grad_full, up_grad_full = swiglu_pull(act_grad)
    gate_grad = gate_grad_full.astype(jnp.bfloat16)
    up_grad = up_grad_full.astype(jnp.bfloat16)
    gate_bias_grad = jnp.sum(gate_grad.astype(jnp.float32), axis=0)
    up_bias_grad = jnp.sum(up_grad.astype(jnp.float32), axis=0)
    gate_weight_grad = inner_rows(expert_rows, gate_grad)
    up_weight_grad = inner_rows(expert_rows, up_grad)
    rows_grad = gradients_back(gate_grad, up_grad, gate_weight[0], up_weight[0], experts, capacity)
    normed_moe_grad = jnp.einsum(
        "ts,sd->td",
        dispatch.astype(jnp.float32),
        rows_grad.reshape(experts * capacity, width),
        precision=highest,
    )
    hidden_norm_grad, moe_gain_grad = moe_norm_pull(normed_moe_grad)
    hidden_grad = upstream + hidden_norm_grad
    attn_out_grad = hidden_grad.astype(jnp.bfloat16)
    output_bias_grad = jnp.sum(attn_out_grad.astype(jnp.float32), axis=0)
    full_query, full_key, full_value, full_output = (
        lax.all_gather(query_weight, ("seq", "exp", "dp"), axis=1, tiled=True),
        lax.all_gather(key_weight, ("seq", "exp", "dp"), axis=1, tiled=True),
        lax.all_gather(value_weight, ("seq", "exp", "dp"), axis=1, tiled=True),
        lax.all_gather(output_weight, ("seq", "exp", "dp"), axis=0, tiled=True),
    )
    mixed_grad = (
        times_transposed(attn_out_grad, full_output)
        .astype(jnp.bfloat16)
        .reshape(count_rows, kv_count, group, HD)
    )
    scores = score_block()
    probs = jnp.exp(scores - log_total[..., None])
    prob_grad = jnp.einsum(
        "qkgd,skd->kgqs", mixed_grad, all_values, preferred_element_type=jnp.float32
    )
    delta = jnp.sum(probs * prob_grad, axis=-1)
    score_grad = (probs * (prob_grad - delta[..., None])).astype(jnp.bfloat16)
    sink_grad = -jnp.sum(jnp.exp(sink_grid - log_total) * delta, axis=-1).reshape(head_count)
    value_grad = jnp.einsum(
        "kgqs,qkgd->skd", probs.astype(jnp.bfloat16), mixed_grad, preferred_element_type=jnp.float32
    )
    key_grad = (
        jnp.einsum("kgqs,qkgd->skd", score_grad, query_group, preferred_element_type=jnp.float32)
        * scale
    )
    query_grad = (
        jnp.einsum("kgqs,skd->qkgd", score_grad, all_keys, preferred_element_type=jnp.float32)
        * scale
    )
    key_share, value_share = (
        lax.psum_scatter(
            key_grad.reshape(seq_len, kv_count * HD), "seq", scatter_dimension=0, tiled=True
        ),
        lax.psum_scatter(
            value_grad.reshape(seq_len, kv_count * HD), "seq", scatter_dimension=0, tiled=True
        ),
    )
    query_lin_grad = (
        rotate(query_grad.reshape(count_rows, head_count, HD), cosine, -sine)
        .reshape(count_rows, head_count * HD)
        .astype(jnp.bfloat16)
    )
    key_lin_grad = (
        rotate(key_share.reshape(count_rows, kv_count, HD), cosine, -sine)
        .reshape(count_rows, kv_count * HD)
        .astype(jnp.bfloat16)
    )
    value_lin_grad = value_share.astype(jnp.bfloat16)
    query_bias_grad = jnp.sum(query_lin_grad.astype(jnp.float32), axis=0)
    key_bias_grad = jnp.sum(key_lin_grad.astype(jnp.float32), axis=0)
    value_bias_grad = jnp.sum(value_lin_grad.astype(jnp.float32), axis=0)
    normed_grad = (
        times_transposed(query_lin_grad, full_query)
        + times_transposed(key_lin_grad, full_key)
        + times_transposed(value_lin_grad, full_value)
    )
    resid_norm_grad, attn_gain_grad = attn_norm_pull(normed_grad)
    input_grad = hidden_grad + resid_norm_grad
    query_weight_grad = inner_rows(normed, query_lin_grad)
    key_weight_grad = inner_rows(normed, key_lin_grad)
    value_weight_grad = inner_rows(normed, value_lin_grad)
    output_weight_grad = inner_rows(mixed, attn_out_grad)
    query_owned, key_owned, value_owned, output_owned = (
        lax.psum_scatter(query_weight_grad, ("seq", "exp", "dp"), scatter_dimension=1, tiled=True),
        lax.psum_scatter(key_weight_grad, ("seq", "exp", "dp"), scatter_dimension=1, tiled=True),
        lax.psum_scatter(value_weight_grad, ("seq", "exp", "dp"), scatter_dimension=1, tiled=True),
        lax.psum_scatter(output_weight_grad, ("seq", "exp", "dp"), scatter_dimension=0, tiled=True),
    )
    summed = lax.psum(
        (
            attn_gain_grad,
            query_bias_grad,
            key_bias_grad,
            value_bias_grad,
            output_bias_grad,
            sink_grad,
            moe_gain_grad,
        ),
        ("seq", "exp", "dp"),
    )
    return (
        output[None],
        input_grad[None],
        summed[0],
        query_owned,
        summed[1],
        key_owned,
        summed[2],
        value_owned,
        summed[3],
        output_owned,
        summed[4],
        summed[5],
        summed[6],
        gate_weight_grad[None],
        gate_bias_grad[None],
        up_weight_grad[None],
        up_bias_grad[None],
        down_weight_grad[None],
        down_bias_grad[None],
    )

MESH = pl.DeviceIdType.MESH
HERE = (0, 0, 0)
SIBLING = (0, 1, 0)
ACROSS = (1, 0, 0)
ALONG = (0, 0, 1)
NEAR = (0, 2, 0)
FAR = (0, 4, 0)
ENDS = (0, 6, 0)


def flip(place, mask):
    x, e, y = place
    if mask[0]:
        x = 1 - x
    if mask[2]:
        y = 1 - y
    step = 0
    for bit in (1, 2, 4):
        if mask[1] & bit:
            step = step + bit - 2 * bit * lax.rem(lax.div(e, bit), 2)
    return x, e + step, y


def both(left, right):
    return tuple(a ^ b for a, b in zip(left, right))


def place_here():
    return lax.axis_index("seq"), lax.axis_index("exp"), lax.axis_index("dp")


def block_of_all(place):
    x, e, y = place
    return (e * 2 + x) * 2 + y


def block_of_tokens(place):
    x, e, y = place
    return lax.rem(lax.div(e, 2), 2) * 2 + x


def block_of_heads(place):
    x, e, y = place
    return (lax.div(e, 4) * 2 + lax.rem(e, 2)) * 2 + y


GROUPS = {
    "all": (block_of_all, 32, SIBLING, ACROSS, ALONG, (NEAR, FAR, ENDS), 0.5),
    "tokens": (block_of_tokens, 4, None, ACROSS, NEAR, (), 0.5),
    "heads": (block_of_heads, 8, SIBLING, FAR, ALONG, (), 1.0),
}


def partners(group):
    _, _, sibling, first, second, line, _ = GROUPS[group]
    return ([sibling] if sibling else []) + [first, second] + list(line)


def copies(group):
    _, _, sibling, _, _, line, _ = GROUPS[group]
    rounds = 1 + len(line)
    return rounds * (8 if sibling else 4) + len(line)


class Sender:
    def __init__(self, place, send, recv):
        self.place, self.send, self.recv, self.started = place, send, recv, []

    def push(self, source, target, mask):
        number = len(self.started)
        copy = pltpu.make_async_remote_copy(
            src_ref=source,
            dst_ref=target,
            send_sem=self.send.at[number],
            recv_sem=self.recv.at[number],
            device_id=flip(self.place, mask),
            device_id_type=MESH,
        )
        copy.start()
        self.started.append(copy)
        return copy

    def finish(self):
        for copy in self.started:
            copy.wait_send()


class Gather:
    def __init__(self, group, place, source, result, send, recv, local):
        self.index, _, self.sibling, self.first, self.second, self.line, share = GROUPS[group]
        self.place, self.source, self.result = place, source, result
        self.rows = source.shape[0]
        self.cut = int(self.rows * share) // 16 * 16
        self.out = Sender(place, send, recv)
        self.own = pltpu.make_async_copy(source, self.at(HERE), local.at[0])
        self.masks = [HERE] + list(self.line)
        self.reach, self.ways, self.halves = {}, {}, {}
        self.tails = {step: [] for step in range(len(self.masks))}

    def at(self, mask):
        return self.result.at[self.index(flip(self.place, mask))]

    def start(self):
        self.own.start()
        self.reached(self.line[:2])

    def reached(self, line):
        for mask in line:
            self.reach[mask] = self.out.push(self.source, self.at(HERE), mask)

    def pass_on(self, step, block, place):
        if self.sibling:
            self.tails[step].append(self.out.push(block, place, self.sibling))

    def plane(self, step):
        mask = self.masks[step]
        if step:
            self.reach[mask].wait_recv()
        block = self.at(mask) if step else self.source
        self.ways[step] = (
            self.out.push(block, self.at(mask), self.first),
            self.out.push(block, self.at(mask), self.second),
        )
        self.pass_on(step, block, self.at(mask))
        if step == 1:
            self.reached(self.line[2:])

    def turn(self, step):
        halves = []
        mask, cut = self.masks[step], self.cut
        self.ways[step][0].wait_recv()
        seen = self.at(both(mask, self.first))
        if cut:
            halves.append(self.out.push(seen.at[:cut], seen.at[:cut], self.second))
        self.pass_on(step, seen, seen)
        self.ways[step][1].wait_recv()
        seen = self.at(both(mask, self.second))
        if cut < self.rows:
            halves.append(self.out.push(seen.at[cut:], seen.at[cut:], self.first))
        self.pass_on(step, seen, seen)
        self.halves[step] = halves

    def close(self, step):
        for half in self.halves[step]:
            half.wait_recv()
        seen = self.at(both(self.masks[step], both(self.first, self.second)))
        self.pass_on(step, seen, seen)

    def passed(self, step):
        for copy in self.tails[step]:
            copy.wait_recv()

    def finish(self):
        self.out.finish()


def gather_steps(group, place, source, result, send, recv, local):
    work = Gather(group, place, source, result, send, recv, local)
    work.start()
    count = len(work.masks)
    for step in range(count + 2):
        if step < count:
            work.plane(step)
            yield
        if 0 <= step - 1 < count:
            work.turn(step - 1)
            yield
        if 0 <= step - 2 < count:
            work.close(step - 2)
            yield
    for step in range(count):
        work.passed(step)
    work.own.wait()
    work.finish()


def total(parts, low, high, store):
    def body(step, carry):
        rows = pl.ds(pl.multiple_of(low + step * 16, 16), 16)
        value = parts[0][rows].astype(jnp.float32)
        for part in parts[1:]:
            value = value + part[rows].astype(jnp.float32)
        store[rows] = value.astype(store.dtype)
        return carry

    if high > low:
        lax.fori_loop(0, (high - low) // 16, body, 0)


def scatter_steps(group, place, source, result, own, mate, side, arrive, ends, send, recv, local):
    index, _, sibling, first, second, line, share = GROUPS[group]
    rows = result.shape[0]
    cut = int(rows * (1.0 - share)) // 16 * 16
    corner = both(first, second)
    out = Sender(place, send, recv)
    masks = list(line)[::-1] + [HERE]
    corners = (corner, first, second, HERE)
    fetched, sent = {}, {}
    for step, mask in enumerate(masks):
        for spot, shift in enumerate(corners):
            seat = step * 4 + spot
            goal = both(mask, shift)
            if sibling:
                sent[seat] = out.push(
                    source.at[index(flip(place, both(goal, sibling)))], mate.at[seat], sibling
                )
            fetched[seat] = pltpu.make_async_copy(
                source.at[index(flip(place, goal))], own.at[seat], local.at[seat]
            )
            fetched[seat].start()
    yield

    def ready(seat):
        fetched[seat].wait()
        if sibling:
            sent[seat].wait_recv()
            return [own.at[seat], mate.at[seat]]
        return [own.at[seat]]

    def outward(step):
        seat = step * 4
        parts = ready(seat)
        if sibling:
            total(parts, 0, rows, own.at[seat])
        halves = []
        if cut:
            halves.append(out.push(own.at[seat].at[:cut], side.at[step].at[:cut], first))
        if cut < rows:
            halves.append(out.push(own.at[seat].at[cut:], side.at[step].at[cut:], second))
        return halves

    def inward(step, halves):
        by_first, by_second = ready(step * 4 + 1), ready(step * 4 + 2)
        for half in halves:
            half.wait_recv()
        total(by_second + [side.at[step]], 0, cut, own.at[step * 4 + 2])
        total(by_first + [side.at[step]], cut, rows, own.at[step * 4 + 1])
        if sibling:
            total(by_second, cut, rows, own.at[step * 4 + 2])
            total(by_first, 0, cut, own.at[step * 4 + 1])
        return (
            out.push(own.at[step * 4 + 1], arrive.at[step * 2], first),
            out.push(own.at[step * 4 + 2], arrive.at[step * 2 + 1], second),
        )

    def close(step, ways):
        parts = ready(step * 4 + 3)
        for way in ways:
            way.wait_recv()
        parts = parts + [arrive.at[step * 2], arrive.at[step * 2 + 1]]
        if masks[step] != HERE:
            total(parts, 0, rows, own.at[step * 4 + 3])
            return out.push(own.at[step * 4 + 3], ends.at[step], masks[step])
        for number, copy in enumerate(reach):
            copy.wait_recv()
            parts.append(ends.at[number])
        total(parts, 0, rows, result)

    halves, ways, reach = {}, {}, []
    for step in range(len(masks) + 2):
        if step < len(masks):
            halves[step] = outward(step)
            yield
        if 0 <= step - 1 < len(masks):
            ways[step - 1] = inward(step - 1, halves[step - 1])
            yield
        if 0 <= step - 2 < len(masks):
            copy = close(step - 2, ways[step - 2])
            if copy is not None:
                reach.append(copy)
            yield
    out.finish()


def exchange(jobs, collective, name):
    in_specs, out_specs, out_shape, scratch, plans = [], [], [], [], []
    for kind, group, array in jobs:
        _, blocks, sibling, _, _, line, _ = GROUPS[group]
        rounds = 1 + len(line)
        in_specs.append(pl.BlockSpec(memory_space=pl.ANY))
        sems = [pltpu.SemaphoreType.DMA((copies(group),)), pltpu.SemaphoreType.DMA((copies(group),))]
        if kind == "gather":
            shape = array.shape
            out_shape.append(jax.ShapeDtypeStruct((blocks,) + shape, array.dtype))
            out_specs.append(pl.BlockSpec(memory_space=pl.ANY))
            need = sems + [pltpu.SemaphoreType.DMA((1,))]
        else:
            shape = array.shape[1:]
            out_shape.append(jax.ShapeDtypeStruct(shape, jnp.float32))
            out_specs.append(pl.BlockSpec(memory_space=pltpu.VMEM))
            slots = [4 * rounds, 4 * rounds if sibling else 1, rounds, 2 * rounds, max(1, rounds - 1)]
            if not sibling:
                slots[1] = 1
            need = [
                pltpu.VMEM((count,) + (shape if count > 1 or number != 1 else (16, 128)), array.dtype)
                for number, count in enumerate(slots)
            ]
            need = need + sems + [pltpu.SemaphoreType.DMA((4 * rounds,))]
        plans.append((kind, group, len(need)))
        scratch += need
    greet = []
    for _, group, _ in jobs:
        greet += [mask for mask in partners(group) if mask not in greet]

    def body(*refs):
        count = len(jobs)
        sources, results, rest = refs[:count], refs[count : 2 * count], list(refs[2 * count :])
        place = place_here()
        barrier = pltpu.get_barrier_semaphore()
        for mask in greet:
            pl.semaphore_signal(barrier, inc=1, device_id=flip(place, mask), device_id_type=MESH)
        pl.semaphore_wait(barrier, len(greet))
        running = []
        for number, (kind, group, width) in enumerate(plans):
            own, rest = rest[:width], rest[width:]
            steps = gather_steps if kind == "gather" else scatter_steps
            running.append(steps(group, place, sources[number], results[number], *own))
        while running:
            for steps in list(running):
                if next(steps, "end") == "end":
                    running.remove(steps)

    return pl.pallas_call(
        body,
        out_shape=out_shape,
        in_specs=in_specs,
        out_specs=out_specs,
        scratch_shapes=scratch,
        compiler_params=pltpu.CompilerParams(
            collective_id=collective, has_side_effects=True, vmem_limit_bytes=60 * 1024 * 1024
        ),
        name=name,
    )(*[array for _, _, array in jobs])


TILE = 512


def spans(width):
    return [(low, min(TILE, width - low)) for low in range(0, width, TILE)]


def seat_hot(seats, capacity, kind):
    lines = lax.broadcasted_iota(jnp.int32, (2 * capacity, seats.shape[-1]), 0)
    return (lines == seats).astype(kind)


def expert_sums(kind, rows, weights, seats, extra, collective, name):
    experts, pairs = seats.shape[1], seats.shape[2]
    tokens = seats.shape[4] // 2
    half_rows = rows[0].shape[0] // experts
    pair_rows = half_rows // pairs
    capacity = pair_rows // 2
    hidden = rows[0].shape[1]
    width = weights[0].shape[0] if kind == "gradient" else weights[0].shape[1]
    first, second, line = ACROSS, ALONG, (ENDS, FAR, NEAR)
    masks = list(line) + [HERE]
    rounds = len(masks)
    cut = tokens // 2
    count_rows, count_extra = len(rows), len(extra)
    copies_out = rounds * (pairs + 4) + len(line)

    def body(*refs):
        refs = list(refs)
        left = refs[:count_rows]
        wide = refs[count_rows : 2 * count_rows]
        seat_ref = refs[2 * count_rows]
        more = refs[2 * count_rows + 1 : 2 * count_rows + 1 + count_extra]
        rest = refs[2 * count_rows + 1 + count_extra :]
        result, staged, away, joined, own, side, arrive, ends, send, recv, local = rest
        place = place_here()
        x, e, y = place
        greet = [SIBLING, first, second] + list(line)
        barrier = pltpu.get_barrier_semaphore()
        for mask in greet:
            pl.semaphore_signal(barrier, inc=1, device_id=flip(place, mask), device_id_type=MESH)
        pl.semaphore_wait(barrier, len(greet))
        out = Sender(place, send, recv)

        def block(mask):
            there = flip(place, mask)
            return there[0] * 2 + there[2]

        halves = []
        for mask in masks:
            halves.append((flip(place, both(mask, SIBLING))[1], True))
            halves.append((flip(place, mask)[1], False))
        loads = {}

        def load(number):
            if number < len(halves):
                begin = pl.multiple_of(halves[number][0] * half_rows, 16)
                for item in range(count_rows):
                    copy = pltpu.make_async_copy(
                        left[item].at[pl.ds(begin, half_rows)],
                        staged.at[number % 2, item],
                        local.at[number % 2, item],
                    )
                    copy.start()
                    loads[number, item] = copy

        def make(number, store):
            load(number + 1)
            for item in range(count_rows):
                loads[number, item].wait()
            values = [staged[number % 2, item] for item in range(count_rows)]
            if kind == "result":
                part = halves[number][0]
                factors = []
                for pair in range(pairs):
                    hot = seat_hot(seat_ref[0, part, pair], capacity, jnp.float32)
                    factors.append(jnp.sum(hot * more[0][part, pair], axis=1, keepdims=True))
                factor = jnp.concatenate(factors, axis=0)
                once = jnp.where((x == 0) & (y == 0), 1.0, 0.0).astype(jnp.float32)

            def tile(low, size):
                if kind == "gradient":
                    value = times_transposed(values[0], wide[0][pl.ds(low, size), :])
                    value = value + times_transposed(values[1], wide[1][pl.ds(low, size), :])
                else:
                    value = jnp.dot(
                        values[0], wide[0][:, pl.ds(low, size)], preferred_element_type=jnp.float32
                    )
                    value = (value + once * more[1][:, pl.ds(low, size)]) * factor
                store(low, size, value.astype(jnp.bfloat16))

            by_tiles(width, tile)

        def to_sibling(step):
            slot = step % 2

            def store(low, size, value):
                away[slot, :, pl.ds(low, size)] = value

            if step >= 2:
                for copy in sent[step - 2]:
                    copy.wait_send()
            make(2 * step, store)
            sent[step] = [
                out.push(
                    away.at[slot].at[pair * pair_rows : (pair + 1) * pair_rows],
                    joined.at[step, pair].at[pair_rows : 2 * pair_rows],
                    SIBLING,
                )
                for pair in range(pairs)
            ]

        def to_here(step):
            def store(low, size, value):
                for pair in range(pairs):
                    joined[step, pair, :pair_rows, pl.ds(low, size)] = value[
                        pair * pair_rows : (pair + 1) * pair_rows
                    ]

            make(2 * step + 1, store)

        def combine(step):
            for copy in sent[step]:
                copy.wait_recv()
            part = halves[2 * step + 1][0]
            for pair in range(pairs):
                hot = jnp.concatenate(
                    [seat_hot(seat_ref[mate, part, pair], capacity, jnp.bfloat16) for mate in range(2)],
                    axis=0,
                )

                def tile(low, size):
                    value = inner_rows(hot, joined[step, pair, :, pl.ds(low, size)])
                    value = value.astype(jnp.bfloat16)
                    own[step * 4 + pair * 2, :, pl.ds(low, size)] = value[:tokens]
                    own[step * 4 + pair * 2 + 1, :, pl.ds(low, size)] = value[tokens:]

                by_tiles(width, tile)

        def outward(step):
            corner = own.at[step * 4 + block(both(first, second))]
            return [
                out.push(corner.at[:cut], side.at[step].at[:cut], first),
                out.push(corner.at[cut:], side.at[step].at[cut:], second),
            ]

        def inward(step, parts):
            by_first = own.at[step * 4 + block(first)]
            by_second = own.at[step * 4 + block(second)]
            for part in parts:
                part.wait_recv()
            total([by_second, side.at[step]], 0, cut, by_second)
            total([by_first, side.at[step]], cut, tokens, by_first)
            return (
                out.push(by_first, arrive.at[step * 2], first),
                out.push(by_second, arrive.at[step * 2 + 1], second),
            )

        def close(step, ways):
            kept = own.at[step * 4 + block(HERE)]
            for way in ways:
                way.wait_recv()
            parts = [kept, arrive.at[step * 2], arrive.at[step * 2 + 1]]
            if masks[step] != HERE:
                total(parts, 0, tokens, kept)
                reach.append(out.push(kept, ends.at[step], masks[step]))
                return
            for number, copy in enumerate(reach):
                copy.wait_recv()
                parts.append(ends.at[number])
            total(parts, 0, tokens, result)

        sent, corners, ways, reach = {}, {}, {}, []
        load(0)
        for step in range(rounds + 2):
            if step < rounds:
                to_sibling(step)
                to_here(step)
                combine(step)
                corners[step] = outward(step)
            if 0 <= step - 1 < rounds:
                ways[step - 1] = inward(step - 1, corners[step - 1])
            if 0 <= step - 2 < rounds:
                close(step - 2, ways[step - 2])
        for step in range(rounds):
            if step >= rounds - 2:
                for copy in sent[step]:
                    copy.wait_send()
        exchanged = {id(copy) for step in range(rounds) for copy in sent[step]}
        for copy in out.started:
            if id(copy) not in exchanged:
                copy.wait_send()

    vmem = pl.BlockSpec(memory_space=pltpu.VMEM)
    return pl.pallas_call(
        body,
        out_shape=jax.ShapeDtypeStruct((tokens, width), jnp.float32),
        in_specs=[pl.BlockSpec(memory_space=pl.ANY)] * count_rows
        + [vmem] * (count_rows + 1 + count_extra),
        out_specs=vmem,
        scratch_shapes=[
            pltpu.VMEM((2, count_rows, half_rows, hidden), jnp.bfloat16),
            pltpu.VMEM((2, half_rows, width), jnp.bfloat16),
            pltpu.VMEM((rounds, pairs, 2 * pair_rows, width), jnp.bfloat16),
            pltpu.VMEM((rounds * 4, tokens, width), jnp.bfloat16),
            pltpu.VMEM((rounds, tokens, width), jnp.bfloat16),
            pltpu.VMEM((rounds * 2, tokens, width), jnp.bfloat16),
            pltpu.VMEM((len(line), tokens, width), jnp.bfloat16),
            pltpu.SemaphoreType.DMA((copies_out,)),
            pltpu.SemaphoreType.DMA((copies_out,)),
            pltpu.SemaphoreType.DMA((2, count_rows)),
        ],
        compiler_params=pltpu.CompilerParams(
            collective_id=collective, has_side_effects=True, vmem_limit_bytes=60 * 1024 * 1024
        ),
        name=name,
    )(*rows, *weights, seats, *extra)


def by_tiles(width, tile):
    whole = width // TILE

    def step(number, carry):
        tile(pl.multiple_of(number * TILE, TILE), TILE)
        return carry

    lax.fori_loop(0, whole, step, 0)
    if width % TILE:
        tile(whole * TILE, width % TILE)


def expert_rows_kernel(own_block, cotangents, weights, biases, seats, shares, capacity, collective, name):
    experts, pairs = seats.shape[0], seats.shape[1]
    tokens, width = own_block.shape
    blocks = cotangents.shape[0]
    hidden = weights[0].shape[1]
    pair_rows = 2 * capacity
    half_rows = pairs * pair_rows
    row_count = experts * half_rows
    copies_out = copies("all")

    def body(*refs):
        (own_ref, cot_ref, gate, up, down, gate_bias, up_bias, seat_ref, share_ref) = refs[:9]
        (rows_out, grads_out, act_out, dgate_out, dup_out, gate_sum, up_sum, down_sum, held) = refs[9:18]
        (stage, lines, thin, pre, back, send, recv, local, load_sem, line_sem, thin_sem) = refs[18:]
        place = place_here()
        x, e, y = place
        greet = partners("all")
        barrier = pltpu.get_barrier_semaphore()
        for mask in greet:
            pl.semaphore_signal(barrier, inc=1, device_id=flip(place, mask), device_id_type=MESH)
        pl.semaphore_wait(barrier, len(greet))
        work = Gather("all", place, own_ref, held, send, recv, local)
        work.start()
        gate_sum[...] = jnp.zeros_like(gate_sum)
        up_sum[...] = jnp.zeros_like(up_sum)
        down_sum[...] = jnp.zeros_like(down_sum)
        halves = []
        for mask in work.masks:
            halves.append(flip(place, mask)[1])
            halves.append(flip(place, both(mask, SIBLING))[1])
        turnstile = {"load": 0, "line": 0}
        line_copies, thin_copies = [], []

        def fetch(source, part, pair):
            slot = pair % 2
            copy = pltpu.make_async_copy(
                source.at[pl.ds(pl.multiple_of((part * pairs + pair) * 2, 2), 2)],
                stage.at[slot],
                load_sem.at[slot],
            )
            copy.start()
            return copy

        def pick(source, part, scaled):
            slot = turnstile["line"] % 2
            turnstile["line"] += 1
            if len(line_copies) >= 2:
                line_copies[-2].wait()
            fetched = [fetch(source, part, pair) for pair in range(pairs)]
            for pair in range(pairs):
                fetched[pair].wait()
                hot = seat_hot(seat_ref[part, pair], capacity, jnp.float32)
                if scaled:
                    factor = jnp.sum(hot * share_ref[part, pair], axis=1, keepdims=True)
                hot = hot.astype(jnp.bfloat16)

                def tile(low, size):
                    area = pl.ds(low, size)
                    value = jnp.dot(
                        hot[:, :tokens], stage[pair % 2, 0, :, area], preferred_element_type=jnp.float32
                    ) + jnp.dot(
                        hot[:, tokens:], stage[pair % 2, 1, :, area], preferred_element_type=jnp.float32
                    )
                    if scaled:
                        value = value * factor
                    value = value.astype(jnp.bfloat16)
                    lines[slot, pair * pair_rows : (pair + 1) * pair_rows, area] = value
                    if scaled:
                        down_sum[:, area] += jnp.sum(value.astype(jnp.float32), axis=0, keepdims=True)

                by_tiles(width, tile)
            copy = pltpu.make_async_copy(
                lines.at[slot],
                (grads_out if scaled else rows_out).at[
                    pl.ds(pl.multiple_of(part * half_rows, 16), half_rows)
                ],
                line_sem.at[slot],
            )
            copy.start()
            line_copies.append(copy)
            return lines.at[slot]

        def backward(number):
            picked = pick(cot_ref, halves[number], True)
            back[number] = times_transposed(picked[...], down[...])

        def forward(number):
            if number % 2 == 0:
                if number == 0:
                    work.own.wait()
            else:
                work.passed(number // 2)
            part = halves[number]
            picked = pick(held, part, False)
            pre[0] = jnp.dot(picked[...], gate[...], preferred_element_type=jnp.float32)
            pre[1] = jnp.dot(picked[...], up[...], preferred_element_type=jnp.float32)
            slot = number % 2
            if number >= 2:
                for copy in thin_copies[-6:-3]:
                    copy.wait()

            def chunk(step, sums):
                area = pl.ds(pl.multiple_of(step * 16, 16), 16)
                gate_tanh = jnp.tanh((pre[0, area] + gate_bias[...]) * (1.0 / clip_level))
                up_tanh = jnp.tanh((pre[1, area] + up_bias[...]) * (1.0 / clip_level))
                gate_soft = clip_level * gate_tanh
                up_more = clip_level * up_tanh + 1.0
                bend = jax.nn.sigmoid(glu_alpha * gate_soft)
                glow = gate_soft * bend
                grad = back[number, area]
                dgate = grad * up_more * (bend + glu_alpha * glow * (1.0 - bend))
                dgate = (dgate * (1.0 - gate_tanh * gate_tanh)).astype(jnp.bfloat16)
                dup = (grad * glow * (1.0 - up_tanh * up_tanh)).astype(jnp.bfloat16)
                thin[slot, 0, area] = (glow * up_more).astype(jnp.bfloat16)
                thin[slot, 1, area] = dgate
                thin[slot, 2, area] = dup
                return sums[0] + dgate.astype(jnp.float32), sums[1] + dup.astype(jnp.float32)

            zero = jnp.zeros((16, hidden), jnp.float32)
            sums = lax.fori_loop(0, half_rows // 16, chunk, (zero, zero))
            gate_sum[...] += jnp.sum(sums[0], axis=0, keepdims=True)
            up_sum[...] += jnp.sum(sums[1], axis=0, keepdims=True)
            for item, goal in enumerate((act_out, dgate_out, dup_out)):
                copy = pltpu.make_async_copy(
                    thin.at[slot, item],
                    goal.at[pl.ds(pl.multiple_of(part * half_rows, 16), half_rows)],
                    thin_sem.at[slot, item],
                )
                copy.start()
                thin_copies.append(copy)

        work.plane(0)
        backward(0)
        backward(1)
        work.turn(0)
        work.plane(1)
        backward(2)
        work.close(0)
        backward(3)
        forward(0)
        work.turn(1)
        work.plane(2)
        forward(1)
        work.close(1)
        backward(4)
        backward(5)
        forward(2)
        work.turn(2)
        work.plane(3)
        forward(3)
        work.close(2)
        backward(6)
        work.turn(3)
        backward(7)
        work.close(3)
        for number in range(4, 8):
            forward(number)
        for copy in line_copies[-2:] + thin_copies[-6:]:
            copy.wait()
        work.finish()

    vmem, anywhere = pl.BlockSpec(memory_space=pltpu.VMEM), pl.BlockSpec(memory_space=pl.ANY)
    bf16, f32 = jnp.bfloat16, jnp.float32
    return pl.pallas_call(
        body,
        out_shape=[
            jax.ShapeDtypeStruct((row_count, width), bf16),
            jax.ShapeDtypeStruct((row_count, width), bf16),
            jax.ShapeDtypeStruct((row_count, hidden), bf16),
            jax.ShapeDtypeStruct((row_count, hidden), bf16),
            jax.ShapeDtypeStruct((row_count, hidden), bf16),
            jax.ShapeDtypeStruct((1, hidden), f32),
            jax.ShapeDtypeStruct((1, hidden), f32),
            jax.ShapeDtypeStruct((1, width), f32),
            jax.ShapeDtypeStruct((blocks, tokens, width), bf16),
        ],
        in_specs=[anywhere] * 2 + [vmem] * 7,
        out_specs=[anywhere] * 5 + [vmem] * 3 + [anywhere],
        scratch_shapes=[
            pltpu.VMEM((2, 2, tokens, width), bf16),
            pltpu.VMEM((2, half_rows, width), bf16),
            pltpu.VMEM((2, 3, half_rows, hidden), bf16),
            pltpu.VMEM((2, half_rows, hidden), f32),
            pltpu.VMEM((experts, half_rows, hidden), f32),
            pltpu.SemaphoreType.DMA((copies_out,)),
            pltpu.SemaphoreType.DMA((copies_out,)),
            pltpu.SemaphoreType.DMA((1,)),
            pltpu.SemaphoreType.DMA((2,)),
            pltpu.SemaphoreType.DMA((2,)),
            pltpu.SemaphoreType.DMA((2, 3)),
        ],
        compiler_params=pltpu.CompilerParams(
            collective_id=collective, has_side_effects=True, vmem_limit_bytes=60 * 1024 * 1024
        ),
        name=name,
    )(own_block, cotangents, *weights, *biases, seats, shares)


def pair_steps(mesh_exp, bit):
    return [(e, e ^ bit) for e in range(mesh_exp)]


def close_by(
    tokens,
    segments,
    routes,
    gate_share,
    attn_gain,
    query_weight,
    query_bias,
    key_weight,
    key_bias,
    value_weight,
    value_bias,
    output_weight,
    output_bias,
    sink_logits,
    moe_gain,
    gate_weight,
    gate_bias,
    up_weight,
    up_bias,
    down_weight,
    down_bias,
    cotangent,
):
    count_rows = tokens.shape[1]
    width = tokens.shape[2]
    head_count = sink_logits.shape[0]
    kv_count = key_bias.shape[0] // HD
    group = head_count // kv_count
    scale = 1.0 / math.sqrt(HD)
    experts = lax.axis_size("exp")
    devices = 4 * experts
    topk = routes.shape[2]
    capacity = count_rows * topk * 9 // (8 * experts)
    x, e, y = place_here()
    near_bit = lax.rem(lax.div(e, 2), 2)
    seq_len = 2 * count_rows
    own_cols = query_weight.shape[1]
    own_kv = key_weight.shape[1]

    chosen = routes[0].reshape(-1)
    expert_hot = (chosen[:, None] == jnp.arange(experts, dtype=jnp.int32)[None, :]).astype(
        jnp.int32
    )
    earlier = (jnp.cumsum(expert_hot, axis=0) - expert_hot).reshape(count_rows, topk, experts)
    named = expert_hot.reshape(count_rows, topk, experts)
    slot_table = jnp.sum((earlier + 1) * named, axis=1) - 1
    share_table = jnp.sum(named.astype(jnp.float32) * gate_share[0][:, :, None], axis=1)
    table = jnp.concatenate([slot_table.astype(jnp.float32).T, share_table.T], axis=0)

    resid = tokens[0].astype(jnp.float32)
    attn_norm, attn_norm_pull = jax.vjp(rms_apply, resid, attn_gain)
    normed = attn_norm.astype(jnp.bfloat16)
    kv_rows = jnp.concatenate([key_weight.T, value_weight.T], axis=0)
    tables, group_tokens, group_query, group_kv, group_output = exchange(
        [
            ("gather", "all", table),
            ("gather", "tokens", normed),
            ("gather", "heads", query_weight.T),
            ("gather", "heads", kv_rows),
            ("gather", "heads", output_weight),
        ],
        0,
        "gather_attention",
    )
    late_cotangent, group_tokens = lax.optimization_barrier((cotangent[0], group_tokens))
    all_cotangents = lax.all_gather(late_cotangent, ("exp", "seq", "dp"), axis=0, tiled=True)
    block_tokens = 4 * count_rows
    held_tokens = group_tokens.reshape(block_tokens, width)
    held_query = group_query.reshape(-1, width)
    held_key = group_kv[:, :own_kv].reshape(-1, width)
    held_value = group_kv[:, own_kv:].reshape(-1, width)
    held_output = group_output.reshape(-1, width)
    held_kv = 2
    held_heads = held_kv * group

    def own_part(vector):
        parts = vector.reshape(2, 2, 2, -1)
        parts = lax.dynamic_index_in_dim(parts, x, 0, keepdims=False)
        return lax.dynamic_index_in_dim(parts, near_bit, 1, keepdims=False)

    query_lin = times_transposed(held_tokens, held_query) + own_part(query_bias).reshape(-1)
    key_lin = times_transposed(held_tokens, held_key) + own_part(key_bias).reshape(-1)
    value_low = (
        times_transposed(held_tokens, held_value) + own_part(value_bias).reshape(-1)
    ).astype(jnp.bfloat16)
    position = jnp.arange(seq_len, dtype=jnp.int32)
    cosine, sine = rope_tables(position, HD)
    cosine = cosine[None, :, None]
    sine = sine[None, :, None]
    query_rot = rotate(query_lin.reshape(2, seq_len, held_heads, HD), cosine, sine).astype(
        jnp.bfloat16
    )
    key_rot = rotate(key_lin.reshape(2, seq_len, held_kv, HD), cosine, sine).astype(jnp.bfloat16)
    values = value_low.reshape(2, seq_len, held_kv, HD)
    mine = segments[0]
    other = lax.ppermute(mine, "exp", pair_steps(experts, 2))
    doc_ids = jnp.where(near_bit == 0, jnp.stack([mine, other]), jnp.stack([other, mine]))
    visible = (position[:, None] >= position[None, :])[None] & (
        doc_ids[:, :, None] == doc_ids[:, None, :]
    )
    query_group = query_rot.reshape(2, seq_len, held_kv, group, HD)
    sink_grid = own_part(sink_logits).reshape(held_kv, group)[None, :, :, None]

    def score_block():
        raw = (
            jnp.einsum("bqkgd,bskd->bkgqs", query_group, key_rot, preferred_element_type=jnp.float32)
            * scale
        )
        return jnp.where(visible[:, None, None], raw, masked_score)

    scores = score_block()
    peak = jnp.maximum(jnp.max(scores, axis=-1), sink_grid)
    total_mass = jnp.sum(jnp.exp(scores - peak[..., None]), axis=-1) + jnp.exp(sink_grid - peak)
    log_total = peak + jnp.log(total_mass)
    probs = jnp.exp(scores - log_total[..., None])
    mixed = jnp.einsum(
        "bkgqs,bskd->bqkgd", probs.astype(jnp.bfloat16), values, preferred_element_type=jnp.float32
    )
    mixed = mixed.reshape(block_tokens, held_heads * HD).astype(jnp.bfloat16)
    attn_part = jnp.dot(mixed, held_output, preferred_element_type=jnp.float32)
    (attn_out,) = exchange(
        [("scatter", "tokens", attn_part.astype(jnp.bfloat16).reshape(4, count_rows, width))],
        1,
        "sum_attention",
    )
    hidden = resid + (attn_out + output_bias)
    moe_norm, moe_norm_pull = jax.vjp(rms_apply, hidden, moe_gain)
    normed_moe = moe_norm.astype(jnp.bfloat16)

    def by_pairs(part):
        part = jnp.moveaxis(part.reshape(experts, 2, 2, experts, count_rows), 3, 0)
        return part.reshape(experts, experts, 2, 1, 2 * count_rows)

    slots = tables[:, :experts].astype(jnp.int32)
    second_block = jnp.arange(devices, dtype=jnp.int32)[:, None, None] % 2
    seats = by_pairs(jnp.where(slots >= 0, slots + capacity * second_block, -1))
    sibling = e + 1 - 2 * lax.rem(e, 2)
    seats = jnp.stack(
        [
            lax.dynamic_index_in_dim(seats, e, 0, keepdims=False),
            lax.dynamic_index_in_dim(seats, sibling, 0, keepdims=False),
        ]
    )
    shares = lax.dynamic_index_in_dim(by_pairs(tables[:, experts:]), e, 0, keepdims=False)
    (
        expert_rows,
        grad_rows,
        activation,
        gate_grad,
        up_grad,
        gate_bias_grad,
        up_bias_grad,
        down_bias_grad,
        _,
    ) = expert_rows_kernel(
        normed_moe,
        all_cotangents.reshape(devices, count_rows, width),
        (gate_weight[0], up_weight[0], down_weight[0]),
        (gate_bias, up_bias),
        seats[0],
        shares,
        capacity,
        2,
        "route_rows",
    )
    normed_moe_grad = expert_sums(
        "gradient", (gate_grad, up_grad), (gate_weight[0], up_weight[0]), seats, (), 3, "sum_rows"
    )
    moe_out = expert_sums(
        "result", (activation,), (down_weight[0],), seats, (shares, down_bias), 4, "sum_results"
    )
    output = (hidden + moe_out).astype(jnp.bfloat16)
    down_weight_grad = inner_rows(activation, grad_rows)
    gate_weight_grad = inner_rows(expert_rows, gate_grad)
    up_weight_grad = inner_rows(expert_rows, up_grad)

    upstream = cotangent[0].astype(jnp.float32)
    hidden_norm_grad, moe_gain_grad = moe_norm_pull(normed_moe_grad)
    hidden_grad = upstream + hidden_norm_grad
    attn_out_grad = hidden_grad.astype(jnp.bfloat16)
    output_bias_grad = jnp.sum(attn_out_grad.astype(jnp.float32), axis=0)
    (group_grad,) = exchange([("gather", "tokens", attn_out_grad)], 5, "gather_gradient")
    held_grad = group_grad.reshape(block_tokens, width)
    mixed_grad = (
        times_transposed(held_grad, held_output)
        .astype(jnp.bfloat16)
        .reshape(2, seq_len, held_kv, group, HD)
    )
    scores = score_block()
    probs = jnp.exp(scores - log_total[..., None])
    prob_grad = jnp.einsum(
        "bqkgd,bskd->bkgqs", mixed_grad, values, preferred_element_type=jnp.float32
    )
    delta = jnp.sum(probs * prob_grad, axis=-1)
    score_grad = (probs * (prob_grad - delta[..., None])).astype(jnp.bfloat16)
    sink_part = -jnp.sum(jnp.exp(sink_grid - log_total) * delta, axis=(0, 3))
    value_grad = jnp.einsum(
        "bkgqs,bqkgd->bskd", probs.astype(jnp.bfloat16), mixed_grad, preferred_element_type=jnp.float32
    )
    key_grad = (
        jnp.einsum("bkgqs,bqkgd->bskd", score_grad, query_group, preferred_element_type=jnp.float32)
        * scale
    )
    query_grad = (
        jnp.einsum("bkgqs,bskd->bqkgd", score_grad, key_rot, preferred_element_type=jnp.float32)
        * scale
    )
    query_lin_grad = (
        rotate(query_grad.reshape(2, seq_len, held_heads, HD), cosine, -sine)
        .reshape(block_tokens, held_heads * HD)
        .astype(jnp.bfloat16)
    )
    key_lin_grad = (
        rotate(key_grad, cosine, -sine).reshape(block_tokens, held_kv * HD).astype(jnp.bfloat16)
    )
    value_lin_grad = value_grad.reshape(block_tokens, held_kv * HD).astype(jnp.bfloat16)
    normed_part = (
        jnp.dot(query_lin_grad, held_query, preferred_element_type=jnp.float32)
        + jnp.dot(key_lin_grad, held_key, preferred_element_type=jnp.float32)
        + jnp.dot(value_lin_grad, held_value, preferred_element_type=jnp.float32)
    )
    query_rows = inner_rows(query_lin_grad, held_tokens).astype(jnp.bfloat16)
    key_rows = inner_rows(key_lin_grad, held_tokens).astype(jnp.bfloat16)
    value_rows = inner_rows(value_lin_grad, held_tokens).astype(jnp.bfloat16)
    output_rows = inner_rows(mixed, held_grad).astype(jnp.bfloat16)
    own_blocks = held_query.shape[0] // own_cols
    kv_part = jnp.concatenate(
        [
            key_rows.reshape(own_blocks, own_kv, width),
            value_rows.reshape(own_blocks, own_kv, width),
        ],
        axis=1,
    )
    small = jnp.concatenate(
        [
            jnp.sum(query_lin_grad.astype(jnp.float32), axis=0),
            jnp.sum(key_lin_grad.astype(jnp.float32), axis=0),
            jnp.sum(value_lin_grad.astype(jnp.float32), axis=0),
            sink_part.reshape(-1),
        ]
    )
    lengths = (held_heads * HD, held_kv * HD, held_kv * HD, held_heads)
    small = jnp.pad(small, (0, width - small.shape[0]))
    small = jnp.stack([moe_gain_grad, output_bias_grad, small])
    small = jnp.pad(small, ((0, 5), (0, 0)))
    normed_grad, query_owned, kv_owned, output_owned, all_small = exchange(
        [
            ("scatter", "tokens", normed_part.astype(jnp.bfloat16).reshape(4, count_rows, width)),
            ("scatter", "heads", query_rows.reshape(own_blocks, own_cols, width)),
            ("scatter", "heads", kv_part),
            ("scatter", "heads", output_rows.reshape(own_blocks, own_cols, width)),
            ("gather", "all", small),
        ],
        6,
        "sum_weights",
    )
    resid_norm_grad, attn_gain_grad = attn_norm_pull(normed_grad)
    input_grad = hidden_grad + resid_norm_grad
    gain_block = jnp.pad(attn_gain_grad[None], ((0, 7), (0, 0)))
    (all_gains,) = exchange([("gather", "all", gain_block)], 7, "gather_gain")
    by_heads = jnp.sum(all_small[:, 2].reshape(2, 2, 2, 2, 2, width), axis=(0, 2, 4))
    pieces = []
    for low, length in zip((0, lengths[0], sum(lengths[:2]), sum(lengths[:3])), lengths):
        piece = by_heads[:, :, low : low + length].reshape(2, 2, held_kv, -1)
        pieces.append(jnp.transpose(piece, (1, 2, 0, 3)).reshape(-1))
    query_bias_grad, key_bias_grad, value_bias_grad, sink_grad = pieces
    return (
        output[None],
        input_grad[None],
        jnp.sum(all_gains[:, 0], axis=0),
        query_owned.T,
        query_bias_grad,
        kv_owned[:own_kv].T,
        key_bias_grad,
        kv_owned[own_kv:].T,
        value_bias_grad,
        output_owned,
        jnp.sum(all_small[:, 1], axis=0),
        sink_grad,
        jnp.sum(all_small[:, 0], axis=0),
        gate_weight_grad[None],
        gate_bias_grad,
        up_weight_grad[None],
        up_bias_grad,
        down_weight_grad[None],
        down_bias_grad,
    )


def solution(mesh):
    placed = (
        P(("exp", "dp"), "seq", None),
        P(("exp", "dp"), None),
        P(("exp", "dp"), "seq", None),
        P(("exp", "dp"), "seq", None),
        P(),
        P(None, ("seq", "exp", "dp")),
        P(),
        P(None, ("seq", "exp", "dp")),
        P(),
        P(None, ("seq", "exp", "dp")),
        P(),
        P(("seq", "exp", "dp"), None),
        P(),
        P(),
        P(),
        P("exp", None, ("seq", "dp")),
        P("exp", ("seq", "dp")),
        P("exp", None, ("seq", "dp")),
        P("exp", ("seq", "dp")),
        P("exp", ("seq", "dp"), None),
        P("exp", None),
        P(("exp", "dp"), "seq", None),
    )
    shape = mesh.shape
    small = shape["seq"] == 2 and shape["dp"] == 2 and shape["exp"] == 8
    return jax.shard_map(
        close_by if small else local,
        mesh=mesh,
        in_specs=placed,
        out_specs=(
            P(("exp", "dp"), "seq", None),
            P(("exp", "dp"), "seq", None),
            P(),
            P(None, ("seq", "exp", "dp")),
            P(),
            P(None, ("seq", "exp", "dp")),
            P(),
            P(None, ("seq", "exp", "dp")),
            P(),
            P(("seq", "exp", "dp"), None),
            P(),
            P(),
            P(),
            P("exp", None, ("seq", "dp")),
            P("exp", ("seq", "dp")),
            P("exp", None, ("seq", "dp")),
            P("exp", ("seq", "dp")),
            P("exp", ("seq", "dp"), None),
            P("exp", None),
        ),
        check_vma=False,
    )
```

```python
import math

import jax
import jax.numpy as jnp
from jax import lax
from jax.experimental import pallas as pl
from jax.experimental.pallas import tpu as pltpu
from jax.sharding import PartitionSpec as P

HD = 64


highest = lax.Precision.HIGHEST
norm_eps = 1e-05
rope_base = 150000.0
clip_level = 7.0
glu_alpha = 1.702
masked_score = -1000000000.0


def rms_apply(values, gain):
    return values * lax.rsqrt(jnp.mean(values * values, axis=-1, keepdims=True) + norm_eps) * gain


def rope_tables(position, width):
    exponent = jnp.arange(width // 2).astype(jnp.float32) * (2.0 / width)
    freqs = jnp.exp(-math.log(rope_base) * exponent)
    angles = position.astype(jnp.float32)[:, None] * freqs[None, :]
    return (jnp.cos(angles), jnp.sin(angles))


def rotate(values, cosine, sine):
    half = values.shape[-1] // 2
    first = values[..., :half]
    second = values[..., half:]
    return jnp.concatenate(
        [first * cosine - second * sine, second * cosine + first * sine], axis=-1
    )


def swiglu(gate_pre, up_pre):
    gate_soft = clip_level * jnp.tanh(gate_pre / clip_level)
    up_soft = clip_level * jnp.tanh(up_pre / clip_level)
    return gate_soft * jax.nn.sigmoid(glu_alpha * gate_soft) * (up_soft + 1.0)


def inner_rows(left, right):
    return lax.dot_general(
        left, right, (((0,), (0,)), ((), ())), preferred_element_type=jnp.float32
    )


def times_transposed(left, right):
    return lax.dot_general(
        left, right, (((1,), (1,)), ((), ())), preferred_element_type=jnp.float32
    )


def to_experts(outgoing):
    width = outgoing.shape[2]
    arrived = lax.all_to_all(outgoing, "exp", split_axis=0, concat_axis=0, tiled=True)
    arrived = lax.all_gather(arrived, ("seq", "dp"), axis=0, tiled=True)
    return arrived.reshape(-1, width)


def results_back(activation, down_matrix, down_vector, experts, capacity):
    width = down_matrix.shape[1]
    share = lax.psum_scatter(
        jnp.dot(activation, down_matrix, preferred_element_type=jnp.float32).astype(jnp.bfloat16),
        ("seq", "dp"),
        scatter_dimension=0,
        tiled=True,
    ).astype(jnp.float32)
    finished = (share + down_vector).astype(jnp.bfloat16).reshape(experts, capacity, width)
    return lax.all_to_all(finished, "exp", split_axis=0, concat_axis=0, tiled=True)


def gradients_back(gate_grad, up_grad, gate_matrix, up_matrix, experts, capacity):
    share = lax.psum_scatter(
        times_transposed(gate_grad, gate_matrix) + times_transposed(up_grad, up_matrix),
        ("seq", "dp"),
        scatter_dimension=0,
        tiled=True,
    )
    return lax.all_to_all(
        share.reshape(experts, capacity, share.shape[1]),
        "exp",
        split_axis=0,
        concat_axis=0,
        tiled=True,
    )


def local(
    tokens,
    segments,
    routes,
    gate_share,
    attn_gain,
    query_weight,
    query_bias,
    key_weight,
    key_bias,
    value_weight,
    value_bias,
    output_weight,
    output_bias,
    sink_logits,
    moe_gain,
    gate_weight,
    gate_bias,
    up_weight,
    up_bias,
    down_weight,
    down_bias,
    cotangent,
):
    count_rows = tokens.shape[1]
    width = tokens.shape[2]
    head_count = sink_logits.shape[0]
    kv_count = key_bias.shape[0] // HD
    group = head_count // kv_count
    scale = 1.0 / math.sqrt(HD)
    experts = lax.axis_size("exp")
    topk = routes.shape[2]
    capacity = count_rows * topk * 9 // (8 * experts)
    resid = tokens[0].astype(jnp.float32)
    full_query, full_key, full_value, full_output = (
        lax.all_gather(query_weight, ("seq", "exp", "dp"), axis=1, tiled=True),
        lax.all_gather(key_weight, ("seq", "exp", "dp"), axis=1, tiled=True),
        lax.all_gather(value_weight, ("seq", "exp", "dp"), axis=1, tiled=True),
        lax.all_gather(output_weight, ("seq", "exp", "dp"), axis=0, tiled=True),
    )
    attn_norm, attn_norm_pull = jax.vjp(rms_apply, resid, attn_gain)
    normed = attn_norm.astype(jnp.bfloat16)
    query_lin = jnp.dot(normed, full_query, preferred_element_type=jnp.float32) + query_bias
    key_lin = jnp.dot(normed, full_key, preferred_element_type=jnp.float32) + key_bias
    value_low = (
        jnp.dot(normed, full_value, preferred_element_type=jnp.float32) + value_bias
    ).astype(jnp.bfloat16)
    offset = lax.axis_index("seq") * count_rows
    position = offset + jnp.arange(count_rows, dtype=jnp.int32)
    cosine, sine = rope_tables(position, HD)
    cosine = cosine[:, None]
    sine = sine[:, None]
    query_rot = rotate(query_lin.reshape(count_rows, head_count, HD), cosine, sine).astype(
        jnp.bfloat16
    )
    key_rot = rotate(key_lin.reshape(count_rows, kv_count, HD), cosine, sine).astype(jnp.bfloat16)
    all_keys, all_values = (
        lax.all_gather(key_rot.reshape(count_rows, kv_count * HD), "seq", axis=0, tiled=True),
        lax.all_gather(value_low, "seq", axis=0, tiled=True),
    )
    seq_len = all_keys.shape[0]
    all_keys = all_keys.reshape(seq_len, kv_count, HD)
    all_values = all_values.reshape(seq_len, kv_count, HD)
    doc_ids = segments[0]
    own_ids = lax.dynamic_slice_in_dim(doc_ids, offset, count_rows, 0)
    key_place = jnp.arange(seq_len, dtype=jnp.int32)
    visible = (position[:, None] >= key_place[None, :]) & (own_ids[:, None] == doc_ids[None, :])
    query_group = query_rot.reshape(count_rows, kv_count, group, HD)
    sink_grid = sink_logits.reshape(kv_count, group)[:, :, None]

    def score_block():
        raw = (
            jnp.einsum("qkgd,skd->kgqs", query_group, all_keys, preferred_element_type=jnp.float32)
            * scale
        )
        return jnp.where(visible[None, None], raw, masked_score)

    scores = score_block()
    peak = jnp.maximum(jnp.max(scores, axis=-1), sink_grid)
    total = jnp.sum(jnp.exp(scores - peak[..., None]), axis=-1) + jnp.exp(sink_grid - peak)
    log_total = peak + jnp.log(total)
    probs = jnp.exp(scores - log_total[..., None])
    mixed = jnp.einsum(
        "kgqs,skd->qkgd", probs.astype(jnp.bfloat16), all_values, preferred_element_type=jnp.float32
    )
    mixed = mixed.reshape(count_rows, head_count * HD).astype(jnp.bfloat16)
    attn_out = jnp.dot(mixed, full_output, preferred_element_type=jnp.float32) + output_bias
    hidden = resid + attn_out
    moe_norm, moe_norm_pull = jax.vjp(rms_apply, hidden, moe_gain)
    normed_moe = moe_norm.astype(jnp.bfloat16)
    chosen = routes[0].reshape(-1)
    expert_hot = (chosen[:, None] == jnp.arange(experts, dtype=jnp.int32)[None, :]).astype(
        jnp.int32
    )
    slot_index = jnp.sum((jnp.cumsum(expert_hot, axis=0) - expert_hot) * expert_hot, axis=1)
    target = chosen * capacity + slot_index
    slot_hot = (
        target[:, None] == jnp.arange(experts * capacity, dtype=jnp.int32)[None, :]
    ).reshape(count_rows, topk, experts * capacity)
    dispatch = jnp.sum(slot_hot.astype(jnp.bfloat16), axis=1)
    weighted = jnp.sum(slot_hot.astype(jnp.float32) * gate_share[0][:, :, None], axis=1)
    outgoing = jnp.einsum("ts,td->sd", dispatch, normed_moe, preferred_element_type=jnp.float32)
    outgoing = outgoing.astype(jnp.bfloat16).reshape(experts, capacity, width)
    expert_rows = to_experts(outgoing)
    gate_pre = (
        jnp.dot(expert_rows, gate_weight[0], preferred_element_type=jnp.float32) + gate_bias[0]
    )
    up_pre = jnp.dot(expert_rows, up_weight[0], preferred_element_type=jnp.float32) + up_bias[0]
    act_full, swiglu_pull = jax.vjp(swiglu, gate_pre, up_pre)
    activation = act_full.astype(jnp.bfloat16)
    returned = results_back(activation, down_weight[0], down_bias[0], experts, capacity)
    moe_out = jnp.dot(
        weighted, returned.reshape(experts * capacity, width).astype(jnp.float32), precision=highest
    )
    output = (hidden + moe_out).astype(jnp.bfloat16)
    upstream = cotangent[0].astype(jnp.float32)
    grad_slots = jnp.einsum("ts,td->sd", weighted, upstream, precision=highest)
    grad_slots = grad_slots.astype(jnp.bfloat16).reshape(experts, capacity, width)
    grad_rows = to_experts(grad_slots)
    down_bias_grad = jnp.sum(grad_rows.astype(jnp.float32), axis=0)
    down_weight_grad = inner_rows(activation, grad_rows)
    act_grad = times_transposed(grad_rows, down_weight[0])
    gate_grad_full, up_grad_full = swiglu_pull(act_grad)
    gate_grad = gate_grad_full.astype(jnp.bfloat16)
    up_grad = up_grad_full.astype(jnp.bfloat16)
    gate_bias_grad = jnp.sum(gate_grad.astype(jnp.float32), axis=0)
    up_bias_grad = jnp.sum(up_grad.astype(jnp.float32), axis=0)
    gate_weight_grad = inner_rows(expert_rows, gate_grad)
    up_weight_grad = inner_rows(expert_rows, up_grad)
    rows_grad = gradients_back(gate_grad, up_grad, gate_weight[0], up_weight[0], experts, capacity)
    normed_moe_grad = jnp.einsum(
        "ts,sd->td",
        dispatch.astype(jnp.float32),
        rows_grad.reshape(experts * capacity, width),
        precision=highest,
    )
    hidden_norm_grad, moe_gain_grad = moe_norm_pull(normed_moe_grad)
    hidden_grad = upstream + hidden_norm_grad
    attn_out_grad = hidden_grad.astype(jnp.bfloat16)
    output_bias_grad = jnp.sum(attn_out_grad.astype(jnp.float32), axis=0)
    full_query, full_key, full_value, full_output = (
        lax.all_gather(query_weight, ("seq", "exp", "dp"), axis=1, tiled=True),
        lax.all_gather(key_weight, ("seq", "exp", "dp"), axis=1, tiled=True),
        lax.all_gather(value_weight, ("seq", "exp", "dp"), axis=1, tiled=True),
        lax.all_gather(output_weight, ("seq", "exp", "dp"), axis=0, tiled=True),
    )
    mixed_grad = (
        times_transposed(attn_out_grad, full_output)
        .astype(jnp.bfloat16)
        .reshape(count_rows, kv_count, group, HD)
    )
    scores = score_block()
    probs = jnp.exp(scores - log_total[..., None])
    prob_grad = jnp.einsum(
        "qkgd,skd->kgqs", mixed_grad, all_values, preferred_element_type=jnp.float32
    )
    delta = jnp.sum(probs * prob_grad, axis=-1)
    score_grad = (probs * (prob_grad - delta[..., None])).astype(jnp.bfloat16)
    sink_grad = -jnp.sum(jnp.exp(sink_grid - log_total) * delta, axis=-1).reshape(head_count)
    value_grad = jnp.einsum(
        "kgqs,qkgd->skd", probs.astype(jnp.bfloat16), mixed_grad, preferred_element_type=jnp.float32
    )
    key_grad = (
        jnp.einsum("kgqs,qkgd->skd", score_grad, query_group, preferred_element_type=jnp.float32)
        * scale
    )
    query_grad = (
        jnp.einsum("kgqs,skd->qkgd", score_grad, all_keys, preferred_element_type=jnp.float32)
        * scale
    )
    key_share, value_share = (
        lax.psum_scatter(
            key_grad.reshape(seq_len, kv_count * HD), "seq", scatter_dimension=0, tiled=True
        ),
        lax.psum_scatter(
            value_grad.reshape(seq_len, kv_count * HD), "seq", scatter_dimension=0, tiled=True
        ),
    )
    query_lin_grad = (
        rotate(query_grad.reshape(count_rows, head_count, HD), cosine, -sine)
        .reshape(count_rows, head_count * HD)
        .astype(jnp.bfloat16)
    )
    key_lin_grad = (
        rotate(key_share.reshape(count_rows, kv_count, HD), cosine, -sine)
        .reshape(count_rows, kv_count * HD)
        .astype(jnp.bfloat16)
    )
    value_lin_grad = value_share.astype(jnp.bfloat16)
    query_bias_grad = jnp.sum(query_lin_grad.astype(jnp.float32), axis=0)
    key_bias_grad = jnp.sum(key_lin_grad.astype(jnp.float32), axis=0)
    value_bias_grad = jnp.sum(value_lin_grad.astype(jnp.float32), axis=0)
    normed_grad = (
        times_transposed(query_lin_grad, full_query)
        + times_transposed(key_lin_grad, full_key)
        + times_transposed(value_lin_grad, full_value)
    )
    resid_norm_grad, attn_gain_grad = attn_norm_pull(normed_grad)
    input_grad = hidden_grad + resid_norm_grad
    query_weight_grad = inner_rows(normed, query_lin_grad)
    key_weight_grad = inner_rows(normed, key_lin_grad)
    value_weight_grad = inner_rows(normed, value_lin_grad)
    output_weight_grad = inner_rows(mixed, attn_out_grad)
    query_owned, key_owned, value_owned, output_owned = (
        lax.psum_scatter(query_weight_grad, ("seq", "exp", "dp"), scatter_dimension=1, tiled=True),
        lax.psum_scatter(key_weight_grad, ("seq", "exp", "dp"), scatter_dimension=1, tiled=True),
        lax.psum_scatter(value_weight_grad, ("seq", "exp", "dp"), scatter_dimension=1, tiled=True),
        lax.psum_scatter(output_weight_grad, ("seq", "exp", "dp"), scatter_dimension=0, tiled=True),
    )
    summed = lax.psum(
        (
            attn_gain_grad,
            query_bias_grad,
            key_bias_grad,
            value_bias_grad,
            output_bias_grad,
            sink_grad,
            moe_gain_grad,
        ),
        ("seq", "exp", "dp"),
    )
    return (
        output[None],
        input_grad[None],
        summed[0],
        query_owned,
        summed[1],
        key_owned,
        summed[2],
        value_owned,
        summed[3],
        output_owned,
        summed[4],
        summed[5],
        summed[6],
        gate_weight_grad[None],
        gate_bias_grad[None],
        up_weight_grad[None],
        up_bias_grad[None],
        down_weight_grad[None],
        down_bias_grad[None],
    )

MESH = pl.DeviceIdType.MESH
HERE = (0, 0, 0)
SIBLING = (0, 1, 0)
ACROSS = (1, 0, 0)
ALONG = (0, 0, 1)
NEAR = (0, 2, 0)
FAR = (0, 4, 0)
ENDS = (0, 6, 0)


def flip(place, mask):
    x, e, y = place
    if mask[0]:
        x = 1 - x
    if mask[2]:
        y = 1 - y
    step = 0
    for bit in (1, 2, 4):
        if mask[1] & bit:
            step = step + bit - 2 * bit * lax.rem(lax.div(e, bit), 2)
    return x, e + step, y


def both(left, right):
    return tuple(a ^ b for a, b in zip(left, right))


def place_here():
    return lax.axis_index("seq"), lax.axis_index("exp"), lax.axis_index("dp")


def block_of_all(place):
    x, e, y = place
    return (e * 2 + x) * 2 + y


def block_of_tokens(place):
    x, e, y = place
    return lax.rem(lax.div(e, 2), 2) * 2 + x


def block_of_heads(place):
    x, e, y = place
    return (lax.div(e, 4) * 2 + lax.rem(e, 2)) * 2 + y


GROUPS = {
    "all": (block_of_all, 32, SIBLING, ACROSS, ALONG, (NEAR, FAR, ENDS), 0.5),
    "tokens": (block_of_tokens, 4, None, ACROSS, NEAR, (), 0.5),
    "heads": (block_of_heads, 8, SIBLING, FAR, ALONG, (), 1.0),
}


def partners(group):
    _, _, sibling, first, second, line, _ = GROUPS[group]
    return ([sibling] if sibling else []) + [first, second] + list(line)


def copies(group):
    _, _, sibling, _, _, line, _ = GROUPS[group]
    rounds = 1 + len(line)
    return rounds * (8 if sibling else 4) + len(line)


class Sender:
    def __init__(self, place, send, recv):
        self.place, self.send, self.recv, self.started = place, send, recv, []

    def push(self, source, target, mask):
        number = len(self.started)
        copy = pltpu.make_async_remote_copy(
            src_ref=source,
            dst_ref=target,
            send_sem=self.send.at[number],
            recv_sem=self.recv.at[number],
            device_id=flip(self.place, mask),
            device_id_type=MESH,
        )
        copy.start()
        self.started.append(copy)
        return copy

    def finish(self):
        for copy in self.started:
            copy.wait_send()


class Gather:
    def __init__(self, group, place, source, result, send, recv, local, share=None):
        self.index, _, self.sibling, self.first, self.second, self.line, usual = GROUPS[group]
        self.place, self.source, self.result = place, source, result
        self.rows = source.shape[0]
        share = usual if share is None else share
        self.cut = int(self.rows * share) // 16 * 16
        self.out = Sender(place, send, recv)
        self.own = pltpu.make_async_copy(source, self.at(HERE), local.at[0])
        self.masks = [HERE] + list(self.line)
        self.reach, self.ways, self.halves = {}, {}, {}
        self.tails = {step: [] for step in range(len(self.masks))}

    def at(self, mask):
        return self.result.at[self.index(flip(self.place, mask))]

    def start(self):
        self.own.start()
        self.reached(self.line[:2])

    def reached(self, line):
        for mask in line:
            self.reach[mask] = self.out.push(self.source, self.at(HERE), mask)

    def pass_on(self, step, block, place):
        if self.sibling:
            self.tails[step].append(self.out.push(block, place, self.sibling))

    def plane(self, step):
        mask = self.masks[step]
        if step:
            self.reach[mask].wait_recv()
        block = self.at(mask) if step else self.source
        self.ways[step] = (
            self.out.push(block, self.at(mask), self.first),
            self.out.push(block, self.at(mask), self.second),
        )
        self.pass_on(step, block, self.at(mask))
        if step == 1:
            self.reached(self.line[2:])

    def turn(self, step):
        halves = []
        mask, cut = self.masks[step], self.cut
        self.ways[step][0].wait_recv()
        seen = self.at(both(mask, self.first))
        if cut:
            halves.append(self.out.push(seen.at[:cut], seen.at[:cut], self.second))
        self.pass_on(step, seen, seen)
        self.ways[step][1].wait_recv()
        seen = self.at(both(mask, self.second))
        if cut < self.rows:
            halves.append(self.out.push(seen.at[cut:], seen.at[cut:], self.first))
        self.pass_on(step, seen, seen)
        self.halves[step] = halves

    def close(self, step):
        for half in self.halves[step]:
            half.wait_recv()
        seen = self.at(both(self.masks[step], both(self.first, self.second)))
        self.pass_on(step, seen, seen)

    def passed(self, step):
        for copy in self.tails[step]:
            copy.wait_recv()

    def finish(self):
        self.out.finish()


def gather_steps(group, place, source, result, send, recv, local):
    work = Gather(group, place, source, result, send, recv, local)
    work.start()
    count = len(work.masks)
    for step in range(count + 2):
        if step < count:
            work.plane(step)
            yield
        if 0 <= step - 1 < count:
            work.turn(step - 1)
            yield
        if 0 <= step - 2 < count:
            work.close(step - 2)
            yield
    for step in range(count):
        work.passed(step)
    work.own.wait()
    work.finish()


def total(parts, low, high, store):
    def body(step, carry):
        rows = pl.ds(pl.multiple_of(low + step * 16, 16), 16)
        value = parts[0][rows].astype(jnp.float32)
        for part in parts[1:]:
            value = value + part[rows].astype(jnp.float32)
        store[rows] = value.astype(store.dtype)
        return carry

    if high > low:
        lax.fori_loop(0, (high - low) // 16, body, 0)


def scatter_steps(group, place, source, result, own, mate, side, arrive, ends, send, recv, local):
    index, _, sibling, first, second, line, share = GROUPS[group]
    rows = result.shape[0]
    cut = int(rows * (1.0 - share)) // 16 * 16
    corner = both(first, second)
    out = Sender(place, send, recv)
    masks = list(line)[::-1] + [HERE]
    corners = (corner, first, second, HERE)
    fetched, sent = {}, {}
    for step, mask in enumerate(masks):
        for spot, shift in enumerate(corners):
            seat = step * 4 + spot
            goal = both(mask, shift)
            if sibling:
                sent[seat] = out.push(
                    source.at[index(flip(place, both(goal, sibling)))], mate.at[seat], sibling
                )
            fetched[seat] = pltpu.make_async_copy(
                source.at[index(flip(place, goal))], own.at[seat], local.at[seat]
            )
            fetched[seat].start()
    yield

    def ready(seat):
        fetched[seat].wait()
        if sibling:
            sent[seat].wait_recv()
            return [own.at[seat], mate.at[seat]]
        return [own.at[seat]]

    def outward(step):
        seat = step * 4
        parts = ready(seat)
        if sibling:
            total(parts, 0, rows, own.at[seat])
        halves = []
        if cut:
            halves.append(out.push(own.at[seat].at[:cut], side.at[step].at[:cut], first))
        if cut < rows:
            halves.append(out.push(own.at[seat].at[cut:], side.at[step].at[cut:], second))
        return halves

    def inward(step, halves):
        by_first, by_second = ready(step * 4 + 1), ready(step * 4 + 2)
        for half in halves:
            half.wait_recv()
        total(by_second + [side.at[step]], 0, cut, own.at[step * 4 + 2])
        total(by_first + [side.at[step]], cut, rows, own.at[step * 4 + 1])
        if sibling:
            total(by_second, cut, rows, own.at[step * 4 + 2])
            total(by_first, 0, cut, own.at[step * 4 + 1])
        return (
            out.push(own.at[step * 4 + 1], arrive.at[step * 2], first),
            out.push(own.at[step * 4 + 2], arrive.at[step * 2 + 1], second),
        )

    def close(step, ways):
        parts = ready(step * 4 + 3)
        for way in ways:
            way.wait_recv()
        parts = parts + [arrive.at[step * 2], arrive.at[step * 2 + 1]]
        if masks[step] != HERE:
            total(parts, 0, rows, own.at[step * 4 + 3])
            return out.push(own.at[step * 4 + 3], ends.at[step], masks[step])
        for number, copy in enumerate(reach):
            copy.wait_recv()
            parts.append(ends.at[number])
        total(parts, 0, rows, result)

    halves, ways, reach = {}, {}, []
    for step in range(len(masks) + 2):
        if step < len(masks):
            halves[step] = outward(step)
            yield
        if 0 <= step - 1 < len(masks):
            ways[step - 1] = inward(step - 1, halves[step - 1])
            yield
        if 0 <= step - 2 < len(masks):
            copy = close(step - 2, ways[step - 2])
            if copy is not None:
                reach.append(copy)
            yield
    out.finish()


def exchange(jobs, collective, name):
    in_specs, out_specs, out_shape, scratch, plans = [], [], [], [], []
    for kind, group, array in jobs:
        _, blocks, sibling, _, _, line, _ = GROUPS[group]
        rounds = 1 + len(line)
        in_specs.append(pl.BlockSpec(memory_space=pl.ANY))
        sems = [pltpu.SemaphoreType.DMA((copies(group),)), pltpu.SemaphoreType.DMA((copies(group),))]
        if kind == "gather":
            shape = array.shape
            out_shape.append(jax.ShapeDtypeStruct((blocks,) + shape, array.dtype))
            out_specs.append(pl.BlockSpec(memory_space=pl.ANY))
            need = sems + [pltpu.SemaphoreType.DMA((1,))]
        else:
            shape = array.shape[1:]
            out_shape.append(jax.ShapeDtypeStruct(shape, jnp.float32))
            out_specs.append(pl.BlockSpec(memory_space=pltpu.VMEM))
            slots = [4 * rounds, 4 * rounds if sibling else 1, rounds, 2 * rounds, max(1, rounds - 1)]
            if not sibling:
                slots[1] = 1
            need = [
                pltpu.VMEM((count,) + (shape if count > 1 or number != 1 else (16, 128)), array.dtype)
                for number, count in enumerate(slots)
            ]
            need = need + sems + [pltpu.SemaphoreType.DMA((4 * rounds,))]
        plans.append((kind, group, len(need)))
        scratch += need
    greet = []
    for _, group, _ in jobs:
        greet += [mask for mask in partners(group) if mask not in greet]

    def body(*refs):
        count = len(jobs)
        sources, results, rest = refs[:count], refs[count : 2 * count], list(refs[2 * count :])
        place = place_here()
        barrier = pltpu.get_barrier_semaphore()
        for mask in greet:
            pl.semaphore_signal(barrier, inc=1, device_id=flip(place, mask), device_id_type=MESH)
        pl.semaphore_wait(barrier, len(greet))
        running = []
        for number, (kind, group, width) in enumerate(plans):
            own, rest = rest[:width], rest[width:]
            steps = gather_steps if kind == "gather" else scatter_steps
            running.append(steps(group, place, sources[number], results[number], *own))
        while running:
            for steps in list(running):
                if next(steps, "end") == "end":
                    running.remove(steps)

    return pl.pallas_call(
        body,
        out_shape=out_shape,
        in_specs=in_specs,
        out_specs=out_specs,
        scratch_shapes=scratch,
        compiler_params=pltpu.CompilerParams(
            collective_id=collective, has_side_effects=True, vmem_limit_bytes=60 * 1024 * 1024
        ),
        name=name,
    )(*[array for _, _, array in jobs])


def by_tiles(width, tile, parts=2):
    size = -(-width // (128 * parts)) * 128
    for low in range(0, width, size):
        tile(low, min(size, width - low))


def seat_hot(seats, capacity, kind):
    lines = lax.broadcasted_iota(jnp.int32, (2 * capacity, seats.shape[-1]), 0)
    return (lines == seats).astype(kind)


def expert_sums(kind, rows, weights, seats, extra, collective, name, products=()):
    experts, pairs = seats.shape[1], seats.shape[2]
    thick = seats.shape[4]
    tokens = seats.shape[4] // 2
    half_rows = rows[0].shape[0] // experts
    pair_rows = half_rows // pairs
    capacity = pair_rows // 2
    hidden = rows[0].shape[1]
    width = weights[0].shape[1]
    first, second, line = ACROSS, ALONG, (ENDS, FAR, NEAR)
    masks = list(line) + [HERE]
    rounds = len(masks)
    cut = tokens // 2
    count_rows, count_extra = len(rows), len(extra)
    copies_out = rounds * (pairs + 4) + len(line)

    def body(*refs):
        refs = list(refs)
        left = refs[:count_rows]
        wide = refs[count_rows : 2 * count_rows]
        seat_ref = refs[2 * count_rows]
        more = refs[2 * count_rows + 1 : 2 * count_rows + 1 + count_extra]
        rest = refs[2 * count_rows + 1 + count_extra :]
        thin_wide, rest = rest[: 2 * len(products)], rest[2 * len(products) :]
        result, rest = rest[0], rest[1:]
        made, rest = rest[: len(products)], rest[len(products) :]
        staged, away, joined, own, side, arrive, ends, send, recv, local = rest[:10]
        if products:
            thin_stage, wide_stage, gross, product_sem, made_sem = rest[10:]
        place = place_here()
        x, e, y = place
        greet = [SIBLING, first, second] + list(line)
        barrier = pltpu.get_barrier_semaphore()
        for mask in greet:
            pl.semaphore_signal(barrier, inc=1, device_id=flip(place, mask), device_id_type=MESH)
        pl.semaphore_wait(barrier, len(greet))
        out = Sender(place, send, recv)

        def block(mask):
            there = flip(place, mask)
            return there[0] * 2 + there[2]

        halves = []
        for mask in masks:
            halves.append((flip(place, both(mask, SIBLING))[1], True))
            halves.append((flip(place, mask)[1], False))
        loads = {}

        def load(number):
            if number < len(halves):
                begin = pl.multiple_of(halves[number][0] * half_rows, 16)
                for item in range(count_rows):
                    copy = pltpu.make_async_copy(
                        left[item].at[pl.ds(begin, half_rows)],
                        staged.at[number % 2, item],
                        local.at[number % 2, item],
                    )
                    copy.start()
                    loads[number, item] = copy

        def make(number, store):
            load(number + 1)
            for item in range(count_rows):
                loads[number, item].wait()
            values = [staged[number % 2, item] for item in range(count_rows)]
            if kind == "result":
                part = halves[number][0]
                factors = []
                for pair in range(pairs):
                    hot = seat_hot(seat_ref[0, part, pair], capacity, jnp.float32)
                    factors.append(jnp.sum(hot * more[0][part, pair], axis=1, keepdims=True))
                factor = jnp.concatenate(factors, axis=0)
                once = jnp.where((x == 0) & (y == 0), 1.0, 0.0).astype(jnp.float32)

            def tile(low, size):
                area = pl.ds(low, size)
                value = jnp.dot(values[0], wide[0][:, area], preferred_element_type=jnp.float32)
                if kind == "gradient":
                    value += jnp.dot(values[1], wide[1][:, area], preferred_element_type=jnp.float32)
                else:
                    value = (value + once * more[1][:, area]) * factor
                store(low, size, value.astype(jnp.bfloat16))

            by_tiles(width, tile)

        def to_sibling(step):
            slot = step % 2

            def store(low, size, value):
                away[slot, :, pl.ds(low, size)] = value

            if step >= 2:
                for copy in sent[step - 2]:
                    copy.wait_send()
            make(2 * step, store)
            sent[step] = [
                out.push(
                    away.at[slot].at[pair * pair_rows : (pair + 1) * pair_rows],
                    joined.at[step, pair].at[pair_rows : 2 * pair_rows],
                    SIBLING,
                )
                for pair in range(pairs)
            ]

        def to_here(step):
            def store(low, size, value):
                for pair in range(pairs):
                    joined[step, pair, :pair_rows, pl.ds(low, size)] = value[
                        pair * pair_rows : (pair + 1) * pair_rows
                    ]

            make(2 * step + 1, store)

        def combine(step):
            for copy in sent[step]:
                copy.wait_recv()
            part = halves[2 * step + 1][0]
            for pair in range(pairs):
                hot = jnp.concatenate(
                    [seat_hot(seat_ref[mate, part, pair], capacity, jnp.bfloat16) for mate in range(2)],
                    axis=0,
                )

                def tile(low, size):
                    value = inner_rows(hot, joined[step, pair, :, pl.ds(low, size)])
                    value = value.astype(jnp.bfloat16)
                    own[step * 4 + pair * 2, :, pl.ds(low, size)] = value[:tokens]
                    own[step * 4 + pair * 2 + 1, :, pl.ds(low, size)] = value[tokens:]

                by_tiles(width, tile)

        def outward(step):
            corner = own.at[step * 4 + block(both(first, second))]
            return [
                out.push(corner.at[:cut], side.at[step].at[:cut], first),
                out.push(corner.at[cut:], side.at[step].at[cut:], second),
            ]

        def inward(step, parts):
            by_first = own.at[step * 4 + block(first)]
            by_second = own.at[step * 4 + block(second)]
            for part in parts:
                part.wait_recv()
            total([by_second, side.at[step]], 0, cut, by_second)
            total([by_first, side.at[step]], cut, tokens, by_first)
            return (
                out.push(by_first, arrive.at[step * 2], first),
                out.push(by_second, arrive.at[step * 2 + 1], second),
            )

        def close(step, ways):
            kept = own.at[step * 4 + block(HERE)]
            for way in ways:
                way.wait_recv()
            parts = [kept, arrive.at[step * 2], arrive.at[step * 2 + 1]]
            if masks[step] != HERE:
                total(parts, 0, tokens, kept)
                reach.append(out.push(kept, ends.at[step], masks[step]))
                return
            for number, copy in enumerate(reach):
                copy.wait_recv()
                parts.append(ends.at[number])
            total(parts, 0, tokens, result)

        chunks = rows[0].shape[0] // thick

        def product_loads(item, number):
            slot = lax.rem(number, 2)
            begin = pl.multiple_of(number * thick, 16)
            return [
                pltpu.make_async_copy(
                    thin_wide[2 * item + part].at[pl.ds(begin, thick)], stage.at[slot], product_sem.at[slot, part]
                )
                for part, stage in enumerate((thin_stage, wide_stage))
            ]

        written = []

        def multiply(item, begin, end):
            if begin == 0:
                for copy in product_loads(item, 0):
                    copy.start()
                if written:
                    written[-1].wait()
                else:
                    gross[...] = jnp.zeros_like(gross)

            def step(number, carry):
                @pl.when(number + 1 < chunks)
                def _():
                    for copy in product_loads(item, number + 1):
                        copy.start()

                for copy in product_loads(item, number):
                    copy.wait()
                slot = lax.rem(number, 2)
                keep = jnp.where(number == 0, 0.0, 1.0).astype(jnp.float32)

                def tile(low, size):
                    area = pl.ds(low, size)
                    value = inner_rows(thin_stage[slot], wide_stage[slot, :, area])
                    gross[:, area] = gross[:, area] * keep + value

                by_tiles(width, tile, 3)
                return carry

            lax.fori_loop(begin, end, step, 0)
            if end == chunks:
                copy = pltpu.make_async_copy(gross, made[item], made_sem.at[0])
                copy.start()
                written.append(copy)

        todo = [(item, begin) for item in range(len(products)) for begin in range(0, chunks, 3)]

        def some(number):
            for item, begin in todo[:number]:
                multiply(item, begin, min(begin + 3, chunks))
            del todo[:number]

        sent, corners, ways, reach = {}, {}, {}, []
        load(0)
        for step in range(rounds + 2):
            if step < rounds:
                to_sibling(step)
                to_here(step)
                combine(step)
                corners[step] = outward(step)
            if 0 <= step - 1 < rounds:
                ways[step - 1] = inward(step - 1, corners[step - 1])
            if 0 <= step - 2 < rounds:
                close(step - 2, ways[step - 2])
            some((2, 2, 3, 2, 0, 0)[step])
        some(len(todo))
        if written:
            written[-1].wait()
        for step in range(rounds):
            if step >= rounds - 2:
                for copy in sent[step]:
                    copy.wait_send()
        exchanged = {id(copy) for step in range(rounds) for copy in sent[step]}
        for copy in out.started:
            if id(copy) not in exchanged:
                copy.wait_send()

    vmem, anywhere = pl.BlockSpec(memory_space=pltpu.VMEM), pl.BlockSpec(memory_space=pl.ANY)
    for_products = []
    if products:
        for_products = [
            pltpu.VMEM((2, thick, hidden), jnp.bfloat16),
            pltpu.VMEM((2, thick, width), jnp.bfloat16),
            pltpu.VMEM((hidden, width), jnp.float32),
            pltpu.SemaphoreType.DMA((2, 2)),
            pltpu.SemaphoreType.DMA((1,)),
        ]
    return pl.pallas_call(
        body,
        out_shape=[jax.ShapeDtypeStruct((tokens, width), jnp.float32)]
        + [jax.ShapeDtypeStruct((hidden, width), jnp.float32)] * len(products),
        in_specs=[anywhere] * count_rows
        + [vmem] * (count_rows + 1 + count_extra)
        + [anywhere] * (2 * len(products)),
        out_specs=[vmem] + [anywhere] * len(products),
        scratch_shapes=[
            pltpu.VMEM((2, count_rows, half_rows, hidden), jnp.bfloat16),
            pltpu.VMEM((2, half_rows, width), jnp.bfloat16),
            pltpu.VMEM((rounds, pairs, 2 * pair_rows, width), jnp.bfloat16),
            pltpu.VMEM((rounds * 4, tokens, width), jnp.bfloat16),
            pltpu.VMEM((rounds, tokens, width), jnp.bfloat16),
            pltpu.VMEM((rounds * 2, tokens, width), jnp.bfloat16),
            pltpu.VMEM((len(line), tokens, width), jnp.bfloat16),
            pltpu.SemaphoreType.DMA((copies_out,)),
            pltpu.SemaphoreType.DMA((copies_out,)),
            pltpu.SemaphoreType.DMA((2, count_rows)),
        ]
        + for_products,
        compiler_params=pltpu.CompilerParams(
            collective_id=collective, has_side_effects=True, vmem_limit_bytes=62 * 1024 * 1024
        ),
        name=name,
    )(*rows, *weights, seats, *extra, *[array for pair in products for array in pair])


def expert_rows_kernel(own_block, cotangents, weights, biases, seats, shares, capacity, collective, name):
    experts, pairs = seats.shape[0], seats.shape[1]
    tokens, width = own_block.shape
    blocks = cotangents.shape[0]
    hidden = weights[0].shape[0]
    pair_rows = 2 * capacity
    half_rows = pairs * pair_rows
    row_count = experts * half_rows
    copies_out = copies("all")

    def body(*refs):
        (own_ref, cot_ref, gate, up, down, gate_bias, up_bias, seat_ref, share_ref) = refs[:9]
        (rows_out, grads_out, act_out, dgate_out, dup_out, gate_sum, up_sum, down_sum, held) = refs[9:18]
        (stage, lines, thin, pre, back, send, recv, local, load_sem, line_sem, thin_sem) = refs[18:]
        place = place_here()
        x, e, y = place
        greet = partners("all")
        barrier = pltpu.get_barrier_semaphore()
        for mask in greet:
            pl.semaphore_signal(barrier, inc=1, device_id=flip(place, mask), device_id_type=MESH)
        pl.semaphore_wait(barrier, len(greet))
        work = Gather("all", place, own_ref, held, send, recv, local)
        work.start()
        gate_sum[...] = jnp.zeros_like(gate_sum)
        up_sum[...] = jnp.zeros_like(up_sum)
        down_sum[...] = jnp.zeros_like(down_sum)
        halves = []
        for mask in work.masks:
            halves.append(flip(place, mask)[1])
            halves.append(flip(place, both(mask, SIBLING))[1])
        turnstile = {"load": 0, "line": 0}
        line_copies, thin_copies = [], []

        def fetch(source, part, pair):
            slot = pair % 2
            copy = pltpu.make_async_copy(
                source.at[pl.ds(pl.multiple_of((part * pairs + pair) * 2, 2), 2)],
                stage.at[slot],
                load_sem.at[slot],
            )
            copy.start()
            return copy

        def pick(source, part, scaled):
            slot = turnstile["line"] % 2
            turnstile["line"] += 1
            if len(line_copies) >= 2:
                line_copies[-2].wait()
            fetched = [fetch(source, part, pair) for pair in range(pairs)]
            for pair in range(pairs):
                fetched[pair].wait()
                hot = seat_hot(seat_ref[part, pair], capacity, jnp.float32)
                if scaled:
                    factor = jnp.sum(hot * share_ref[part, pair], axis=1, keepdims=True)
                hot = hot.astype(jnp.bfloat16)

                blocks_here = stage[pair % 2].reshape(2 * tokens, width)
                value = jnp.dot(hot, blocks_here, preferred_element_type=jnp.float32)
                if scaled:
                    value = value * factor
                value = value.astype(jnp.bfloat16)
                lines[slot, pair * pair_rows : (pair + 1) * pair_rows] = value
                if scaled:
                    down_sum[...] += jnp.sum(value.astype(jnp.float32), axis=0, keepdims=True)
            copy = pltpu.make_async_copy(
                lines.at[slot],
                (grads_out if scaled else rows_out).at[
                    pl.ds(pl.multiple_of(part * half_rows, 16), half_rows)
                ],
                line_sem.at[slot],
            )
            copy.start()
            line_copies.append(copy)
            return lines.at[slot]

        def backward(number):
            picked = pick(cot_ref, halves[number], True)
            back[number] = times_transposed(picked[...], down[...])

        def forward(number):
            if number % 2 == 0:
                if number == 0:
                    work.own.wait()
            else:
                work.passed(number // 2)
            part = halves[number]
            picked = pick(held, part, False)
            pre[0] = times_transposed(picked[...], gate[...])
            pre[1] = times_transposed(picked[...], up[...])
            slot = number % 2
            if number >= 2:
                for copy in thin_copies[-6:-3]:
                    copy.wait()

            def chunk(step, sums):
                area = pl.ds(pl.multiple_of(step * 16, 16), 16)
                gate_tanh = jnp.tanh((pre[0, area] + gate_bias[...]) * (1.0 / clip_level))
                up_tanh = jnp.tanh((pre[1, area] + up_bias[...]) * (1.0 / clip_level))
                gate_soft = clip_level * gate_tanh
                up_more = clip_level * up_tanh + 1.0
                bend = jax.nn.sigmoid(glu_alpha * gate_soft)
                glow = gate_soft * bend
                grad = back[number, area]
                dgate = grad * up_more * (bend + glu_alpha * glow * (1.0 - bend))
                dgate = (dgate * (1.0 - gate_tanh * gate_tanh)).astype(jnp.bfloat16)
                dup = (grad * glow * (1.0 - up_tanh * up_tanh)).astype(jnp.bfloat16)
                thin[slot, 0, area] = (glow * up_more).astype(jnp.bfloat16)
                thin[slot, 1, area] = dgate
                thin[slot, 2, area] = dup
                return sums[0] + dgate.astype(jnp.float32), sums[1] + dup.astype(jnp.float32)

            zero = jnp.zeros((16, hidden), jnp.float32)
            sums = lax.fori_loop(0, half_rows // 16, chunk, (zero, zero))
            gate_sum[...] += jnp.sum(sums[0], axis=0, keepdims=True)
            up_sum[...] += jnp.sum(sums[1], axis=0, keepdims=True)
            for item, goal in enumerate((act_out, dgate_out, dup_out)):
                copy = pltpu.make_async_copy(
                    thin.at[slot, item],
                    goal.at[pl.ds(pl.multiple_of(part * half_rows, 16), half_rows)],
                    thin_sem.at[slot, item],
                )
                copy.start()
                thin_copies.append(copy)

        work.plane(0)
        backward(0)
        backward(1)
        backward(2)
        work.turn(0)
        work.plane(1)
        backward(3)
        work.close(0)
        forward(0)
        work.turn(1)
        work.plane(2)
        forward(1)
        backward(4)
        work.close(1)
        backward(5)
        forward(2)
        work.turn(2)
        work.plane(3)
        forward(3)
        work.close(2)
        backward(6)
        backward(7)
        work.turn(3)
        forward(4)
        work.close(3)
        forward(5)
        forward(6)
        forward(7)
        for copy in line_copies[-2:] + thin_copies[-6:]:
            copy.wait()
        work.finish()

    vmem, anywhere = pl.BlockSpec(memory_space=pltpu.VMEM), pl.BlockSpec(memory_space=pl.ANY)
    bf16, f32 = jnp.bfloat16, jnp.float32
    return pl.pallas_call(
        body,
        out_shape=[
            jax.ShapeDtypeStruct((row_count, width), bf16),
            jax.ShapeDtypeStruct((row_count, width), bf16),
            jax.ShapeDtypeStruct((row_count, hidden), bf16),
            jax.ShapeDtypeStruct((row_count, hidden), bf16),
            jax.ShapeDtypeStruct((row_count, hidden), bf16),
            jax.ShapeDtypeStruct((1, hidden), f32),
            jax.ShapeDtypeStruct((1, hidden), f32),
            jax.ShapeDtypeStruct((1, width), f32),
            jax.ShapeDtypeStruct((blocks, tokens, width), bf16),
        ],
        in_specs=[anywhere] * 2 + [vmem] * 7,
        out_specs=[anywhere] * 5 + [vmem] * 3 + [anywhere],
        scratch_shapes=[
            pltpu.VMEM((2, 2, tokens, width), bf16),
            pltpu.VMEM((2, half_rows, width), bf16),
            pltpu.VMEM((2, 3, half_rows, hidden), bf16),
            pltpu.VMEM((2, half_rows, hidden), f32),
            pltpu.VMEM((experts, half_rows, hidden), f32),
            pltpu.SemaphoreType.DMA((copies_out,)),
            pltpu.SemaphoreType.DMA((copies_out,)),
            pltpu.SemaphoreType.DMA((1,)),
            pltpu.SemaphoreType.DMA((2,)),
            pltpu.SemaphoreType.DMA((2,)),
            pltpu.SemaphoreType.DMA((2, 3)),
        ],
        compiler_params=pltpu.CompilerParams(
            collective_id=collective, has_side_effects=True, vmem_limit_bytes=60 * 1024 * 1024
        ),
        name=name,
    )(own_block, cotangents, *weights, *biases, seats, shares)


class Scatter:
    def __init__(self, group, place, source, result, side, arrive, send, recv, spare, mate=None):
        self.index, _, self.sibling, self.first, self.second, _, share = GROUPS[group]
        self.place, self.source, self.result = place, source, result
        self.side, self.arrive, self.mate = side, arrive, mate
        self.rows = result.shape[0]
        self.cut = int(self.rows * (1.0 - share)) // 16 * 16
        self.corner = both(self.first, self.second)
        self.out = Sender(place, send, recv)
        self.crossing = {}

    def at(self, mask):
        return self.source.at[self.index(flip(self.place, mask))]

    def cross(self):
        for spot, mask in enumerate((self.corner, self.first, self.second, HERE)):
            self.crossing[mask] = (
                self.out.push(self.at(both(mask, self.sibling)), self.mate.at[spot], self.sibling),
                self.mate.at[spot],
            )

    def ready(self, mask):
        if not self.sibling:
            return [self.at(mask)]
        copy, block = self.crossing[mask]
        copy.wait_recv()
        return [self.at(mask), block]

    def outward(self):
        corner, cut = self.at(self.corner), self.cut
        parts = self.ready(self.corner)
        if len(parts) > 1:
            total(parts, 0, self.rows, corner)
        self.halves = []
        if cut:
            self.halves.append(self.out.push(corner.at[:cut], self.side.at[:cut], self.first))
        if cut < self.rows:
            self.halves.append(self.out.push(corner.at[cut:], self.side.at[cut:], self.second))

    def inward(self):
        by_first, by_second = self.ready(self.first), self.ready(self.second)
        for half in self.halves:
            half.wait_recv()
        cut, rows = self.cut, self.rows
        total(by_second + [self.side], 0, cut, by_second[0])
        total(by_first + [self.side], cut, rows, by_first[0])
        if self.sibling:
            total(by_second, cut, rows, by_second[0])
            total(by_first, 0, cut, by_first[0])
        self.ways = (
            self.out.push(by_first[0], self.arrive.at[0], self.first),
            self.out.push(by_second[0], self.arrive.at[1], self.second),
        )

    def close(self):
        parts = self.ready(HERE)
        for way in self.ways:
            way.wait_recv()
        total(parts + [self.arrive.at[0], self.arrive.at[1]], 0, self.rows, self.result)

    def finish(self):
        self.out.finish()


def lanes(shape):
    return lax.broadcasted_iota(jnp.int32, shape, len(shape) - 1)


def swapped(value):
    width = value.shape[-1]
    upper = pltpu.roll(value, width - HD // 2, len(value.shape) - 1)
    lower = pltpu.roll(value, HD // 2, len(value.shape) - 1)
    return jnp.where(lanes(value.shape) % HD < HD // 2, upper, lower)


def halves_of(value, member):
    low = lanes(value.shape) < HD
    zero = jnp.zeros_like(value)
    if member == 0:
        kept = jnp.where(low, value, zero)
        return kept, pltpu.roll(kept, HD, 1)
    kept = jnp.where(low, zero, value)
    return pltpu.roll(kept, HD, 1), kept


def seen(marks, held, first_key=0):
    rows = marks.shape[1]
    lines = []
    for query in range(2):
        parts = []
        for key in range(2):
            if key > query:
                parts.append(jnp.zeros((rows, rows), jnp.bool_))
                continue
            same = marks[held + query] == marks[held + key].T
            if key == query:
                down = lax.broadcasted_iota(jnp.int32, (rows, rows), 0)
                same = same & (down >= lanes((rows, rows)))
            parts.append(same)
        lines.append(parts)
    return lines


def mask_of(marks, held):
    lines = seen(marks, held)
    return jnp.concatenate(
        [
            jnp.concatenate([jnp.where(part, 1.0, 0.0) for part in parts], axis=1)
            for parts in lines
        ],
        axis=0,
    )


def pick_lane(value, number):
    return jnp.sum(jnp.where(lanes(value.shape) == number, value, 0.0), axis=1, keepdims=True)


def attention_forward(
    normed, query_rows, key_rows, value_rows, output_rows, marks, table, extra, biases, tables, sinks, collective, name
):
    tokens, width = normed.shape
    block = 4 * tokens
    seq_len = 2 * tokens
    columns = 8 * query_rows.shape[0]
    pairs = columns // 128
    scale = 1.0 / math.sqrt(HD)
    bf16, f32 = jnp.bfloat16, jnp.float32
    gathers = [
        ("tokens", normed),
        ("heads", query_rows),
        ("heads", key_rows),
        ("heads", value_rows),
        ("tokens", marks),
        ("heads", output_rows),
        ("all", table),
        ("all", extra),
    ]
    count = len(gathers)

    def body(*refs):
        refs = list(refs)

        def take(number):
            got = refs[:number]
            del refs[:number]
            return got

        sources = take(count)
        query_bias, key_bias, value_bias, cosine, sine, sink_ref = take(6)
        (result, query_out, key_out, value_out, mixed_out, lse_out, mask) = take(7)
        kept_out = take(5)
        far_out = take(2)
        held = take(count - 2)
        (key_half, value_half, partial, side, arrive) = take(5)
        sems = [take(3) for _ in range(count)]
        sum_sems = take(3)
        (keep_sem,) = take(1)
        place = place_here()
        greet = []
        for group, _ in gathers:
            greet += [step for step in partners(group) if step not in greet]
        barrier = pltpu.get_barrier_semaphore()
        for step in greet:
            pl.semaphore_signal(barrier, inc=1, device_id=flip(place, step), device_id_type=MESH)
        pl.semaphore_wait(barrier, len(greet))
        works = [
            Gather(
                group, place, sources[item], (held + far_out)[item], *sems[item], share=0.25 if item == 7 else None
            )
            for item, (group, _) in enumerate(gathers)
        ]
        all_tokens, all_query, all_key, all_value, all_marks, all_output = held
        early, output_work, table_work, extra_work = works[:5], works[5], works[6], works[7]
        for work in early + [table_work]:
            work.start()
            work.plane(0)
        for work in early:
            work.turn(0)
        output_work.start()
        output_work.plane(0)
        extra_work.start()
        extra_work.plane(0)
        for work in early:
            work.close(0)
        table_work.turn(0)
        table_work.plane(1)
        for work in early:
            work.passed(0)
            work.own.wait()
        keeps = []

        def keep(item, goal):
            copy = pltpu.make_async_copy(held[item], kept_out[goal], keep_sem.at[goal])
            copy.start()
            keeps.append(copy)

        for item in range(4):
            keep(item, item)
        x_all = all_tokens[...].reshape(block, width)

        def turned(value, low):
            return value * cosine[...] + swapped(value) * sine[...]

        def project(number, carry):
            weight = all_query[pl.ds(pl.multiple_of(2 * number, 2), 2)].reshape(256, width)
            value = times_transposed(x_all, weight)
            for part in range(2):
                area = pl.ds(pl.multiple_of((2 * number + part) * 128, 128), 128)
                head = value[:, part * 128 : (part + 1) * 128] + query_bias[:, area]
                query_out[:, area] = turned(head, 0).astype(bf16)
            return carry

        lax.fori_loop(0, pairs // 2, project, 0)
        key = times_transposed(x_all, all_key[...].reshape(128, width)) + key_bias[...]
        key = turned(key, 0).astype(bf16)
        key_out[...] = key
        value = times_transposed(x_all, all_value[...].reshape(128, width)) + value_bias[...]
        value = value.astype(bf16)
        value_out[...] = value
        for member in range(2):
            for part, half in enumerate(halves_of(key, member)):
                key_half[2 * member + part] = half
            for part, half in enumerate(halves_of(value, member)):
                value_half[2 * member + part] = half
        for half in range(2):
            mask[half] = mask_of(all_marks, 2 * half)
        output_work.turn(0)
        extra_work.turn(0)
        extra_work.plane(1)
        table_work.turn(1)
        table_work.close(0)
        table_work.plane(2)
        lse_out[...] = jnp.zeros_like(lse_out)

        def attend(number, carry):
            pair = lax.div(number, 2)
            half = lax.rem(number, 2)
            member = lax.div(pair, pairs // 2)
            rows = pl.ds(pl.multiple_of(half * seq_len, seq_len), seq_len)
            area = pl.ds(pl.multiple_of(pair * 128, 128), 128)
            query = query_out[rows, area]
            mixed = jnp.zeros((seq_len, 128), f32)
            for part in range(2):
                raw = times_transposed(query, key_half[2 * member + part, rows]) * scale
                raw = jnp.where(mask[half] > 0.0, raw, masked_score)
                sink = sink_ref[0, 2 * pair + part]
                peak = jnp.maximum(jnp.max(raw, axis=1, keepdims=True), sink)
                mass = jnp.sum(jnp.exp(raw - peak), axis=1, keepdims=True) + jnp.exp(sink - peak)
                lse = peak + jnp.log(mass)
                probs = jnp.exp(raw - lse).astype(bf16)
                mixed = mixed + jnp.dot(
                    probs, value_half[2 * member + part, rows], preferred_element_type=f32
                )
                spot = lanes((seq_len, 128)) == 2 * pair + part
                lse_out[rows] = jnp.where(spot, lse, lse_out[rows])
            mixed_out[rows, area] = mixed.astype(bf16)
            return carry

        lax.fori_loop(0, pairs, attend, 0)
        output_work.close(0)
        extra_work.close(0)
        table_work.turn(2)
        table_work.plane(3)
        table_work.close(1)
        lax.fori_loop(pairs, 2 * pairs, attend, 0)
        output_work.passed(0)
        output_work.own.wait()
        keep(5, 4)
        extra_work.turn(1)
        extra_work.plane(2)
        table_work.turn(3)
        table_work.close(2)

        def tile(low, size):
            weight = all_output[:, :, pl.ds(low, size)].reshape(columns, size)
            value = jnp.dot(mixed_out[...], weight, preferred_element_type=f32).astype(bf16)
            partial[:, :, pl.ds(low, size)] = value.reshape(4, tokens, size)

        by_tiles(width, tile)
        run = Scatter("tokens", place, partial, result, side, arrive, *sum_sems)
        run.outward()
        extra_work.close(1)
        table_work.close(3)
        run.inward()
        extra_work.turn(2)
        extra_work.plane(3)
        run.close()
        extra_work.close(2)
        extra_work.turn(3)
        extra_work.close(3)
        for work in (table_work, extra_work):
            for step in range(4):
                work.passed(step)
            work.own.wait()
        run.finish()
        for copy in keeps:
            copy.wait()
        for work in works:
            work.finish()

    vmem, anywhere = pl.BlockSpec(memory_space=pltpu.VMEM), pl.BlockSpec(memory_space=pl.ANY)
    smem = pl.BlockSpec(memory_space=pltpu.SMEM)
    kept = [(4,) + normed.shape] + [(8,) + rows.shape for rows in (query_rows, key_rows, value_rows, output_rows)]
    blocks = [GROUPS[group][1] for group, _ in gathers]
    return pl.pallas_call(
        body,
        out_shape=[
            jax.ShapeDtypeStruct((tokens, width), f32),
            jax.ShapeDtypeStruct((block, columns), bf16),
            jax.ShapeDtypeStruct((block, 128), bf16),
            jax.ShapeDtypeStruct((block, 128), bf16),
            jax.ShapeDtypeStruct((block, columns), bf16),
            jax.ShapeDtypeStruct((block, 128), f32),
            jax.ShapeDtypeStruct((2, seq_len, seq_len), f32),
        ]
        + [jax.ShapeDtypeStruct(shape, bf16) for shape in kept]
        + [
            jax.ShapeDtypeStruct((blocks[item],) + array.shape, array.dtype)
            for item, (_, array) in list(enumerate(gathers))[-2:]
        ],
        in_specs=[anywhere] * count + [vmem] * 5 + [smem],
        out_specs=[vmem] * 7 + [anywhere] * 7,
        scratch_shapes=[
            pltpu.VMEM((blocks[item],) + array.shape, array.dtype)
            for item, (_, array) in enumerate(gathers[:-2])
        ]
        + [
            pltpu.VMEM((4, block, 128), bf16),
            pltpu.VMEM((4, block, 128), bf16),
            pltpu.VMEM((4, tokens, width), bf16),
            pltpu.VMEM((tokens, width), bf16),
            pltpu.VMEM((2, tokens, width), bf16),
        ]
        + [
            pltpu.SemaphoreType.DMA((size,))
            for group, _ in gathers
            for size in (copies(group), copies(group), 1)
        ]
        + [pltpu.SemaphoreType.DMA((copies("tokens"),))] * 2
        + [pltpu.SemaphoreType.DMA((1,)), pltpu.SemaphoreType.DMA((5,))],
        compiler_params=pltpu.CompilerParams(
            collective_id=collective, has_side_effects=True, vmem_limit_bytes=60 * 1024 * 1024
        ),
        name=name,
    )(*[array for _, array in gathers], *biases, *tables, sinks)


def attention_backward(
    outer, query, key, value, mixed, log_total, mask, tokens_kept, weights, tables, sinks, plain, small, collective, name
):
    tokens, width = outer.shape
    block = 4 * tokens
    seq_len = 2 * tokens
    columns = query.shape[1]
    pairs = columns // 128
    scale = 1.0 / math.sqrt(HD)
    bf16, f32 = jnp.bfloat16, jnp.float32
    owned = [rows.shape[1] for rows in weights]
    groups = ["heads"] * 4 + ["tokens"]

    def body(*refs):
        refs = list(refs)

        def take(number):
            got = refs[:number]
            del refs[:number]
            return got

        (outer_ref,) = take(1)
        query_ref, key_ref, value_ref, mixed_ref, lse_ref, mask_ref = take(6)
        stored = take(5)
        cosine, sine, sink_ref, plain_ref, small_ref = take(5)
        results = take(5)
        (small_out,) = take(1)
        held = take(5)
        grads, key_half, value_half = take(3)
        mixed_grad, query_grad, key_grad, value_grad = take(4)
        key_sum, value_sum, sink_sum, small_own = take(4)
        output_part, key_part, value_part = take(3)
        mates, sides, arrives = take(4), take(5), take(5)
        load_sem, gather_sems, small_sems = take(1)[0], take(3), take(3)
        sum_sems = [take(3) for _ in groups]
        place = place_here()
        greet = []
        for group in ("tokens", "heads", "all"):
            greet += [step for step in partners(group) if step not in greet]
        barrier = pltpu.get_barrier_semaphore()
        for step in greet:
            pl.semaphore_signal(barrier, inc=1, device_id=flip(place, step), device_id_type=MESH)
        pl.semaphore_wait(barrier, len(greet))
        work = Gather("tokens", place, outer_ref, grads, *gather_sems)
        work.start()
        work.plane(0)
        loads = []
        for item in (4, 1, 2, 3, 0):
            copy = pltpu.make_async_copy(stored[item], held[item], load_sem.at[item])
            copy.start()
            loads.append(copy)
        all_tokens, all_query, all_key, all_value, all_output = held
        for member in range(2):
            for part, half in enumerate(halves_of(key_ref[...], member)):
                key_half[2 * member + part] = half
            for part, half in enumerate(halves_of(value_ref[...], member)):
                value_half[2 * member + part] = half
        key_sum[...] = jnp.zeros_like(key_sum)
        value_sum[...] = jnp.zeros_like(value_sum)
        sink_sum[...] = jnp.zeros_like(sink_sum)
        small_own[...] = small_ref[...]
        work.turn(0)
        work.close(0)
        work.own.wait()
        work.finish()

        parts = [all_output, key_part, value_part, output_part, grads]
        sums = [
            Scatter(
                group,
                place,
                parts[item],
                results[item],
                sides[item],
                arrives[item],
                *sum_sems[item],
                mate=mates[item] if group == "heads" else None,
            )
            for item, group in enumerate(groups)
        ]
        of_query, of_key, of_value, of_output, of_tokens = sums

        def output_gradient(number, carry):
            area = pl.ds(pl.multiple_of(number * 128, 128), 128)
            rows = inner_rows(mixed_ref[:, area], grads[...].reshape(block, width))
            output_part[number] = rows.astype(bf16)
            return carry

        lax.fori_loop(0, pairs, output_gradient, 0)
        of_output.cross()
        loads[0].wait()

        def project(number, carry):
            weight = all_output[pl.ds(pl.multiple_of(2 * number, 2), 2)].reshape(256, width)
            area = pl.ds(pl.multiple_of(number * 256, 256), 256)
            mixed_grad[:, area] = times_transposed(
                grads[...].reshape(block, width), weight
            ).astype(bf16)
            return carry

        lax.fori_loop(0, pairs // 2, project, 0)
        of_output.outward()

        def back(value):
            return value * cosine[:seq_len] - swapped(value) * sine[:seq_len]

        def attend(number, carry):
            pair = lax.div(number, 2)
            half = lax.rem(number, 2)
            member = lax.div(pair, pairs // 2)
            rows = pl.ds(pl.multiple_of(half * seq_len, seq_len), seq_len)
            area = pl.ds(pl.multiple_of(pair * 128, 128), 128)
            queries = query_ref[rows, area]
            upstream = mixed_grad[rows, area]
            low = lanes((seq_len, 128)) < HD
            made = jnp.zeros((seq_len, 128), f32)
            for part in range(2):
                head = 2 * pair + part
                keys = key_half[2 * member + part, rows]
                lse = pick_lane(lse_ref[rows], head)
                raw = times_transposed(queries, keys) * scale
                raw = jnp.where(mask_ref[half] > 0.0, raw, masked_score)
                probs = jnp.exp(raw - lse)
                grad = times_transposed(upstream, value_half[2 * member + part, rows])
                delta = jnp.sum(probs * grad, axis=1, keepdims=True)
                inner = (probs * (grad - delta)).astype(bf16)
                made = made + jnp.dot(inner, keys, preferred_element_type=f32)
                mine = low if part == 0 else jnp.logical_not(low)
                value_sum[member, rows] += jnp.where(mine, inner_rows(probs.astype(bf16), upstream), 0.0)
                key_sum[member, rows] += jnp.where(mine, inner_rows(inner, queries), 0.0)
                lost = jnp.sum(jnp.exp(sink_ref[0, head] - lse) * delta, axis=0, keepdims=True)
                sink_sum[...] -= jnp.where(lanes((1, 128)) == head, lost, 0.0)
            query_grad[rows, area] = back(made * scale).astype(bf16)
            return carry

        lax.fori_loop(0, pairs, attend, 0)
        of_output.inward()
        lax.fori_loop(pairs, 2 * pairs, attend, 0)
        of_output.close()
        low = lanes((seq_len, 128)) < HD
        for half in range(2):
            rows = pl.ds(half * seq_len, seq_len)

            def joined(sums):
                first = sums[0, rows] + pltpu.roll(sums[0, rows], HD, 1)
                second = sums[1, rows] + pltpu.roll(sums[1, rows], HD, 1)
                return jnp.where(low, first, second)

            key_grad[rows] = back(joined(key_sum) * scale).astype(bf16)
            value_grad[rows] = joined(value_sum).astype(bf16)
        for copy in loads[1:]:
            copy.wait()

        def tile(low_column, size):
            area = pl.ds(low_column, size)

            def rows_of(weight):
                return weight[:, :, area].reshape(-1, size)

            total_grad = jnp.dot(query_grad[...], rows_of(all_query), preferred_element_type=f32)
            total_grad += jnp.dot(key_grad[...], rows_of(all_key), preferred_element_type=f32)
            total_grad += jnp.dot(value_grad[...], rows_of(all_value), preferred_element_type=f32)
            grads[:, :, area] = total_grad.astype(bf16).reshape(4, tokens, size)

        by_tiles(width, tile)
        of_tokens.outward()

        def query_gradient(number, carry):
            area = pl.ds(pl.multiple_of(number * 128, 128), 128)
            rows = inner_rows(query_grad[:, area], all_tokens[...].reshape(block, width))
            all_output[number] = rows.astype(bf16)
            return carry

        lax.fori_loop(0, pairs, query_gradient, 0)
        of_query.cross()
        for goal, grad in ((key_part, key_grad), (value_part, value_grad)):
            rows = inner_rows(grad[...], all_tokens[...].reshape(block, width))
            goal[...] = rows.astype(bf16).reshape(goal.shape)
        of_key.cross()
        of_value.cross()
        of_tokens.inward()
        low_column = 0
        for array in (query_grad, key_grad, value_grad):
            size = array.shape[1]
            small_own[3:4, low_column : low_column + size] = jnp.sum(
                array[...].astype(f32), axis=0, keepdims=True
            )
            low_column += size
        small_own[3:4, low_column : low_column + 128] = sink_sum[...]
        of_query.outward()
        of_key.outward()
        of_value.outward()
        of_tokens.close()
        small_own[0:1] = jnp.sum(results[4][...] * plain_ref[...], axis=0, keepdims=True)
        spread = Gather("all", place, small_own, small_out, *small_sems)
        spread.start()
        spread.plane(0)
        of_query.inward()
        of_key.inward()
        of_value.inward()
        spread.turn(0)
        spread.plane(1)
        spread.turn(1)
        spread.close(0)
        spread.plane(2)
        spread.turn(2)
        spread.close(1)
        spread.plane(3)
        spread.turn(3)
        spread.close(2)
        spread.close(3)
        of_query.close()
        of_key.close()
        of_value.close()
        for step in range(4):
            spread.passed(step)
        spread.own.wait()
        spread.finish()
        for part in sums:
            part.finish()

    vmem, anywhere = pl.BlockSpec(memory_space=pltpu.VMEM), pl.BlockSpec(memory_space=pl.ANY)
    smem = pl.BlockSpec(memory_space=pltpu.SMEM)
    rows_of = owned + [tokens]
    kept = [tokens_kept] + list(weights)
    return pl.pallas_call(
        body,
        out_shape=[jax.ShapeDtypeStruct((rows, width), f32) for rows in rows_of]
        + [jax.ShapeDtypeStruct((GROUPS["all"][1],) + small.shape, f32)],
        in_specs=[anywhere] + [vmem] * 6 + [anywhere] * 5 + [vmem] * 2 + [smem] + [vmem] * 2,
        out_specs=[vmem] * 5 + [anywhere],
        scratch_shapes=[pltpu.VMEM(array.shape, bf16) for array in kept]
        + [
            pltpu.VMEM((4, tokens, width), bf16),
            pltpu.VMEM((4, block, 128), bf16),
            pltpu.VMEM((4, block, 128), bf16),
            pltpu.VMEM((block, columns), bf16),
            pltpu.VMEM((block, columns), bf16),
            pltpu.VMEM((block, 128), bf16),
            pltpu.VMEM((block, 128), bf16),
            pltpu.VMEM((2, block, 128), f32),
            pltpu.VMEM((2, block, 128), f32),
            pltpu.VMEM((1, 128), f32),
            pltpu.VMEM(small.shape, f32),
            pltpu.VMEM(weights[3].shape, bf16),
            pltpu.VMEM(weights[1].shape, bf16),
            pltpu.VMEM(weights[2].shape, bf16),
        ]
        + [pltpu.VMEM((4, rows, width), bf16) for rows in owned]
        + [pltpu.VMEM((rows, width), bf16) for rows in rows_of]
        + [pltpu.VMEM((2, rows, width), bf16) for rows in rows_of]
        + [pltpu.SemaphoreType.DMA((5,))]
        + [
            pltpu.SemaphoreType.DMA((size,))
            for group in ["tokens", "all"] + groups
            for size in (copies(group), copies(group), 1)
        ],
        compiler_params=pltpu.CompilerParams(
            collective_id=collective, has_side_effects=True, vmem_limit_bytes=62 * 1024 * 1024
        ),
        name=name,
    )(outer, query, key, value, mixed, log_total, mask, *kept, *tables, sinks, plain, small)


def close_by(
    tokens,
    segments,
    routes,
    gate_share,
    attn_gain,
    query_weight,
    query_bias,
    key_weight,
    key_bias,
    value_weight,
    value_bias,
    output_weight,
    output_bias,
    sink_logits,
    moe_gain,
    gate_weight,
    gate_bias,
    up_weight,
    up_bias,
    down_weight,
    down_bias,
    cotangent,
):
    count_rows = tokens.shape[1]
    width = tokens.shape[2]
    head_count = sink_logits.shape[0]
    kv_count = key_bias.shape[0] // HD
    group = head_count // kv_count
    experts = lax.axis_size("exp")
    devices = 4 * experts
    topk = routes.shape[2]
    capacity = count_rows * topk * 9 // (8 * experts)
    x, e, y = place_here()
    near_bit = lax.rem(lax.div(e, 2), 2)
    seq_len = 2 * count_rows

    chosen = routes[0].reshape(-1)
    expert_hot = (chosen[:, None] == jnp.arange(experts, dtype=jnp.int32)[None, :]).astype(
        jnp.int32
    )
    earlier = (jnp.cumsum(expert_hot, axis=0) - expert_hot).reshape(count_rows, topk, experts)
    named = expert_hot.reshape(count_rows, topk, experts)
    slot_table = jnp.sum((earlier + 1) * named, axis=1) - 1
    share_table = jnp.sum(named.astype(jnp.float32) * gate_share[0][:, :, None], axis=1)
    table = jnp.concatenate([slot_table.astype(jnp.float32).T, share_table.T], axis=0)

    resid = tokens[0].astype(jnp.float32)
    attn_norm, attn_norm_pull = jax.vjp(rms_apply, resid, attn_gain)
    normed = attn_norm.astype(jnp.bfloat16)
    block_tokens = 4 * count_rows
    held_kv = 2
    held_heads = held_kv * group

    def own_part(vector):
        parts = vector.reshape(2, 2, 2, -1)
        parts = lax.dynamic_index_in_dim(parts, x, 0, keepdims=False)
        return lax.dynamic_index_in_dim(parts, near_bit, 1, keepdims=False).reshape(1, -1)

    position = jnp.arange(seq_len, dtype=jnp.int32)
    cosine, sine = rope_tables(position, HD)
    cosine = jnp.tile(cosine, (2, 4))
    sine = jnp.tile(jnp.concatenate([-sine, sine], axis=1), (2, 2))
    own_ids = lax.dynamic_slice_in_dim(segments[0], x * count_rows, count_rows, 0)
    marks = jnp.broadcast_to(own_ids.astype(jnp.float32)[:, None], (count_rows, count_rows))
    sinks = own_part(sink_logits)
    (
        attn_out,
        query_rot,
        key_rot,
        value_low,
        mixed,
        log_total,
        mask,
        group_tokens,
        group_query,
        group_key,
        group_value,
        group_output,
        tables,
        all_cotangents,
    ) = attention_forward(
        normed,
        query_weight.T,
        key_weight.T,
        value_weight.T,
        output_weight,
        marks,
        table,
        cotangent[0],
        (own_part(query_bias), own_part(key_bias), own_part(value_bias)),
        (cosine, sine),
        sinks,
        0,
        "attention_forward",
    )
    hidden = resid + (attn_out + output_bias)
    moe_norm, moe_norm_pull = jax.vjp(rms_apply, hidden, moe_gain)
    normed_moe = moe_norm.astype(jnp.bfloat16)

    def by_pairs(part):
        part = jnp.moveaxis(part.reshape(experts, 2, 2, experts, count_rows), 3, 0)
        return part.reshape(experts, experts, 2, 1, 2 * count_rows)

    slots = tables[:, :experts].astype(jnp.int32)
    second_block = jnp.arange(devices, dtype=jnp.int32)[:, None, None] % 2
    seats = by_pairs(jnp.where(slots >= 0, slots + capacity * second_block, -1))
    sibling = e + 1 - 2 * lax.rem(e, 2)
    seats = jnp.stack(
        [
            lax.dynamic_index_in_dim(seats, e, 0, keepdims=False),
            lax.dynamic_index_in_dim(seats, sibling, 0, keepdims=False),
        ]
    )
    gate_rows, up_rows = gate_weight[0].T, up_weight[0].T
    shares = lax.dynamic_index_in_dim(by_pairs(tables[:, experts:]), e, 0, keepdims=False)
    (
        expert_rows,
        grad_rows,
        activation,
        gate_grad,
        up_grad,
        gate_bias_grad,
        up_bias_grad,
        down_bias_grad,
        _,
    ) = expert_rows_kernel(
        normed_moe,
        all_cotangents,
        (gate_rows, up_rows, down_weight[0]),
        (gate_bias, up_bias),
        seats[0],
        shares,
        capacity,
        2,
        "route_rows",
    )
    (normed_moe_grad,) = expert_sums(
        "gradient", (gate_grad, up_grad), (gate_rows, up_rows), seats, (), 3, "sum_rows"
    )
    moe_out, gate_weight_grad, up_weight_grad, down_weight_grad = expert_sums(
        "result",
        (activation,),
        (down_weight[0],),
        seats,
        (shares, down_bias),
        4,
        "sum_results",
        ((gate_grad, expert_rows), (up_grad, expert_rows), (activation, grad_rows)),
    )
    output = (hidden + moe_out).astype(jnp.bfloat16)

    upstream = cotangent[0].astype(jnp.float32)
    hidden_norm_grad, moe_gain_grad = moe_norm_pull(normed_moe_grad)
    hidden_grad = upstream + hidden_norm_grad
    attn_out_grad = hidden_grad.astype(jnp.bfloat16)
    output_bias_grad = jnp.sum(attn_out_grad.astype(jnp.float32), axis=0)
    plain = resid * lax.rsqrt(jnp.mean(resid * resid, axis=-1, keepdims=True) + norm_eps)
    small = jnp.concatenate(
        [
            jnp.zeros((1, width), jnp.float32),
            moe_gain_grad[None],
            output_bias_grad[None],
            jnp.zeros((5, width), jnp.float32),
        ],
        axis=0,
    )
    query_owned, key_owned, value_owned, output_owned, normed_grad, all_small = attention_backward(
        attn_out_grad,
        query_rot,
        key_rot,
        value_low,
        mixed,
        log_total,
        mask,
        group_tokens,
        (group_query, group_key, group_value, group_output),
        (cosine, sine),
        sinks,
        plain,
        small,
        5,
        "attention_backward",
    )
    lengths = (held_heads * HD, held_kv * HD, held_kv * HD, held_heads)
    resid_norm_grad, _ = attn_norm_pull(normed_grad)
    input_grad = hidden_grad + resid_norm_grad
    by_heads = jnp.sum(all_small[:, 3].reshape(2, 2, 2, 2, 2, width), axis=(0, 2, 4))
    pieces = []
    for low, length in zip((0, lengths[0], sum(lengths[:2]), sum(lengths[:3])), lengths):
        piece = by_heads[:, :, low : low + length].reshape(2, 2, held_kv, -1)
        pieces.append(jnp.transpose(piece, (1, 2, 0, 3)).reshape(-1))
    query_bias_grad, key_bias_grad, value_bias_grad, sink_grad = pieces
    return (
        output[None],
        input_grad[None],
        jnp.sum(all_small[:, 0], axis=0),
        query_owned.T,
        query_bias_grad,
        key_owned.T,
        key_bias_grad,
        value_owned.T,
        value_bias_grad,
        output_owned,
        jnp.sum(all_small[:, 2], axis=0),
        sink_grad,
        jnp.sum(all_small[:, 1], axis=0),
        gate_weight_grad.T[None],
        gate_bias_grad,
        up_weight_grad.T[None],
        up_bias_grad,
        down_weight_grad[None],
        down_bias_grad,
    )


def solution(mesh):
    placed = (
        P(("exp", "dp"), "seq", None),
        P(("exp", "dp"), None),
        P(("exp", "dp"), "seq", None),
        P(("exp", "dp"), "seq", None),
        P(),
        P(None, ("seq", "exp", "dp")),
        P(),
        P(None, ("seq", "exp", "dp")),
        P(),
        P(None, ("seq", "exp", "dp")),
        P(),
        P(("seq", "exp", "dp"), None),
        P(),
        P(),
        P(),
        P("exp", None, ("seq", "dp")),
        P("exp", ("seq", "dp")),
        P("exp", None, ("seq", "dp")),
        P("exp", ("seq", "dp")),
        P("exp", ("seq", "dp"), None),
        P("exp", None),
        P(("exp", "dp"), "seq", None),
    )
    shape = mesh.shape
    small = shape["seq"] == 2 and shape["dp"] == 2 and shape["exp"] == 8
    return jax.shard_map(
        close_by if small else local,
        mesh=mesh,
        in_specs=placed,
        out_specs=(
            P(("exp", "dp"), "seq", None),
            P(("exp", "dp"), "seq", None),
            P(),
            P(None, ("seq", "exp", "dp")),
            P(),
            P(None, ("seq", "exp", "dp")),
            P(),
            P(None, ("seq", "exp", "dp")),
            P(),
            P(("seq", "exp", "dp"), None),
            P(),
            P(),
            P(),
            P("exp", None, ("seq", "dp")),
            P("exp", ("seq", "dp")),
            P("exp", None, ("seq", "dp")),
            P("exp", ("seq", "dp")),
            P("exp", ("seq", "dp"), None),
            P("exp", None),
        ),
        check_vma=False,
    )
```

```python
import math

import jax
import jax.numpy as jnp
from jax import lax
from jax.experimental import pallas as pl
from jax.experimental.pallas import tpu as pltpu
from jax.sharding import PartitionSpec as P

HD = 64


highest = lax.Precision.HIGHEST
norm_eps = 1e-05
rope_base = 150000.0
clip_level = 7.0
glu_alpha = 1.702
masked_score = -1000000000.0


def rms_apply(values, gain):
    return values * lax.rsqrt(jnp.mean(values * values, axis=-1, keepdims=True) + norm_eps) * gain


def rope_tables(position, width):
    exponent = jnp.arange(width // 2).astype(jnp.float32) * (2.0 / width)
    freqs = jnp.exp(-math.log(rope_base) * exponent)
    angles = position.astype(jnp.float32)[:, None] * freqs[None, :]
    return (jnp.cos(angles), jnp.sin(angles))


def rotate(values, cosine, sine):
    half = values.shape[-1] // 2
    first = values[..., :half]
    second = values[..., half:]
    return jnp.concatenate(
        [first * cosine - second * sine, second * cosine + first * sine], axis=-1
    )


def swiglu(gate_pre, up_pre):
    gate_soft = clip_level * jnp.tanh(gate_pre / clip_level)
    up_soft = clip_level * jnp.tanh(up_pre / clip_level)
    return gate_soft * jax.nn.sigmoid(glu_alpha * gate_soft) * (up_soft + 1.0)


def inner_rows(left, right):
    return lax.dot_general(
        left, right, (((0,), (0,)), ((), ())), preferred_element_type=jnp.float32
    )


def times_transposed(left, right):
    return lax.dot_general(
        left, right, (((1,), (1,)), ((), ())), preferred_element_type=jnp.float32
    )


def to_experts(outgoing):
    width = outgoing.shape[2]
    arrived = lax.all_to_all(outgoing, "exp", split_axis=0, concat_axis=0, tiled=True)
    arrived = lax.all_gather(arrived, ("seq", "dp"), axis=0, tiled=True)
    return arrived.reshape(-1, width)


def results_back(activation, down_matrix, down_vector, experts, capacity):
    width = down_matrix.shape[1]
    share = lax.psum_scatter(
        jnp.dot(activation, down_matrix, preferred_element_type=jnp.float32).astype(jnp.bfloat16),
        ("seq", "dp"),
        scatter_dimension=0,
        tiled=True,
    ).astype(jnp.float32)
    finished = (share + down_vector).astype(jnp.bfloat16).reshape(experts, capacity, width)
    return lax.all_to_all(finished, "exp", split_axis=0, concat_axis=0, tiled=True)


def gradients_back(gate_grad, up_grad, gate_matrix, up_matrix, experts, capacity):
    share = lax.psum_scatter(
        times_transposed(gate_grad, gate_matrix) + times_transposed(up_grad, up_matrix),
        ("seq", "dp"),
        scatter_dimension=0,
        tiled=True,
    )
    return lax.all_to_all(
        share.reshape(experts, capacity, share.shape[1]),
        "exp",
        split_axis=0,
        concat_axis=0,
        tiled=True,
    )


def local(
    tokens,
    segments,
    routes,
    gate_share,
    attn_gain,
    query_weight,
    query_bias,
    key_weight,
    key_bias,
    value_weight,
    value_bias,
    output_weight,
    output_bias,
    sink_logits,
    moe_gain,
    gate_weight,
    gate_bias,
    up_weight,
    up_bias,
    down_weight,
    down_bias,
    cotangent,
):
    count_rows = tokens.shape[1]
    width = tokens.shape[2]
    head_count = sink_logits.shape[0]
    kv_count = key_bias.shape[0] // HD
    group = head_count // kv_count
    scale = 1.0 / math.sqrt(HD)
    experts = lax.axis_size("exp")
    topk = routes.shape[2]
    capacity = count_rows * topk * 9 // (8 * experts)
    resid = tokens[0].astype(jnp.float32)
    full_query, full_key, full_value, full_output = (
        lax.all_gather(query_weight, ("seq", "exp", "dp"), axis=1, tiled=True),
        lax.all_gather(key_weight, ("seq", "exp", "dp"), axis=1, tiled=True),
        lax.all_gather(value_weight, ("seq", "exp", "dp"), axis=1, tiled=True),
        lax.all_gather(output_weight, ("seq", "exp", "dp"), axis=0, tiled=True),
    )
    attn_norm, attn_norm_pull = jax.vjp(rms_apply, resid, attn_gain)
    normed = attn_norm.astype(jnp.bfloat16)
    query_lin = jnp.dot(normed, full_query, preferred_element_type=jnp.float32) + query_bias
    key_lin = jnp.dot(normed, full_key, preferred_element_type=jnp.float32) + key_bias
    value_low = (
        jnp.dot(normed, full_value, preferred_element_type=jnp.float32) + value_bias
    ).astype(jnp.bfloat16)
    offset = lax.axis_index("seq") * count_rows
    position = offset + jnp.arange(count_rows, dtype=jnp.int32)
    cosine, sine = rope_tables(position, HD)
    cosine = cosine[:, None]
    sine = sine[:, None]
    query_rot = rotate(query_lin.reshape(count_rows, head_count, HD), cosine, sine).astype(
        jnp.bfloat16
    )
    key_rot = rotate(key_lin.reshape(count_rows, kv_count, HD), cosine, sine).astype(jnp.bfloat16)
    all_keys, all_values = (
        lax.all_gather(key_rot.reshape(count_rows, kv_count * HD), "seq", axis=0, tiled=True),
        lax.all_gather(value_low, "seq", axis=0, tiled=True),
    )
    seq_len = all_keys.shape[0]
    all_keys = all_keys.reshape(seq_len, kv_count, HD)
    all_values = all_values.reshape(seq_len, kv_count, HD)
    doc_ids = segments[0]
    own_ids = lax.dynamic_slice_in_dim(doc_ids, offset, count_rows, 0)
    key_place = jnp.arange(seq_len, dtype=jnp.int32)
    visible = (position[:, None] >= key_place[None, :]) & (own_ids[:, None] == doc_ids[None, :])
    query_group = query_rot.reshape(count_rows, kv_count, group, HD)
    sink_grid = sink_logits.reshape(kv_count, group)[:, :, None]

    def score_block():
        raw = (
            jnp.einsum("qkgd,skd->kgqs", query_group, all_keys, preferred_element_type=jnp.float32)
            * scale
        )
        return jnp.where(visible[None, None], raw, masked_score)

    scores = score_block()
    peak = jnp.maximum(jnp.max(scores, axis=-1), sink_grid)
    total = jnp.sum(jnp.exp(scores - peak[..., None]), axis=-1) + jnp.exp(sink_grid - peak)
    log_total = peak + jnp.log(total)
    probs = jnp.exp(scores - log_total[..., None])
    mixed = jnp.einsum(
        "kgqs,skd->qkgd", probs.astype(jnp.bfloat16), all_values, preferred_element_type=jnp.float32
    )
    mixed = mixed.reshape(count_rows, head_count * HD).astype(jnp.bfloat16)
    attn_out = jnp.dot(mixed, full_output, preferred_element_type=jnp.float32) + output_bias
    hidden = resid + attn_out
    moe_norm, moe_norm_pull = jax.vjp(rms_apply, hidden, moe_gain)
    normed_moe = moe_norm.astype(jnp.bfloat16)
    chosen = routes[0].reshape(-1)
    expert_hot = (chosen[:, None] == jnp.arange(experts, dtype=jnp.int32)[None, :]).astype(
        jnp.int32
    )
    slot_index = jnp.sum((jnp.cumsum(expert_hot, axis=0) - expert_hot) * expert_hot, axis=1)
    target = chosen * capacity + slot_index
    slot_hot = (
        target[:, None] == jnp.arange(experts * capacity, dtype=jnp.int32)[None, :]
    ).reshape(count_rows, topk, experts * capacity)
    dispatch = jnp.sum(slot_hot.astype(jnp.bfloat16), axis=1)
    weighted = jnp.sum(slot_hot.astype(jnp.float32) * gate_share[0][:, :, None], axis=1)
    outgoing = jnp.einsum("ts,td->sd", dispatch, normed_moe, preferred_element_type=jnp.float32)
    outgoing = outgoing.astype(jnp.bfloat16).reshape(experts, capacity, width)
    expert_rows = to_experts(outgoing)
    gate_pre = (
        jnp.dot(expert_rows, gate_weight[0], preferred_element_type=jnp.float32) + gate_bias[0]
    )
    up_pre = jnp.dot(expert_rows, up_weight[0], preferred_element_type=jnp.float32) + up_bias[0]
    act_full, swiglu_pull = jax.vjp(swiglu, gate_pre, up_pre)
    activation = act_full.astype(jnp.bfloat16)
    returned = results_back(activation, down_weight[0], down_bias[0], experts, capacity)
    moe_out = jnp.dot(
        weighted, returned.reshape(experts * capacity, width).astype(jnp.float32), precision=highest
    )
    output = (hidden + moe_out).astype(jnp.bfloat16)
    upstream = cotangent[0].astype(jnp.float32)
    grad_slots = jnp.einsum("ts,td->sd", weighted, upstream, precision=highest)
    grad_slots = grad_slots.astype(jnp.bfloat16).reshape(experts, capacity, width)
    grad_rows = to_experts(grad_slots)
    down_bias_grad = jnp.sum(grad_rows.astype(jnp.float32), axis=0)
    down_weight_grad = inner_rows(activation, grad_rows)
    act_grad = times_transposed(grad_rows, down_weight[0])
    gate_grad_full, up_grad_full = swiglu_pull(act_grad)
    gate_grad = gate_grad_full.astype(jnp.bfloat16)
    up_grad = up_grad_full.astype(jnp.bfloat16)
    gate_bias_grad = jnp.sum(gate_grad.astype(jnp.float32), axis=0)
    up_bias_grad = jnp.sum(up_grad.astype(jnp.float32), axis=0)
    gate_weight_grad = inner_rows(expert_rows, gate_grad)
    up_weight_grad = inner_rows(expert_rows, up_grad)
    rows_grad = gradients_back(gate_grad, up_grad, gate_weight[0], up_weight[0], experts, capacity)
    normed_moe_grad = jnp.einsum(
        "ts,sd->td",
        dispatch.astype(jnp.float32),
        rows_grad.reshape(experts * capacity, width),
        precision=highest,
    )
    hidden_norm_grad, moe_gain_grad = moe_norm_pull(normed_moe_grad)
    hidden_grad = upstream + hidden_norm_grad
    attn_out_grad = hidden_grad.astype(jnp.bfloat16)
    output_bias_grad = jnp.sum(attn_out_grad.astype(jnp.float32), axis=0)
    full_query, full_key, full_value, full_output = (
        lax.all_gather(query_weight, ("seq", "exp", "dp"), axis=1, tiled=True),
        lax.all_gather(key_weight, ("seq", "exp", "dp"), axis=1, tiled=True),
        lax.all_gather(value_weight, ("seq", "exp", "dp"), axis=1, tiled=True),
        lax.all_gather(output_weight, ("seq", "exp", "dp"), axis=0, tiled=True),
    )
    mixed_grad = (
        times_transposed(attn_out_grad, full_output)
        .astype(jnp.bfloat16)
        .reshape(count_rows, kv_count, group, HD)
    )
    scores = score_block()
    probs = jnp.exp(scores - log_total[..., None])
    prob_grad = jnp.einsum(
        "qkgd,skd->kgqs", mixed_grad, all_values, preferred_element_type=jnp.float32
    )
    delta = jnp.sum(probs * prob_grad, axis=-1)
    score_grad = (probs * (prob_grad - delta[..., None])).astype(jnp.bfloat16)
    sink_grad = -jnp.sum(jnp.exp(sink_grid - log_total) * delta, axis=-1).reshape(head_count)
    value_grad = jnp.einsum(
        "kgqs,qkgd->skd", probs.astype(jnp.bfloat16), mixed_grad, preferred_element_type=jnp.float32
    )
    key_grad = (
        jnp.einsum("kgqs,qkgd->skd", score_grad, query_group, preferred_element_type=jnp.float32)
        * scale
    )
    query_grad = (
        jnp.einsum("kgqs,skd->qkgd", score_grad, all_keys, preferred_element_type=jnp.float32)
        * scale
    )
    key_share, value_share = (
        lax.psum_scatter(
            key_grad.reshape(seq_len, kv_count * HD), "seq", scatter_dimension=0, tiled=True
        ),
        lax.psum_scatter(
            value_grad.reshape(seq_len, kv_count * HD), "seq", scatter_dimension=0, tiled=True
        ),
    )
    query_lin_grad = (
        rotate(query_grad.reshape(count_rows, head_count, HD), cosine, -sine)
        .reshape(count_rows, head_count * HD)
        .astype(jnp.bfloat16)
    )
    key_lin_grad = (
        rotate(key_share.reshape(count_rows, kv_count, HD), cosine, -sine)
        .reshape(count_rows, kv_count * HD)
        .astype(jnp.bfloat16)
    )
    value_lin_grad = value_share.astype(jnp.bfloat16)
    query_bias_grad = jnp.sum(query_lin_grad.astype(jnp.float32), axis=0)
    key_bias_grad = jnp.sum(key_lin_grad.astype(jnp.float32), axis=0)
    value_bias_grad = jnp.sum(value_lin_grad.astype(jnp.float32), axis=0)
    normed_grad = (
        times_transposed(query_lin_grad, full_query)
        + times_transposed(key_lin_grad, full_key)
        + times_transposed(value_lin_grad, full_value)
    )
    resid_norm_grad, attn_gain_grad = attn_norm_pull(normed_grad)
    input_grad = hidden_grad + resid_norm_grad
    query_weight_grad = inner_rows(normed, query_lin_grad)
    key_weight_grad = inner_rows(normed, key_lin_grad)
    value_weight_grad = inner_rows(normed, value_lin_grad)
    output_weight_grad = inner_rows(mixed, attn_out_grad)
    query_owned, key_owned, value_owned, output_owned = (
        lax.psum_scatter(query_weight_grad, ("seq", "exp", "dp"), scatter_dimension=1, tiled=True),
        lax.psum_scatter(key_weight_grad, ("seq", "exp", "dp"), scatter_dimension=1, tiled=True),
        lax.psum_scatter(value_weight_grad, ("seq", "exp", "dp"), scatter_dimension=1, tiled=True),
        lax.psum_scatter(output_weight_grad, ("seq", "exp", "dp"), scatter_dimension=0, tiled=True),
    )
    summed = lax.psum(
        (
            attn_gain_grad,
            query_bias_grad,
            key_bias_grad,
            value_bias_grad,
            output_bias_grad,
            sink_grad,
            moe_gain_grad,
        ),
        ("seq", "exp", "dp"),
    )
    return (
        output[None],
        input_grad[None],
        summed[0],
        query_owned,
        summed[1],
        key_owned,
        summed[2],
        value_owned,
        summed[3],
        output_owned,
        summed[4],
        summed[5],
        summed[6],
        gate_weight_grad[None],
        gate_bias_grad[None],
        up_weight_grad[None],
        up_bias_grad[None],
        down_weight_grad[None],
        down_bias_grad[None],
    )

MESH = pl.DeviceIdType.MESH
HERE = (0, 0, 0)
SIBLING = (0, 1, 0)
ACROSS = (1, 0, 0)
ALONG = (0, 0, 1)
NEAR = (0, 2, 0)
FAR = (0, 4, 0)
ENDS = (0, 6, 0)
THIRD = (0, 8, 0)
FOURTH = (0, 16, 0)


def flip(place, mask):
    x, e, y = place
    if mask[0]:
        x = 1 - x
    if mask[2]:
        y = 1 - y
    if mask[1] & 8:
        e = 2 * (2 - lax.div(e, 4)) + lax.rem(e, 2)
    if mask[1] & 16:
        e = 2 * (3 - 3 * lax.div(e, 4)) + lax.rem(e, 2)
    step = 0
    for bit in (1, 2, 4):
        if mask[1] & bit:
            step = step + bit - 2 * bit * lax.rem(lax.div(e, bit), 2)
    return x, e + step, y


def both(left, right):
    return tuple(a ^ b for a, b in zip(left, right))


def place_here():
    return lax.axis_index("seq"), lax.axis_index("exp"), lax.axis_index("dp")


def block_of_all(place):
    x, e, y = place
    return (e * 2 + x) * 2 + y


def block_of_tokens(place):
    x, e, y = place
    return lax.rem(lax.div(e, 2), 2) * 2 + x


def block_of_heads(place):
    x, e, y = place
    return (lax.div(e, 4) * 2 + lax.rem(e, 2)) * 2 + y


GROUPS = {
    "all": (block_of_all, 32, SIBLING, ACROSS, ALONG, (NEAR, ENDS), 0.5),
    "tokens": (block_of_tokens, 4, None, ACROSS, NEAR, (), 0.5),
    "heads": (block_of_heads, 8, SIBLING, FAR, ALONG, (), 1.0),
}


def partners(group):
    _, _, sibling, first, second, line, _ = GROUPS[group]
    return ([sibling] if sibling else []) + [first, second] + list(line)


def copies(group):
    _, _, sibling, _, _, line, _ = GROUPS[group]
    if line:
        return 4 * 8 + 5
    return 8 if sibling else 4


class Sender:
    def __init__(self, place, send, recv):
        self.place, self.send, self.recv, self.started = place, send, recv, []
        self.maybe = []
        line_place = lax.div(place[1], 2)
        self.inner = (line_place == 1) | (line_place == 2)

    def plan(self, source, target, mask, lands=None):
        number = len(self.started) + len(self.maybe)
        return pltpu.make_async_remote_copy(
            src_ref=source,
            dst_ref=target,
            send_sem=self.send.at[number],
            recv_sem=self.recv.at[number if lands is None else lands],
            device_id=flip(self.place, mask),
            device_id_type=MESH,
        )

    def push(self, source, target, mask):
        copy = self.plan(source, target, mask)
        copy.start()
        self.started.append(copy)
        return copy

    def push_within(self, source, target, mask, lands=None):
        copy = self.plan(source, target, mask, lands)
        number = len(self.started) + len(self.maybe)
        self.maybe.append(copy)
        pl.when(self.inner)(copy.start)
        return copy, number

    def finish(self):
        for copy in self.started:
            copy.wait_send()
        for copy in self.maybe:
            pl.when(self.inner)(copy.wait_send)


class Gather:
    def __init__(self, group, place, source, result, send, recv, local, share=None):
        self.index, _, self.sibling, self.first, self.second, line, usual = GROUPS[group]
        self.place, self.source, self.result = place, source, result
        self.rows = source.shape[0]
        share = usual if share is None else share
        self.cut = int(self.rows * share) // 16 * 16
        self.out = Sender(place, send, recv)
        self.own = pltpu.make_async_copy(source, self.at(HERE), local.at[0])
        self.masks = [HERE, NEAR, THIRD, FOURTH] if line else [HERE]
        self.ways, self.halves, self.lands, self.relayed = {}, {}, {}, []
        self.tails = {step: [] for step in range(len(self.masks))}

    def at(self, mask):
        return self.result.at[self.index(flip(self.place, mask))]

    def start(self):
        self.own.start()
        if len(self.masks) > 1:
            self.begin_line()

    def begin_line(self):
        self.near = self.out.push(self.source, self.at(HERE), NEAR)
        self.third, self.lands[2] = self.out.push_within(self.source, self.at(HERE), ENDS)

    def relay(self, step):
        if step in self.relayed:
            return
        self.relayed.append(step)
        if step == 1:
            self.near.wait_recv()
            self.fourth, self.lands[3] = self.out.push_within(self.at(NEAR), self.at(NEAR), ENDS)
            return
        copy = self.third if step == 2 else self.fourth
        pl.when(self.out.inner)(copy.wait_recv)
        block = self.at(self.masks[step])
        self.out.push_within(block, block, NEAR, self.lands[step])

    def reached(self, step):
        self.relay(step)
        if step > 1:
            copy = self.third if step == 2 else self.fourth
            pl.when(jnp.logical_not(self.out.inner))(copy.wait_recv)

    def pass_on(self, step, block, place):
        if self.sibling:
            self.tails[step].append(self.out.push(block, place, self.sibling))

    def plane(self, step):
        mask = self.masks[step]
        if step:
            self.reached(step)
        block = self.at(mask) if step else self.source
        self.ways[step] = (
            self.out.push(block, self.at(mask), self.first),
            self.out.push(block, self.at(mask), self.second),
        )
        self.pass_on(step, block, self.at(mask))

    def turn(self, step):
        halves = []
        mask, cut = self.masks[step], self.cut
        self.ways[step][0].wait_recv()
        seen = self.at(both(mask, self.first))
        if cut:
            halves.append(self.out.push(seen.at[:cut], seen.at[:cut], self.second))
        self.pass_on(step, seen, seen)
        self.ways[step][1].wait_recv()
        seen = self.at(both(mask, self.second))
        if cut < self.rows:
            halves.append(self.out.push(seen.at[cut:], seen.at[cut:], self.first))
        self.pass_on(step, seen, seen)
        self.halves[step] = halves

    def close(self, step):
        for half in self.halves[step]:
            half.wait_recv()
        seen = self.at(both(self.masks[step], both(self.first, self.second)))
        self.pass_on(step, seen, seen)

    def hop(self, number):
        for step in range(len(self.masks)):
            (self.plane, self.turn, self.close)[number](step)

    def passed(self, step):
        for copy in self.tails[step]:
            copy.wait_recv()

    def arrived(self):
        for step in range(len(self.masks)):
            self.passed(step)
        self.own.wait()

    def finish(self):
        self.out.finish()


def total(parts, low, high, store):
    def body(step, carry):
        rows = pl.ds(pl.multiple_of(low + step * 16, 16), 16)
        value = parts[0][rows].astype(jnp.float32)
        for part in parts[1:]:
            value = value + part[rows].astype(jnp.float32)
        store[rows] = value.astype(store.dtype)
        return carry

    if high > low:
        lax.fori_loop(0, (high - low) // 16, body, 0)


def by_tiles(width, tile, parts=2):
    size = -(-width // (128 * parts)) * 128
    for low in range(0, width, size):
        tile(low, min(size, width - low))


def seat_hot(seats, capacity, kind):
    lines = lax.broadcasted_iota(jnp.int32, (2 * capacity, seats.shape[-1]), 0)
    return (lines == seats).astype(kind)


def expert_sums(kind, rows, weights, seats, extra, collective, name, products=()):
    experts, pairs = seats.shape[1], seats.shape[2]
    thick = seats.shape[4]
    tokens = seats.shape[4] // 2
    half_rows = rows[0].shape[0] // experts
    pair_rows = half_rows // pairs
    capacity = pair_rows // 2
    hidden = rows[0].shape[1]
    width = weights[0].shape[1]
    first, second, line = ACROSS, ALONG, (ENDS, FAR, NEAR)
    masks = list(line) + [HERE]
    rounds = len(masks)
    cut = tokens // 2
    count_rows, count_extra = len(rows), len(extra)
    copies_out = rounds * (pairs + 4) + len(line)

    def body(*refs):
        refs = list(refs)
        left = refs[:count_rows]
        stored = refs[count_rows : 2 * count_rows]
        seat_ref = refs[2 * count_rows]
        more = refs[2 * count_rows + 1 : 2 * count_rows + 1 + count_extra]
        rest = refs[2 * count_rows + 1 + count_extra :]
        thin_wide, rest = rest[: 2 * len(products)], rest[2 * len(products) :]
        result, rest = rest[0], rest[1:]
        made, rest = rest[: len(products)], rest[len(products) :]
        wide, rest = rest[:count_rows], rest[count_rows:]
        staged, away, joined, own, side, arrive, ends, send, recv, local, weight_sem = rest[:11]
        if products:
            thin_stage, wide_stage, gross, product_sem, made_sem = rest[11:]
        weight_copies = [
            pltpu.make_async_copy(stored[item], wide[item], weight_sem.at[item])
            for item in range(count_rows)
        ]
        for copy in weight_copies:
            copy.start()
        place = place_here()
        x, e, y = place
        greet = [SIBLING, first, second] + list(line)
        barrier = pltpu.get_barrier_semaphore()
        for mask in greet:
            pl.semaphore_signal(barrier, inc=1, device_id=flip(place, mask), device_id_type=MESH)
        pl.semaphore_wait(barrier, len(greet))
        out = Sender(place, send, recv)

        def block(mask):
            there = flip(place, mask)
            return there[0] * 2 + there[2]

        halves = []
        for mask in masks:
            halves.append((flip(place, both(mask, SIBLING))[1], True))
            halves.append((flip(place, mask)[1], False))
        loads = {}

        def load(number):
            if number < len(halves):
                begin = pl.multiple_of(halves[number][0] * half_rows, 16)
                for item in range(count_rows):
                    copy = pltpu.make_async_copy(
                        left[item].at[pl.ds(begin, half_rows)],
                        staged.at[number % 2, item],
                        local.at[number % 2, item],
                    )
                    copy.start()
                    loads[number, item] = copy

        def make(number, store):
            load(number + 1)
            for item in range(count_rows):
                loads[number, item].wait()
                if number == 0:
                    weight_copies[item].wait()
            values = [staged[number % 2, item] for item in range(count_rows)]
            if kind == "result":
                part = halves[number][0]
                factors = []
                for pair in range(pairs):
                    hot = seat_hot(seat_ref[0, part, pair], capacity, jnp.float32)
                    factors.append(jnp.sum(hot * more[0][part, pair], axis=1, keepdims=True))
                factor = jnp.concatenate(factors, axis=0)
                once = jnp.where((x == 0) & (y == 0), 1.0, 0.0).astype(jnp.float32)

            def tile(low, size):
                area = pl.ds(low, size)
                value = jnp.dot(values[0], wide[0][:, area], preferred_element_type=jnp.float32)
                if kind == "gradient":
                    value += jnp.dot(values[1], wide[1][:, area], preferred_element_type=jnp.float32)
                else:
                    value = (value + once * more[1][:, area]) * factor
                store(low, size, value.astype(jnp.bfloat16))

            by_tiles(width, tile)

        def to_sibling(step):
            slot = step % 2

            def store(low, size, value):
                away[slot, :, pl.ds(low, size)] = value

            if step >= 2:
                for copy in sent[step - 2]:
                    copy.wait_send()
            make(2 * step, store)
            sent[step] = [
                out.push(
                    away.at[slot].at[pair * pair_rows : (pair + 1) * pair_rows],
                    joined.at[step, pair].at[pair_rows : 2 * pair_rows],
                    SIBLING,
                )
                for pair in range(pairs)
            ]

        def to_here(step):
            def store(low, size, value):
                for pair in range(pairs):
                    joined[step, pair, :pair_rows, pl.ds(low, size)] = value[
                        pair * pair_rows : (pair + 1) * pair_rows
                    ]

            make(2 * step + 1, store)

        def combine(step):
            for copy in sent[step]:
                copy.wait_recv()
            part = halves[2 * step + 1][0]
            for pair in range(pairs):
                hot = jnp.concatenate(
                    [seat_hot(seat_ref[mate, part, pair], capacity, jnp.bfloat16) for mate in range(2)],
                    axis=0,
                )

                def tile(low, size):
                    value = inner_rows(hot, joined[step, pair, :, pl.ds(low, size)])
                    value = value.astype(jnp.bfloat16)
                    own[step * 4 + pair * 2, :, pl.ds(low, size)] = value[:tokens]
                    own[step * 4 + pair * 2 + 1, :, pl.ds(low, size)] = value[tokens:]

                by_tiles(width, tile)

        def outward(step):
            corner = own.at[step * 4 + block(both(first, second))]
            return [
                out.push(corner.at[:cut], side.at[step].at[:cut], first),
                out.push(corner.at[cut:], side.at[step].at[cut:], second),
            ]

        def inward(step, parts):
            by_first = own.at[step * 4 + block(first)]
            by_second = own.at[step * 4 + block(second)]
            for part in parts:
                part.wait_recv()
            total([by_second, side.at[step]], 0, cut, by_second)
            total([by_first, side.at[step]], cut, tokens, by_first)
            return (
                out.push(by_first, arrive.at[step * 2], first),
                out.push(by_second, arrive.at[step * 2 + 1], second),
            )

        def close(step, ways):
            kept = own.at[step * 4 + block(HERE)]
            for way in ways:
                way.wait_recv()
            parts = [kept, arrive.at[step * 2], arrive.at[step * 2 + 1]]
            if masks[step] != HERE:
                total(parts, 0, tokens, kept)
                reach.append(out.push(kept, ends.at[step], masks[step]))
                return
            for number, copy in enumerate(reach):
                copy.wait_recv()
                parts.append(ends.at[number])
            total(parts, 0, tokens, result)

        chunks = rows[0].shape[0] // thick

        def product_loads(item, number):
            slot = lax.rem(number, 2)
            begin = pl.multiple_of(number * thick, 16)
            return [
                pltpu.make_async_copy(
                    thin_wide[2 * item + part].at[pl.ds(begin, thick)], stage.at[slot], product_sem.at[slot, part]
                )
                for part, stage in enumerate((thin_stage, wide_stage))
            ]

        written = []

        def multiply(item, begin, end):
            if begin == 0:
                for copy in product_loads(item, 0):
                    copy.start()
                if written:
                    written[-1].wait()
                else:
                    gross[...] = jnp.zeros_like(gross)

            def step(number, carry):
                @pl.when(number + 1 < chunks)
                def _():
                    for copy in product_loads(item, number + 1):
                        copy.start()

                for copy in product_loads(item, number):
                    copy.wait()
                slot = lax.rem(number, 2)
                keep = jnp.where(number == 0, 0.0, 1.0).astype(jnp.float32)

                def tile(low, size):
                    area = pl.ds(low, size)
                    value = inner_rows(thin_stage[slot], wide_stage[slot, :, area])
                    gross[:, area] = gross[:, area] * keep + value

                by_tiles(width, tile, 3)
                return carry

            lax.fori_loop(begin, end, step, 0)
            if end == chunks:
                copy = pltpu.make_async_copy(gross, made[item], made_sem.at[0])
                copy.start()
                written.append(copy)

        todo = [(item, begin) for item in range(len(products)) for begin in range(0, chunks, 3)]

        def some(number):
            for item, begin in todo[:number]:
                multiply(item, begin, min(begin + 3, chunks))
            del todo[:number]

        sent, corners, ways, reach = {}, {}, {}, []
        load(0)
        for step in range(rounds + 2):
            if step < rounds:
                to_sibling(step)
                to_here(step)
                combine(step)
                corners[step] = outward(step)
            if 0 <= step - 1 < rounds:
                ways[step - 1] = inward(step - 1, corners[step - 1])
            if 0 <= step - 2 < rounds:
                close(step - 2, ways[step - 2])
            some((2, 2, 3, 2, 0, 0)[step])
        some(len(todo))
        if written:
            written[-1].wait()
        for step in range(rounds):
            if step >= rounds - 2:
                for copy in sent[step]:
                    copy.wait_send()
        exchanged = {id(copy) for step in range(rounds) for copy in sent[step]}
        for copy in out.started:
            if id(copy) not in exchanged:
                copy.wait_send()

    vmem, anywhere = pl.BlockSpec(memory_space=pltpu.VMEM), pl.BlockSpec(memory_space=pl.ANY)
    for_products = []
    if products:
        for_products = [
            pltpu.VMEM((2, thick, hidden), jnp.bfloat16),
            pltpu.VMEM((2, thick, width), jnp.bfloat16),
            pltpu.VMEM((hidden, width), jnp.float32),
            pltpu.SemaphoreType.DMA((2, 2)),
            pltpu.SemaphoreType.DMA((1,)),
        ]
    return pl.pallas_call(
        body,
        out_shape=[jax.ShapeDtypeStruct((tokens, width), jnp.float32)]
        + [jax.ShapeDtypeStruct((hidden, width), jnp.float32)] * len(products),
        in_specs=[anywhere] * (2 * count_rows)
        + [vmem] * (1 + count_extra)
        + [anywhere] * (2 * len(products)),
        out_specs=[vmem] + [anywhere] * len(products),
        scratch_shapes=[pltpu.VMEM(weight.shape, jnp.bfloat16) for weight in weights]
        + [
            pltpu.VMEM((2, count_rows, half_rows, hidden), jnp.bfloat16),
            pltpu.VMEM((2, half_rows, width), jnp.bfloat16),
            pltpu.VMEM((rounds, pairs, 2 * pair_rows, width), jnp.bfloat16),
            pltpu.VMEM((rounds * 4, tokens, width), jnp.bfloat16),
            pltpu.VMEM((rounds, tokens, width), jnp.bfloat16),
            pltpu.VMEM((rounds * 2, tokens, width), jnp.bfloat16),
            pltpu.VMEM((len(line), tokens, width), jnp.bfloat16),
            pltpu.SemaphoreType.DMA((copies_out,)),
            pltpu.SemaphoreType.DMA((copies_out,)),
            pltpu.SemaphoreType.DMA((2, count_rows)),
            pltpu.SemaphoreType.DMA((count_rows,)),
        ]
        + for_products,
        compiler_params=pltpu.CompilerParams(
            collective_id=collective, has_side_effects=True, vmem_limit_bytes=62 * 1024 * 1024
        ),
        name=name,
    )(*rows, *weights, seats, *extra, *[array for pair in products for array in pair])


def expert_rows_kernel(own_block, cotangents, weights, biases, seats, shares, capacity, collective, name):
    experts, pairs = seats.shape[0], seats.shape[1]
    tokens, width = own_block.shape
    blocks = cotangents.shape[0]
    hidden = weights[0].shape[0]
    pair_rows = 2 * capacity
    half_rows = pairs * pair_rows
    row_count = experts * half_rows
    copies_out = copies("all")

    def body(*refs):
        (own_ref, cot_ref, *stored, gate_bias, up_bias, seat_ref, share_ref) = refs[:9]
        (rows_out, grads_out, act_out, dgate_out, dup_out, gate_sum, up_sum, down_sum, held) = refs[9:18]
        (stage, lines, thin, pre, back, gate, up, down) = refs[18:26]
        (send, recv, local, load_sem, line_sem, thin_sem, weight_sem) = refs[26:]
        weight_copies = [
            pltpu.make_async_copy(stored[item], goal, weight_sem.at[item])
            for item, goal in enumerate((gate, up, down))
        ]
        for copy in weight_copies[::-1]:
            copy.start()
        place = place_here()
        x, e, y = place
        greet = partners("all")
        barrier = pltpu.get_barrier_semaphore()
        for mask in greet:
            pl.semaphore_signal(barrier, inc=1, device_id=flip(place, mask), device_id_type=MESH)
        pl.semaphore_wait(barrier, len(greet))
        work = Gather("all", place, own_ref, held, send, recv, local)
        work.start()
        gate_sum[...] = jnp.zeros_like(gate_sum)
        up_sum[...] = jnp.zeros_like(up_sum)
        down_sum[...] = jnp.zeros_like(down_sum)
        halves = []
        for mask in work.masks:
            halves.append(flip(place, mask)[1])
            halves.append(flip(place, both(mask, SIBLING))[1])
        turnstile = {"load": 0, "line": 0}
        line_copies, thin_copies = [], []

        fetched = {}

        def fetch(scaled, number):
            bank = len(fetched) % 2
            begin = halves[number] * pairs * 2
            copies_in = [
                pltpu.make_async_copy(
                    (cot_ref if scaled else held).at[pl.ds(begin + 2 * pair, 2)],
                    stage.at[2 * bank + pair],
                    load_sem.at[2 * bank + pair],
                )
                for pair in range(pairs)
            ]
            for copy in copies_in:
                copy.start()
            fetched[scaled, number] = (bank, copies_in)

        def pick(scaled, number):
            part = halves[number]
            bank, copies_in = fetched[scaled, number]
            slot = turnstile["line"] % 2
            turnstile["line"] += 1
            if len(line_copies) >= 2:
                line_copies[-2].wait()
            for pair in range(pairs):
                copies_in[pair].wait()
                hot = seat_hot(seat_ref[part, pair], capacity, jnp.float32)
                if scaled:
                    factor = jnp.sum(hot * share_ref[part, pair], axis=1, keepdims=True)
                hot = hot.astype(jnp.bfloat16)
                blocks_here = stage[2 * bank + pair].reshape(2 * tokens, width)
                value = jnp.dot(hot, blocks_here, preferred_element_type=jnp.float32)
                if scaled:
                    value = value * factor
                value = value.astype(jnp.bfloat16)
                lines[slot, pair * pair_rows : (pair + 1) * pair_rows] = value
                if scaled:
                    down_sum[...] += jnp.sum(value.astype(jnp.float32), axis=0, keepdims=True)
            copy = pltpu.make_async_copy(
                lines.at[slot],
                (grads_out if scaled else rows_out).at[
                    pl.ds(pl.multiple_of(part * half_rows, 16), half_rows)
                ],
                line_sem.at[slot],
            )
            copy.start()
            line_copies.append(copy)
            return lines.at[slot]

        def backward(number):
            picked = pick(True, number)
            if number == 0:
                weight_copies[2].wait()
            back[number] = times_transposed(picked[...], down[...])

        def forward(number):
            part = halves[number]
            picked = pick(False, number)
            if number == 0:
                weight_copies[0].wait()
                weight_copies[1].wait()
            pre[0] = times_transposed(picked[...], gate[...])
            pre[1] = times_transposed(picked[...], up[...])
            slot = number % 2
            if number >= 2:
                for copy in thin_copies[-6:-3]:
                    copy.wait()

            def chunk(step, sums):
                area = pl.ds(pl.multiple_of(step * 16, 16), 16)
                gate_tanh = jnp.tanh((pre[0, area] + gate_bias[...]) * (1.0 / clip_level))
                up_tanh = jnp.tanh((pre[1, area] + up_bias[...]) * (1.0 / clip_level))
                gate_soft = clip_level * gate_tanh
                up_more = clip_level * up_tanh + 1.0
                bend = jax.nn.sigmoid(glu_alpha * gate_soft)
                glow = gate_soft * bend
                grad = back[number, area]
                dgate = grad * up_more * (bend + glu_alpha * glow * (1.0 - bend))
                dgate = (dgate * (1.0 - gate_tanh * gate_tanh)).astype(jnp.bfloat16)
                dup = (grad * glow * (1.0 - up_tanh * up_tanh)).astype(jnp.bfloat16)
                thin[slot, 0, area] = (glow * up_more).astype(jnp.bfloat16)
                thin[slot, 1, area] = dgate
                thin[slot, 2, area] = dup
                return sums[0] + dgate.astype(jnp.float32), sums[1] + dup.astype(jnp.float32)

            zero = jnp.zeros((16, hidden), jnp.float32)
            sums = lax.fori_loop(0, half_rows // 16, chunk, (zero, zero))
            gate_sum[...] += jnp.sum(sums[0], axis=0, keepdims=True)
            up_sum[...] += jnp.sum(sums[1], axis=0, keepdims=True)
            for item, goal in enumerate((act_out, dgate_out, dup_out)):
                copy = pltpu.make_async_copy(
                    thin.at[slot, item],
                    goal.at[pl.ds(pl.multiple_of(part * half_rows, 16), half_rows)],
                    thin_sem.at[slot, item],
                )
                copy.start()
                thin_copies.append(copy)

        order = ["p0B0B1b0B2b1t0p1r2B3b2c0o0F0b3r3p2t1w0F1f0B4f1c1F2b4"]
        order += ["p3t2w1F3f2B5f3B6b5c2F4b6w2F5f4t3B7f5b7c3F6w3F7f6f7"]
        acts = {
            "p": work.plane,
            "t": work.turn,
            "c": work.close,
            "w": work.passed,
            "r": work.relay,
            "o": lambda number: work.own.wait(),
            "B": lambda number: fetch(True, number),
            "F": lambda number: fetch(False, number),
            "b": backward,
            "f": forward,
        }
        order = "".join(order)
        for low in range(0, len(order), 2):
            acts[order[low]](int(order[low + 1]))
        for copy in line_copies[-2:] + thin_copies[-6:]:
            copy.wait()
        work.finish()

    vmem, anywhere = pl.BlockSpec(memory_space=pltpu.VMEM), pl.BlockSpec(memory_space=pl.ANY)
    bf16, f32 = jnp.bfloat16, jnp.float32
    return pl.pallas_call(
        body,
        out_shape=[
            jax.ShapeDtypeStruct((row_count, width), bf16),
            jax.ShapeDtypeStruct((row_count, width), bf16),
            jax.ShapeDtypeStruct((row_count, hidden), bf16),
            jax.ShapeDtypeStruct((row_count, hidden), bf16),
            jax.ShapeDtypeStruct((row_count, hidden), bf16),
            jax.ShapeDtypeStruct((1, hidden), f32),
            jax.ShapeDtypeStruct((1, hidden), f32),
            jax.ShapeDtypeStruct((1, width), f32),
            jax.ShapeDtypeStruct((blocks, tokens, width), bf16),
        ],
        in_specs=[anywhere] * 5 + [vmem] * 4,
        out_specs=[anywhere] * 5 + [vmem] * 3 + [anywhere],
        scratch_shapes=[
            pltpu.VMEM((4, 2, tokens, width), bf16),
            pltpu.VMEM((2, half_rows, width), bf16),
            pltpu.VMEM((2, 3, half_rows, hidden), bf16),
            pltpu.VMEM((2, half_rows, hidden), f32),
            pltpu.VMEM((experts, half_rows, hidden), f32),
        ]
        + [pltpu.VMEM(weight.shape, bf16) for weight in weights]
        + [
            pltpu.SemaphoreType.DMA((copies_out,)),
            pltpu.SemaphoreType.DMA((copies_out,)),
            pltpu.SemaphoreType.DMA((1,)),
            pltpu.SemaphoreType.DMA((4,)),
            pltpu.SemaphoreType.DMA((2,)),
            pltpu.SemaphoreType.DMA((2, 3)),
            pltpu.SemaphoreType.DMA((3,)),
        ],
        compiler_params=pltpu.CompilerParams(
            collective_id=collective, has_side_effects=True, vmem_limit_bytes=60 * 1024 * 1024
        ),
        name=name,
    )(own_block, cotangents, *weights, *biases, seats, shares)


class Scatter:
    def __init__(self, group, place, source, result, side, arrive, send, recv, spare, mate=None):
        self.index, _, self.sibling, self.first, self.second, _, share = GROUPS[group]
        self.place, self.source, self.result = place, source, result
        self.side, self.arrive, self.mate = side, arrive, mate
        self.rows = result.shape[0]
        self.cut = int(self.rows * (1.0 - share)) // 16 * 16
        self.corner = both(self.first, self.second)
        self.out = Sender(place, send, recv)
        self.crossing = {}

    def at(self, mask):
        return self.source.at[self.index(flip(self.place, mask))]

    def cross(self):
        for spot, mask in enumerate((self.corner, self.first, self.second, HERE)):
            self.crossing[mask] = (
                self.out.push(self.at(both(mask, self.sibling)), self.mate.at[spot], self.sibling),
                self.mate.at[spot],
            )

    def ready(self, mask):
        if not self.sibling:
            return [self.at(mask)]
        copy, block = self.crossing[mask]
        copy.wait_recv()
        return [self.at(mask), block]

    def outward(self):
        corner, cut = self.at(self.corner), self.cut
        parts = self.ready(self.corner)
        if len(parts) > 1:
            total(parts, 0, self.rows, corner)
        self.halves = []
        if cut:
            self.halves.append(self.out.push(corner.at[:cut], self.side.at[:cut], self.first))
        if cut < self.rows:
            self.halves.append(self.out.push(corner.at[cut:], self.side.at[cut:], self.second))

    def inward(self):
        by_first, by_second = self.ready(self.first), self.ready(self.second)
        for half in self.halves:
            half.wait_recv()
        cut, rows = self.cut, self.rows
        total(by_second + [self.side], 0, cut, by_second[0])
        total(by_first + [self.side], cut, rows, by_first[0])
        if self.sibling:
            total(by_second, cut, rows, by_second[0])
            total(by_first, 0, cut, by_first[0])
        self.ways = (
            self.out.push(by_first[0], self.arrive.at[0], self.first),
            self.out.push(by_second[0], self.arrive.at[1], self.second),
        )

    def close(self):
        parts = self.ready(HERE)
        for way in self.ways:
            way.wait_recv()
        total(parts + [self.arrive.at[0], self.arrive.at[1]], 0, self.rows, self.result)

    def finish(self):
        self.out.finish()


def lanes(shape):
    return lax.broadcasted_iota(jnp.int32, shape, len(shape) - 1)


def swapped(value):
    width = value.shape[-1]
    upper = pltpu.roll(value, width - HD // 2, len(value.shape) - 1)
    lower = pltpu.roll(value, HD // 2, len(value.shape) - 1)
    return jnp.where(lanes(value.shape) % HD < HD // 2, upper, lower)


def halves_of(value, member):
    low = lanes(value.shape) < HD
    zero = jnp.zeros_like(value)
    if member == 0:
        kept = jnp.where(low, value, zero)
        return kept, pltpu.roll(kept, HD, 1)
    kept = jnp.where(low, zero, value)
    return pltpu.roll(kept, HD, 1), kept


def seen(marks, held, first_key=0):
    rows = marks.shape[1]
    lines = []
    for query in range(2):
        parts = []
        for key in range(2):
            if key > query:
                parts.append(jnp.zeros((rows, rows), jnp.bool_))
                continue
            same = marks[held + query] == marks[held + key].T
            if key == query:
                down = lax.broadcasted_iota(jnp.int32, (rows, rows), 0)
                same = same & (down >= lanes((rows, rows)))
            parts.append(same)
        lines.append(parts)
    return lines


def mask_of(marks, held):
    lines = seen(marks, held)
    return jnp.concatenate(
        [
            jnp.concatenate([jnp.where(part, 1.0, 0.0) for part in parts], axis=1)
            for parts in lines
        ],
        axis=0,
    )


def pick_lane(value, number):
    return jnp.sum(jnp.where(lanes(value.shape) == number, value, 0.0), axis=1, keepdims=True)


def attention_forward(
    normed, query_rows, key_rows, value_rows, output_rows, marks, table, extra, biases, tables, sinks, collective, name
):
    tokens, width = normed.shape
    block = 4 * tokens
    seq_len = 2 * tokens
    columns = 8 * query_rows.shape[0]
    pairs = columns // 128
    scale = 1.0 / math.sqrt(HD)
    bf16, f32 = jnp.bfloat16, jnp.float32
    gathers = [
        ("tokens", normed),
        ("heads", query_rows),
        ("heads", key_rows),
        ("heads", value_rows),
        ("tokens", marks),
        ("heads", output_rows),
        ("all", table),
        ("all", extra),
    ]
    count = len(gathers)

    def body(*refs):
        refs = list(refs)

        def take(number):
            got = refs[:number]
            del refs[:number]
            return got

        sources = take(count)
        query_bias, key_bias, value_bias, cosine, sine, sink_ref = take(6)
        (result, query_out, key_out, value_out, mixed_out, lse_out, mask) = take(7)
        kept_out = take(5)
        far_out = take(2)
        held = take(count - 2)
        (key_half, value_half, partial, side, arrive) = take(5)
        sems = [take(3) for _ in range(count)]
        sum_sems = take(3)
        (keep_sem,) = take(1)
        place = place_here()
        greet = []
        for group, _ in gathers:
            greet += [step for step in partners(group) if step not in greet]
        barrier = pltpu.get_barrier_semaphore()
        for step in greet:
            pl.semaphore_signal(barrier, inc=1, device_id=flip(place, step), device_id_type=MESH)
        pl.semaphore_wait(barrier, len(greet))
        works = [
            Gather(
                group, place, sources[item], (held + far_out)[item], *sems[item], share=0.25 if item == 7 else None
            )
            for item, (group, _) in enumerate(gathers)
        ]
        all_tokens, all_query, all_key, all_value, all_marks, all_output = held
        early, output_work, table_work, extra_work = works[:5], works[5], works[6], works[7]
        early = [early[4]] + early[:4]
        table_work.start()
        for work in early:
            work.start()
            work.plane(0)
        extra_work.start()
        extra_work.plane(0)
        early[0].turn(0)
        table_work.relay(1)
        table_work.relay(2)
        for work in early[1:]:
            work.turn(0)
        extra_work.turn(0)
        extra_work.plane(1)
        extra_work.relay(2)
        output_work.start()
        output_work.plane(0)
        for work in early:
            work.close(0)
        for work in early:
            work.passed(0)
            work.own.wait()
        keeps = []

        def keep(item, goal):
            copy = pltpu.make_async_copy(held[item], kept_out[goal], keep_sem.at[goal])
            copy.start()
            keeps.append(copy)

        for item in range(4):
            keep(item, item)
        x_all = all_tokens[...].reshape(block, width)

        def turned(value, low):
            return value * cosine[...] + swapped(value) * sine[...]

        def project(number, carry):
            weight = all_query[pl.ds(pl.multiple_of(2 * number, 2), 2)].reshape(256, width)
            value = times_transposed(x_all, weight)
            for part in range(2):
                area = pl.ds(pl.multiple_of((2 * number + part) * 128, 128), 128)
                head = value[:, part * 128 : (part + 1) * 128] + query_bias[:, area]
                query_out[:, area] = turned(head, 0).astype(bf16)
            return carry

        lax.fori_loop(0, pairs // 2, project, 0)
        key = times_transposed(x_all, all_key[...].reshape(128, width)) + key_bias[...]
        key = turned(key, 0).astype(bf16)
        key_out[...] = key
        value = times_transposed(x_all, all_value[...].reshape(128, width)) + value_bias[...]
        value = value.astype(bf16)
        value_out[...] = value
        for member in range(2):
            for part, half in enumerate(halves_of(key, member)):
                key_half[2 * member + part] = half
            for part, half in enumerate(halves_of(value, member)):
                value_half[2 * member + part] = half
        for half in range(2):
            mask[half] = mask_of(all_marks, 2 * half)
        table_work.relay(3)
        extra_work.close(0)
        extra_work.relay(3)
        extra_work.plane(2)
        lse_out[...] = jnp.zeros_like(lse_out)

        def attend(number, carry):
            pair = lax.div(number, 2)
            half = lax.rem(number, 2)
            member = lax.div(pair, pairs // 2)
            rows = pl.ds(pl.multiple_of(half * seq_len, seq_len), seq_len)
            area = pl.ds(pl.multiple_of(pair * 128, 128), 128)
            query = query_out[rows, area]
            mixed = jnp.zeros((seq_len, 128), f32)
            for part in range(2):
                raw = times_transposed(query, key_half[2 * member + part, rows]) * scale
                raw = jnp.where(mask[half] > 0.0, raw, masked_score)
                sink = sink_ref[0, 2 * pair + part]
                peak = jnp.maximum(jnp.max(raw, axis=1, keepdims=True), sink)
                mass = jnp.sum(jnp.exp(raw - peak), axis=1, keepdims=True) + jnp.exp(sink - peak)
                lse = peak + jnp.log(mass)
                probs = jnp.exp(raw - lse).astype(bf16)
                mixed = mixed + jnp.dot(
                    probs, value_half[2 * member + part, rows], preferred_element_type=f32
                )
                spot = lanes((seq_len, 128)) == 2 * pair + part
                lse_out[rows] = jnp.where(spot, lse, lse_out[rows])
            mixed_out[rows, area] = mixed.astype(bf16)
            return carry

        lax.fori_loop(0, pairs, attend, 0)
        extra_work.turn(1)
        output_work.turn(0)
        lax.fori_loop(pairs, 2 * pairs, attend, 0)
        table_work.hop(0)
        extra_work.plane(3)
        output_work.close(0)
        output_work.passed(0)
        output_work.own.wait()
        keep(5, 4)

        def tile(low, size):
            weight = all_output[:, :, pl.ds(low, size)].reshape(columns, size)
            value = jnp.dot(mixed_out[...], weight, preferred_element_type=f32).astype(bf16)
            partial[:, :, pl.ds(low, size)] = value.reshape(4, tokens, size)

        by_tiles(width, tile)
        run = Scatter("tokens", place, partial, result, side, arrive, *sum_sems)
        run.outward()
        extra_work.close(1)
        extra_work.turn(2)
        run.inward()
        extra_work.close(2)
        table_work.hop(1)
        extra_work.turn(3)
        run.close()
        table_work.hop(2)
        extra_work.close(3)
        for work in (table_work, extra_work):
            work.arrived()
        run.finish()
        for copy in keeps:
            copy.wait()
        for work in works:
            work.finish()

    vmem, anywhere = pl.BlockSpec(memory_space=pltpu.VMEM), pl.BlockSpec(memory_space=pl.ANY)
    smem = pl.BlockSpec(memory_space=pltpu.SMEM)
    kept = [(4,) + normed.shape] + [(8,) + rows.shape for rows in (query_rows, key_rows, value_rows, output_rows)]
    blocks = [GROUPS[group][1] for group, _ in gathers]
    return pl.pallas_call(
        body,
        out_shape=[
            jax.ShapeDtypeStruct((tokens, width), f32),
            jax.ShapeDtypeStruct((block, columns), bf16),
            jax.ShapeDtypeStruct((block, 128), bf16),
            jax.ShapeDtypeStruct((block, 128), bf16),
            jax.ShapeDtypeStruct((block, columns), bf16),
            jax.ShapeDtypeStruct((block, 128), f32),
            jax.ShapeDtypeStruct((2, seq_len, seq_len), f32),
        ]
        + [jax.ShapeDtypeStruct(shape, bf16) for shape in kept]
        + [
            jax.ShapeDtypeStruct((blocks[item],) + array.shape, array.dtype)
            for item, (_, array) in list(enumerate(gathers))[-2:]
        ],
        in_specs=[anywhere] * count + [vmem] * 5 + [smem],
        out_specs=[vmem] * 7 + [anywhere] * 7,
        scratch_shapes=[
            pltpu.VMEM((blocks[item],) + array.shape, array.dtype)
            for item, (_, array) in enumerate(gathers[:-2])
        ]
        + [
            pltpu.VMEM((4, block, 128), bf16),
            pltpu.VMEM((4, block, 128), bf16),
            pltpu.VMEM((4, tokens, width), bf16),
            pltpu.VMEM((tokens, width), bf16),
            pltpu.VMEM((2, tokens, width), bf16),
        ]
        + [
            pltpu.SemaphoreType.DMA((size,))
            for group, _ in gathers
            for size in (copies(group), copies(group), 1)
        ]
        + [pltpu.SemaphoreType.DMA((copies("tokens"),))] * 2
        + [pltpu.SemaphoreType.DMA((1,)), pltpu.SemaphoreType.DMA((5,))],
        compiler_params=pltpu.CompilerParams(
            collective_id=collective, has_side_effects=True, vmem_limit_bytes=60 * 1024 * 1024
        ),
        name=name,
    )(*[array for _, array in gathers], *biases, *tables, sinks)


def attention_backward(
    outer, query, key, value, mixed, log_total, mask, tokens_kept, weights, tables, sinks, plain, small, collective, name
):
    tokens, width = outer.shape
    block = 4 * tokens
    seq_len = 2 * tokens
    columns = query.shape[1]
    pairs = columns // 128
    scale = 1.0 / math.sqrt(HD)
    bf16, f32 = jnp.bfloat16, jnp.float32
    owned = [rows.shape[1] for rows in weights]
    groups = ["heads"] * 4 + ["tokens"]

    def body(*refs):
        refs = list(refs)

        def take(number):
            got = refs[:number]
            del refs[:number]
            return got

        (outer_ref,) = take(1)
        query_ref, key_ref, value_ref, mixed_ref, lse_ref, mask_ref = take(6)
        stored = take(5)
        cosine, sine, sink_ref, plain_ref, small_ref = take(5)
        results = take(5)
        (small_out,) = take(1)
        held = take(5)
        grads, key_half, value_half = take(3)
        mixed_grad, query_grad, key_grad, value_grad = take(4)
        key_sum, value_sum, sink_sum, small_own, small_all = take(5)
        output_part, key_part, value_part = take(3)
        mates, sides, arrives = take(4), take(5), take(5)
        load_sem, gather_sems, small_sems = take(1)[0], take(3), take(3)
        sum_sems = [take(3) for _ in groups]
        place = place_here()
        greet = []
        for group in ("tokens", "heads", "all"):
            greet += [step for step in partners(group) if step not in greet]
        barrier = pltpu.get_barrier_semaphore()
        for step in greet:
            pl.semaphore_signal(barrier, inc=1, device_id=flip(place, step), device_id_type=MESH)
        pl.semaphore_wait(barrier, len(greet))
        work = Gather("tokens", place, outer_ref, grads, *gather_sems)
        work.start()
        work.plane(0)
        loads = []
        for item in (4, 1, 2, 3, 0):
            copy = pltpu.make_async_copy(stored[item], held[item], load_sem.at[item])
            copy.start()
            loads.append(copy)
        all_tokens, all_query, all_key, all_value, all_output = held
        for member in range(2):
            for part, half in enumerate(halves_of(key_ref[...], member)):
                key_half[2 * member + part] = half
            for part, half in enumerate(halves_of(value_ref[...], member)):
                value_half[2 * member + part] = half
        key_sum[...] = jnp.zeros_like(key_sum)
        value_sum[...] = jnp.zeros_like(value_sum)
        sink_sum[...] = jnp.zeros_like(sink_sum)
        small_own[...] = small_ref[...]
        work.turn(0)
        work.close(0)
        work.own.wait()
        work.finish()

        parts = [all_output, key_part, value_part, output_part, grads]
        sums = [
            Scatter(
                group,
                place,
                parts[item],
                results[item],
                sides[item],
                arrives[item],
                *sum_sems[item],
                mate=mates[item] if group == "heads" else None,
            )
            for item, group in enumerate(groups)
        ]
        of_query, of_key, of_value, of_output, of_tokens = sums

        def output_gradient(number, carry):
            area = pl.ds(pl.multiple_of(number * 128, 128), 128)
            rows = inner_rows(mixed_ref[:, area], grads[...].reshape(block, width))
            output_part[number] = rows.astype(bf16)
            return carry

        lax.fori_loop(0, pairs, output_gradient, 0)
        of_output.cross()
        loads[0].wait()

        def project(number, carry):
            weight = all_output[pl.ds(pl.multiple_of(2 * number, 2), 2)].reshape(256, width)
            area = pl.ds(pl.multiple_of(number * 256, 256), 256)
            mixed_grad[:, area] = times_transposed(
                grads[...].reshape(block, width), weight
            ).astype(bf16)
            return carry

        lax.fori_loop(0, pairs // 2, project, 0)
        of_output.outward()

        def back(value):
            return value * cosine[:seq_len] - swapped(value) * sine[:seq_len]

        def attend(number, carry):
            pair = lax.div(number, 2)
            half = lax.rem(number, 2)
            member = lax.div(pair, pairs // 2)
            rows = pl.ds(pl.multiple_of(half * seq_len, seq_len), seq_len)
            area = pl.ds(pl.multiple_of(pair * 128, 128), 128)
            queries = query_ref[rows, area]
            upstream = mixed_grad[rows, area]
            low = lanes((seq_len, 128)) < HD
            made = jnp.zeros((seq_len, 128), f32)
            for part in range(2):
                head = 2 * pair + part
                keys = key_half[2 * member + part, rows]
                lse = pick_lane(lse_ref[rows], head)
                raw = times_transposed(queries, keys) * scale
                raw = jnp.where(mask_ref[half] > 0.0, raw, masked_score)
                probs = jnp.exp(raw - lse)
                grad = times_transposed(upstream, value_half[2 * member + part, rows])
                delta = jnp.sum(probs * grad, axis=1, keepdims=True)
                inner = (probs * (grad - delta)).astype(bf16)
                made = made + jnp.dot(inner, keys, preferred_element_type=f32)
                mine = low if part == 0 else jnp.logical_not(low)
                value_sum[member, rows] += jnp.where(mine, inner_rows(probs.astype(bf16), upstream), 0.0)
                key_sum[member, rows] += jnp.where(mine, inner_rows(inner, queries), 0.0)
                lost = jnp.sum(jnp.exp(sink_ref[0, head] - lse) * delta, axis=0, keepdims=True)
                sink_sum[...] -= jnp.where(lanes((1, 128)) == head, lost, 0.0)
            query_grad[rows, area] = back(made * scale).astype(bf16)
            return carry

        lax.fori_loop(0, pairs, attend, 0)
        of_output.inward()
        lax.fori_loop(pairs, 2 * pairs, attend, 0)
        low = lanes((seq_len, 128)) < HD
        for half in range(2):
            rows = pl.ds(half * seq_len, seq_len)

            def joined(sums):
                first = sums[0, rows] + pltpu.roll(sums[0, rows], HD, 1)
                second = sums[1, rows] + pltpu.roll(sums[1, rows], HD, 1)
                return jnp.where(low, first, second)

            key_grad[rows] = back(joined(key_sum) * scale).astype(bf16)
            value_grad[rows] = joined(value_sum).astype(bf16)
        for copy in loads[1:]:
            copy.wait()

        def tile(low_column, size):
            area = pl.ds(low_column, size)

            def rows_of(weight):
                return weight[:, :, area].reshape(-1, size)

            total_grad = jnp.dot(query_grad[...], rows_of(all_query), preferred_element_type=f32)
            total_grad += jnp.dot(key_grad[...], rows_of(all_key), preferred_element_type=f32)
            total_grad += jnp.dot(value_grad[...], rows_of(all_value), preferred_element_type=f32)
            grads[:, :, area] = total_grad.astype(bf16).reshape(4, tokens, size)

        by_tiles(width, tile)
        of_tokens.outward()

        def query_gradient(number, carry):
            area = pl.ds(pl.multiple_of(number * 128, 128), 128)
            rows = inner_rows(query_grad[:, area], all_tokens[...].reshape(block, width))
            all_output[number] = rows.astype(bf16)
            return carry

        lax.fori_loop(0, pairs, query_gradient, 0)
        of_query.cross()
        for goal, grad in ((key_part, key_grad), (value_part, value_grad)):
            rows = inner_rows(grad[...], all_tokens[...].reshape(block, width))
            goal[...] = rows.astype(bf16).reshape(goal.shape)
        of_key.cross()
        of_value.cross()
        of_query.outward()
        of_key.outward()
        of_value.outward()
        low_column = 0
        for array in (query_grad, key_grad, value_grad):
            size = array.shape[1]
            small_own[3:4, low_column : low_column + size] = jnp.sum(
                array[...].astype(f32), axis=0, keepdims=True
            )
            low_column += size
        small_own[3:4, low_column : low_column + 128] = sink_sum[...]
        of_tokens.inward()
        of_query.inward()
        of_key.inward()
        of_value.inward()
        of_tokens.close()
        small_own[0:1] = jnp.sum(results[4][...] * plain_ref[...], axis=0, keepdims=True)
        spread = Gather("all", place, small_own, small_all, *small_sems)
        spread.start()
        spread.hop(0)
        spread.hop(1)
        spread.hop(2)
        of_output.close()
        of_query.close()
        of_key.close()
        of_value.close()
        spread.arrived()
        spread.finish()
        blocks = small_all.shape[0]
        whole = small_all[0]
        for number in range(1, blocks):
            whole = whole + small_all[number]
        small_out[0:4] = whole[0:4]
        for near in range(2):
            for side in range(2):
                chosen = [
                    number for number in range(blocks) if (number // 8 % 2, number // 2 % 2) == (near, side)
                ]
                part = small_all[chosen[0], 3:4]
                for number in chosen[1:]:
                    part = part + small_all[number, 3:4]
                small_out[4 + 2 * near + side : 5 + 2 * near + side] = part
        for part in sums:
            part.finish()

    vmem, anywhere = pl.BlockSpec(memory_space=pltpu.VMEM), pl.BlockSpec(memory_space=pl.ANY)
    smem = pl.BlockSpec(memory_space=pltpu.SMEM)
    rows_of = owned + [tokens]
    kept = [tokens_kept] + list(weights)
    return pl.pallas_call(
        body,
        out_shape=[jax.ShapeDtypeStruct((rows, width), f32) for rows in rows_of]
        + [jax.ShapeDtypeStruct(small.shape, f32)],
        in_specs=[anywhere] + [vmem] * 6 + [anywhere] * 5 + [vmem] * 2 + [smem] + [vmem] * 2,
        out_specs=[vmem] * 6,
        scratch_shapes=[pltpu.VMEM(array.shape, bf16) for array in kept]
        + [
            pltpu.VMEM((4, tokens, width), bf16),
            pltpu.VMEM((4, block, 128), bf16),
            pltpu.VMEM((4, block, 128), bf16),
            pltpu.VMEM((block, columns), bf16),
            pltpu.VMEM((block, columns), bf16),
            pltpu.VMEM((block, 128), bf16),
            pltpu.VMEM((block, 128), bf16),
            pltpu.VMEM((2, block, 128), f32),
            pltpu.VMEM((2, block, 128), f32),
            pltpu.VMEM((1, 128), f32),
            pltpu.VMEM(small.shape, f32),
            pltpu.VMEM((GROUPS["all"][1],) + small.shape, f32),
            pltpu.VMEM(weights[3].shape, bf16),
            pltpu.VMEM(weights[1].shape, bf16),
            pltpu.VMEM(weights[2].shape, bf16),
        ]
        + [pltpu.VMEM((4, rows, width), bf16) for rows in owned]
        + [pltpu.VMEM((rows, width), bf16) for rows in rows_of]
        + [pltpu.VMEM((2, rows, width), bf16) for rows in rows_of]
        + [pltpu.SemaphoreType.DMA((5,))]
        + [
            pltpu.SemaphoreType.DMA((size,))
            for group in ["tokens", "all"] + groups
            for size in (copies(group), copies(group), 1)
        ],
        compiler_params=pltpu.CompilerParams(
            collective_id=collective, has_side_effects=True, vmem_limit_bytes=62 * 1024 * 1024
        ),
        name=name,
    )(outer, query, key, value, mixed, log_total, mask, *kept, *tables, sinks, plain, small)


def close_by(
    tokens,
    segments,
    routes,
    gate_share,
    attn_gain,
    query_weight,
    query_bias,
    key_weight,
    key_bias,
    value_weight,
    value_bias,
    output_weight,
    output_bias,
    sink_logits,
    moe_gain,
    gate_weight,
    gate_bias,
    up_weight,
    up_bias,
    down_weight,
    down_bias,
    cotangent,
):
    count_rows = tokens.shape[1]
    width = tokens.shape[2]
    head_count = sink_logits.shape[0]
    kv_count = key_bias.shape[0] // HD
    group = head_count // kv_count
    experts = lax.axis_size("exp")
    devices = 4 * experts
    topk = routes.shape[2]
    capacity = count_rows * topk * 9 // (8 * experts)
    x, e, y = place_here()
    near_bit = lax.rem(lax.div(e, 2), 2)
    seq_len = 2 * count_rows

    chosen = routes[0].reshape(-1)
    expert_hot = (chosen[:, None] == jnp.arange(experts, dtype=jnp.int32)[None, :]).astype(
        jnp.int32
    )
    earlier = (jnp.cumsum(expert_hot, axis=0) - expert_hot).reshape(count_rows, topk, experts)
    named = expert_hot.reshape(count_rows, topk, experts)
    slot_table = jnp.sum((earlier + 1) * named, axis=1) - 1
    share_table = jnp.sum(named.astype(jnp.float32) * gate_share[0][:, :, None], axis=1)
    table = jnp.concatenate([slot_table.astype(jnp.float32).T, share_table.T], axis=0)

    resid = tokens[0].astype(jnp.float32)
    attn_norm, attn_norm_pull = jax.vjp(rms_apply, resid, attn_gain)
    normed = attn_norm.astype(jnp.bfloat16)
    block_tokens = 4 * count_rows
    held_kv = 2
    held_heads = held_kv * group

    def own_part(vector):
        parts = vector.reshape(2, 2, 2, -1)
        parts = lax.dynamic_index_in_dim(parts, x, 0, keepdims=False)
        return lax.dynamic_index_in_dim(parts, near_bit, 1, keepdims=False).reshape(1, -1)

    position = jnp.arange(seq_len, dtype=jnp.int32)
    cosine, sine = rope_tables(position, HD)
    cosine = jnp.tile(cosine, (2, 4))
    sine = jnp.tile(jnp.concatenate([-sine, sine], axis=1), (2, 2))
    own_ids = lax.dynamic_slice_in_dim(segments[0], x * count_rows, count_rows, 0)
    marks = jnp.broadcast_to(own_ids.astype(jnp.float32)[:, None], (count_rows, count_rows))
    sinks = own_part(sink_logits)
    (
        attn_out,
        query_rot,
        key_rot,
        value_low,
        mixed,
        log_total,
        mask,
        group_tokens,
        group_query,
        group_key,
        group_value,
        group_output,
        tables,
        all_cotangents,
    ) = attention_forward(
        normed,
        query_weight.T,
        key_weight.T,
        value_weight.T,
        output_weight,
        marks,
        table,
        cotangent[0],
        (own_part(query_bias), own_part(key_bias), own_part(value_bias)),
        (cosine, sine),
        sinks,
        0,
        "attention_forward",
    )
    hidden = resid + (attn_out + output_bias)
    moe_norm, moe_norm_pull = jax.vjp(rms_apply, hidden, moe_gain)
    normed_moe = moe_norm.astype(jnp.bfloat16)

    def by_pairs(part):
        part = jnp.moveaxis(part.reshape(experts, 2, 2, experts, count_rows), 3, 0)
        return part.reshape(experts, experts, 2, 1, 2 * count_rows)

    slots = tables[:, :experts].astype(jnp.int32)
    second_block = jnp.arange(devices, dtype=jnp.int32)[:, None, None] % 2
    seats = by_pairs(jnp.where(slots >= 0, slots + capacity * second_block, -1))
    sibling = e + 1 - 2 * lax.rem(e, 2)
    seats = jnp.stack(
        [
            lax.dynamic_index_in_dim(seats, e, 0, keepdims=False),
            lax.dynamic_index_in_dim(seats, sibling, 0, keepdims=False),
        ]
    )
    gate_rows, up_rows = gate_weight[0].T, up_weight[0].T
    shares = lax.dynamic_index_in_dim(by_pairs(tables[:, experts:]), e, 0, keepdims=False)
    (
        expert_rows,
        grad_rows,
        activation,
        gate_grad,
        up_grad,
        gate_bias_grad,
        up_bias_grad,
        down_bias_grad,
        _,
    ) = expert_rows_kernel(
        normed_moe,
        all_cotangents,
        (gate_rows, up_rows, down_weight[0]),
        (gate_bias, up_bias),
        seats[0],
        shares,
        capacity,
        2,
        "route_rows",
    )
    (normed_moe_grad,) = expert_sums(
        "gradient", (gate_grad, up_grad), (gate_rows, up_rows), seats, (), 3, "sum_rows"
    )
    moe_out, gate_weight_grad, up_weight_grad, down_weight_grad = expert_sums(
        "result",
        (activation,),
        (down_weight[0],),
        seats,
        (shares, down_bias),
        4,
        "sum_results",
        ((gate_grad, expert_rows), (up_grad, expert_rows), (activation, grad_rows)),
    )
    output = (hidden + moe_out).astype(jnp.bfloat16)

    upstream = cotangent[0].astype(jnp.float32)
    hidden_norm_grad, moe_gain_grad = moe_norm_pull(normed_moe_grad)
    hidden_grad = upstream + hidden_norm_grad
    attn_out_grad = hidden_grad.astype(jnp.bfloat16)
    output_bias_grad = jnp.sum(attn_out_grad.astype(jnp.float32), axis=0)
    plain = resid * lax.rsqrt(jnp.mean(resid * resid, axis=-1, keepdims=True) + norm_eps)
    small = jnp.concatenate(
        [
            jnp.zeros((1, width), jnp.float32),
            moe_gain_grad[None],
            output_bias_grad[None],
            jnp.zeros((5, width), jnp.float32),
        ],
        axis=0,
    )
    query_owned, key_owned, value_owned, output_owned, normed_grad, small_sums = attention_backward(
        attn_out_grad,
        query_rot,
        key_rot,
        value_low,
        mixed,
        log_total,
        mask,
        group_tokens,
        (group_query, group_key, group_value, group_output),
        (cosine, sine),
        sinks,
        plain,
        small,
        5,
        "attention_backward",
    )
    lengths = (held_heads * HD, held_kv * HD, held_kv * HD, held_heads)
    resid_norm_grad, _ = attn_norm_pull(normed_grad)
    input_grad = hidden_grad + resid_norm_grad
    pieces = []
    for low, length in zip((0, lengths[0], sum(lengths[:2]), sum(lengths[:3])), lengths):
        piece = small_sums[4:, low : low + length].reshape(2, 2, held_kv, -1)
        pieces.append(jnp.transpose(piece, (1, 2, 0, 3)).reshape(-1))
    query_bias_grad, key_bias_grad, value_bias_grad, sink_grad = pieces
    return (
        output[None],
        input_grad[None],
        small_sums[0],
        query_owned.T,
        query_bias_grad,
        key_owned.T,
        key_bias_grad,
        value_owned.T,
        value_bias_grad,
        output_owned,
        small_sums[2],
        sink_grad,
        small_sums[1],
        gate_weight_grad.T[None],
        gate_bias_grad,
        up_weight_grad.T[None],
        up_bias_grad,
        down_weight_grad[None],
        down_bias_grad,
    )


def solution(mesh):
    placed = (
        P(("exp", "dp"), "seq", None),
        P(("exp", "dp"), None),
        P(("exp", "dp"), "seq", None),
        P(("exp", "dp"), "seq", None),
        P(),
        P(None, ("seq", "exp", "dp")),
        P(),
        P(None, ("seq", "exp", "dp")),
        P(),
        P(None, ("seq", "exp", "dp")),
        P(),
        P(("seq", "exp", "dp"), None),
        P(),
        P(),
        P(),
        P("exp", None, ("seq", "dp")),
        P("exp", ("seq", "dp")),
        P("exp", None, ("seq", "dp")),
        P("exp", ("seq", "dp")),
        P("exp", ("seq", "dp"), None),
        P("exp", None),
        P(("exp", "dp"), "seq", None),
    )
    shape = mesh.shape
    small = shape["seq"] == 2 and shape["dp"] == 2 and shape["exp"] == 8
    return jax.shard_map(
        close_by if small else local,
        mesh=mesh,
        in_specs=placed,
        out_specs=(
            P(("exp", "dp"), "seq", None),
            P(("exp", "dp"), "seq", None),
            P(),
            P(None, ("seq", "exp", "dp")),
            P(),
            P(None, ("seq", "exp", "dp")),
            P(),
            P(None, ("seq", "exp", "dp")),
            P(),
            P(("seq", "exp", "dp"), None),
            P(),
            P(),
            P(),
            P("exp", None, ("seq", "dp")),
            P("exp", ("seq", "dp")),
            P("exp", None, ("seq", "dp")),
            P("exp", ("seq", "dp")),
            P("exp", ("seq", "dp"), None),
            P("exp", None),
        ),
        check_vma=False,
    )
```

```python
import math

import jax
import jax.numpy as jnp
from jax import lax
from jax.experimental import pallas as pl
from jax.experimental.pallas import tpu as pltpu
from jax.sharding import PartitionSpec as P

HD = 64


highest = lax.Precision.HIGHEST
norm_eps = 1e-05
rope_base = 150000.0
clip_level = 7.0
glu_alpha = 1.702
masked_score = -1000000000.0


def rms_apply(values, gain):
    return values * lax.rsqrt(jnp.mean(values * values, axis=-1, keepdims=True) + norm_eps) * gain


def rope_tables(position, width):
    exponent = jnp.arange(width // 2).astype(jnp.float32) * (2.0 / width)
    freqs = jnp.exp(-math.log(rope_base) * exponent)
    angles = position.astype(jnp.float32)[:, None] * freqs[None, :]
    return (jnp.cos(angles), jnp.sin(angles))


def rotate(values, cosine, sine):
    half = values.shape[-1] // 2
    first = values[..., :half]
    second = values[..., half:]
    return jnp.concatenate(
        [first * cosine - second * sine, second * cosine + first * sine], axis=-1
    )


def swiglu(gate_pre, up_pre):
    gate_soft = clip_level * jnp.tanh(gate_pre / clip_level)
    up_soft = clip_level * jnp.tanh(up_pre / clip_level)
    return gate_soft * jax.nn.sigmoid(glu_alpha * gate_soft) * (up_soft + 1.0)


def inner_rows(left, right):
    return lax.dot_general(
        left, right, (((0,), (0,)), ((), ())), preferred_element_type=jnp.float32
    )


def times_transposed(left, right):
    return lax.dot_general(
        left, right, (((1,), (1,)), ((), ())), preferred_element_type=jnp.float32
    )


def to_experts(outgoing):
    width = outgoing.shape[2]
    arrived = lax.all_to_all(outgoing, "exp", split_axis=0, concat_axis=0, tiled=True)
    arrived = lax.all_gather(arrived, ("seq", "dp"), axis=0, tiled=True)
    return arrived.reshape(-1, width)


def results_back(activation, down_matrix, down_vector, experts, capacity):
    width = down_matrix.shape[1]
    share = lax.psum_scatter(
        jnp.dot(activation, down_matrix, preferred_element_type=jnp.float32).astype(jnp.bfloat16),
        ("seq", "dp"),
        scatter_dimension=0,
        tiled=True,
    ).astype(jnp.float32)
    finished = (share + down_vector).astype(jnp.bfloat16).reshape(experts, capacity, width)
    return lax.all_to_all(finished, "exp", split_axis=0, concat_axis=0, tiled=True)


def gradients_back(gate_grad, up_grad, gate_matrix, up_matrix, experts, capacity):
    share = lax.psum_scatter(
        times_transposed(gate_grad, gate_matrix) + times_transposed(up_grad, up_matrix),
        ("seq", "dp"),
        scatter_dimension=0,
        tiled=True,
    )
    return lax.all_to_all(
        share.reshape(experts, capacity, share.shape[1]),
        "exp",
        split_axis=0,
        concat_axis=0,
        tiled=True,
    )


def local(
    tokens,
    segments,
    routes,
    gate_share,
    attn_gain,
    query_weight,
    query_bias,
    key_weight,
    key_bias,
    value_weight,
    value_bias,
    output_weight,
    output_bias,
    sink_logits,
    moe_gain,
    gate_weight,
    gate_bias,
    up_weight,
    up_bias,
    down_weight,
    down_bias,
    cotangent,
):
    count_rows = tokens.shape[1]
    width = tokens.shape[2]
    head_count = sink_logits.shape[0]
    kv_count = key_bias.shape[0] // HD
    group = head_count // kv_count
    scale = 1.0 / math.sqrt(HD)
    experts = lax.axis_size("exp")
    topk = routes.shape[2]
    capacity = count_rows * topk * 9 // (8 * experts)
    resid = tokens[0].astype(jnp.float32)
    full_query, full_key, full_value, full_output = (
        lax.all_gather(query_weight, ("seq", "exp", "dp"), axis=1, tiled=True),
        lax.all_gather(key_weight, ("seq", "exp", "dp"), axis=1, tiled=True),
        lax.all_gather(value_weight, ("seq", "exp", "dp"), axis=1, tiled=True),
        lax.all_gather(output_weight, ("seq", "exp", "dp"), axis=0, tiled=True),
    )
    attn_norm, attn_norm_pull = jax.vjp(rms_apply, resid, attn_gain)
    normed = attn_norm.astype(jnp.bfloat16)
    query_lin = jnp.dot(normed, full_query, preferred_element_type=jnp.float32) + query_bias
    key_lin = jnp.dot(normed, full_key, preferred_element_type=jnp.float32) + key_bias
    value_low = (
        jnp.dot(normed, full_value, preferred_element_type=jnp.float32) + value_bias
    ).astype(jnp.bfloat16)
    offset = lax.axis_index("seq") * count_rows
    position = offset + jnp.arange(count_rows, dtype=jnp.int32)
    cosine, sine = rope_tables(position, HD)
    cosine = cosine[:, None]
    sine = sine[:, None]
    query_rot = rotate(query_lin.reshape(count_rows, head_count, HD), cosine, sine).astype(
        jnp.bfloat16
    )
    key_rot = rotate(key_lin.reshape(count_rows, kv_count, HD), cosine, sine).astype(jnp.bfloat16)
    all_keys, all_values = (
        lax.all_gather(key_rot.reshape(count_rows, kv_count * HD), "seq", axis=0, tiled=True),
        lax.all_gather(value_low, "seq", axis=0, tiled=True),
    )
    seq_len = all_keys.shape[0]
    all_keys = all_keys.reshape(seq_len, kv_count, HD)
    all_values = all_values.reshape(seq_len, kv_count, HD)
    doc_ids = segments[0]
    own_ids = lax.dynamic_slice_in_dim(doc_ids, offset, count_rows, 0)
    key_place = jnp.arange(seq_len, dtype=jnp.int32)
    visible = (position[:, None] >= key_place[None, :]) & (own_ids[:, None] == doc_ids[None, :])
    query_group = query_rot.reshape(count_rows, kv_count, group, HD)
    sink_grid = sink_logits.reshape(kv_count, group)[:, :, None]

    def score_block():
        raw = (
            jnp.einsum("qkgd,skd->kgqs", query_group, all_keys, preferred_element_type=jnp.float32)
            * scale
        )
        return jnp.where(visible[None, None], raw, masked_score)

    scores = score_block()
    peak = jnp.maximum(jnp.max(scores, axis=-1), sink_grid)
    total = jnp.sum(jnp.exp(scores - peak[..., None]), axis=-1) + jnp.exp(sink_grid - peak)
    log_total = peak + jnp.log(total)
    probs = jnp.exp(scores - log_total[..., None])
    mixed = jnp.einsum(
        "kgqs,skd->qkgd", probs.astype(jnp.bfloat16), all_values, preferred_element_type=jnp.float32
    )
    mixed = mixed.reshape(count_rows, head_count * HD).astype(jnp.bfloat16)
    attn_out = jnp.dot(mixed, full_output, preferred_element_type=jnp.float32) + output_bias
    hidden = resid + attn_out
    moe_norm, moe_norm_pull = jax.vjp(rms_apply, hidden, moe_gain)
    normed_moe = moe_norm.astype(jnp.bfloat16)
    chosen = routes[0].reshape(-1)
    expert_hot = (chosen[:, None] == jnp.arange(experts, dtype=jnp.int32)[None, :]).astype(
        jnp.int32
    )
    slot_index = jnp.sum((jnp.cumsum(expert_hot, axis=0) - expert_hot) * expert_hot, axis=1)
    target = chosen * capacity + slot_index
    slot_hot = (
        target[:, None] == jnp.arange(experts * capacity, dtype=jnp.int32)[None, :]
    ).reshape(count_rows, topk, experts * capacity)
    dispatch = jnp.sum(slot_hot.astype(jnp.bfloat16), axis=1)
    weighted = jnp.sum(slot_hot.astype(jnp.float32) * gate_share[0][:, :, None], axis=1)
    outgoing = jnp.einsum("ts,td->sd", dispatch, normed_moe, preferred_element_type=jnp.float32)
    outgoing = outgoing.astype(jnp.bfloat16).reshape(experts, capacity, width)
    expert_rows = to_experts(outgoing)
    gate_pre = (
        jnp.dot(expert_rows, gate_weight[0], preferred_element_type=jnp.float32) + gate_bias[0]
    )
    up_pre = jnp.dot(expert_rows, up_weight[0], preferred_element_type=jnp.float32) + up_bias[0]
    act_full, swiglu_pull = jax.vjp(swiglu, gate_pre, up_pre)
    activation = act_full.astype(jnp.bfloat16)
    returned = results_back(activation, down_weight[0], down_bias[0], experts, capacity)
    moe_out = jnp.dot(
        weighted, returned.reshape(experts * capacity, width).astype(jnp.float32), precision=highest
    )
    output = (hidden + moe_out).astype(jnp.bfloat16)
    upstream = cotangent[0].astype(jnp.float32)
    grad_slots = jnp.einsum("ts,td->sd", weighted, upstream, precision=highest)
    grad_slots = grad_slots.astype(jnp.bfloat16).reshape(experts, capacity, width)
    grad_rows = to_experts(grad_slots)
    down_bias_grad = jnp.sum(grad_rows.astype(jnp.float32), axis=0)
    down_weight_grad = inner_rows(activation, grad_rows)
    act_grad = times_transposed(grad_rows, down_weight[0])
    gate_grad_full, up_grad_full = swiglu_pull(act_grad)
    gate_grad = gate_grad_full.astype(jnp.bfloat16)
    up_grad = up_grad_full.astype(jnp.bfloat16)
    gate_bias_grad = jnp.sum(gate_grad.astype(jnp.float32), axis=0)
    up_bias_grad = jnp.sum(up_grad.astype(jnp.float32), axis=0)
    gate_weight_grad = inner_rows(expert_rows, gate_grad)
    up_weight_grad = inner_rows(expert_rows, up_grad)
    rows_grad = gradients_back(gate_grad, up_grad, gate_weight[0], up_weight[0], experts, capacity)
    normed_moe_grad = jnp.einsum(
        "ts,sd->td",
        dispatch.astype(jnp.float32),
        rows_grad.reshape(experts * capacity, width),
        precision=highest,
    )
    hidden_norm_grad, moe_gain_grad = moe_norm_pull(normed_moe_grad)
    hidden_grad = upstream + hidden_norm_grad
    attn_out_grad = hidden_grad.astype(jnp.bfloat16)
    output_bias_grad = jnp.sum(attn_out_grad.astype(jnp.float32), axis=0)
    full_query, full_key, full_value, full_output = (
        lax.all_gather(query_weight, ("seq", "exp", "dp"), axis=1, tiled=True),
        lax.all_gather(key_weight, ("seq", "exp", "dp"), axis=1, tiled=True),
        lax.all_gather(value_weight, ("seq", "exp", "dp"), axis=1, tiled=True),
        lax.all_gather(output_weight, ("seq", "exp", "dp"), axis=0, tiled=True),
    )
    mixed_grad = (
        times_transposed(attn_out_grad, full_output)
        .astype(jnp.bfloat16)
        .reshape(count_rows, kv_count, group, HD)
    )
    scores = score_block()
    probs = jnp.exp(scores - log_total[..., None])
    prob_grad = jnp.einsum(
        "qkgd,skd->kgqs", mixed_grad, all_values, preferred_element_type=jnp.float32
    )
    delta = jnp.sum(probs * prob_grad, axis=-1)
    score_grad = (probs * (prob_grad - delta[..., None])).astype(jnp.bfloat16)
    sink_grad = -jnp.sum(jnp.exp(sink_grid - log_total) * delta, axis=-1).reshape(head_count)
    value_grad = jnp.einsum(
        "kgqs,qkgd->skd", probs.astype(jnp.bfloat16), mixed_grad, preferred_element_type=jnp.float32
    )
    key_grad = (
        jnp.einsum("kgqs,qkgd->skd", score_grad, query_group, preferred_element_type=jnp.float32)
        * scale
    )
    query_grad = (
        jnp.einsum("kgqs,skd->qkgd", score_grad, all_keys, preferred_element_type=jnp.float32)
        * scale
    )
    key_share, value_share = (
        lax.psum_scatter(
            key_grad.reshape(seq_len, kv_count * HD), "seq", scatter_dimension=0, tiled=True
        ),
        lax.psum_scatter(
            value_grad.reshape(seq_len, kv_count * HD), "seq", scatter_dimension=0, tiled=True
        ),
    )
    query_lin_grad = (
        rotate(query_grad.reshape(count_rows, head_count, HD), cosine, -sine)
        .reshape(count_rows, head_count * HD)
        .astype(jnp.bfloat16)
    )
    key_lin_grad = (
        rotate(key_share.reshape(count_rows, kv_count, HD), cosine, -sine)
        .reshape(count_rows, kv_count * HD)
        .astype(jnp.bfloat16)
    )
    value_lin_grad = value_share.astype(jnp.bfloat16)
    query_bias_grad = jnp.sum(query_lin_grad.astype(jnp.float32), axis=0)
    key_bias_grad = jnp.sum(key_lin_grad.astype(jnp.float32), axis=0)
    value_bias_grad = jnp.sum(value_lin_grad.astype(jnp.float32), axis=0)
    normed_grad = (
        times_transposed(query_lin_grad, full_query)
        + times_transposed(key_lin_grad, full_key)
        + times_transposed(value_lin_grad, full_value)
    )
    resid_norm_grad, attn_gain_grad = attn_norm_pull(normed_grad)
    input_grad = hidden_grad + resid_norm_grad
    query_weight_grad = inner_rows(normed, query_lin_grad)
    key_weight_grad = inner_rows(normed, key_lin_grad)
    value_weight_grad = inner_rows(normed, value_lin_grad)
    output_weight_grad = inner_rows(mixed, attn_out_grad)
    query_owned, key_owned, value_owned, output_owned = (
        lax.psum_scatter(query_weight_grad, ("seq", "exp", "dp"), scatter_dimension=1, tiled=True),
        lax.psum_scatter(key_weight_grad, ("seq", "exp", "dp"), scatter_dimension=1, tiled=True),
        lax.psum_scatter(value_weight_grad, ("seq", "exp", "dp"), scatter_dimension=1, tiled=True),
        lax.psum_scatter(output_weight_grad, ("seq", "exp", "dp"), scatter_dimension=0, tiled=True),
    )
    summed = lax.psum(
        (
            attn_gain_grad,
            query_bias_grad,
            key_bias_grad,
            value_bias_grad,
            output_bias_grad,
            sink_grad,
            moe_gain_grad,
        ),
        ("seq", "exp", "dp"),
    )
    return (
        output[None],
        input_grad[None],
        summed[0],
        query_owned,
        summed[1],
        key_owned,
        summed[2],
        value_owned,
        summed[3],
        output_owned,
        summed[4],
        summed[5],
        summed[6],
        gate_weight_grad[None],
        gate_bias_grad[None],
        up_weight_grad[None],
        up_bias_grad[None],
        down_weight_grad[None],
        down_bias_grad[None],
    )

MESH = pl.DeviceIdType.MESH
HERE = (0, 0, 0)
SIBLING = (0, 1, 0)
ACROSS = (1, 0, 0)
ALONG = (0, 0, 1)
NEAR = (0, 2, 0)
FAR = (0, 4, 0)
ENDS = (0, 6, 0)
THIRD = (0, 8, 0)
FOURTH = (0, 16, 0)


def flip(place, mask):
    x, e, y = place
    if mask[0]:
        x = 1 - x
    if mask[2]:
        y = 1 - y
    if mask[1] & 8:
        e = 2 * (2 - lax.div(e, 4)) + lax.rem(e, 2)
    if mask[1] & 16:
        e = 2 * (3 - 3 * lax.div(e, 4)) + lax.rem(e, 2)
    step = 0
    for bit in (1, 2, 4):
        if mask[1] & bit:
            step = step + bit - 2 * bit * lax.rem(lax.div(e, bit), 2)
    return x, e + step, y


def both(left, right):
    return tuple(a ^ b for a, b in zip(left, right))


def place_here():
    return lax.axis_index("seq"), lax.axis_index("exp"), lax.axis_index("dp")


def block_of_all(place):
    x, e, y = place
    return (e * 2 + x) * 2 + y


def block_of_tokens(place):
    x, e, y = place
    return lax.rem(lax.div(e, 2), 2) * 2 + x


def block_of_heads(place):
    x, e, y = place
    return (lax.div(e, 4) * 2 + lax.rem(e, 2)) * 2 + y


GROUPS = {
    "all": (block_of_all, 32, SIBLING, ACROSS, ALONG, (NEAR, ENDS), 0.5),
    "tokens": (block_of_tokens, 4, None, ACROSS, NEAR, (), 0.5),
    "heads": (block_of_heads, 8, SIBLING, FAR, ALONG, (), 1.0),
}


def partners(group):
    _, _, sibling, first, second, line, _ = GROUPS[group]
    return ([sibling] if sibling else []) + [first, second] + list(line)


def copies(group):
    _, _, sibling, _, _, line, _ = GROUPS[group]
    if line:
        return 4 * 8 + 5
    return 8 if sibling else 4


class Sender:
    def __init__(self, place, send, recv):
        self.place, self.send, self.recv, self.started = place, send, recv, []
        self.maybe = []
        line_place = lax.div(place[1], 2)
        self.inner = (line_place == 1) | (line_place == 2)

    def plan(self, source, target, mask, lands=None):
        number = len(self.started) + len(self.maybe)
        return pltpu.make_async_remote_copy(
            src_ref=source,
            dst_ref=target,
            send_sem=self.send.at[number],
            recv_sem=self.recv.at[number if lands is None else lands],
            device_id=flip(self.place, mask),
            device_id_type=MESH,
        )

    def push(self, source, target, mask):
        copy = self.plan(source, target, mask)
        copy.start()
        self.started.append(copy)
        return copy

    def push_within(self, source, target, mask, lands=None, inner=True):
        copy = self.plan(source, target, mask, lands)
        number = len(self.started) + len(self.maybe)
        here = self.inner if inner else jnp.logical_not(self.inner)
        self.maybe.append((here, copy))
        pl.when(here)(copy.start)
        return copy, number

    def finish(self):
        for copy in self.started:
            copy.wait_send()
        for here, copy in self.maybe:
            pl.when(here)(copy.wait_send)


class Gather:
    def __init__(self, group, place, source, result, send, recv, local, share=None):
        self.index, _, self.sibling, self.first, self.second, line, usual = GROUPS[group]
        self.place, self.source, self.result = place, source, result
        self.rows = source.shape[0]
        share = usual if share is None else share
        self.cut = int(self.rows * share) // 16 * 16
        self.out = Sender(place, send, recv)
        self.own = pltpu.make_async_copy(source, self.at(HERE), local.at[0])
        self.masks = [HERE, NEAR, THIRD, FOURTH] if line else [HERE]
        self.ways, self.halves, self.lands, self.relayed = {}, {}, {}, []
        self.tails = {step: [] for step in range(len(self.masks))}

    def at(self, mask):
        return self.result.at[self.index(flip(self.place, mask))]

    def start(self):
        self.own.start()
        if len(self.masks) > 1:
            self.begin_line()

    def begin_line(self):
        self.near = self.out.push(self.source, self.at(HERE), NEAR)
        self.third, self.lands[2] = self.out.push_within(self.source, self.at(HERE), ENDS)

    def relay(self, step):
        if step in self.relayed:
            return
        self.relayed.append(step)
        if step == 1:
            self.near.wait_recv()
            self.fourth, self.lands[3] = self.out.push_within(self.at(NEAR), self.at(NEAR), ENDS)
            return
        copy = self.third if step == 2 else self.fourth
        pl.when(self.out.inner)(copy.wait_recv)
        block = self.at(self.masks[step])
        self.out.push_within(block, block, NEAR, self.lands[step])

    def reached(self, step):
        self.relay(step)
        if step > 1:
            copy = self.third if step == 2 else self.fourth
            pl.when(jnp.logical_not(self.out.inner))(copy.wait_recv)

    def pass_on(self, step, block, place):
        if self.sibling:
            self.tails[step].append(self.out.push(block, place, self.sibling))

    def plane(self, step):
        mask = self.masks[step]
        if step:
            self.reached(step)
        block = self.at(mask) if step else self.source
        self.ways[step] = (
            self.out.push(block, self.at(mask), self.first),
            self.out.push(block, self.at(mask), self.second),
        )
        self.pass_on(step, block, self.at(mask))

    def turn(self, step):
        halves = []
        mask, cut = self.masks[step], self.cut
        self.ways[step][0].wait_recv()
        seen = self.at(both(mask, self.first))
        if cut:
            halves.append(self.out.push(seen.at[:cut], seen.at[:cut], self.second))
        self.pass_on(step, seen, seen)
        self.ways[step][1].wait_recv()
        seen = self.at(both(mask, self.second))
        if cut < self.rows:
            halves.append(self.out.push(seen.at[cut:], seen.at[cut:], self.first))
        self.pass_on(step, seen, seen)
        self.halves[step] = halves

    def close(self, step):
        for half in self.halves[step]:
            half.wait_recv()
        seen = self.at(both(self.masks[step], both(self.first, self.second)))
        self.pass_on(step, seen, seen)

    def hop(self, number):
        for step in range(len(self.masks)):
            (self.plane, self.turn, self.close)[number](step)

    def passed(self, step):
        for copy in self.tails[step]:
            copy.wait_recv()

    def arrived(self):
        for step in range(len(self.masks)):
            self.passed(step)
        self.own.wait()

    def finish(self):
        self.out.finish()


def total(parts, low, high, store):
    def body(step, carry):
        rows = pl.ds(pl.multiple_of(low + step * 16, 16), 16)
        value = parts[0][rows].astype(jnp.float32)
        for part in parts[1:]:
            value = value + part[rows].astype(jnp.float32)
        store[rows] = value.astype(store.dtype)
        return carry

    if high > low:
        lax.fori_loop(0, (high - low) // 16, body, 0)


def by_tiles(width, tile, parts=2):
    size = -(-width // (128 * parts)) * 128
    for low in range(0, width, size):
        tile(low, min(size, width - low))


def seat_hot(seats, capacity, kind):
    lines = lax.broadcasted_iota(jnp.int32, (2 * capacity, seats.shape[-1]), 0)
    return (lines == seats).astype(kind)


def expert_sums(kind, rows, weights, seats, extra, collective, name, products=()):
    experts, pairs = seats.shape[1], seats.shape[2]
    thick = seats.shape[4]
    tokens = seats.shape[4] // 2
    half_rows = rows[0].shape[0] // experts
    pair_rows = half_rows // pairs
    capacity = pair_rows // 2
    hidden = rows[0].shape[1]
    width = weights[0].shape[1]
    first, second = ACROSS, ALONG
    masks = [FOURTH, THIRD, NEAR, HERE]
    rounds = len(masks)
    cut = tokens // 2
    count_rows, count_extra = len(rows), len(extra)
    copies_out = rounds * (pairs + 4) + 5

    def body(*refs):
        refs = list(refs)
        left = refs[:count_rows]
        stored = refs[count_rows : 2 * count_rows]
        seat_ref = refs[2 * count_rows]
        more = refs[2 * count_rows + 1 : 2 * count_rows + 1 + count_extra]
        rest = refs[2 * count_rows + 1 + count_extra :]
        thin_wide, rest = rest[: 2 * len(products)], rest[2 * len(products) :]
        result, rest = rest[0], rest[1:]
        made, rest = rest[: len(products)], rest[len(products) :]
        wide, rest = rest[:count_rows], rest[count_rows:]
        staged, away, joined, own, side, arrive, ends, send, recv, local, weight_sem = rest[:11]
        if products:
            thin_stage, wide_stage, gross, product_sem, made_sem = rest[11:]
        weight_copies = [
            pltpu.make_async_copy(stored[item], wide[item], weight_sem.at[item])
            for item in range(count_rows)
        ]
        for copy in weight_copies:
            copy.start()
        place = place_here()
        x, e, y = place
        greet = [SIBLING, first, second, NEAR, FAR, ENDS]
        barrier = pltpu.get_barrier_semaphore()
        for mask in greet:
            pl.semaphore_signal(barrier, inc=1, device_id=flip(place, mask), device_id_type=MESH)
        pl.semaphore_wait(barrier, len(greet))
        out = Sender(place, send, recv)

        def block(mask):
            there = flip(place, mask)
            return there[0] * 2 + there[2]

        halves = []
        for mask in masks:
            halves.append((flip(place, both(mask, SIBLING))[1], True))
            halves.append((flip(place, mask)[1], False))
        loads = {}

        def load(number):
            if number < len(halves):
                begin = pl.multiple_of(halves[number][0] * half_rows, 16)
                for item in range(count_rows):
                    copy = pltpu.make_async_copy(
                        left[item].at[pl.ds(begin, half_rows)],
                        staged.at[number % 2, item],
                        local.at[number % 2, item],
                    )
                    copy.start()
                    loads[number, item] = copy

        def make(number, store):
            load(number + 1)
            for item in range(count_rows):
                loads[number, item].wait()
                if number == 0:
                    weight_copies[item].wait()
            values = [staged[number % 2, item] for item in range(count_rows)]
            if kind == "result":
                part = halves[number][0]
                factors = []
                for pair in range(pairs):
                    hot = seat_hot(seat_ref[0, part, pair], capacity, jnp.float32)
                    factors.append(jnp.sum(hot * more[0][part, pair], axis=1, keepdims=True))
                factor = jnp.concatenate(factors, axis=0)
                once = jnp.where((x == 0) & (y == 0), 1.0, 0.0).astype(jnp.float32)

            def tile(low, size):
                area = pl.ds(low, size)
                value = jnp.dot(values[0], wide[0][:, area], preferred_element_type=jnp.float32)
                if kind == "gradient":
                    value += jnp.dot(values[1], wide[1][:, area], preferred_element_type=jnp.float32)
                else:
                    value = (value + once * more[1][:, area]) * factor
                store(low, size, value.astype(jnp.bfloat16))

            by_tiles(width, tile)

        def to_sibling(step):
            slot = step % 2

            def store(low, size, value):
                away[slot, :, pl.ds(low, size)] = value

            if step >= 2:
                for copy in sent[step - 2]:
                    copy.wait_send()
            make(2 * step, store)
            sent[step] = [
                out.push(
                    away.at[slot].at[pair * pair_rows : (pair + 1) * pair_rows],
                    joined.at[step, pair].at[pair_rows : 2 * pair_rows],
                    SIBLING,
                )
                for pair in range(pairs)
            ]

        def to_here(step):
            def store(low, size, value):
                for pair in range(pairs):
                    joined[step, pair, :pair_rows, pl.ds(low, size)] = value[
                        pair * pair_rows : (pair + 1) * pair_rows
                    ]

            make(2 * step + 1, store)

        def combine(step):
            for copy in sent[step]:
                copy.wait_recv()
            part = halves[2 * step + 1][0]
            for pair in range(pairs):
                hot = jnp.concatenate(
                    [seat_hot(seat_ref[mate, part, pair], capacity, jnp.bfloat16) for mate in range(2)],
                    axis=0,
                )

                def tile(low, size):
                    value = inner_rows(hot, joined[step, pair, :, pl.ds(low, size)])
                    value = value.astype(jnp.bfloat16)
                    own[step * 4 + pair * 2, :, pl.ds(low, size)] = value[:tokens]
                    own[step * 4 + pair * 2 + 1, :, pl.ds(low, size)] = value[tokens:]

                by_tiles(width, tile)

        def outward(step):
            corner = own.at[step * 4 + block(both(first, second))]
            return [
                out.push(corner.at[:cut], side.at[step].at[:cut], first),
                out.push(corner.at[cut:], side.at[step].at[cut:], second),
            ]

        def inward(step, parts):
            by_first = own.at[step * 4 + block(first)]
            by_second = own.at[step * 4 + block(second)]
            for part in parts:
                part.wait_recv()
            total([by_second, side.at[step]], 0, cut, by_second)
            total([by_first, side.at[step]], cut, tokens, by_first)
            return (
                out.push(by_first, arrive.at[step * 2], first),
                out.push(by_second, arrive.at[step * 2 + 1], second),
            )

        def close(step, ways):
            kept = own.at[step * 4 + block(HERE)]
            for way in ways:
                way.wait_recv()
            parts = [kept, arrive.at[step * 2], arrive.at[step * 2 + 1]]
            if masks[step] in (FOURTH, THIRD):
                total(parts, 0, tokens, kept)
                shared[step], _ = out.push_within(kept, ends.at[1 + step], NEAR, inner=False)
                return
            if masks[step] == NEAR:
                total(parts, 0, tokens, kept)
                reach.append((out.push(kept, ends.at[3], NEAR), None))
                return
            for copy, _ in reach:
                copy.wait_recv()
            parts += [ends.at[0], ends.at[3]]
            total(parts, 0, tokens, result)

        def across(step):
            kept = own.at[step * 4 + block(HERE)]

            @pl.when(out.inner)
            def _():
                shared[step].wait_recv()
                total([kept, ends.at[1 + step]], 0, tokens, kept)

            copy, number = out.push_within(kept, ends.at[0], masks[step], lands=reach[0][1] if reach else None)
            if not reach:
                reach.append((copy, number))

        chunks = rows[0].shape[0] // thick

        def product_loads(item, number):
            slot = lax.rem(number, 2)
            begin = pl.multiple_of(number * thick, 16)
            return [
                pltpu.make_async_copy(
                    thin_wide[2 * item + part].at[pl.ds(begin, thick)], stage.at[slot], product_sem.at[slot, part]
                )
                for part, stage in enumerate((thin_stage, wide_stage))
            ]

        written = []

        def multiply(item, begin, end):
            if begin == 0:
                for copy in product_loads(item, 0):
                    copy.start()
                if written:
                    written[-1].wait()
                else:
                    gross[...] = jnp.zeros_like(gross)

            def step(number, carry):
                @pl.when(number + 1 < chunks)
                def _():
                    for copy in product_loads(item, number + 1):
                        copy.start()

                for copy in product_loads(item, number):
                    copy.wait()
                slot = lax.rem(number, 2)
                keep = jnp.where(number == 0, 0.0, 1.0).astype(jnp.float32)

                def tile(low, size):
                    area = pl.ds(low, size)
                    value = inner_rows(thin_stage[slot], wide_stage[slot, :, area])
                    gross[:, area] = gross[:, area] * keep + value

                by_tiles(width, tile, 3)
                return carry

            lax.fori_loop(begin, end, step, 0)
            if end == chunks:
                copy = pltpu.make_async_copy(gross, made[item], made_sem.at[0])
                copy.start()
                written.append(copy)

        todo = [(item, begin) for item in range(len(products)) for begin in range(0, chunks, 3)]

        def some(number):
            for item, begin in todo[:number]:
                multiply(item, begin, min(begin + 3, chunks))
            del todo[:number]

        sent, corners, ways, reach, shared = {}, {}, {}, [], {}
        load(0)
        for step in range(rounds + 2):
            if step < rounds:
                to_sibling(step)
                to_here(step)
                combine(step)
                corners[step] = outward(step)
            if 0 <= step - 1 < rounds:
                ways[step - 1] = inward(step - 1, corners[step - 1])
            if step - 3 in (0, 1):
                across(step - 3)
            if 0 <= step - 2 < rounds:
                close(step - 2, ways[step - 2])
            some((2, 2, 3, 2, 0, 0)[step])
        some(len(todo))
        if written:
            written[-1].wait()
        for step in range(rounds):
            if step >= rounds - 2:
                for copy in sent[step]:
                    copy.wait_send()
        exchanged = {id(copy) for step in range(rounds) for copy in sent[step]}
        out.started = [copy for copy in out.started if id(copy) not in exchanged]
        out.finish()

    vmem, anywhere = pl.BlockSpec(memory_space=pltpu.VMEM), pl.BlockSpec(memory_space=pl.ANY)
    for_products = []
    if products:
        for_products = [
            pltpu.VMEM((2, thick, hidden), jnp.bfloat16),
            pltpu.VMEM((2, thick, width), jnp.bfloat16),
            pltpu.VMEM((hidden, width), jnp.float32),
            pltpu.SemaphoreType.DMA((2, 2)),
            pltpu.SemaphoreType.DMA((1,)),
        ]
    return pl.pallas_call(
        body,
        out_shape=[jax.ShapeDtypeStruct((tokens, width), jnp.float32)]
        + [jax.ShapeDtypeStruct((hidden, width), jnp.float32)] * len(products),
        in_specs=[anywhere] * (2 * count_rows)
        + [vmem] * (1 + count_extra)
        + [anywhere] * (2 * len(products)),
        out_specs=[vmem] + [anywhere] * len(products),
        scratch_shapes=[pltpu.VMEM(weight.shape, jnp.bfloat16) for weight in weights]
        + [
            pltpu.VMEM((2, count_rows, half_rows, hidden), jnp.bfloat16),
            pltpu.VMEM((2, half_rows, width), jnp.bfloat16),
            pltpu.VMEM((rounds, pairs, 2 * pair_rows, width), jnp.bfloat16),
            pltpu.VMEM((rounds * 4, tokens, width), jnp.bfloat16),
            pltpu.VMEM((rounds, tokens, width), jnp.bfloat16),
            pltpu.VMEM((rounds * 2, tokens, width), jnp.bfloat16),
            pltpu.VMEM((4, tokens, width), jnp.bfloat16),
            pltpu.SemaphoreType.DMA((copies_out,)),
            pltpu.SemaphoreType.DMA((copies_out,)),
            pltpu.SemaphoreType.DMA((2, count_rows)),
            pltpu.SemaphoreType.DMA((count_rows,)),
        ]
        + for_products,
        compiler_params=pltpu.CompilerParams(
            collective_id=collective, has_side_effects=True, vmem_limit_bytes=62 * 1024 * 1024
        ),
        name=name,
    )(*rows, *weights, seats, *extra, *[array for pair in products for array in pair])


def expert_rows_kernel(own_block, cotangents, weights, biases, seats, shares, capacity, collective, name):
    experts, pairs = seats.shape[0], seats.shape[1]
    tokens, width = own_block.shape
    blocks = cotangents.shape[0]
    hidden = weights[0].shape[0]
    pair_rows = 2 * capacity
    half_rows = pairs * pair_rows
    row_count = experts * half_rows
    copies_out = copies("all")

    def body(*refs):
        (own_ref, cot_ref, *stored, gate_bias, up_bias, seat_ref, share_ref) = refs[:9]
        (rows_out, grads_out, act_out, dgate_out, dup_out, gate_sum, up_sum, down_sum, held) = refs[9:18]
        (stage, lines, thin, pre, back, gate, up, down) = refs[18:26]
        (send, recv, local, load_sem, line_sem, thin_sem, weight_sem) = refs[26:]
        weight_copies = [
            pltpu.make_async_copy(stored[item], goal, weight_sem.at[item])
            for item, goal in enumerate((gate, up, down))
        ]
        for copy in weight_copies[::-1]:
            copy.start()
        place = place_here()
        x, e, y = place
        greet = partners("all")
        barrier = pltpu.get_barrier_semaphore()
        for mask in greet:
            pl.semaphore_signal(barrier, inc=1, device_id=flip(place, mask), device_id_type=MESH)
        pl.semaphore_wait(barrier, len(greet))
        work = Gather("all", place, own_ref, held, send, recv, local)
        work.start()
        gate_sum[...] = jnp.zeros_like(gate_sum)
        up_sum[...] = jnp.zeros_like(up_sum)
        down_sum[...] = jnp.zeros_like(down_sum)
        halves = []
        for mask in work.masks:
            halves.append(flip(place, mask)[1])
            halves.append(flip(place, both(mask, SIBLING))[1])
        turnstile = {"load": 0, "line": 0}
        line_copies, thin_copies = [], []

        fetched = {}

        def fetch(scaled, number):
            bank = len(fetched) % 2
            begin = halves[number] * pairs * 2
            copies_in = [
                pltpu.make_async_copy(
                    (cot_ref if scaled else held).at[pl.ds(begin + 2 * pair, 2)],
                    stage.at[2 * bank + pair],
                    load_sem.at[2 * bank + pair],
                )
                for pair in range(pairs)
            ]
            for copy in copies_in:
                copy.start()
            fetched[scaled, number] = (bank, copies_in)

        def pick(scaled, number):
            part = halves[number]
            bank, copies_in = fetched[scaled, number]
            slot = turnstile["line"] % 2
            turnstile["line"] += 1
            if len(line_copies) >= 2:
                line_copies[-2].wait()
            for pair in range(pairs):
                copies_in[pair].wait()
                hot = seat_hot(seat_ref[part, pair], capacity, jnp.float32)
                if scaled:
                    factor = jnp.sum(hot * share_ref[part, pair], axis=1, keepdims=True)
                hot = hot.astype(jnp.bfloat16)
                blocks_here = stage[2 * bank + pair].reshape(2 * tokens, width)
                value = jnp.dot(hot, blocks_here, preferred_element_type=jnp.float32)
                if scaled:
                    value = value * factor
                value = value.astype(jnp.bfloat16)
                lines[slot, pair * pair_rows : (pair + 1) * pair_rows] = value
                if scaled:
                    down_sum[...] += jnp.sum(value.astype(jnp.float32), axis=0, keepdims=True)
            copy = pltpu.make_async_copy(
                lines.at[slot],
                (grads_out if scaled else rows_out).at[
                    pl.ds(pl.multiple_of(part * half_rows, 16), half_rows)
                ],
                line_sem.at[slot],
            )
            copy.start()
            line_copies.append(copy)
            return lines.at[slot]

        def backward(number):
            picked = pick(True, number)
            if number == 0:
                weight_copies[2].wait()
            back[number] = times_transposed(picked[...], down[...])

        def forward(number):
            part = halves[number]
            picked = pick(False, number)
            if number == 0:
                weight_copies[0].wait()
                weight_copies[1].wait()
            pre[0] = times_transposed(picked[...], gate[...])
            pre[1] = times_transposed(picked[...], up[...])
            slot = number % 2
            if number >= 2:
                for copy in thin_copies[-6:-3]:
                    copy.wait()

            def chunk(step, sums):
                area = pl.ds(pl.multiple_of(step * 16, 16), 16)
                gate_tanh = jnp.tanh((pre[0, area] + gate_bias[...]) * (1.0 / clip_level))
                up_tanh = jnp.tanh((pre[1, area] + up_bias[...]) * (1.0 / clip_level))
                gate_soft = clip_level * gate_tanh
                up_more = clip_level * up_tanh + 1.0
                bend = jax.nn.sigmoid(glu_alpha * gate_soft)
                glow = gate_soft * bend
                grad = back[number, area]
                dgate = grad * up_more * (bend + glu_alpha * glow * (1.0 - bend))
                dgate = (dgate * (1.0 - gate_tanh * gate_tanh)).astype(jnp.bfloat16)
                dup = (grad * glow * (1.0 - up_tanh * up_tanh)).astype(jnp.bfloat16)
                thin[slot, 0, area] = (glow * up_more).astype(jnp.bfloat16)
                thin[slot, 1, area] = dgate
                thin[slot, 2, area] = dup
                return sums[0] + dgate.astype(jnp.float32), sums[1] + dup.astype(jnp.float32)

            zero = jnp.zeros((16, hidden), jnp.float32)
            sums = lax.fori_loop(0, half_rows // 16, chunk, (zero, zero))
            gate_sum[...] += jnp.sum(sums[0], axis=0, keepdims=True)
            up_sum[...] += jnp.sum(sums[1], axis=0, keepdims=True)
            for item, goal in enumerate((act_out, dgate_out, dup_out)):
                copy = pltpu.make_async_copy(
                    thin.at[slot, item],
                    goal.at[pl.ds(pl.multiple_of(part * half_rows, 16), half_rows)],
                    thin_sem.at[slot, item],
                )
                copy.start()
                thin_copies.append(copy)

        order = ["p0B0B1b0B2b1t0p1r2B3b2c0o0F0b3r3p2t1w0F1f0B4f1c1F2b4"]
        order += ["p3t2w1F3f2B5f3B6b5c2F4b6w2F5f4t3B7f5b7c3F6w3F7f6f7"]
        acts = {
            "p": work.plane,
            "t": work.turn,
            "c": work.close,
            "w": work.passed,
            "r": work.relay,
            "o": lambda number: work.own.wait(),
            "B": lambda number: fetch(True, number),
            "F": lambda number: fetch(False, number),
            "b": backward,
            "f": forward,
        }
        order = "".join(order)
        for low in range(0, len(order), 2):
            acts[order[low]](int(order[low + 1]))
        for copy in line_copies[-2:] + thin_copies[-6:]:
            copy.wait()
        work.finish()

    vmem, anywhere = pl.BlockSpec(memory_space=pltpu.VMEM), pl.BlockSpec(memory_space=pl.ANY)
    bf16, f32 = jnp.bfloat16, jnp.float32
    return pl.pallas_call(
        body,
        out_shape=[
            jax.ShapeDtypeStruct((row_count, width), bf16),
            jax.ShapeDtypeStruct((row_count, width), bf16),
            jax.ShapeDtypeStruct((row_count, hidden), bf16),
            jax.ShapeDtypeStruct((row_count, hidden), bf16),
            jax.ShapeDtypeStruct((row_count, hidden), bf16),
            jax.ShapeDtypeStruct((1, hidden), f32),
            jax.ShapeDtypeStruct((1, hidden), f32),
            jax.ShapeDtypeStruct((1, width), f32),
            jax.ShapeDtypeStruct((blocks, tokens, width), bf16),
        ],
        in_specs=[anywhere] * 5 + [vmem] * 4,
        out_specs=[anywhere] * 5 + [vmem] * 3 + [anywhere],
        scratch_shapes=[
            pltpu.VMEM((4, 2, tokens, width), bf16),
            pltpu.VMEM((2, half_rows, width), bf16),
            pltpu.VMEM((2, 3, half_rows, hidden), bf16),
            pltpu.VMEM((2, half_rows, hidden), f32),
            pltpu.VMEM((experts, half_rows, hidden), f32),
        ]
        + [pltpu.VMEM(weight.shape, bf16) for weight in weights]
        + [
            pltpu.SemaphoreType.DMA((copies_out,)),
            pltpu.SemaphoreType.DMA((copies_out,)),
            pltpu.SemaphoreType.DMA((1,)),
            pltpu.SemaphoreType.DMA((4,)),
            pltpu.SemaphoreType.DMA((2,)),
            pltpu.SemaphoreType.DMA((2, 3)),
            pltpu.SemaphoreType.DMA((3,)),
        ],
        compiler_params=pltpu.CompilerParams(
            collective_id=collective, has_side_effects=True, vmem_limit_bytes=60 * 1024 * 1024
        ),
        name=name,
    )(own_block, cotangents, *weights, *biases, seats, shares)


class Scatter:
    def __init__(self, group, place, source, result, side, arrive, send, recv, spare, mate=None):
        self.index, _, self.sibling, self.first, self.second, _, share = GROUPS[group]
        self.place, self.source, self.result = place, source, result
        self.side, self.arrive, self.mate = side, arrive, mate
        self.rows = result.shape[0]
        self.cut = int(self.rows * (1.0 - share)) // 16 * 16
        self.corner = both(self.first, self.second)
        self.out = Sender(place, send, recv)
        self.crossing = {}

    def at(self, mask):
        return self.source.at[self.index(flip(self.place, mask))]

    def cross(self):
        for spot, mask in enumerate((self.corner, self.first, self.second, HERE)):
            self.crossing[mask] = (
                self.out.push(self.at(both(mask, self.sibling)), self.mate.at[spot], self.sibling),
                self.mate.at[spot],
            )

    def ready(self, mask):
        if not self.sibling:
            return [self.at(mask)]
        copy, block = self.crossing[mask]
        copy.wait_recv()
        return [self.at(mask), block]

    def outward(self):
        corner, cut = self.at(self.corner), self.cut
        parts = self.ready(self.corner)
        if len(parts) > 1:
            total(parts, 0, self.rows, corner)
        self.halves = []
        if cut:
            self.halves.append(self.out.push(corner.at[:cut], self.side.at[:cut], self.first))
        if cut < self.rows:
            self.halves.append(self.out.push(corner.at[cut:], self.side.at[cut:], self.second))

    def inward(self):
        by_first, by_second = self.ready(self.first), self.ready(self.second)
        for half in self.halves:
            half.wait_recv()
        cut, rows = self.cut, self.rows
        total(by_second + [self.side], 0, cut, by_second[0])
        total(by_first + [self.side], cut, rows, by_first[0])
        if self.sibling:
            total(by_second, cut, rows, by_second[0])
            total(by_first, 0, cut, by_first[0])
        self.ways = (
            self.out.push(by_first[0], self.arrive.at[0], self.first),
            self.out.push(by_second[0], self.arrive.at[1], self.second),
        )

    def close(self):
        parts = self.ready(HERE)
        for way in self.ways:
            way.wait_recv()
        total(parts + [self.arrive.at[0], self.arrive.at[1]], 0, self.rows, self.result)

    def finish(self):
        self.out.finish()


def lanes(shape):
    return lax.broadcasted_iota(jnp.int32, shape, len(shape) - 1)


def swapped(value):
    width = value.shape[-1]
    upper = pltpu.roll(value, width - HD // 2, len(value.shape) - 1)
    lower = pltpu.roll(value, HD // 2, len(value.shape) - 1)
    return jnp.where(lanes(value.shape) % HD < HD // 2, upper, lower)


def halves_of(value, member):
    low = lanes(value.shape) < HD
    zero = jnp.zeros_like(value)
    if member == 0:
        kept = jnp.where(low, value, zero)
        return kept, pltpu.roll(kept, HD, 1)
    kept = jnp.where(low, zero, value)
    return pltpu.roll(kept, HD, 1), kept


def seen(marks, held, first_key=0):
    rows = marks.shape[1]
    lines = []
    for query in range(2):
        parts = []
        for key in range(2):
            if key > query:
                parts.append(jnp.zeros((rows, rows), jnp.bool_))
                continue
            same = marks[held + query] == marks[held + key].T
            if key == query:
                down = lax.broadcasted_iota(jnp.int32, (rows, rows), 0)
                same = same & (down >= lanes((rows, rows)))
            parts.append(same)
        lines.append(parts)
    return lines


def mask_of(marks, held):
    lines = seen(marks, held)
    return jnp.concatenate(
        [
            jnp.concatenate([jnp.where(part, 1.0, 0.0) for part in parts], axis=1)
            for parts in lines
        ],
        axis=0,
    )


def pick_lane(value, number):
    return jnp.sum(jnp.where(lanes(value.shape) == number, value, 0.0), axis=1, keepdims=True)


def attention_forward(
    normed, query_rows, key_rows, value_rows, output_rows, marks, table, extra, biases, tables, sinks, collective, name
):
    tokens, width = normed.shape
    block = 4 * tokens
    seq_len = 2 * tokens
    columns = 8 * query_rows.shape[0]
    pairs = columns // 128
    scale = 1.0 / math.sqrt(HD)
    bf16, f32 = jnp.bfloat16, jnp.float32
    gathers = [
        ("tokens", normed),
        ("heads", query_rows),
        ("heads", key_rows),
        ("heads", value_rows),
        ("tokens", marks),
        ("heads", output_rows),
        ("all", table),
        ("all", extra),
    ]
    count = len(gathers)

    def body(*refs):
        refs = list(refs)

        def take(number):
            got = refs[:number]
            del refs[:number]
            return got

        sources = take(count)
        query_bias, key_bias, value_bias, cosine, sine, sink_ref = take(6)
        (result, query_out, key_out, value_out, mixed_out, lse_out, mask) = take(7)
        kept_out = take(5)
        far_out = take(2)
        held = take(count - 2)
        (key_half, value_half, partial, side, arrive) = take(5)
        sems = [take(3) for _ in range(count)]
        sum_sems = take(3)
        (keep_sem,) = take(1)
        place = place_here()
        greet = []
        for group, _ in gathers:
            greet += [step for step in partners(group) if step not in greet]
        barrier = pltpu.get_barrier_semaphore()
        for step in greet:
            pl.semaphore_signal(barrier, inc=1, device_id=flip(place, step), device_id_type=MESH)
        pl.semaphore_wait(barrier, len(greet))
        works = [
            Gather(
                group, place, sources[item], (held + far_out)[item], *sems[item], share=0.25 if item == 7 else None
            )
            for item, (group, _) in enumerate(gathers)
        ]
        all_tokens, all_query, all_key, all_value, all_marks, all_output = held
        early, output_work, table_work, extra_work = works[:5], works[5], works[6], works[7]
        early = [early[4]] + early[:4]
        table_work.start()
        for work in early:
            work.start()
            work.plane(0)
        extra_work.start()
        extra_work.plane(0)
        early[0].turn(0)
        table_work.relay(1)
        table_work.relay(2)
        for work in early[1:]:
            work.turn(0)
        extra_work.turn(0)
        extra_work.plane(1)
        extra_work.relay(2)
        output_work.start()
        output_work.plane(0)
        for work in early:
            work.close(0)
        for work in early:
            work.passed(0)
            work.own.wait()
        keeps = []

        def keep(item, goal):
            copy = pltpu.make_async_copy(held[item], kept_out[goal], keep_sem.at[goal])
            copy.start()
            keeps.append(copy)

        for item in range(4):
            keep(item, item)
        x_all = all_tokens[...].reshape(block, width)

        def turned(value, low):
            return value * cosine[...] + swapped(value) * sine[...]

        def project(number, carry):
            weight = all_query[pl.ds(pl.multiple_of(2 * number, 2), 2)].reshape(256, width)
            value = times_transposed(x_all, weight)
            for part in range(2):
                area = pl.ds(pl.multiple_of((2 * number + part) * 128, 128), 128)
                head = value[:, part * 128 : (part + 1) * 128] + query_bias[:, area]
                query_out[:, area] = turned(head, 0).astype(bf16)
            return carry

        lax.fori_loop(0, pairs // 2, project, 0)
        key = times_transposed(x_all, all_key[...].reshape(128, width)) + key_bias[...]
        key = turned(key, 0).astype(bf16)
        key_out[...] = key
        value = times_transposed(x_all, all_value[...].reshape(128, width)) + value_bias[...]
        value = value.astype(bf16)
        value_out[...] = value
        for member in range(2):
            for part, half in enumerate(halves_of(key, member)):
                key_half[2 * member + part] = half
            for part, half in enumerate(halves_of(value, member)):
                value_half[2 * member + part] = half
        for half in range(2):
            mask[half] = mask_of(all_marks, 2 * half)
        table_work.relay(3)
        extra_work.close(0)
        extra_work.relay(3)
        extra_work.plane(2)
        lse_out[...] = jnp.zeros_like(lse_out)

        def attend(number, carry):
            pair = lax.div(number, 2)
            half = lax.rem(number, 2)
            member = lax.div(pair, pairs // 2)
            rows = pl.ds(pl.multiple_of(half * seq_len, seq_len), seq_len)
            area = pl.ds(pl.multiple_of(pair * 128, 128), 128)
            query = query_out[rows, area]
            mixed = jnp.zeros((seq_len, 128), f32)
            for part in range(2):
                raw = times_transposed(query, key_half[2 * member + part, rows]) * scale
                raw = jnp.where(mask[half] > 0.0, raw, masked_score)
                sink = sink_ref[0, 2 * pair + part]
                peak = jnp.maximum(jnp.max(raw, axis=1, keepdims=True), sink)
                mass = jnp.sum(jnp.exp(raw - peak), axis=1, keepdims=True) + jnp.exp(sink - peak)
                lse = peak + jnp.log(mass)
                probs = jnp.exp(raw - lse).astype(bf16)
                mixed = mixed + jnp.dot(
                    probs, value_half[2 * member + part, rows], preferred_element_type=f32
                )
                spot = lanes((seq_len, 128)) == 2 * pair + part
                lse_out[rows] = jnp.where(spot, lse, lse_out[rows])
            mixed_out[rows, area] = mixed.astype(bf16)
            return carry

        lax.fori_loop(0, pairs, attend, 0)
        extra_work.turn(1)
        output_work.turn(0)
        lax.fori_loop(pairs, 2 * pairs, attend, 0)
        table_work.hop(0)
        extra_work.plane(3)
        output_work.close(0)
        output_work.passed(0)
        output_work.own.wait()
        keep(5, 4)

        def tile(low, size):
            weight = all_output[:, :, pl.ds(low, size)].reshape(columns, size)
            value = jnp.dot(mixed_out[...], weight, preferred_element_type=f32).astype(bf16)
            partial[:, :, pl.ds(low, size)] = value.reshape(4, tokens, size)

        by_tiles(width, tile)
        run = Scatter("tokens", place, partial, result, side, arrive, *sum_sems)
        run.outward()
        extra_work.close(1)
        extra_work.turn(2)
        run.inward()
        extra_work.close(2)
        table_work.hop(1)
        extra_work.turn(3)
        run.close()
        table_work.hop(2)
        extra_work.close(3)
        for work in (table_work, extra_work):
            work.arrived()
        run.finish()
        for copy in keeps:
            copy.wait()
        for work in works:
            work.finish()

    vmem, anywhere = pl.BlockSpec(memory_space=pltpu.VMEM), pl.BlockSpec(memory_space=pl.ANY)
    smem = pl.BlockSpec(memory_space=pltpu.SMEM)
    kept = [(4,) + normed.shape] + [(8,) + rows.shape for rows in (query_rows, key_rows, value_rows, output_rows)]
    blocks = [GROUPS[group][1] for group, _ in gathers]
    return pl.pallas_call(
        body,
        out_shape=[
            jax.ShapeDtypeStruct((tokens, width), f32),
            jax.ShapeDtypeStruct((block, columns), bf16),
            jax.ShapeDtypeStruct((block, 128), bf16),
            jax.ShapeDtypeStruct((block, 128), bf16),
            jax.ShapeDtypeStruct((block, columns), bf16),
            jax.ShapeDtypeStruct((block, 128), f32),
            jax.ShapeDtypeStruct((2, seq_len, seq_len), f32),
        ]
        + [jax.ShapeDtypeStruct(shape, bf16) for shape in kept]
        + [
            jax.ShapeDtypeStruct((blocks[item],) + array.shape, array.dtype)
            for item, (_, array) in list(enumerate(gathers))[-2:]
        ],
        in_specs=[anywhere] * count + [vmem] * 5 + [smem],
        out_specs=[vmem] * 7 + [anywhere] * 7,
        scratch_shapes=[
            pltpu.VMEM((blocks[item],) + array.shape, array.dtype)
            for item, (_, array) in enumerate(gathers[:-2])
        ]
        + [
            pltpu.VMEM((4, block, 128), bf16),
            pltpu.VMEM((4, block, 128), bf16),
            pltpu.VMEM((4, tokens, width), bf16),
            pltpu.VMEM((tokens, width), bf16),
            pltpu.VMEM((2, tokens, width), bf16),
        ]
        + [
            pltpu.SemaphoreType.DMA((size,))
            for group, _ in gathers
            for size in (copies(group), copies(group), 1)
        ]
        + [pltpu.SemaphoreType.DMA((copies("tokens"),))] * 2
        + [pltpu.SemaphoreType.DMA((1,)), pltpu.SemaphoreType.DMA((5,))],
        compiler_params=pltpu.CompilerParams(
            collective_id=collective, has_side_effects=True, vmem_limit_bytes=60 * 1024 * 1024
        ),
        name=name,
    )(*[array for _, array in gathers], *biases, *tables, sinks)


def attention_backward(
    outer, query, key, value, mixed, log_total, mask, tokens_kept, weights, tables, sinks, gain, small, collective, name
):
    tokens, width = outer.shape
    block = 4 * tokens
    seq_len = 2 * tokens
    columns = query.shape[1]
    pairs = columns // 128
    scale = 1.0 / math.sqrt(HD)
    bf16, f32 = jnp.bfloat16, jnp.float32
    owned = [rows.shape[1] for rows in weights]
    groups = ["heads"] * 4 + ["tokens"]

    def body(*refs):
        refs = list(refs)

        def take(number):
            got = refs[:number]
            del refs[:number]
            return got

        (outer_ref,) = take(1)
        query_ref, key_ref, value_ref, mixed_ref, lse_ref, mask_ref = take(6)
        stored = take(5)
        cosine, sine, sink_ref, gain_ref, small_ref = take(5)
        results = take(5)
        (small_out,) = take(1)
        held = take(5)
        grads, key_half, value_half = take(3)
        mixed_grad, query_grad, key_grad, value_grad = take(4)
        key_sum, value_sum, sink_sum, small_own, small_all = take(5)
        output_part, key_part, value_part = take(3)
        mates, sides, arrives = take(4), take(5), take(5)
        load_sem, gather_sems, small_sems = take(1)[0], take(3), take(3)
        sum_sems = [take(3) for _ in groups]
        place = place_here()
        greet = []
        for group in ("tokens", "heads", "all"):
            greet += [step for step in partners(group) if step not in greet]
        barrier = pltpu.get_barrier_semaphore()
        for step in greet:
            pl.semaphore_signal(barrier, inc=1, device_id=flip(place, step), device_id_type=MESH)
        pl.semaphore_wait(barrier, len(greet))
        work = Gather("tokens", place, outer_ref, grads, *gather_sems)
        work.start()
        work.plane(0)
        loads = []
        for item in (4, 1, 2, 3, 0):
            copy = pltpu.make_async_copy(stored[item], held[item], load_sem.at[item])
            copy.start()
            loads.append(copy)
        all_tokens, all_query, all_key, all_value, all_output = held
        for member in range(2):
            for part, half in enumerate(halves_of(key_ref[...], member)):
                key_half[2 * member + part] = half
            for part, half in enumerate(halves_of(value_ref[...], member)):
                value_half[2 * member + part] = half
        key_sum[...] = jnp.zeros_like(key_sum)
        value_sum[...] = jnp.zeros_like(value_sum)
        sink_sum[...] = jnp.zeros_like(sink_sum)
        small_own[...] = small_ref[...]
        work.turn(0)
        work.close(0)
        work.own.wait()
        work.finish()

        parts = [all_output, key_part, value_part, output_part, grads]
        sums = [
            Scatter(
                group,
                place,
                parts[item],
                results[item],
                sides[item],
                arrives[item],
                *sum_sems[item],
                mate=mates[item] if group == "heads" else None,
            )
            for item, group in enumerate(groups)
        ]
        of_query, of_key, of_value, of_output, of_tokens = sums

        def output_gradient(number, carry):
            area = pl.ds(pl.multiple_of(number * 128, 128), 128)
            rows = inner_rows(mixed_ref[:, area], grads[...].reshape(block, width))
            output_part[number] = rows.astype(bf16)
            return carry

        lax.fori_loop(0, pairs, output_gradient, 0)
        of_output.cross()
        loads[0].wait()

        def project(number, carry):
            weight = all_output[pl.ds(pl.multiple_of(2 * number, 2), 2)].reshape(256, width)
            area = pl.ds(pl.multiple_of(number * 256, 256), 256)
            mixed_grad[:, area] = times_transposed(
                grads[...].reshape(block, width), weight
            ).astype(bf16)
            return carry

        lax.fori_loop(0, pairs // 2, project, 0)
        of_output.outward()

        def back(value):
            return value * cosine[:seq_len] - swapped(value) * sine[:seq_len]

        def attend(number, carry):
            pair = lax.div(number, 2)
            half = lax.rem(number, 2)
            member = lax.div(pair, pairs // 2)
            rows = pl.ds(pl.multiple_of(half * seq_len, seq_len), seq_len)
            area = pl.ds(pl.multiple_of(pair * 128, 128), 128)
            queries = query_ref[rows, area]
            upstream = mixed_grad[rows, area]
            low = lanes((seq_len, 128)) < HD
            made = jnp.zeros((seq_len, 128), f32)
            for part in range(2):
                head = 2 * pair + part
                keys = key_half[2 * member + part, rows]
                lse = pick_lane(lse_ref[rows], head)
                raw = times_transposed(queries, keys) * scale
                raw = jnp.where(mask_ref[half] > 0.0, raw, masked_score)
                probs = jnp.exp(raw - lse)
                grad = times_transposed(upstream, value_half[2 * member + part, rows])
                delta = jnp.sum(probs * grad, axis=1, keepdims=True)
                inner = (probs * (grad - delta)).astype(bf16)
                made = made + jnp.dot(inner, keys, preferred_element_type=f32)
                mine = low if part == 0 else jnp.logical_not(low)
                value_sum[member, rows] += jnp.where(mine, inner_rows(probs.astype(bf16), upstream), 0.0)
                key_sum[member, rows] += jnp.where(mine, inner_rows(inner, queries), 0.0)
                lost = jnp.sum(jnp.exp(sink_ref[0, head] - lse) * delta, axis=0, keepdims=True)
                sink_sum[...] -= jnp.where(lanes((1, 128)) == head, lost, 0.0)
            query_grad[rows, area] = back(made * scale).astype(bf16)
            return carry

        lax.fori_loop(0, pairs, attend, 0)
        of_output.inward()
        lax.fori_loop(pairs, 2 * pairs, attend, 0)
        low = lanes((seq_len, 128)) < HD
        for half in range(2):
            rows = pl.ds(half * seq_len, seq_len)

            def joined(sums):
                first = sums[0, rows] + pltpu.roll(sums[0, rows], HD, 1)
                second = sums[1, rows] + pltpu.roll(sums[1, rows], HD, 1)
                return jnp.where(low, first, second)

            key_grad[rows] = back(joined(key_sum) * scale).astype(bf16)
            value_grad[rows] = joined(value_sum).astype(bf16)
        for copy in loads[1:]:
            copy.wait()

        def tile(low_column, size):
            area = pl.ds(low_column, size)

            def rows_of(weight):
                return weight[:, :, area].reshape(-1, size)

            total_grad = jnp.dot(query_grad[...], rows_of(all_query), preferred_element_type=f32)
            total_grad += jnp.dot(key_grad[...], rows_of(all_key), preferred_element_type=f32)
            total_grad += jnp.dot(value_grad[...], rows_of(all_value), preferred_element_type=f32)
            gained = total_grad * all_tokens[:, :, area].reshape(block, size).astype(f32)
            small_own[0:1, area] = jnp.sum(gained, axis=0, keepdims=True) / gain_ref[:, area]
            grads[:, :, area] = total_grad.astype(bf16).reshape(4, tokens, size)

        by_tiles(width, tile)
        low_column = 0
        for array in (query_grad, key_grad, value_grad):
            size = array.shape[1]
            small_own[3:4, low_column : low_column + size] = jnp.sum(
                array[...].astype(f32), axis=0, keepdims=True
            )
            low_column += size
        small_own[3:4, low_column : low_column + 128] = sink_sum[...]
        spread = Gather("all", place, small_own, small_all, *small_sems)
        spread.start()
        of_tokens.outward()

        def query_gradient(number, carry):
            area = pl.ds(pl.multiple_of(number * 128, 128), 128)
            rows = inner_rows(query_grad[:, area], all_tokens[...].reshape(block, width))
            all_output[number] = rows.astype(bf16)
            return carry

        lax.fori_loop(0, pairs, query_gradient, 0)
        of_query.cross()
        for goal, grad in ((key_part, key_grad), (value_part, value_grad)):
            rows = inner_rows(grad[...], all_tokens[...].reshape(block, width))
            goal[...] = rows.astype(bf16).reshape(goal.shape)
        of_key.cross()
        of_value.cross()
        spread.relay(1)
        spread.relay(2)
        of_query.outward()
        of_key.outward()
        of_value.outward()
        spread.relay(3)
        of_tokens.inward()
        spread.hop(0)
        of_query.inward()
        of_key.inward()
        of_value.inward()
        spread.hop(1)
        of_tokens.close()
        spread.hop(2)
        of_output.close()
        of_query.close()
        of_key.close()
        of_value.close()
        spread.arrived()
        spread.finish()
        blocks = small_all.shape[0]
        whole = small_all[0]
        for number in range(1, blocks):
            whole = whole + small_all[number]
        small_out[0:4] = whole[0:4]
        for near in range(2):
            for side in range(2):
                chosen = [
                    number for number in range(blocks) if (number // 8 % 2, number // 2 % 2) == (near, side)
                ]
                part = small_all[chosen[0], 3:4]
                for number in chosen[1:]:
                    part = part + small_all[number, 3:4]
                small_out[4 + 2 * near + side : 5 + 2 * near + side] = part
        for part in sums:
            part.finish()

    vmem, anywhere = pl.BlockSpec(memory_space=pltpu.VMEM), pl.BlockSpec(memory_space=pl.ANY)
    smem = pl.BlockSpec(memory_space=pltpu.SMEM)
    rows_of = owned + [tokens]
    kept = [tokens_kept] + list(weights)
    return pl.pallas_call(
        body,
        out_shape=[jax.ShapeDtypeStruct((rows, width), f32) for rows in rows_of]
        + [jax.ShapeDtypeStruct(small.shape, f32)],
        in_specs=[anywhere] + [vmem] * 6 + [anywhere] * 5 + [vmem] * 2 + [smem] + [vmem] * 2,
        out_specs=[vmem] * 6,
        scratch_shapes=[pltpu.VMEM(array.shape, bf16) for array in kept]
        + [
            pltpu.VMEM((4, tokens, width), bf16),
            pltpu.VMEM((4, block, 128), bf16),
            pltpu.VMEM((4, block, 128), bf16),
            pltpu.VMEM((block, columns), bf16),
            pltpu.VMEM((block, columns), bf16),
            pltpu.VMEM((block, 128), bf16),
            pltpu.VMEM((block, 128), bf16),
            pltpu.VMEM((2, block, 128), f32),
            pltpu.VMEM((2, block, 128), f32),
            pltpu.VMEM((1, 128), f32),
            pltpu.VMEM(small.shape, f32),
            pltpu.VMEM((GROUPS["all"][1],) + small.shape, f32),
            pltpu.VMEM(weights[3].shape, bf16),
            pltpu.VMEM(weights[1].shape, bf16),
            pltpu.VMEM(weights[2].shape, bf16),
        ]
        + [pltpu.VMEM((4, rows, width), bf16) for rows in owned]
        + [pltpu.VMEM((rows, width), bf16) for rows in rows_of]
        + [pltpu.VMEM((2, rows, width), bf16) for rows in rows_of]
        + [pltpu.SemaphoreType.DMA((5,))]
        + [
            pltpu.SemaphoreType.DMA((size,))
            for group in ["tokens", "all"] + groups
            for size in (copies(group), copies(group), 1)
        ],
        compiler_params=pltpu.CompilerParams(
            collective_id=collective, has_side_effects=True, vmem_limit_bytes=62 * 1024 * 1024
        ),
        name=name,
    )(outer, query, key, value, mixed, log_total, mask, *kept, *tables, sinks, gain, small)


def close_by(
    tokens,
    segments,
    routes,
    gate_share,
    attn_gain,
    query_weight,
    query_bias,
    key_weight,
    key_bias,
    value_weight,
    value_bias,
    output_weight,
    output_bias,
    sink_logits,
    moe_gain,
    gate_weight,
    gate_bias,
    up_weight,
    up_bias,
    down_weight,
    down_bias,
    cotangent,
):
    count_rows = tokens.shape[1]
    width = tokens.shape[2]
    head_count = sink_logits.shape[0]
    kv_count = key_bias.shape[0] // HD
    group = head_count // kv_count
    experts = lax.axis_size("exp")
    devices = 4 * experts
    topk = routes.shape[2]
    capacity = count_rows * topk * 9 // (8 * experts)
    x, e, y = place_here()
    near_bit = lax.rem(lax.div(e, 2), 2)
    seq_len = 2 * count_rows

    chosen = routes[0].reshape(-1)
    expert_hot = (chosen[:, None] == jnp.arange(experts, dtype=jnp.int32)[None, :]).astype(
        jnp.int32
    )
    earlier = (jnp.cumsum(expert_hot, axis=0) - expert_hot).reshape(count_rows, topk, experts)
    named = expert_hot.reshape(count_rows, topk, experts)
    slot_table = jnp.sum((earlier + 1) * named, axis=1) - 1
    share_table = jnp.sum(named.astype(jnp.float32) * gate_share[0][:, :, None], axis=1)
    table = jnp.concatenate([slot_table.astype(jnp.float32).T, share_table.T], axis=0)

    resid = tokens[0].astype(jnp.float32)
    attn_norm, attn_norm_pull = jax.vjp(rms_apply, resid, attn_gain)
    normed = attn_norm.astype(jnp.bfloat16)
    block_tokens = 4 * count_rows
    held_kv = 2
    held_heads = held_kv * group

    def own_part(vector):
        size = vector.shape[0] // 8
        first = (4 * x + near_bit) * size
        parts = [lax.dynamic_slice(vector, (first + 2 * far * size,), (size,)) for far in range(2)]
        return jnp.concatenate(parts)[None]

    position = jnp.arange(seq_len, dtype=jnp.int32)
    cosine, sine = rope_tables(position, HD)
    cosine = jnp.tile(cosine, (2, 4))
    sine = jnp.tile(jnp.concatenate([-sine, sine], axis=1), (2, 2))
    own_ids = lax.dynamic_slice_in_dim(segments[0], x * count_rows, count_rows, 0)
    marks = jnp.broadcast_to(own_ids.astype(jnp.float32)[:, None], (count_rows, count_rows))
    sinks = own_part(sink_logits)
    (
        attn_out,
        query_rot,
        key_rot,
        value_low,
        mixed,
        log_total,
        mask,
        group_tokens,
        group_query,
        group_key,
        group_value,
        group_output,
        tables,
        all_cotangents,
    ) = attention_forward(
        normed,
        query_weight.T,
        key_weight.T,
        value_weight.T,
        output_weight,
        marks,
        table,
        cotangent[0],
        (own_part(query_bias), own_part(key_bias), own_part(value_bias)),
        (cosine, sine),
        sinks,
        0,
        "attention_forward",
    )
    hidden = resid + (attn_out + output_bias)
    moe_norm, moe_norm_pull = jax.vjp(rms_apply, hidden, moe_gain)
    normed_moe = moe_norm.astype(jnp.bfloat16)

    def by_pairs(part):
        part = jnp.moveaxis(part.reshape(experts, 2, 2, experts, count_rows), 3, 0)
        return part.reshape(experts, experts, 2, 1, 2 * count_rows)

    slots = tables[:, :experts].astype(jnp.int32)
    second_block = jnp.arange(devices, dtype=jnp.int32)[:, None, None] % 2
    seats = by_pairs(jnp.where(slots >= 0, slots + capacity * second_block, -1))
    sibling = e + 1 - 2 * lax.rem(e, 2)
    seats = jnp.stack(
        [
            lax.dynamic_index_in_dim(seats, e, 0, keepdims=False),
            lax.dynamic_index_in_dim(seats, sibling, 0, keepdims=False),
        ]
    )
    gate_rows, up_rows = gate_weight[0].T, up_weight[0].T
    shares = lax.dynamic_index_in_dim(by_pairs(tables[:, experts:]), e, 0, keepdims=False)
    (
        expert_rows,
        grad_rows,
        activation,
        gate_grad,
        up_grad,
        gate_bias_grad,
        up_bias_grad,
        down_bias_grad,
        _,
    ) = expert_rows_kernel(
        normed_moe,
        all_cotangents,
        (gate_rows, up_rows, down_weight[0]),
        (gate_bias, up_bias),
        seats[0],
        shares,
        capacity,
        2,
        "route_rows",
    )
    (normed_moe_grad,) = expert_sums(
        "gradient", (gate_grad, up_grad), (gate_rows, up_rows), seats, (), 3, "sum_rows"
    )
    moe_out, gate_weight_grad, up_weight_grad, down_weight_grad = expert_sums(
        "result",
        (activation,),
        (down_weight[0],),
        seats,
        (shares, down_bias),
        4,
        "sum_results",
        ((gate_grad, expert_rows), (up_grad, expert_rows), (activation, grad_rows)),
    )
    output = (hidden + moe_out).astype(jnp.bfloat16)

    upstream = cotangent[0].astype(jnp.float32)
    hidden_norm_grad, moe_gain_grad = moe_norm_pull(normed_moe_grad)
    hidden_grad = upstream + hidden_norm_grad
    attn_out_grad = hidden_grad.astype(jnp.bfloat16)
    output_bias_grad = jnp.sum(attn_out_grad.astype(jnp.float32), axis=0)
    small = jnp.concatenate(
        [
            jnp.zeros((1, width), jnp.float32),
            moe_gain_grad[None],
            output_bias_grad[None],
            jnp.zeros((5, width), jnp.float32),
        ],
        axis=0,
    )
    query_owned, key_owned, value_owned, output_owned, normed_grad, small_sums = attention_backward(
        attn_out_grad,
        query_rot,
        key_rot,
        value_low,
        mixed,
        log_total,
        mask,
        group_tokens,
        (group_query, group_key, group_value, group_output),
        (cosine, sine),
        sinks,
        attn_gain[None],
        small,
        5,
        "attention_backward",
    )
    lengths = (held_heads * HD, held_kv * HD, held_kv * HD, held_heads)
    resid_norm_grad, _ = attn_norm_pull(normed_grad)
    input_grad = hidden_grad + resid_norm_grad
    pieces = []
    for low, length in zip((0, lengths[0], sum(lengths[:2]), sum(lengths[:3])), lengths):
        piece = small_sums[4:, low : low + length].reshape(2, 2, held_kv, -1)
        pieces.append(jnp.transpose(piece, (1, 2, 0, 3)).reshape(-1))
    query_bias_grad, key_bias_grad, value_bias_grad, sink_grad = pieces
    return (
        output[None],
        input_grad[None],
        small_sums[0],
        query_owned.T,
        query_bias_grad,
        key_owned.T,
        key_bias_grad,
        value_owned.T,
        value_bias_grad,
        output_owned,
        small_sums[2],
        sink_grad,
        small_sums[1],
        gate_weight_grad.T[None],
        gate_bias_grad,
        up_weight_grad.T[None],
        up_bias_grad,
        down_weight_grad[None],
        down_bias_grad,
    )


def solution(mesh):
    placed = (
        P(("exp", "dp"), "seq", None),
        P(("exp", "dp"), None),
        P(("exp", "dp"), "seq", None),
        P(("exp", "dp"), "seq", None),
        P(),
        P(None, ("seq", "exp", "dp")),
        P(),
        P(None, ("seq", "exp", "dp")),
        P(),
        P(None, ("seq", "exp", "dp")),
        P(),
        P(("seq", "exp", "dp"), None),
        P(),
        P(),
        P(),
        P("exp", None, ("seq", "dp")),
        P("exp", ("seq", "dp")),
        P("exp", None, ("seq", "dp")),
        P("exp", ("seq", "dp")),
        P("exp", ("seq", "dp"), None),
        P("exp", None),
        P(("exp", "dp"), "seq", None),
    )
    shape = mesh.shape
    small = shape["seq"] == 2 and shape["dp"] == 2 and shape["exp"] == 8
    return jax.shard_map(
        close_by if small else local,
        mesh=mesh,
        in_specs=placed,
        out_specs=(
            P(("exp", "dp"), "seq", None),
            P(("exp", "dp"), "seq", None),
            P(),
            P(None, ("seq", "exp", "dp")),
            P(),
            P(None, ("seq", "exp", "dp")),
            P(),
            P(None, ("seq", "exp", "dp")),
            P(),
            P(("seq", "exp", "dp"), None),
            P(),
            P(),
            P(),
            P("exp", None, ("seq", "dp")),
            P("exp", ("seq", "dp")),
            P("exp", None, ("seq", "dp")),
            P("exp", ("seq", "dp")),
            P("exp", ("seq", "dp"), None),
            P("exp", None),
        ),
        check_vma=False,
    )
```

```python
import math

import jax
import jax.numpy as jnp
from jax import lax
from jax.experimental import pallas as pl
from jax.experimental.pallas import tpu as pltpu
from jax.sharding import PartitionSpec as P

HD = 64


highest = lax.Precision.HIGHEST
norm_eps = 1e-05
rope_base = 150000.0
clip_level = 7.0
glu_alpha = 1.702
masked_score = -1000000000.0


def rms_apply(values, gain):
    return values * lax.rsqrt(jnp.mean(values * values, axis=-1, keepdims=True) + norm_eps) * gain


def rope_tables(position, width):
    exponent = jnp.arange(width // 2).astype(jnp.float32) * (2.0 / width)
    freqs = jnp.exp(-math.log(rope_base) * exponent)
    angles = position.astype(jnp.float32)[:, None] * freqs[None, :]
    return (jnp.cos(angles), jnp.sin(angles))


def rotate(values, cosine, sine):
    half = values.shape[-1] // 2
    first = values[..., :half]
    second = values[..., half:]
    return jnp.concatenate(
        [first * cosine - second * sine, second * cosine + first * sine], axis=-1
    )


def swiglu(gate_pre, up_pre):
    gate_soft = clip_level * jnp.tanh(gate_pre / clip_level)
    up_soft = clip_level * jnp.tanh(up_pre / clip_level)
    return gate_soft * jax.nn.sigmoid(glu_alpha * gate_soft) * (up_soft + 1.0)


def inner_rows(left, right):
    return lax.dot_general(
        left, right, (((0,), (0,)), ((), ())), preferred_element_type=jnp.float32
    )


def times_transposed(left, right):
    return lax.dot_general(
        left, right, (((1,), (1,)), ((), ())), preferred_element_type=jnp.float32
    )


def to_experts(outgoing):
    width = outgoing.shape[2]
    arrived = lax.all_to_all(outgoing, "exp", split_axis=0, concat_axis=0, tiled=True)
    arrived = lax.all_gather(arrived, ("seq", "dp"), axis=0, tiled=True)
    return arrived.reshape(-1, width)


def results_back(activation, down_matrix, down_vector, experts, capacity):
    width = down_matrix.shape[1]
    share = lax.psum_scatter(
        jnp.dot(activation, down_matrix, preferred_element_type=jnp.float32).astype(jnp.bfloat16),
        ("seq", "dp"),
        scatter_dimension=0,
        tiled=True,
    ).astype(jnp.float32)
    finished = (share + down_vector).astype(jnp.bfloat16).reshape(experts, capacity, width)
    return lax.all_to_all(finished, "exp", split_axis=0, concat_axis=0, tiled=True)


def gradients_back(gate_grad, up_grad, gate_matrix, up_matrix, experts, capacity):
    share = lax.psum_scatter(
        times_transposed(gate_grad, gate_matrix) + times_transposed(up_grad, up_matrix),
        ("seq", "dp"),
        scatter_dimension=0,
        tiled=True,
    )
    return lax.all_to_all(
        share.reshape(experts, capacity, share.shape[1]),
        "exp",
        split_axis=0,
        concat_axis=0,
        tiled=True,
    )


def local(
    tokens,
    segments,
    routes,
    gate_share,
    attn_gain,
    query_weight,
    query_bias,
    key_weight,
    key_bias,
    value_weight,
    value_bias,
    output_weight,
    output_bias,
    sink_logits,
    moe_gain,
    gate_weight,
    gate_bias,
    up_weight,
    up_bias,
    down_weight,
    down_bias,
    cotangent,
):
    count_rows = tokens.shape[1]
    width = tokens.shape[2]
    head_count = sink_logits.shape[0]
    kv_count = key_bias.shape[0] // HD
    group = head_count // kv_count
    scale = 1.0 / math.sqrt(HD)
    experts = lax.axis_size("exp")
    topk = routes.shape[2]
    capacity = count_rows * topk * 9 // (8 * experts)
    resid = tokens[0].astype(jnp.float32)
    full_query, full_key, full_value, full_output = (
        lax.all_gather(query_weight, ("seq", "exp", "dp"), axis=1, tiled=True),
        lax.all_gather(key_weight, ("seq", "exp", "dp"), axis=1, tiled=True),
        lax.all_gather(value_weight, ("seq", "exp", "dp"), axis=1, tiled=True),
        lax.all_gather(output_weight, ("seq", "exp", "dp"), axis=0, tiled=True),
    )
    attn_norm, attn_norm_pull = jax.vjp(rms_apply, resid, attn_gain)
    normed = attn_norm.astype(jnp.bfloat16)
    query_lin = jnp.dot(normed, full_query, preferred_element_type=jnp.float32) + query_bias
    key_lin = jnp.dot(normed, full_key, preferred_element_type=jnp.float32) + key_bias
    value_low = (
        jnp.dot(normed, full_value, preferred_element_type=jnp.float32) + value_bias
    ).astype(jnp.bfloat16)
    offset = lax.axis_index("seq") * count_rows
    position = offset + jnp.arange(count_rows, dtype=jnp.int32)
    cosine, sine = rope_tables(position, HD)
    cosine = cosine[:, None]
    sine = sine[:, None]
    query_rot = rotate(query_lin.reshape(count_rows, head_count, HD), cosine, sine).astype(
        jnp.bfloat16
    )
    key_rot = rotate(key_lin.reshape(count_rows, kv_count, HD), cosine, sine).astype(jnp.bfloat16)
    all_keys, all_values = (
        lax.all_gather(key_rot.reshape(count_rows, kv_count * HD), "seq", axis=0, tiled=True),
        lax.all_gather(value_low, "seq", axis=0, tiled=True),
    )
    seq_len = all_keys.shape[0]
    all_keys = all_keys.reshape(seq_len, kv_count, HD)
    all_values = all_values.reshape(seq_len, kv_count, HD)
    doc_ids = segments[0]
    own_ids = lax.dynamic_slice_in_dim(doc_ids, offset, count_rows, 0)
    key_place = jnp.arange(seq_len, dtype=jnp.int32)
    visible = (position[:, None] >= key_place[None, :]) & (own_ids[:, None] == doc_ids[None, :])
    query_group = query_rot.reshape(count_rows, kv_count, group, HD)
    sink_grid = sink_logits.reshape(kv_count, group)[:, :, None]

    def score_block():
        raw = (
            jnp.einsum("qkgd,skd->kgqs", query_group, all_keys, preferred_element_type=jnp.float32)
            * scale
        )
        return jnp.where(visible[None, None], raw, masked_score)

    scores = score_block()
    peak = jnp.maximum(jnp.max(scores, axis=-1), sink_grid)
    total = jnp.sum(jnp.exp(scores - peak[..., None]), axis=-1) + jnp.exp(sink_grid - peak)
    log_total = peak + jnp.log(total)
    probs = jnp.exp(scores - log_total[..., None])
    mixed = jnp.einsum(
        "kgqs,skd->qkgd", probs.astype(jnp.bfloat16), all_values, preferred_element_type=jnp.float32
    )
    mixed = mixed.reshape(count_rows, head_count * HD).astype(jnp.bfloat16)
    attn_out = jnp.dot(mixed, full_output, preferred_element_type=jnp.float32) + output_bias
    hidden = resid + attn_out
    moe_norm, moe_norm_pull = jax.vjp(rms_apply, hidden, moe_gain)
    normed_moe = moe_norm.astype(jnp.bfloat16)
    chosen = routes[0].reshape(-1)
    expert_hot = (chosen[:, None] == jnp.arange(experts, dtype=jnp.int32)[None, :]).astype(
        jnp.int32
    )
    slot_index = jnp.sum((jnp.cumsum(expert_hot, axis=0) - expert_hot) * expert_hot, axis=1)
    target = chosen * capacity + slot_index
    slot_hot = (
        target[:, None] == jnp.arange(experts * capacity, dtype=jnp.int32)[None, :]
    ).reshape(count_rows, topk, experts * capacity)
    dispatch = jnp.sum(slot_hot.astype(jnp.bfloat16), axis=1)
    weighted = jnp.sum(slot_hot.astype(jnp.float32) * gate_share[0][:, :, None], axis=1)
    outgoing = jnp.einsum("ts,td->sd", dispatch, normed_moe, preferred_element_type=jnp.float32)
    outgoing = outgoing.astype(jnp.bfloat16).reshape(experts, capacity, width)
    expert_rows = to_experts(outgoing)
    gate_pre = (
        jnp.dot(expert_rows, gate_weight[0], preferred_element_type=jnp.float32) + gate_bias[0]
    )
    up_pre = jnp.dot(expert_rows, up_weight[0], preferred_element_type=jnp.float32) + up_bias[0]
    act_full, swiglu_pull = jax.vjp(swiglu, gate_pre, up_pre)
    activation = act_full.astype(jnp.bfloat16)
    returned = results_back(activation, down_weight[0], down_bias[0], experts, capacity)
    moe_out = jnp.dot(
        weighted, returned.reshape(experts * capacity, width).astype(jnp.float32), precision=highest
    )
    output = (hidden + moe_out).astype(jnp.bfloat16)
    upstream = cotangent[0].astype(jnp.float32)
    grad_slots = jnp.einsum("ts,td->sd", weighted, upstream, precision=highest)
    grad_slots = grad_slots.astype(jnp.bfloat16).reshape(experts, capacity, width)
    grad_rows = to_experts(grad_slots)
    down_bias_grad = jnp.sum(grad_rows.astype(jnp.float32), axis=0)
    down_weight_grad = inner_rows(activation, grad_rows)
    act_grad = times_transposed(grad_rows, down_weight[0])
    gate_grad_full, up_grad_full = swiglu_pull(act_grad)
    gate_grad = gate_grad_full.astype(jnp.bfloat16)
    up_grad = up_grad_full.astype(jnp.bfloat16)
    gate_bias_grad = jnp.sum(gate_grad.astype(jnp.float32), axis=0)
    up_bias_grad = jnp.sum(up_grad.astype(jnp.float32), axis=0)
    gate_weight_grad = inner_rows(expert_rows, gate_grad)
    up_weight_grad = inner_rows(expert_rows, up_grad)
    rows_grad = gradients_back(gate_grad, up_grad, gate_weight[0], up_weight[0], experts, capacity)
    normed_moe_grad = jnp.einsum(
        "ts,sd->td",
        dispatch.astype(jnp.float32),
        rows_grad.reshape(experts * capacity, width),
        precision=highest,
    )
    hidden_norm_grad, moe_gain_grad = moe_norm_pull(normed_moe_grad)
    hidden_grad = upstream + hidden_norm_grad
    attn_out_grad = hidden_grad.astype(jnp.bfloat16)
    output_bias_grad = jnp.sum(attn_out_grad.astype(jnp.float32), axis=0)
    full_query, full_key, full_value, full_output = (
        lax.all_gather(query_weight, ("seq", "exp", "dp"), axis=1, tiled=True),
        lax.all_gather(key_weight, ("seq", "exp", "dp"), axis=1, tiled=True),
        lax.all_gather(value_weight, ("seq", "exp", "dp"), axis=1, tiled=True),
        lax.all_gather(output_weight, ("seq", "exp", "dp"), axis=0, tiled=True),
    )
    mixed_grad = (
        times_transposed(attn_out_grad, full_output)
        .astype(jnp.bfloat16)
        .reshape(count_rows, kv_count, group, HD)
    )
    scores = score_block()
    probs = jnp.exp(scores - log_total[..., None])
    prob_grad = jnp.einsum(
        "qkgd,skd->kgqs", mixed_grad, all_values, preferred_element_type=jnp.float32
    )
    delta = jnp.sum(probs * prob_grad, axis=-1)
    score_grad = (probs * (prob_grad - delta[..., None])).astype(jnp.bfloat16)
    sink_grad = -jnp.sum(jnp.exp(sink_grid - log_total) * delta, axis=-1).reshape(head_count)
    value_grad = jnp.einsum(
        "kgqs,qkgd->skd", probs.astype(jnp.bfloat16), mixed_grad, preferred_element_type=jnp.float32
    )
    key_grad = (
        jnp.einsum("kgqs,qkgd->skd", score_grad, query_group, preferred_element_type=jnp.float32)
        * scale
    )
    query_grad = (
        jnp.einsum("kgqs,skd->qkgd", score_grad, all_keys, preferred_element_type=jnp.float32)
        * scale
    )
    key_share, value_share = (
        lax.psum_scatter(
            key_grad.reshape(seq_len, kv_count * HD), "seq", scatter_dimension=0, tiled=True
        ),
        lax.psum_scatter(
            value_grad.reshape(seq_len, kv_count * HD), "seq", scatter_dimension=0, tiled=True
        ),
    )
    query_lin_grad = (
        rotate(query_grad.reshape(count_rows, head_count, HD), cosine, -sine)
        .reshape(count_rows, head_count * HD)
        .astype(jnp.bfloat16)
    )
    key_lin_grad = (
        rotate(key_share.reshape(count_rows, kv_count, HD), cosine, -sine)
        .reshape(count_rows, kv_count * HD)
        .astype(jnp.bfloat16)
    )
    value_lin_grad = value_share.astype(jnp.bfloat16)
    query_bias_grad = jnp.sum(query_lin_grad.astype(jnp.float32), axis=0)
    key_bias_grad = jnp.sum(key_lin_grad.astype(jnp.float32), axis=0)
    value_bias_grad = jnp.sum(value_lin_grad.astype(jnp.float32), axis=0)
    normed_grad = (
        times_transposed(query_lin_grad, full_query)
        + times_transposed(key_lin_grad, full_key)
        + times_transposed(value_lin_grad, full_value)
    )
    resid_norm_grad, attn_gain_grad = attn_norm_pull(normed_grad)
    input_grad = hidden_grad + resid_norm_grad
    query_weight_grad = inner_rows(normed, query_lin_grad)
    key_weight_grad = inner_rows(normed, key_lin_grad)
    value_weight_grad = inner_rows(normed, value_lin_grad)
    output_weight_grad = inner_rows(mixed, attn_out_grad)
    query_owned, key_owned, value_owned, output_owned = (
        lax.psum_scatter(query_weight_grad, ("seq", "exp", "dp"), scatter_dimension=1, tiled=True),
        lax.psum_scatter(key_weight_grad, ("seq", "exp", "dp"), scatter_dimension=1, tiled=True),
        lax.psum_scatter(value_weight_grad, ("seq", "exp", "dp"), scatter_dimension=1, tiled=True),
        lax.psum_scatter(output_weight_grad, ("seq", "exp", "dp"), scatter_dimension=0, tiled=True),
    )
    summed = lax.psum(
        (
            attn_gain_grad,
            query_bias_grad,
            key_bias_grad,
            value_bias_grad,
            output_bias_grad,
            sink_grad,
            moe_gain_grad,
        ),
        ("seq", "exp", "dp"),
    )
    return (
        output[None],
        input_grad[None],
        summed[0],
        query_owned,
        summed[1],
        key_owned,
        summed[2],
        value_owned,
        summed[3],
        output_owned,
        summed[4],
        summed[5],
        summed[6],
        gate_weight_grad[None],
        gate_bias_grad[None],
        up_weight_grad[None],
        up_bias_grad[None],
        down_weight_grad[None],
        down_bias_grad[None],
    )

MESH = pl.DeviceIdType.MESH
HERE = (0, 0, 0)
SIBLING = (0, 1, 0)
ACROSS = (1, 0, 0)
ALONG = (0, 0, 1)
NEAR = (0, 2, 0)
FAR = (0, 4, 0)
ENDS = (0, 6, 0)
THIRD = (0, 8, 0)
FOURTH = (0, 16, 0)


def flip(place, mask):
    x, e, y = place
    if mask[0]:
        x = 1 - x
    if mask[2]:
        y = 1 - y
    if mask[1] & 8:
        e = 2 * (2 - lax.div(e, 4)) + lax.rem(e, 2)
    if mask[1] & 16:
        e = 2 * (3 - 3 * lax.div(e, 4)) + lax.rem(e, 2)
    step = 0
    for bit in (1, 2, 4):
        if mask[1] & bit:
            step = step + bit - 2 * bit * lax.rem(lax.div(e, bit), 2)
    return x, e + step, y


def both(left, right):
    return tuple(a ^ b for a, b in zip(left, right))


def place_here():
    return lax.axis_index("seq"), lax.axis_index("exp"), lax.axis_index("dp")


def block_of_all(place):
    x, e, y = place
    return (e * 2 + x) * 2 + y


def block_of_tokens(place):
    x, e, y = place
    return lax.rem(lax.div(e, 2), 2) * 2 + x


def block_of_heads(place):
    x, e, y = place
    return (lax.div(e, 4) * 2 + lax.rem(e, 2)) * 2 + y


GROUPS = {
    "all": (block_of_all, 32, SIBLING, ACROSS, ALONG, (NEAR, ENDS), 0.5),
    "tokens": (block_of_tokens, 4, None, ACROSS, NEAR, (), 0.5),
    "heads": (block_of_heads, 8, SIBLING, FAR, ALONG, (), 1.0),
}


def partners(group):
    _, _, sibling, first, second, line, _ = GROUPS[group]
    return ([sibling] if sibling else []) + [first, second] + list(line)


def copies(group):
    _, _, sibling, _, _, line, _ = GROUPS[group]
    if line:
        return 4 * 8 + 5
    return 8 if sibling else 4


class Sender:
    def __init__(self, place, send, recv):
        self.place, self.send, self.recv, self.started = place, send, recv, []
        self.maybe = []
        line_place = lax.div(place[1], 2)
        self.inner = (line_place == 1) | (line_place == 2)

    def plan(self, source, target, mask, lands=None):
        number = len(self.started) + len(self.maybe)
        return pltpu.make_async_remote_copy(
            src_ref=source,
            dst_ref=target,
            send_sem=self.send.at[number],
            recv_sem=self.recv.at[number if lands is None else lands],
            device_id=flip(self.place, mask),
            device_id_type=MESH,
        )

    def push(self, source, target, mask):
        copy = self.plan(source, target, mask)
        copy.start()
        self.started.append(copy)
        return copy

    def push_within(self, source, target, mask, lands=None, inner=True):
        copy = self.plan(source, target, mask, lands)
        number = len(self.started) + len(self.maybe)
        here = self.inner if inner else jnp.logical_not(self.inner)
        self.maybe.append((here, copy))
        pl.when(here)(copy.start)
        return copy, number

    def finish(self):
        for copy in self.started:
            copy.wait_send()
        for here, copy in self.maybe:
            pl.when(here)(copy.wait_send)


class Gather:
    def __init__(self, group, place, source, result, send, recv, local, share=None):
        self.index, _, self.sibling, self.first, self.second, line, usual = GROUPS[group]
        self.place, self.source, self.result = place, source, result
        self.rows = source.shape[0]
        share = usual if share is None else share
        self.cut = int(self.rows * share) // 16 * 16
        self.out = Sender(place, send, recv)
        self.own = pltpu.make_async_copy(source, self.at(HERE), local.at[0])
        self.masks = [HERE, NEAR, THIRD, FOURTH] if line else [HERE]
        self.ways, self.halves, self.lands, self.relayed = {}, {}, {}, []
        self.tails = {step: [] for step in range(len(self.masks))}

    def at(self, mask):
        return self.result.at[self.index(flip(self.place, mask))]

    def start(self):
        self.own.start()
        if len(self.masks) > 1:
            self.begin_line()

    def begin_line(self):
        self.near = self.out.push(self.source, self.at(HERE), NEAR)
        self.third, self.lands[2] = self.out.push_within(self.source, self.at(HERE), ENDS)

    def relay(self, step):
        if step in self.relayed:
            return
        self.relayed.append(step)
        if step == 1:
            self.near.wait_recv()
            self.fourth, self.lands[3] = self.out.push_within(self.at(NEAR), self.at(NEAR), ENDS)
            return
        copy = self.third if step == 2 else self.fourth
        pl.when(self.out.inner)(copy.wait_recv)
        block = self.at(self.masks[step])
        self.out.push_within(block, block, NEAR, self.lands[step])

    def reached(self, step):
        self.relay(step)
        if step > 1:
            copy = self.third if step == 2 else self.fourth
            pl.when(jnp.logical_not(self.out.inner))(copy.wait_recv)

    def pass_on(self, step, block, place):
        if self.sibling:
            self.tails[step].append(self.out.push(block, place, self.sibling))

    def plane(self, step):
        mask = self.masks[step]
        if step:
            self.reached(step)
        block = self.at(mask) if step else self.source
        self.ways[step] = (
            self.out.push(block, self.at(mask), self.first),
            self.out.push(block, self.at(mask), self.second),
        )
        self.pass_on(step, block, self.at(mask))

    def turn(self, step):
        halves = []
        mask, cut = self.masks[step], self.cut
        self.ways[step][0].wait_recv()
        seen = self.at(both(mask, self.first))
        if cut:
            halves.append(self.out.push(seen.at[:cut], seen.at[:cut], self.second))
        self.pass_on(step, seen, seen)
        self.ways[step][1].wait_recv()
        seen = self.at(both(mask, self.second))
        if cut < self.rows:
            halves.append(self.out.push(seen.at[cut:], seen.at[cut:], self.first))
        self.pass_on(step, seen, seen)
        self.halves[step] = halves

    def close(self, step):
        for half in self.halves[step]:
            half.wait_recv()
        seen = self.at(both(self.masks[step], both(self.first, self.second)))
        self.pass_on(step, seen, seen)

    def hop(self, number):
        for step in range(len(self.masks)):
            (self.plane, self.turn, self.close)[number](step)

    def passed(self, step):
        for copy in self.tails[step]:
            copy.wait_recv()

    def arrived(self):
        for step in range(len(self.masks)):
            self.passed(step)
        self.own.wait()

    def finish(self):
        self.out.finish()


def total(parts, low, high, store):
    def body(step, carry):
        rows = pl.ds(pl.multiple_of(low + step * 16, 16), 16)
        value = parts[0][rows].astype(jnp.float32)
        for part in parts[1:]:
            value = value + part[rows].astype(jnp.float32)
        store[rows] = value.astype(store.dtype)
        return carry

    if high > low:
        lax.fori_loop(0, (high - low) // 16, body, 0)


def by_tiles(width, tile, parts=2):
    size = -(-width // (128 * parts)) * 128
    for low in range(0, width, size):
        tile(low, min(size, width - low))


def seat_hot(seats, capacity, kind):
    lines = lax.broadcasted_iota(jnp.int32, (2 * capacity, seats.shape[-1]), 0)
    return (lines == seats).astype(kind)


def expert_sums(kind, rows, weights, seats, extra, collective, name, products=()):
    experts, pairs = seats.shape[1], seats.shape[2]
    thick = seats.shape[4]
    tokens = seats.shape[4] // 2
    half_rows = rows[0].shape[0] // experts
    pair_rows = half_rows // pairs
    capacity = pair_rows // 2
    hidden = rows[0].shape[1]
    width = weights[0].shape[1]
    first, second = ACROSS, ALONG
    masks = [FOURTH, THIRD, NEAR, HERE]
    rounds = len(masks)
    cut = tokens // 2
    count_rows, count_extra = len(rows), len(extra)
    copies_out = rounds * (pairs + 4) + 5

    def body(*refs):
        refs = list(refs)
        left = refs[:count_rows]
        stored = refs[count_rows : 2 * count_rows]
        seat_ref = refs[2 * count_rows]
        more = refs[2 * count_rows + 1 : 2 * count_rows + 1 + count_extra]
        rest = refs[2 * count_rows + 1 + count_extra :]
        thin_wide, rest = rest[: 2 * len(products)], rest[2 * len(products) :]
        result, rest = rest[0], rest[1:]
        made, rest = rest[: len(products)], rest[len(products) :]
        wide, rest = rest[:count_rows], rest[count_rows:]
        staged, away, joined, own, side, arrive, ends, send, recv, local, weight_sem = rest[:11]
        if products:
            thin_stage, wide_stage, gross, product_sem, made_sem = rest[11:]
        weight_copies = [
            pltpu.make_async_copy(stored[item], wide[item], weight_sem.at[item])
            for item in range(count_rows)
        ]
        for copy in weight_copies:
            copy.start()
        place = place_here()
        x, e, y = place
        greet = [SIBLING, first, second, NEAR, FAR, ENDS]
        barrier = pltpu.get_barrier_semaphore()
        for mask in greet:
            pl.semaphore_signal(barrier, inc=1, device_id=flip(place, mask), device_id_type=MESH)
        pl.semaphore_wait(barrier, len(greet))
        out = Sender(place, send, recv)

        def block(mask):
            there = flip(place, mask)
            return there[0] * 2 + there[2]

        halves = []
        for mask in masks:
            halves.append((flip(place, both(mask, SIBLING))[1], True))
            halves.append((flip(place, mask)[1], False))
        loads = {}

        def load(number):
            if number < len(halves):
                begin = pl.multiple_of(halves[number][0] * half_rows, 16)
                for item in range(count_rows):
                    copy = pltpu.make_async_copy(
                        left[item].at[pl.ds(begin, half_rows)],
                        staged.at[number % 2, item],
                        local.at[number % 2, item],
                    )
                    copy.start()
                    loads[number, item] = copy

        def make(number, store):
            load(number + 1)
            for item in range(count_rows):
                loads[number, item].wait()
                if number == 0:
                    weight_copies[item].wait()
            values = [staged[number % 2, item] for item in range(count_rows)]
            if kind == "result":
                part = halves[number][0]
                factors = []
                for pair in range(pairs):
                    hot = seat_hot(seat_ref[0, part, pair], capacity, jnp.float32)
                    factors.append(jnp.sum(hot * more[0][part, pair], axis=1, keepdims=True))
                factor = jnp.concatenate(factors, axis=0)
                once = jnp.where((x == 0) & (y == 0), 1.0, 0.0).astype(jnp.float32)

            def tile(low, size):
                area = pl.ds(low, size)
                value = jnp.dot(values[0], wide[0][:, area], preferred_element_type=jnp.float32)
                if kind == "gradient":
                    value += jnp.dot(values[1], wide[1][:, area], preferred_element_type=jnp.float32)
                else:
                    value = (value + once * more[1][:, area]) * factor
                store(low, size, value.astype(jnp.bfloat16))

            by_tiles(width, tile)

        def to_sibling(step):
            slot = step % 2

            def store(low, size, value):
                away[slot, :, pl.ds(low, size)] = value

            if step >= 2:
                for copy in sent[step - 2]:
                    copy.wait_send()
            make(2 * step, store)
            sent[step] = [
                out.push(
                    away.at[slot].at[pair * pair_rows : (pair + 1) * pair_rows],
                    joined.at[step, pair].at[pair_rows : 2 * pair_rows],
                    SIBLING,
                )
                for pair in range(pairs)
            ]

        def to_here(step):
            def store(low, size, value):
                for pair in range(pairs):
                    joined[step, pair, :pair_rows, pl.ds(low, size)] = value[
                        pair * pair_rows : (pair + 1) * pair_rows
                    ]

            make(2 * step + 1, store)

        def combine(step):
            for copy in sent[step]:
                copy.wait_recv()
            part = halves[2 * step + 1][0]
            for pair in range(pairs):
                hot = jnp.concatenate(
                    [seat_hot(seat_ref[mate, part, pair], capacity, jnp.bfloat16) for mate in range(2)],
                    axis=0,
                )

                def tile(low, size):
                    value = inner_rows(hot, joined[step, pair, :, pl.ds(low, size)])
                    value = value.astype(jnp.bfloat16)
                    own[step * 4 + pair * 2, :, pl.ds(low, size)] = value[:tokens]
                    own[step * 4 + pair * 2 + 1, :, pl.ds(low, size)] = value[tokens:]

                by_tiles(width, tile)

        def outward(step):
            corner = own.at[step * 4 + block(both(first, second))]
            return [
                out.push(corner.at[:cut], side.at[step].at[:cut], first),
                out.push(corner.at[cut:], side.at[step].at[cut:], second),
            ]

        def inward(step, parts):
            by_first = own.at[step * 4 + block(first)]
            by_second = own.at[step * 4 + block(second)]
            for part in parts:
                part.wait_recv()
            total([by_second, side.at[step]], 0, cut, by_second)
            total([by_first, side.at[step]], cut, tokens, by_first)
            return (
                out.push(by_first, arrive.at[step * 2], first),
                out.push(by_second, arrive.at[step * 2 + 1], second),
            )

        def close(step, ways):
            kept = own.at[step * 4 + block(HERE)]
            for way in ways:
                way.wait_recv()
            parts = [kept, arrive.at[step * 2], arrive.at[step * 2 + 1]]
            if masks[step] in (FOURTH, THIRD):
                total(parts, 0, tokens, kept)
                shared[step], _ = out.push_within(kept, ends.at[1 + step], NEAR, inner=False)
                return
            if masks[step] == NEAR:
                total(parts, 0, tokens, kept)
                reach.append((out.push(kept, ends.at[3], NEAR), None))
                return
            for copy, _ in reach:
                copy.wait_recv()
            parts += [ends.at[0], ends.at[3]]
            total(parts, 0, tokens, result)

        def across(step):
            kept = own.at[step * 4 + block(HERE)]

            @pl.when(out.inner)
            def _():
                shared[step].wait_recv()
                total([kept, ends.at[1 + step]], 0, tokens, kept)

            copy, number = out.push_within(kept, ends.at[0], masks[step], lands=reach[0][1] if reach else None)
            if not reach:
                reach.append((copy, number))

        chunks = rows[0].shape[0] // thick

        def product_loads(item, number):
            slot = lax.rem(number, 2)
            begin = pl.multiple_of(number * thick, 16)
            return [
                pltpu.make_async_copy(
                    thin_wide[2 * item + part].at[pl.ds(begin, thick)], stage.at[slot], product_sem.at[slot, part]
                )
                for part, stage in enumerate((thin_stage, wide_stage))
            ]

        written = []

        def multiply(item, begin, end):
            if begin == 0:
                for copy in product_loads(item, 0):
                    copy.start()
                if written:
                    written[-1].wait()
                else:
                    gross[...] = jnp.zeros_like(gross)

            def step(number, carry):
                @pl.when(number + 1 < chunks)
                def _():
                    for copy in product_loads(item, number + 1):
                        copy.start()

                for copy in product_loads(item, number):
                    copy.wait()
                slot = lax.rem(number, 2)
                keep = jnp.where(number == 0, 0.0, 1.0).astype(jnp.float32)

                def tile(low, size):
                    area = pl.ds(low, size)
                    value = inner_rows(thin_stage[slot], wide_stage[slot, :, area])
                    gross[:, area] = gross[:, area] * keep + value

                by_tiles(width, tile, 3)
                return carry

            lax.fori_loop(begin, end, step, 0)
            if end == chunks:
                copy = pltpu.make_async_copy(gross, made[item], made_sem.at[0])
                copy.start()
                written.append(copy)

        todo = [(item, begin) for item in range(len(products)) for begin in range(0, chunks, 3)]

        def some(number):
            for item, begin in todo[:number]:
                multiply(item, begin, min(begin + 3, chunks))
            del todo[:number]

        sent, corners, ways, reach, shared = {}, {}, {}, [], {}
        load(0)
        for step in range(rounds + 2):
            if step < rounds:
                to_sibling(step)
                to_here(step)
                combine(step)
                corners[step] = outward(step)
            if 0 <= step - 1 < rounds:
                ways[step - 1] = inward(step - 1, corners[step - 1])
            if step - 3 in (0, 1):
                across(step - 3)
            if 0 <= step - 2 < rounds:
                close(step - 2, ways[step - 2])
            some((2, 2, 3, 2, 0, 0)[step])
        some(len(todo))
        if written:
            written[-1].wait()
        for step in range(rounds):
            if step >= rounds - 2:
                for copy in sent[step]:
                    copy.wait_send()
        exchanged = {id(copy) for step in range(rounds) for copy in sent[step]}
        out.started = [copy for copy in out.started if id(copy) not in exchanged]
        out.finish()

    vmem, anywhere = pl.BlockSpec(memory_space=pltpu.VMEM), pl.BlockSpec(memory_space=pl.ANY)
    for_products = []
    if products:
        for_products = [
            pltpu.VMEM((2, thick, hidden), jnp.bfloat16),
            pltpu.VMEM((2, thick, width), jnp.bfloat16),
            pltpu.VMEM((hidden, width), jnp.float32),
            pltpu.SemaphoreType.DMA((2, 2)),
            pltpu.SemaphoreType.DMA((1,)),
        ]
    return pl.pallas_call(
        body,
        out_shape=[jax.ShapeDtypeStruct((tokens, width), jnp.float32)]
        + [jax.ShapeDtypeStruct((hidden, width), jnp.float32)] * len(products),
        in_specs=[anywhere] * (2 * count_rows)
        + [vmem] * (1 + count_extra)
        + [anywhere] * (2 * len(products)),
        out_specs=[vmem] + [anywhere] * len(products),
        scratch_shapes=[pltpu.VMEM(weight.shape, jnp.bfloat16) for weight in weights]
        + [
            pltpu.VMEM((2, count_rows, half_rows, hidden), jnp.bfloat16),
            pltpu.VMEM((2, half_rows, width), jnp.bfloat16),
            pltpu.VMEM((rounds, pairs, 2 * pair_rows, width), jnp.bfloat16),
            pltpu.VMEM((rounds * 4, tokens, width), jnp.bfloat16),
            pltpu.VMEM((rounds, tokens, width), jnp.bfloat16),
            pltpu.VMEM((rounds * 2, tokens, width), jnp.bfloat16),
            pltpu.VMEM((4, tokens, width), jnp.bfloat16),
            pltpu.SemaphoreType.DMA((copies_out,)),
            pltpu.SemaphoreType.DMA((copies_out,)),
            pltpu.SemaphoreType.DMA((2, count_rows)),
            pltpu.SemaphoreType.DMA((count_rows,)),
        ]
        + for_products,
        compiler_params=pltpu.CompilerParams(
            collective_id=collective, has_side_effects=True, vmem_limit_bytes=62 * 1024 * 1024
        ),
        name=name,
    )(*rows, *weights, seats, *extra, *[array for pair in products for array in pair])


def expert_rows_kernel(own_block, cotangents, weights, biases, seats, shares, capacity, collective, name):
    experts, pairs = seats.shape[0], seats.shape[1]
    tokens, width = own_block.shape
    blocks = cotangents.shape[0]
    hidden = weights[0].shape[0]
    pair_rows = 2 * capacity
    half_rows = pairs * pair_rows
    row_count = experts * half_rows
    copies_out = copies("all")

    def body(*refs):
        (own_ref, cot_ref, *stored, gate_bias, up_bias, seat_ref, share_ref) = refs[:9]
        (rows_out, grads_out, act_out, dgate_out, dup_out, gate_sum, up_sum, down_sum, held) = refs[9:18]
        (stage, lines, thin, pre, back, gate, up, down) = refs[18:26]
        (send, recv, local, load_sem, line_sem, thin_sem, weight_sem) = refs[26:]
        weight_copies = [
            pltpu.make_async_copy(stored[item], goal, weight_sem.at[item])
            for item, goal in enumerate((gate, up, down))
        ]
        for copy in weight_copies[::-1]:
            copy.start()
        place = place_here()
        x, e, y = place
        greet = partners("all")
        barrier = pltpu.get_barrier_semaphore()
        for mask in greet:
            pl.semaphore_signal(barrier, inc=1, device_id=flip(place, mask), device_id_type=MESH)
        pl.semaphore_wait(barrier, len(greet))
        work = Gather("all", place, own_ref, held, send, recv, local)
        work.start()
        gate_sum[...] = jnp.zeros_like(gate_sum)
        up_sum[...] = jnp.zeros_like(up_sum)
        down_sum[...] = jnp.zeros_like(down_sum)
        halves = []
        for mask in work.masks:
            halves.append(flip(place, mask)[1])
            halves.append(flip(place, both(mask, SIBLING))[1])
        turnstile = {"load": 0, "line": 0}
        line_copies, thin_copies = [], []

        fetched = {}

        def fetch(scaled, number):
            bank = len(fetched) % 2
            begin = halves[number] * pairs * 2
            copies_in = [
                pltpu.make_async_copy(
                    (cot_ref if scaled else held).at[pl.ds(begin + 2 * pair, 2)],
                    stage.at[2 * bank + pair],
                    load_sem.at[2 * bank + pair],
                )
                for pair in range(pairs)
            ]
            for copy in copies_in:
                copy.start()
            fetched[scaled, number] = (bank, copies_in)

        def pick(scaled, number):
            part = halves[number]
            bank, copies_in = fetched[scaled, number]
            slot = turnstile["line"] % 2
            turnstile["line"] += 1
            if len(line_copies) >= 2:
                line_copies[-2].wait()
            for pair in range(pairs):
                copies_in[pair].wait()
                hot = seat_hot(seat_ref[part, pair], capacity, jnp.float32)
                if scaled:
                    factor = jnp.sum(hot * share_ref[part, pair], axis=1, keepdims=True)
                hot = hot.astype(jnp.bfloat16)
                blocks_here = stage[2 * bank + pair].reshape(2 * tokens, width)
                value = jnp.dot(hot, blocks_here, preferred_element_type=jnp.float32)
                if scaled:
                    value = value * factor
                value = value.astype(jnp.bfloat16)
                lines[slot, pair * pair_rows : (pair + 1) * pair_rows] = value
                if scaled:
                    down_sum[...] += jnp.sum(value.astype(jnp.float32), axis=0, keepdims=True)
            copy = pltpu.make_async_copy(
                lines.at[slot],
                (grads_out if scaled else rows_out).at[
                    pl.ds(pl.multiple_of(part * half_rows, 16), half_rows)
                ],
                line_sem.at[slot],
            )
            copy.start()
            line_copies.append(copy)
            return lines.at[slot]

        def backward(number):
            picked = pick(True, number)
            if number == 0:
                weight_copies[2].wait()
            back[number] = times_transposed(picked[...], down[...])

        def forward(number):
            part = halves[number]
            picked = pick(False, number)
            if number == 0:
                weight_copies[0].wait()
                weight_copies[1].wait()
            pre[0] = times_transposed(picked[...], gate[...])
            pre[1] = times_transposed(picked[...], up[...])
            slot = number % 2
            if number >= 2:
                for copy in thin_copies[-6:-3]:
                    copy.wait()

            def chunk(step, sums):
                area = pl.ds(pl.multiple_of(step * 16, 16), 16)
                gate_tanh = jnp.tanh((pre[0, area] + gate_bias[...]) * (1.0 / clip_level))
                up_tanh = jnp.tanh((pre[1, area] + up_bias[...]) * (1.0 / clip_level))
                gate_soft = clip_level * gate_tanh
                up_more = clip_level * up_tanh + 1.0
                bend = jax.nn.sigmoid(glu_alpha * gate_soft)
                glow = gate_soft * bend
                grad = back[number, area]
                dgate = grad * up_more * (bend + glu_alpha * glow * (1.0 - bend))
                dgate = (dgate * (1.0 - gate_tanh * gate_tanh)).astype(jnp.bfloat16)
                dup = (grad * glow * (1.0 - up_tanh * up_tanh)).astype(jnp.bfloat16)
                thin[slot, 0, area] = (glow * up_more).astype(jnp.bfloat16)
                thin[slot, 1, area] = dgate
                thin[slot, 2, area] = dup
                return sums[0] + dgate.astype(jnp.float32), sums[1] + dup.astype(jnp.float32)

            zero = jnp.zeros((16, hidden), jnp.float32)
            sums = lax.fori_loop(0, half_rows // 16, chunk, (zero, zero))
            gate_sum[...] += jnp.sum(sums[0], axis=0, keepdims=True)
            up_sum[...] += jnp.sum(sums[1], axis=0, keepdims=True)
            for item, goal in enumerate((act_out, dgate_out, dup_out)):
                copy = pltpu.make_async_copy(
                    thin.at[slot, item],
                    goal.at[pl.ds(pl.multiple_of(part * half_rows, 16), half_rows)],
                    thin_sem.at[slot, item],
                )
                copy.start()
                thin_copies.append(copy)

        order = ["p0B0B1b0B2b1B3b2B4b3B5b4t0p1r2", "B6b5B7b6b7c0o0F0r3p2f0w0F1f1t1c1"]
        order += ["p3t2w1F2F3f2f3c2F4w2F5f4f5t3c3F6w3F7f6f7"]
        acts = {
            "p": work.plane,
            "t": work.turn,
            "c": work.close,
            "w": work.passed,
            "r": work.relay,
            "o": lambda number: work.own.wait(),
            "B": lambda number: fetch(True, number),
            "F": lambda number: fetch(False, number),
            "b": backward,
            "f": forward,
        }
        order = "".join(order)
        for low in range(0, len(order), 2):
            acts[order[low]](int(order[low + 1]))
        for copy in line_copies[-2:] + thin_copies[-6:]:
            copy.wait()
        work.finish()

    vmem, anywhere = pl.BlockSpec(memory_space=pltpu.VMEM), pl.BlockSpec(memory_space=pl.ANY)
    bf16, f32 = jnp.bfloat16, jnp.float32
    return pl.pallas_call(
        body,
        out_shape=[
            jax.ShapeDtypeStruct((row_count, width), bf16),
            jax.ShapeDtypeStruct((row_count, width), bf16),
            jax.ShapeDtypeStruct((row_count, hidden), bf16),
            jax.ShapeDtypeStruct((row_count, hidden), bf16),
            jax.ShapeDtypeStruct((row_count, hidden), bf16),
            jax.ShapeDtypeStruct((1, hidden), f32),
            jax.ShapeDtypeStruct((1, hidden), f32),
            jax.ShapeDtypeStruct((1, width), f32),
            jax.ShapeDtypeStruct((blocks, tokens, width), bf16),
        ],
        in_specs=[anywhere] * 5 + [vmem] * 4,
        out_specs=[anywhere] * 5 + [vmem] * 3 + [anywhere],
        scratch_shapes=[
            pltpu.VMEM((4, 2, tokens, width), bf16),
            pltpu.VMEM((2, half_rows, width), bf16),
            pltpu.VMEM((2, 3, half_rows, hidden), bf16),
            pltpu.VMEM((2, half_rows, hidden), f32),
            pltpu.VMEM((experts, half_rows, hidden), f32),
        ]
        + [pltpu.VMEM(weight.shape, bf16) for weight in weights]
        + [
            pltpu.SemaphoreType.DMA((copies_out,)),
            pltpu.SemaphoreType.DMA((copies_out,)),
            pltpu.SemaphoreType.DMA((1,)),
            pltpu.SemaphoreType.DMA((4,)),
            pltpu.SemaphoreType.DMA((2,)),
            pltpu.SemaphoreType.DMA((2, 3)),
            pltpu.SemaphoreType.DMA((3,)),
        ],
        compiler_params=pltpu.CompilerParams(
            collective_id=collective, has_side_effects=True, vmem_limit_bytes=60 * 1024 * 1024
        ),
        name=name,
    )(own_block, cotangents, *weights, *biases, seats, shares)


class Scatter:
    def __init__(self, group, place, source, result, side, arrive, send, recv, spare, mate=None):
        self.index, _, self.sibling, self.first, self.second, _, share = GROUPS[group]
        self.place, self.source, self.result = place, source, result
        self.side, self.arrive, self.mate = side, arrive, mate
        self.rows = result.shape[0]
        self.cut = int(self.rows * (1.0 - share)) // 16 * 16
        self.corner = both(self.first, self.second)
        self.out = Sender(place, send, recv)
        self.crossing = {}

    def at(self, mask):
        return self.source.at[self.index(flip(self.place, mask))]

    def cross(self):
        for spot, mask in enumerate((self.corner, self.first, self.second, HERE)):
            self.crossing[mask] = (
                self.out.push(self.at(both(mask, self.sibling)), self.mate.at[spot], self.sibling),
                self.mate.at[spot],
            )

    def ready(self, mask):
        if not self.sibling:
            return [self.at(mask)]
        copy, block = self.crossing[mask]
        copy.wait_recv()
        return [self.at(mask), block]

    def outward(self):
        corner, cut = self.at(self.corner), self.cut
        parts = self.ready(self.corner)
        if len(parts) > 1:
            total(parts, 0, self.rows, corner)
        self.halves = []
        if cut:
            self.halves.append(self.out.push(corner.at[:cut], self.side.at[:cut], self.first))
        if cut < self.rows:
            self.halves.append(self.out.push(corner.at[cut:], self.side.at[cut:], self.second))

    def inward(self):
        by_first, by_second = self.ready(self.first), self.ready(self.second)
        for half in self.halves:
            half.wait_recv()
        cut, rows = self.cut, self.rows
        total(by_second + [self.side], 0, cut, by_second[0])
        total(by_first + [self.side], cut, rows, by_first[0])
        if self.sibling:
            total(by_second, cut, rows, by_second[0])
            total(by_first, 0, cut, by_first[0])
        self.ways = (
            self.out.push(by_first[0], self.arrive.at[0], self.first),
            self.out.push(by_second[0], self.arrive.at[1], self.second),
        )

    def close(self):
        parts = self.ready(HERE)
        for way in self.ways:
            way.wait_recv()
        total(parts + [self.arrive.at[0], self.arrive.at[1]], 0, self.rows, self.result)

    def finish(self):
        self.out.finish()


def lanes(shape):
    return lax.broadcasted_iota(jnp.int32, shape, len(shape) - 1)


def swapped(value):
    width = value.shape[-1]
    upper = pltpu.roll(value, width - HD // 2, len(value.shape) - 1)
    lower = pltpu.roll(value, HD // 2, len(value.shape) - 1)
    return jnp.where(lanes(value.shape) % HD < HD // 2, upper, lower)


def halves_of(value, member):
    low = lanes(value.shape) < HD
    zero = jnp.zeros_like(value)
    if member == 0:
        kept = jnp.where(low, value, zero)
        return kept, pltpu.roll(kept, HD, 1)
    kept = jnp.where(low, zero, value)
    return pltpu.roll(kept, HD, 1), kept


def seen(marks, held, first_key=0):
    rows = marks.shape[1]
    lines = []
    for query in range(2):
        parts = []
        for key in range(2):
            if key > query:
                parts.append(jnp.zeros((rows, rows), jnp.bool_))
                continue
            same = marks[held + query] == marks[held + key].T
            if key == query:
                down = lax.broadcasted_iota(jnp.int32, (rows, rows), 0)
                same = same & (down >= lanes((rows, rows)))
            parts.append(same)
        lines.append(parts)
    return lines


def mask_of(marks, held):
    lines = seen(marks, held)
    return jnp.concatenate(
        [
            jnp.concatenate([jnp.where(part, 1.0, 0.0) for part in parts], axis=1)
            for parts in lines
        ],
        axis=0,
    )


def pick_lane(value, number):
    return jnp.sum(jnp.where(lanes(value.shape) == number, value, 0.0), axis=1, keepdims=True)


def attention_forward(
    normed, query_rows, key_rows, value_rows, output_rows, marks, table, extra, biases, tables, sinks, collective, name
):
    tokens, width = normed.shape
    block = 4 * tokens
    seq_len = 2 * tokens
    columns = 8 * query_rows.shape[0]
    pairs = columns // 128
    scale = 1.0 / math.sqrt(HD)
    bf16, f32 = jnp.bfloat16, jnp.float32
    gathers = [
        ("tokens", normed),
        ("heads", query_rows),
        ("heads", key_rows),
        ("heads", value_rows),
        ("tokens", marks),
        ("heads", output_rows),
        ("all", table),
        ("all", extra),
    ]
    count = len(gathers)

    def body(*refs):
        refs = list(refs)

        def take(number):
            got = refs[:number]
            del refs[:number]
            return got

        sources = take(count)
        query_bias, key_bias, value_bias, cosine, sine, sink_ref = take(6)
        (result, query_out, key_out, value_out, mixed_out, lse_out, mask) = take(7)
        kept_out = take(5)
        far_out = take(2)
        held = take(count - 2)
        (key_half, value_half, partial, side, arrive) = take(5)
        sems = [take(3) for _ in range(count)]
        sum_sems = take(3)
        (keep_sem,) = take(1)
        place = place_here()
        greet = []
        for group, _ in gathers:
            greet += [step for step in partners(group) if step not in greet]
        barrier = pltpu.get_barrier_semaphore()
        for step in greet:
            pl.semaphore_signal(barrier, inc=1, device_id=flip(place, step), device_id_type=MESH)
        pl.semaphore_wait(barrier, len(greet))
        works = [
            Gather(
                group, place, sources[item], (held + far_out)[item], *sems[item], share=0.25 if item == 7 else None
            )
            for item, (group, _) in enumerate(gathers)
        ]
        all_tokens, all_query, all_key, all_value, all_marks, all_output = held
        early, output_work, table_work, extra_work = works[:5], works[5], works[6], works[7]
        early = [early[4]] + early[:4]
        table_work.start()
        for work in early:
            work.start()
            work.plane(0)
        extra_work.start()
        extra_work.plane(0)
        early[0].turn(0)
        table_work.relay(1)
        table_work.relay(2)
        for work in early[1:]:
            work.turn(0)
        extra_work.turn(0)
        extra_work.plane(1)
        extra_work.relay(2)
        output_work.start()
        output_work.plane(0)
        for work in early:
            work.close(0)
        for work in early:
            work.passed(0)
            work.own.wait()
        keeps = []

        def keep(item, goal):
            copy = pltpu.make_async_copy(held[item], kept_out[goal], keep_sem.at[goal])
            copy.start()
            keeps.append(copy)

        for item in range(4):
            keep(item, item)
        x_all = all_tokens[...].reshape(block, width)

        def turned(value, low):
            return value * cosine[...] + swapped(value) * sine[...]

        def project(number, carry):
            weight = all_query[pl.ds(pl.multiple_of(2 * number, 2), 2)].reshape(256, width)
            value = times_transposed(x_all, weight)
            for part in range(2):
                area = pl.ds(pl.multiple_of((2 * number + part) * 128, 128), 128)
                head = value[:, part * 128 : (part + 1) * 128] + query_bias[:, area]
                query_out[:, area] = turned(head, 0).astype(bf16)
            return carry

        lax.fori_loop(0, pairs // 2, project, 0)
        key = times_transposed(x_all, all_key[...].reshape(128, width)) + key_bias[...]
        key = turned(key, 0).astype(bf16)
        key_out[...] = key
        value = times_transposed(x_all, all_value[...].reshape(128, width)) + value_bias[...]
        value = value.astype(bf16)
        value_out[...] = value
        for member in range(2):
            for part, half in enumerate(halves_of(key, member)):
                key_half[2 * member + part] = half
            for part, half in enumerate(halves_of(value, member)):
                value_half[2 * member + part] = half
        for half in range(2):
            mask[half] = mask_of(all_marks, 2 * half)
        table_work.relay(3)
        extra_work.close(0)
        extra_work.relay(3)
        extra_work.plane(2)
        lse_out[...] = jnp.zeros_like(lse_out)

        def attend(number, carry):
            pair = lax.div(number, 2)
            half = lax.rem(number, 2)
            member = lax.div(pair, pairs // 2)
            rows = pl.ds(pl.multiple_of(half * seq_len, seq_len), seq_len)
            area = pl.ds(pl.multiple_of(pair * 128, 128), 128)
            query = query_out[rows, area]
            mixed = jnp.zeros((seq_len, 128), f32)
            for part in range(2):
                raw = times_transposed(query, key_half[2 * member + part, rows]) * scale
                raw = jnp.where(mask[half] > 0.0, raw, masked_score)
                sink = sink_ref[0, 2 * pair + part]
                peak = jnp.maximum(jnp.max(raw, axis=1, keepdims=True), sink)
                mass = jnp.sum(jnp.exp(raw - peak), axis=1, keepdims=True) + jnp.exp(sink - peak)
                lse = peak + jnp.log(mass)
                probs = jnp.exp(raw - lse).astype(bf16)
                mixed = mixed + jnp.dot(
                    probs, value_half[2 * member + part, rows], preferred_element_type=f32
                )
                spot = lanes((seq_len, 128)) == 2 * pair + part
                lse_out[rows] = jnp.where(spot, lse, lse_out[rows])
            mixed_out[rows, area] = mixed.astype(bf16)
            return carry

        lax.fori_loop(0, pairs, attend, 0)
        extra_work.turn(1)
        output_work.turn(0)
        lax.fori_loop(pairs, 2 * pairs, attend, 0)
        table_work.hop(0)
        extra_work.plane(3)
        output_work.close(0)
        output_work.passed(0)
        output_work.own.wait()
        keep(5, 4)

        def tile(low, size):
            weight = all_output[:, :, pl.ds(low, size)].reshape(columns, size)
            value = jnp.dot(mixed_out[...], weight, preferred_element_type=f32).astype(bf16)
            partial[:, :, pl.ds(low, size)] = value.reshape(4, tokens, size)

        by_tiles(width, tile)
        run = Scatter("tokens", place, partial, result, side, arrive, *sum_sems)
        run.outward()
        extra_work.close(1)
        extra_work.turn(2)
        run.inward()
        extra_work.close(2)
        table_work.hop(1)
        extra_work.turn(3)
        run.close()
        table_work.hop(2)
        extra_work.close(3)
        for work in (table_work, extra_work):
            work.arrived()
        run.finish()
        for copy in keeps:
            copy.wait()
        for work in works:
            work.finish()

    vmem, anywhere = pl.BlockSpec(memory_space=pltpu.VMEM), pl.BlockSpec(memory_space=pl.ANY)
    smem = pl.BlockSpec(memory_space=pltpu.SMEM)
    kept = [(4,) + normed.shape] + [(8,) + rows.shape for rows in (query_rows, key_rows, value_rows, output_rows)]
    blocks = [GROUPS[group][1] for group, _ in gathers]
    return pl.pallas_call(
        body,
        out_shape=[
            jax.ShapeDtypeStruct((tokens, width), f32),
            jax.ShapeDtypeStruct((block, columns), bf16),
            jax.ShapeDtypeStruct((block, 128), bf16),
            jax.ShapeDtypeStruct((block, 128), bf16),
            jax.ShapeDtypeStruct((block, columns), bf16),
            jax.ShapeDtypeStruct((block, 128), f32),
            jax.ShapeDtypeStruct((2, seq_len, seq_len), f32),
        ]
        + [jax.ShapeDtypeStruct(shape, bf16) for shape in kept]
        + [
            jax.ShapeDtypeStruct((blocks[item],) + array.shape, array.dtype)
            for item, (_, array) in list(enumerate(gathers))[-2:]
        ],
        in_specs=[anywhere] * count + [vmem] * 5 + [smem],
        out_specs=[vmem] * 7 + [anywhere] * 7,
        scratch_shapes=[
            pltpu.VMEM((blocks[item],) + array.shape, array.dtype)
            for item, (_, array) in enumerate(gathers[:-2])
        ]
        + [
            pltpu.VMEM((4, block, 128), bf16),
            pltpu.VMEM((4, block, 128), bf16),
            pltpu.VMEM((4, tokens, width), bf16),
            pltpu.VMEM((tokens, width), bf16),
            pltpu.VMEM((2, tokens, width), bf16),
        ]
        + [
            pltpu.SemaphoreType.DMA((size,))
            for group, _ in gathers
            for size in (copies(group), copies(group), 1)
        ]
        + [pltpu.SemaphoreType.DMA((copies("tokens"),))] * 2
        + [pltpu.SemaphoreType.DMA((1,)), pltpu.SemaphoreType.DMA((5,))],
        compiler_params=pltpu.CompilerParams(
            collective_id=collective, has_side_effects=True, vmem_limit_bytes=60 * 1024 * 1024
        ),
        name=name,
    )(*[array for _, array in gathers], *biases, *tables, sinks)


def attention_backward(
    outer, query, key, value, mixed, log_total, mask, tokens_kept, weights, tables, sinks, gain, small, collective, name
):
    tokens, width = outer.shape
    block = 4 * tokens
    seq_len = 2 * tokens
    columns = query.shape[1]
    pairs = columns // 128
    scale = 1.0 / math.sqrt(HD)
    bf16, f32 = jnp.bfloat16, jnp.float32
    owned = [rows.shape[1] for rows in weights]
    groups = ["heads"] * 4 + ["tokens"]

    def body(*refs):
        refs = list(refs)

        def take(number):
            got = refs[:number]
            del refs[:number]
            return got

        (outer_ref,) = take(1)
        query_ref, key_ref, value_ref, mixed_ref, lse_ref, mask_ref = take(6)
        stored = take(5)
        cosine, sine, sink_ref, gain_ref, small_ref = take(5)
        results = take(5)
        (small_out,) = take(1)
        held = take(5)
        grads, key_half, value_half = take(3)
        mixed_grad, query_grad, key_grad, value_grad = take(4)
        key_sum, value_sum, sink_sum, small_own, small_all = take(5)
        output_part, key_part, value_part = take(3)
        mates, sides, arrives = take(4), take(5), take(5)
        load_sem, gather_sems, small_sems = take(1)[0], take(3), take(3)
        sum_sems = [take(3) for _ in groups]
        place = place_here()
        greet = []
        for group in ("tokens", "heads", "all"):
            greet += [step for step in partners(group) if step not in greet]
        barrier = pltpu.get_barrier_semaphore()
        for step in greet:
            pl.semaphore_signal(barrier, inc=1, device_id=flip(place, step), device_id_type=MESH)
        pl.semaphore_wait(barrier, len(greet))
        work = Gather("tokens", place, outer_ref, grads, *gather_sems)
        work.start()
        work.plane(0)
        loads = []
        for item in (4, 1, 2, 3, 0):
            copy = pltpu.make_async_copy(stored[item], held[item], load_sem.at[item])
            copy.start()
            loads.append(copy)
        all_tokens, all_query, all_key, all_value, all_output = held
        for member in range(2):
            for part, half in enumerate(halves_of(key_ref[...], member)):
                key_half[2 * member + part] = half
            for part, half in enumerate(halves_of(value_ref[...], member)):
                value_half[2 * member + part] = half
        key_sum[...] = jnp.zeros_like(key_sum)
        value_sum[...] = jnp.zeros_like(value_sum)
        sink_sum[...] = jnp.zeros_like(sink_sum)
        small_own[...] = small_ref[...]
        work.turn(0)
        work.close(0)
        work.own.wait()
        work.finish()

        parts = [all_output, key_part, value_part, output_part, grads]
        sums = [
            Scatter(
                group,
                place,
                parts[item],
                results[item],
                sides[item],
                arrives[item],
                *sum_sems[item],
                mate=mates[item] if group == "heads" else None,
            )
            for item, group in enumerate(groups)
        ]
        of_query, of_key, of_value, of_output, of_tokens = sums

        def output_gradient(number, carry):
            area = pl.ds(pl.multiple_of(number * 128, 128), 128)
            rows = inner_rows(mixed_ref[:, area], grads[...].reshape(block, width))
            output_part[number] = rows.astype(bf16)
            return carry

        lax.fori_loop(0, pairs, output_gradient, 0)
        of_output.cross()
        loads[0].wait()

        def project(number, carry):
            weight = all_output[pl.ds(pl.multiple_of(2 * number, 2), 2)].reshape(256, width)
            area = pl.ds(pl.multiple_of(number * 256, 256), 256)
            mixed_grad[:, area] = times_transposed(
                grads[...].reshape(block, width), weight
            ).astype(bf16)
            return carry

        lax.fori_loop(0, pairs // 2, project, 0)
        of_output.outward()

        def back(value):
            return value * cosine[:seq_len] - swapped(value) * sine[:seq_len]

        def attend(number, carry):
            pair = lax.div(number, 2)
            half = lax.rem(number, 2)
            member = lax.div(pair, pairs // 2)
            rows = pl.ds(pl.multiple_of(half * seq_len, seq_len), seq_len)
            area = pl.ds(pl.multiple_of(pair * 128, 128), 128)
            queries = query_ref[rows, area]
            upstream = mixed_grad[rows, area]
            low = lanes((seq_len, 128)) < HD
            made = jnp.zeros((seq_len, 128), f32)
            for part in range(2):
                head = 2 * pair + part
                keys = key_half[2 * member + part, rows]
                lse = pick_lane(lse_ref[rows], head)
                raw = times_transposed(queries, keys) * scale
                raw = jnp.where(mask_ref[half] > 0.0, raw, masked_score)
                probs = jnp.exp(raw - lse)
                grad = times_transposed(upstream, value_half[2 * member + part, rows])
                delta = jnp.sum(probs * grad, axis=1, keepdims=True)
                inner = (probs * (grad - delta)).astype(bf16)
                made = made + jnp.dot(inner, keys, preferred_element_type=f32)
                mine = low if part == 0 else jnp.logical_not(low)
                value_sum[member, rows] += jnp.where(mine, inner_rows(probs.astype(bf16), upstream), 0.0)
                key_sum[member, rows] += jnp.where(mine, inner_rows(inner, queries), 0.0)
                lost = jnp.sum(jnp.exp(sink_ref[0, head] - lse) * delta, axis=0, keepdims=True)
                sink_sum[...] -= jnp.where(lanes((1, 128)) == head, lost, 0.0)
            query_grad[rows, area] = back(made * scale).astype(bf16)
            return carry

        lax.fori_loop(0, pairs, attend, 0)
        of_output.inward()
        lax.fori_loop(pairs, 2 * pairs, attend, 0)
        low = lanes((seq_len, 128)) < HD
        for half in range(2):
            rows = pl.ds(half * seq_len, seq_len)

            def joined(sums):
                first = sums[0, rows] + pltpu.roll(sums[0, rows], HD, 1)
                second = sums[1, rows] + pltpu.roll(sums[1, rows], HD, 1)
                return jnp.where(low, first, second)

            key_grad[rows] = back(joined(key_sum) * scale).astype(bf16)
            value_grad[rows] = joined(value_sum).astype(bf16)
        for copy in loads[1:]:
            copy.wait()

        def tile(low_column, size):
            area = pl.ds(low_column, size)

            def rows_of(weight):
                return weight[:, :, area].reshape(-1, size)

            total_grad = jnp.dot(query_grad[...], rows_of(all_query), preferred_element_type=f32)
            total_grad += jnp.dot(key_grad[...], rows_of(all_key), preferred_element_type=f32)
            total_grad += jnp.dot(value_grad[...], rows_of(all_value), preferred_element_type=f32)
            gained = total_grad * all_tokens[:, :, area].reshape(block, size).astype(f32)
            small_own[0:1, area] = jnp.sum(gained, axis=0, keepdims=True) / gain_ref[:, area]
            grads[:, :, area] = total_grad.astype(bf16).reshape(4, tokens, size)

        by_tiles(width, tile)
        low_column = 0
        for array in (query_grad, key_grad, value_grad):
            size = array.shape[1]
            small_own[3:4, low_column : low_column + size] = jnp.sum(
                array[...].astype(f32), axis=0, keepdims=True
            )
            low_column += size
        small_own[3:4, low_column : low_column + 128] = sink_sum[...]
        spread = Gather("all", place, small_own, small_all, *small_sems)
        spread.start()
        of_tokens.outward()

        def query_gradient(number, carry):
            area = pl.ds(pl.multiple_of(number * 128, 128), 128)
            rows = inner_rows(query_grad[:, area], all_tokens[...].reshape(block, width))
            all_output[number] = rows.astype(bf16)
            return carry

        lax.fori_loop(0, pairs, query_gradient, 0)
        of_query.cross()
        for goal, grad in ((key_part, key_grad), (value_part, value_grad)):
            rows = inner_rows(grad[...], all_tokens[...].reshape(block, width))
            goal[...] = rows.astype(bf16).reshape(goal.shape)
        of_key.cross()
        of_value.cross()
        spread.relay(1)
        spread.relay(2)
        of_query.outward()
        of_key.outward()
        of_value.outward()
        spread.relay(3)
        of_tokens.inward()
        spread.hop(0)
        of_query.inward()
        of_key.inward()
        of_value.inward()
        spread.hop(1)
        of_tokens.close()
        spread.hop(2)
        of_output.close()
        of_query.close()
        of_key.close()
        of_value.close()
        spread.arrived()
        spread.finish()
        blocks = small_all.shape[0]
        whole = small_all[0]
        for number in range(1, blocks):
            whole = whole + small_all[number]
        small_out[0:4] = whole[0:4]
        for near in range(2):
            for side in range(2):
                chosen = [
                    number for number in range(blocks) if (number // 8 % 2, number // 2 % 2) == (near, side)
                ]
                part = small_all[chosen[0], 3:4]
                for number in chosen[1:]:
                    part = part + small_all[number, 3:4]
                small_out[4 + 2 * near + side : 5 + 2 * near + side] = part
        for part in sums:
            part.finish()

    vmem, anywhere = pl.BlockSpec(memory_space=pltpu.VMEM), pl.BlockSpec(memory_space=pl.ANY)
    smem = pl.BlockSpec(memory_space=pltpu.SMEM)
    rows_of = owned + [tokens]
    kept = [tokens_kept] + list(weights)
    return pl.pallas_call(
        body,
        out_shape=[jax.ShapeDtypeStruct((rows, width), f32) for rows in rows_of]
        + [jax.ShapeDtypeStruct(small.shape, f32)],
        in_specs=[anywhere] + [vmem] * 6 + [anywhere] * 5 + [vmem] * 2 + [smem] + [vmem] * 2,
        out_specs=[vmem] * 6,
        scratch_shapes=[pltpu.VMEM(array.shape, bf16) for array in kept]
        + [
            pltpu.VMEM((4, tokens, width), bf16),
            pltpu.VMEM((4, block, 128), bf16),
            pltpu.VMEM((4, block, 128), bf16),
            pltpu.VMEM((block, columns), bf16),
            pltpu.VMEM((block, columns), bf16),
            pltpu.VMEM((block, 128), bf16),
            pltpu.VMEM((block, 128), bf16),
            pltpu.VMEM((2, block, 128), f32),
            pltpu.VMEM((2, block, 128), f32),
            pltpu.VMEM((1, 128), f32),
            pltpu.VMEM(small.shape, f32),
            pltpu.VMEM((GROUPS["all"][1],) + small.shape, f32),
            pltpu.VMEM(weights[3].shape, bf16),
            pltpu.VMEM(weights[1].shape, bf16),
            pltpu.VMEM(weights[2].shape, bf16),
        ]
        + [pltpu.VMEM((4, rows, width), bf16) for rows in owned]
        + [pltpu.VMEM((rows, width), bf16) for rows in rows_of]
        + [pltpu.VMEM((2, rows, width), bf16) for rows in rows_of]
        + [pltpu.SemaphoreType.DMA((5,))]
        + [
            pltpu.SemaphoreType.DMA((size,))
            for group in ["tokens", "all"] + groups
            for size in (copies(group), copies(group), 1)
        ],
        compiler_params=pltpu.CompilerParams(
            collective_id=collective, has_side_effects=True, vmem_limit_bytes=62 * 1024 * 1024
        ),
        name=name,
    )(outer, query, key, value, mixed, log_total, mask, *kept, *tables, sinks, gain, small)


def close_by(
    tokens,
    segments,
    routes,
    gate_share,
    attn_gain,
    query_weight,
    query_bias,
    key_weight,
    key_bias,
    value_weight,
    value_bias,
    output_weight,
    output_bias,
    sink_logits,
    moe_gain,
    gate_weight,
    gate_bias,
    up_weight,
    up_bias,
    down_weight,
    down_bias,
    cotangent,
):
    count_rows = tokens.shape[1]
    width = tokens.shape[2]
    head_count = sink_logits.shape[0]
    kv_count = key_bias.shape[0] // HD
    group = head_count // kv_count
    experts = lax.axis_size("exp")
    devices = 4 * experts
    topk = routes.shape[2]
    capacity = count_rows * topk * 9 // (8 * experts)
    x, e, y = place_here()
    near_bit = lax.rem(lax.div(e, 2), 2)
    seq_len = 2 * count_rows

    chosen = routes[0].reshape(-1)
    expert_hot = (chosen[:, None] == jnp.arange(experts, dtype=jnp.int32)[None, :]).astype(
        jnp.int32
    )
    earlier = (jnp.cumsum(expert_hot, axis=0) - expert_hot).reshape(count_rows, topk, experts)
    named = expert_hot.reshape(count_rows, topk, experts)
    slot_table = jnp.sum((earlier + 1) * named, axis=1) - 1
    share_table = jnp.sum(named.astype(jnp.float32) * gate_share[0][:, :, None], axis=1)
    table = jnp.concatenate([slot_table.astype(jnp.float32).T, share_table.T], axis=0)

    resid = tokens[0].astype(jnp.float32)
    attn_norm, attn_norm_pull = jax.vjp(rms_apply, resid, attn_gain)
    normed = attn_norm.astype(jnp.bfloat16)
    block_tokens = 4 * count_rows
    held_kv = 2
    held_heads = held_kv * group

    def own_part(vector):
        size = vector.shape[0] // 8
        first = (4 * x + near_bit) * size
        parts = [lax.dynamic_slice(vector, (first + 2 * far * size,), (size,)) for far in range(2)]
        return jnp.concatenate(parts)[None]

    position = jnp.arange(seq_len, dtype=jnp.int32)
    cosine, sine = rope_tables(position, HD)
    cosine = jnp.tile(cosine, (2, 4))
    sine = jnp.tile(jnp.concatenate([-sine, sine], axis=1), (2, 2))
    own_ids = lax.dynamic_slice_in_dim(segments[0], x * count_rows, count_rows, 0)
    marks = jnp.broadcast_to(own_ids.astype(jnp.float32)[:, None], (count_rows, count_rows))
    sinks = own_part(sink_logits)
    (
        attn_out,
        query_rot,
        key_rot,
        value_low,
        mixed,
        log_total,
        mask,
        group_tokens,
        group_query,
        group_key,
        group_value,
        group_output,
        tables,
        all_cotangents,
    ) = attention_forward(
        normed,
        query_weight.T,
        key_weight.T,
        value_weight.T,
        output_weight,
        marks,
        table,
        cotangent[0],
        (own_part(query_bias), own_part(key_bias), own_part(value_bias)),
        (cosine, sine),
        sinks,
        0,
        "attention_forward",
    )
    hidden = resid + (attn_out + output_bias)
    moe_norm, moe_norm_pull = jax.vjp(rms_apply, hidden, moe_gain)
    normed_moe = moe_norm.astype(jnp.bfloat16)

    def by_pairs(part):
        part = jnp.moveaxis(part.reshape(experts, 2, 2, experts, count_rows), 3, 0)
        return part.reshape(experts, experts, 2, 1, 2 * count_rows)

    slots = tables[:, :experts].astype(jnp.int32)
    second_block = jnp.arange(devices, dtype=jnp.int32)[:, None, None] % 2
    seats = by_pairs(jnp.where(slots >= 0, slots + capacity * second_block, -1))
    sibling = e + 1 - 2 * lax.rem(e, 2)
    seats = jnp.stack(
        [
            lax.dynamic_index_in_dim(seats, e, 0, keepdims=False),
            lax.dynamic_index_in_dim(seats, sibling, 0, keepdims=False),
        ]
    )
    gate_rows, up_rows = gate_weight[0].T, up_weight[0].T
    shares = lax.dynamic_index_in_dim(by_pairs(tables[:, experts:]), e, 0, keepdims=False)
    (
        expert_rows,
        grad_rows,
        activation,
        gate_grad,
        up_grad,
        gate_bias_grad,
        up_bias_grad,
        down_bias_grad,
        _,
    ) = expert_rows_kernel(
        normed_moe,
        all_cotangents,
        (gate_rows, up_rows, down_weight[0]),
        (gate_bias, up_bias),
        seats[0],
        shares,
        capacity,
        2,
        "route_rows",
    )
    (normed_moe_grad,) = expert_sums(
        "gradient", (gate_grad, up_grad), (gate_rows, up_rows), seats, (), 3, "sum_rows"
    )
    moe_out, gate_weight_grad, up_weight_grad, down_weight_grad = expert_sums(
        "result",
        (activation,),
        (down_weight[0],),
        seats,
        (shares, down_bias),
        4,
        "sum_results",
        ((gate_grad, expert_rows), (up_grad, expert_rows), (activation, grad_rows)),
    )
    output = (hidden + moe_out).astype(jnp.bfloat16)

    upstream = cotangent[0].astype(jnp.float32)
    hidden_norm_grad, moe_gain_grad = moe_norm_pull(normed_moe_grad)
    hidden_grad = upstream + hidden_norm_grad
    attn_out_grad = hidden_grad.astype(jnp.bfloat16)
    output_bias_grad = jnp.sum(attn_out_grad.astype(jnp.float32), axis=0)
    small = jnp.concatenate(
        [
            jnp.zeros((1, width), jnp.float32),
            moe_gain_grad[None],
            output_bias_grad[None],
            jnp.zeros((5, width), jnp.float32),
        ],
        axis=0,
    )
    query_owned, key_owned, value_owned, output_owned, normed_grad, small_sums = attention_backward(
        attn_out_grad,
        query_rot,
        key_rot,
        value_low,
        mixed,
        log_total,
        mask,
        group_tokens,
        (group_query, group_key, group_value, group_output),
        (cosine, sine),
        sinks,
        attn_gain[None],
        small,
        5,
        "attention_backward",
    )
    lengths = (held_heads * HD, held_kv * HD, held_kv * HD, held_heads)
    resid_norm_grad, _ = attn_norm_pull(normed_grad)
    input_grad = hidden_grad + resid_norm_grad
    pieces = []
    for low, length in zip((0, lengths[0], sum(lengths[:2]), sum(lengths[:3])), lengths):
        piece = small_sums[4:, low : low + length].reshape(2, 2, held_kv, -1)
        pieces.append(jnp.transpose(piece, (1, 2, 0, 3)).reshape(-1))
    query_bias_grad, key_bias_grad, value_bias_grad, sink_grad = pieces
    return (
        output[None],
        input_grad[None],
        small_sums[0],
        query_owned.T,
        query_bias_grad,
        key_owned.T,
        key_bias_grad,
        value_owned.T,
        value_bias_grad,
        output_owned,
        small_sums[2],
        sink_grad,
        small_sums[1],
        gate_weight_grad.T[None],
        gate_bias_grad,
        up_weight_grad.T[None],
        up_bias_grad,
        down_weight_grad[None],
        down_bias_grad,
    )


def solution(mesh):
    placed = (
        P(("exp", "dp"), "seq", None),
        P(("exp", "dp"), None),
        P(("exp", "dp"), "seq", None),
        P(("exp", "dp"), "seq", None),
        P(),
        P(None, ("seq", "exp", "dp")),
        P(),
        P(None, ("seq", "exp", "dp")),
        P(),
        P(None, ("seq", "exp", "dp")),
        P(),
        P(("seq", "exp", "dp"), None),
        P(),
        P(),
        P(),
        P("exp", None, ("seq", "dp")),
        P("exp", ("seq", "dp")),
        P("exp", None, ("seq", "dp")),
        P("exp", ("seq", "dp")),
        P("exp", ("seq", "dp"), None),
        P("exp", None),
        P(("exp", "dp"), "seq", None),
    )
    shape = mesh.shape
    small = shape["seq"] == 2 and shape["dp"] == 2 and shape["exp"] == 8
    return jax.shard_map(
        close_by if small else local,
        mesh=mesh,
        in_specs=placed,
        out_specs=(
            P(("exp", "dp"), "seq", None),
            P(("exp", "dp"), "seq", None),
            P(),
            P(None, ("seq", "exp", "dp")),
            P(),
            P(None, ("seq", "exp", "dp")),
            P(),
            P(None, ("seq", "exp", "dp")),
            P(),
            P(("seq", "exp", "dp"), None),
            P(),
            P(),
            P(),
            P("exp", None, ("seq", "dp")),
            P("exp", ("seq", "dp")),
            P("exp", None, ("seq", "dp")),
            P("exp", ("seq", "dp")),
            P("exp", ("seq", "dp"), None),
            P("exp", None),
        ),
        check_vma=False,
    )
```
